32 devices in a mesh: ctx: 4 (over y, core), fsdp: 8 (over z, x).
Axes of the slice: x: 2, y: 2, z: 4, core: 2. Of those that a mesh axis runs over, the one named last changes fastest.
Arguments:
- inputs: bfloat16 [8, 512, 1024], P('fsdp', 'ctx'), may hold values from -6 to 6
- cotangent: bfloat16 [8, 512, 1024], P('fsdp', 'ctx'), may hold values from -6 to 6
- w_query: bfloat16 [1024, 1024], P('fsdp'), may hold values from -0.078125 to 0.078125
- w_key: bfloat16 [1024, 1024], P('fsdp'), may hold values from -0.078125 to 0.078125
- w_value: bfloat16 [1024, 1024], P('fsdp'), may hold values from -0.1875 to 0.1875
- w_out: bfloat16 [1024, 1024], P('fsdp'), may hold values from -1.5 to 1.5
- w_in: bfloat16 [1024, 4096], P('fsdp'), may hold values from -0.1875 to 0.1875
- w_down: bfloat16 [4096, 1024], P('fsdp'), may hold values from -0.125 to 0.125
- gain_attn: bfloat16 [1024], P('fsdp'), may hold values from 0.25 to 1.75
- gain_mlp: bfloat16 [1024], P('fsdp'), may hold values from 0.25 to 1.75
- rel_bias: bfloat16 [512], P('fsdp'), may hold values from -4 to 4
- buckets: int32 [1023], replicated, may hold values from 0 to 31, as said below
Outputs:
- output: bfloat16 [8, 512, 1024], P('fsdp', 'ctx')
- grad_inputs: bfloat16 [8, 512, 1024], P('fsdp', 'ctx')
- grad_w_query: float32 [1024, 1024], P('fsdp')
- grad_w_key: float32 [1024, 1024], P('fsdp')
- grad_w_value: float32 [1024, 1024], P('fsdp')
- grad_w_out: float32 [1024, 1024], P('fsdp')
- grad_w_in: float32 [1024, 4096], P('fsdp')
- grad_w_down: float32 [4096, 1024], P('fsdp')
- grad_gain_attn: float32 [1024], P('fsdp')
- grad_gain_mlp: float32 [1024], P('fsdp')
- grad_rel_bias: float32 [512], P('fsdp')
The draws below stay inside these ranges and needn't reach their ends.
Inputs may be any that keep to these rules, and one draw needn't show every extreme that they name: `buckets`: entry 511 + k - q is the bucket of key position k for query position q: 0 where k = q; below 16 and not falling as q - k grows where k < q; 16 or more and not falling as k - q grows where k > q; each side reaches its top bucket.
All inputs are finite; a program needn't handle non-finite values.
Results may differ from the reference program's by a relative error of at most 0.019.
Values may be sent and summed in bfloat16 or wider, within the bound.
A program may use at most 192 MiB of HBM per device.

```python
import jax
import jax.numpy as jnp
from jax import lax

D = 1024
HEADS = 16
HEAD = 64
FF = 4096
BUCKETS = 32
LENGTH = 512
SEQS = 8


def bucket_side(key):
    half = BUCKETS // 2
    widest = max(2, (LENGTH - 1) // (half - 1))
    widths = jax.random.randint(key, (half - 1,), 1, widest + 1, dtype=jnp.int32)
    bounds = jnp.cumsum(widths)
    distance = jnp.arange(LENGTH, dtype=jnp.int32)
    return jnp.sum((distance[:, None] >= bounds[None, :]).astype(jnp.int32), axis=1)


def draw_buckets(key, part):
    key = jax.random.fold_in(key, 5)
    before = bucket_side(jax.random.fold_in(key, 11))
    after = bucket_side(jax.random.fold_in(key, 23)) + BUCKETS // 2
    return jnp.concatenate([before[::-1], after[1:]]).astype(jnp.int32)


def raised(values, own_key, source, target, shards_of, factor):
    owner, partner = [(jnp.arange(values.shape[dim]) // (values.shape[dim] // shards_of)).reshape([-1 if axis == dim else 1 for axis in range(values.ndim)]) for dim in (source, target)]
    chosen = jax.random.permutation(own_key, shards_of)[partner]
    strong = (owner == chosen) | (owner == (partner + shards_of // 2) % shards_of)
    return jnp.where(strong, factor * values, values)


def shard_levels(rng, extent, shards, least, top_value):
    level, own = 1.0, jax.random.fold_in(rng, 6)
    for dim, parts in shards:
        heights = jnp.exp(jax.random.uniform(jax.random.fold_in(own, dim), (parts,), jnp.float32, least / len(shards), top_value / len(shards)))
        level = level * jnp.repeat(heights, extent[dim] // parts).reshape([-1 if axis == dim else 1 for axis in range(len(extent))])
    return level


def centred(stream_key, dims, deviation, limit, cuts=(), kind=jnp.bfloat16):
    drawn = deviation * jax.random.normal(stream_key, dims, jnp.float32)
    if cuts:
        drawn = drawn * shard_levels(stream_key, dims, cuts, -0.22, 0.18)
    return jnp.clip(drawn, -limit, limit).astype(kind)


def bell_draw_with(rng, shape, deviation, reach, cuts, heavy, held_as=jnp.bfloat16):
    values = deviation * jax.random.normal(rng, shape, jnp.float32)
    if cuts:
        values = values * shard_levels(rng, shape, cuts, -0.22, 0.18)
    return jnp.clip(raised(values, jax.random.fold_in(rng, 3), *heavy), -reach, reach).astype(held_as)


def setup_inputs(seed: int = 0) -> dict:
    streams_of = jax.random.split(jax.random.key(seed), 13)
    return {
        "inputs": bell_draw_with(streams_of[0], (SEQS, LENGTH, D), 1.0, 6.0, ((0, 8), (1, 4)), (0, 2, 8, 2.0)),
        "cotangent": centred(streams_of[1], (SEQS, LENGTH, D), 1.0, 6.0, ((0, 8), (1, 4))),
        "w_query": centred(streams_of[2], (D, D), (5 * D) ** -0.5, 0.078125, ((0, 8),)),
        "w_key": centred(streams_of[3], (D, D), (5 * D) ** -0.5, 0.078125, ((0, 8),)),
        "w_value": centred(streams_of[4], (D, D), D ** -0.5, 0.1875, ((0, 8),)),
        "w_out": centred(streams_of[5], (D, D), (D // 64) ** -0.5, 1.5, ((0, 8),)),
        "w_in": centred(streams_of[6], (D, FF), D ** -0.5, 0.1875, ((0, 8),)),
        "w_down": centred(streams_of[7], (FF, D), (FF // 2) ** -0.5, 0.125, ((0, 8),)),
        "gain_attn": jnp.clip(1.0 + 0.15 * jax.random.normal(streams_of[8], (D,), jnp.float32), 0.25, 1.75).astype(jnp.bfloat16),
        "gain_mlp": jnp.clip(1.0 + 0.15 * jax.random.normal(streams_of[9], (D,), jnp.float32), 0.25, 1.75).astype(jnp.bfloat16),
        "rel_bias": centred(streams_of[10], (BUCKETS * HEADS,), 1.0, 4.0, ((0, 8),)),
        "buckets": draw_buckets(jax.random.fold_in(streams_of[12], 71), 0),
    }


EPS = 1e-06

@jax.custom_vjp
def low(v):
    return lax.optimization_barrier(v.astype(jnp.bfloat16)).astype(jnp.float32)

@jax.custom_vjp
def low_back(v):
    return v

def low_keep(v):
    return (low(v), None)

def low_pass(kept, grad):
    return (grad,)

def back_keep(v):
    return (v, None)

def back_low(kept, grad):
    return (low(grad),)
low.defvjp(low_keep, low_pass)
low_back.defvjp(back_keep, back_low)

def norm_rows(values, gain):
    return values * lax.rsqrt(lax.optimization_barrier(jnp.mean(values * values, axis=-1, keepdims=True)) + EPS) * gain

def smooth_gelu(values):
    return 0.5 * values * (1.0 + jax.scipy.special.erf(values * 0.7071067811865476))

def make_bias(flat_table, buckets, first_query, query_count):
    seq_length = (buckets.shape[0] + 1) // 2
    bias_table = flat_table.reshape(BUCKETS, HEADS)
    one_hot = (buckets[:, None] == jnp.arange(BUCKETS, dtype=jnp.int32)[None, :]).astype(flat_table.dtype)
    per_offset = jnp.dot(one_hot, bias_table, precision=lax.Precision.HIGHEST)
    key_place = jnp.arange(seq_length, dtype=jnp.int32)
    query_place = first_query + jnp.arange(query_count, dtype=jnp.int32)
    offsets = key_place[None, :] - query_place[:, None] + (seq_length - 1)
    return jnp.take(per_offset.T, offsets, axis=1)

def wide_dot(left, right):
    return jnp.dot(left, right, precision=lax.Precision.HIGHEST)

def layer(params, inputs_seq, buckets):
    w_query, w_key, w_value, w_out, w_in, w_down, gain_attn, gain_mlp, rel_bias = params
    seq_length = inputs_seq.shape[0]
    normed_one = low(norm_rows(inputs_seq, gain_attn))
    query = low(low_back(wide_dot(normed_one, w_query))).reshape(seq_length, HEADS, HEAD)
    key_rows = low(low_back(wide_dot(normed_one, w_key))).reshape(seq_length, HEADS, HEAD)
    value_rows = low(low_back(wide_dot(normed_one, w_value))).reshape(seq_length, HEADS, HEAD)
    bias_values = make_bias(rel_bias, buckets, jnp.int32(0), seq_length)
    scores = low_back(jnp.einsum('qhd,khd->hqk', query, key_rows, precision=lax.Precision.HIGHEST) + bias_values)
    top_score = lax.optimization_barrier(jnp.max(scores, axis=-1, keepdims=True))
    weights_exp = jnp.exp(scores - top_score)
    probs = low(weights_exp / lax.optimization_barrier(jnp.sum(weights_exp, axis=-1, keepdims=True)))
    mixed = jnp.einsum('hqk,khd->qhd', probs, value_rows, precision=lax.Precision.HIGHEST)
    attended = low(low_back(mixed.reshape(seq_length, D)))
    hidden_res = inputs_seq + low_back(wide_dot(attended, w_out))
    normed_two = low(norm_rows(hidden_res, gain_mlp))
    pre_act = low_back(wide_dot(normed_two, w_in))
    activated = low(smooth_gelu(pre_act))
    return hidden_res + low_back(wide_dot(activated, w_down))

def reference(inputs, cotangent, w_query, w_key, w_value, w_out, w_in, w_down, gain_attn, gain_mlp, rel_bias, buckets):
    params = tuple((weight.astype(jnp.float32) for weight in (w_query, w_key, w_value, w_out, w_in, w_down, gain_attn, gain_mlp, rel_bias)))

    def one_sequence(carry, pair):
        inputs_seq, cot_seq = pair
        result, pull = jax.vjp(lambda weights, values: layer(weights, values, buckets), params, inputs_seq.astype(jnp.float32))
        grad_params, grad_values = pull(cot_seq.astype(jnp.float32))
        carry = tuple((total + part for total, part in zip(carry, grad_params)))
        return (carry, (result.astype(jnp.bfloat16), grad_values.astype(jnp.bfloat16)))
    zeros = tuple((jnp.zeros(weight.shape, jnp.float32) for weight in params))
    sums, (output, grad_inputs) = lax.scan(one_sequence, zeros, (inputs, cotangent))
    return (output, grad_inputs, sums[0], sums[1], sums[2], sums[3], sums[4], sums[5], sums[6], sums[7], sums[8])
```

```python
import jax
import jax.numpy as jnp
from jax import lax
from jax.experimental import pallas as pl
from jax.experimental.pallas import tpu as pltpu
from jax.sharding import PartitionSpec as P

HEADS = 16
HEAD = 64
BUCKETS = 32


EPS = 1e-06


def norm_rows(values, gain):
    return values * lax.rsqrt(jnp.mean(values * values, axis=-1, keepdims=True) + EPS) * gain


def smooth_gelu(values):
    return 0.5 * values * (1.0 + jax.scipy.special.erf(values * 0.7071067811865476))


def gelu_slope(values):
    return (
        0.5 * (1.0 + jax.scipy.special.erf(values * 0.7071067811865476))
        + values * jnp.exp(-0.5 * values * values) * 0.3989422804014327
    )


def bucket_offsets(buckets, first_query, query_count):
    seq_length = (buckets.shape[0] + 1) // 2
    key_place = jnp.arange(seq_length, dtype=jnp.int32)
    query_place = first_query + jnp.arange(query_count, dtype=jnp.int32)
    return key_place[None, :] - query_place[:, None] + (seq_length - 1)


def make_bias(flat_table, buckets, first_query, query_count):
    bias_table = flat_table.reshape(BUCKETS, HEADS)
    one_hot = (buckets[:, None] == jnp.arange(BUCKETS, dtype=jnp.int32)[None, :]).astype(
        flat_table.dtype
    )
    per_offset = jnp.dot(one_hot, bias_table, precision=lax.Precision.HIGHEST)
    offsets = bucket_offsets(buckets, first_query, query_count)
    return jnp.take(per_offset.T, offsets, axis=1)


def pair_table(buckets, first_query, query_count):
    offsets = bucket_offsets(buckets, first_query, query_count)
    pair_bucket = jnp.take(buckets, offsets.reshape(-1), axis=0)
    return (pair_bucket[:, None] == jnp.arange(BUCKETS, dtype=jnp.int32)[None, :]).astype(
        jnp.bfloat16
    )


def fetch_attention(w_query, w_key, w_value, w_out, gain_attn, rel_bias):
    return (
        lax.all_gather(w_query, "fsdp", axis=0, tiled=True),
        lax.all_gather(w_key, "fsdp", axis=0, tiled=True),
        lax.all_gather(w_value, "fsdp", axis=0, tiled=True),
        lax.all_gather(w_out, "fsdp", axis=0, tiled=True),
        lax.all_gather(gain_attn, "fsdp", axis=0, tiled=True),
        lax.all_gather(rel_bias, "fsdp", axis=0, tiled=True),
    )


def fetch_mlp(w_in, w_down, gain_mlp):
    return (
        lax.all_gather(w_in, "fsdp", axis=0, tiled=True),
        lax.all_gather(w_down, "fsdp", axis=0, tiled=True),
        lax.all_gather(gain_mlp, "fsdp", axis=0, tiled=True),
    )


def share_keys(key_rows, value_rows):
    return (
        lax.all_gather(key_rows, "ctx", axis=1, tiled=True),
        lax.all_gather(value_rows, "ctx", axis=1, tiled=True),
    )


def scores_of(query_part, key_part, bias_values):
    return (
        jnp.einsum("qhd,khd->hqk", query_part, key_part, preferred_element_type=jnp.float32)
        + bias_values
    )


def shards(
    inputs,
    cotangent,
    w_query,
    w_key,
    w_value,
    w_out,
    w_in,
    w_down,
    gain_attn,
    gain_mlp,
    rel_bias,
    buckets,
):
    seq_count, row_count, width = inputs.shape
    total_rows = seq_count * row_count
    first_query = lax.axis_index("ctx") * row_count
    query_w, key_w, value_w, out_w, attn_gain, bias_flat = fetch_attention(
        w_query, w_key, w_value, w_out, gain_attn, rel_bias
    )
    in_w, down_w, mlp_gain = fetch_mlp(w_in, w_down, gain_mlp)
    bias_values = make_bias(bias_flat.astype(jnp.float32), buckets, first_query, row_count)
    inputs_flat = inputs.astype(jnp.float32).reshape(total_rows, width)
    attn_scale = attn_gain.astype(jnp.float32)
    normed_one = norm_rows(inputs_flat, attn_scale).astype(jnp.bfloat16)
    query_rows = jnp.dot(normed_one, query_w, preferred_element_type=jnp.float32).astype(
        jnp.bfloat16
    )
    key_rows = (
        jnp.dot(normed_one, key_w, preferred_element_type=jnp.float32)
        .astype(jnp.bfloat16)
        .reshape(seq_count, row_count, width)
    )
    value_rows = (
        jnp.dot(normed_one, value_w, preferred_element_type=jnp.float32)
        .astype(jnp.bfloat16)
        .reshape(seq_count, row_count, width)
    )
    all_keys, all_values = share_keys(key_rows, value_rows)
    query_heads = query_rows.reshape(seq_count, row_count, HEADS, HEAD)
    seq_index = 0
    key_heads = all_keys[seq_index].reshape(-1, HEADS, HEAD)
    value_heads = all_values[seq_index].reshape(-1, HEADS, HEAD)
    scores = scores_of(query_heads[seq_index], key_heads, bias_values)
    top_score = jnp.max(scores, axis=-1, keepdims=True)
    weights_exp = jnp.exp(scores - top_score)
    totals = jnp.sum(weights_exp, axis=-1, keepdims=True)
    probs_low = (weights_exp / totals).astype(jnp.bfloat16)
    mixed = jnp.einsum("hqk,khd->qhd", probs_low, value_heads, preferred_element_type=jnp.float32)
    mixed_list = mixed.reshape(row_count, width)
    lse_list = [top_score + jnp.log(totals)]
    attended = mixed_list.astype(jnp.bfloat16)
    hidden_res = inputs_flat + jnp.dot(attended, out_w, preferred_element_type=jnp.float32)
    mlp_scale = mlp_gain.astype(jnp.float32)
    normed_two = norm_rows(hidden_res, mlp_scale).astype(jnp.bfloat16)
    pre_act = jnp.dot(normed_two, in_w, preferred_element_type=jnp.float32)
    activated = smooth_gelu(pre_act).astype(jnp.bfloat16)
    result = hidden_res + jnp.dot(activated, down_w, preferred_element_type=jnp.float32)
    in_w, down_w, mlp_gain = fetch_mlp(w_in, w_down, gain_mlp)
    query_w, key_w, value_w, out_w, attn_gain, bias_flat = fetch_attention(
        w_query, w_key, w_value, w_out, gain_attn, rel_bias
    )
    all_keys, all_values = share_keys(key_rows, value_rows)
    grad_rows = cotangent.reshape(total_rows, width)
    grad_down = jnp.einsum("nf,nd->fd", activated, grad_rows, preferred_element_type=jnp.float32)
    grad_act = jnp.einsum("nd,fd->nf", grad_rows, down_w, preferred_element_type=jnp.float32)
    grad_pre = (grad_act * gelu_slope(pre_act)).astype(jnp.bfloat16)
    grad_in = jnp.einsum("nd,nf->df", normed_two, grad_pre, preferred_element_type=jnp.float32)
    grad_normed_two = jnp.einsum("nf,df->nd", grad_pre, in_w, preferred_element_type=jnp.float32)
    back_hidden, grad_mlp_gain = jax.vjp(norm_rows, hidden_res, mlp_scale)[1](grad_normed_two)
    grad_hidden = grad_rows.astype(jnp.float32) + back_hidden
    grad_attn_low = grad_hidden.astype(jnp.bfloat16)
    grad_out = jnp.einsum("nd,ne->de", attended, grad_attn_low, preferred_element_type=jnp.float32)
    grad_attended = jnp.einsum(
        "ne,de->nd", grad_attn_low, out_w, preferred_element_type=jnp.float32
    ).astype(jnp.bfloat16)
    grad_heads = grad_attended.reshape(seq_count, row_count, HEADS, HEAD)
    pair_buckets = pair_table(buckets, first_query, row_count)
    seq_index = 0
    key_heads = all_keys[seq_index].reshape(-1, HEADS, HEAD)
    value_heads = all_values[seq_index].reshape(-1, HEADS, HEAD)
    scores = scores_of(query_heads[seq_index], key_heads, bias_values)
    probs = jnp.exp(scores - lse_list[seq_index])
    grad_probs = jnp.einsum(
        "qhd,khd->hqk", grad_heads[seq_index], value_heads, preferred_element_type=jnp.float32
    )
    row_inner = jnp.sum(probs * grad_probs, axis=-1, keepdims=True)
    grad_scores = (probs * (grad_probs - row_inner)).astype(jnp.bfloat16)
    bias_grad = jnp.dot(
        grad_scores.reshape(HEADS, -1), pair_buckets, preferred_element_type=jnp.float32
    )
    query_grads = jnp.einsum(
        "hqk,khd->qhd", grad_scores, key_heads, preferred_element_type=jnp.float32
    ).reshape(row_count, width)
    key_grads = [
        jnp.einsum(
            "hqk,qhd->khd", grad_scores, query_heads[seq_index], preferred_element_type=jnp.float32
        ).reshape(-1, width)
    ]
    value_grads = [
        jnp.einsum(
            "hqk,qhd->khd",
            probs.astype(jnp.bfloat16),
            grad_heads[seq_index],
            preferred_element_type=jnp.float32,
        ).reshape(-1, width)
    ]
    key_back, value_back = (
        lax.psum_scatter(
            jnp.stack(key_grads).astype(jnp.bfloat16), "ctx", scatter_dimension=1, tiled=True
        ).astype(jnp.float32),
        lax.psum_scatter(
            jnp.stack(value_grads).astype(jnp.bfloat16), "ctx", scatter_dimension=1, tiled=True
        ).astype(jnp.float32),
    )
    grad_query_rows = query_grads.astype(jnp.bfloat16)
    grad_key_rows = key_back.reshape(total_rows, width).astype(jnp.bfloat16)
    grad_value_rows = value_back.reshape(total_rows, width).astype(jnp.bfloat16)
    grad_query = jnp.einsum(
        "nd,ne->de", normed_one, grad_query_rows, preferred_element_type=jnp.float32
    )
    grad_key = jnp.einsum(
        "nd,ne->de", normed_one, grad_key_rows, preferred_element_type=jnp.float32
    )
    grad_value = jnp.einsum(
        "nd,ne->de", normed_one, grad_value_rows, preferred_element_type=jnp.float32
    )
    grad_normed_one = jnp.einsum(
        "ne,de->nd", grad_query_rows, query_w, preferred_element_type=jnp.float32
    )
    grad_normed_one = grad_normed_one + jnp.einsum(
        "ne,de->nd", grad_key_rows, key_w, preferred_element_type=jnp.float32
    )
    grad_normed_one = grad_normed_one + jnp.einsum(
        "ne,de->nd", grad_value_rows, value_w, preferred_element_type=jnp.float32
    )
    back_inputs, grad_attn_gain = jax.vjp(norm_rows, inputs_flat, attn_scale)[1](grad_normed_one)
    grad_inputs = (
        (grad_hidden + back_inputs).astype(jnp.bfloat16).reshape(seq_count, row_count, width)
    )
    grad_bias_flat = bias_grad.T.reshape(BUCKETS * HEADS)
    (
        part_query,
        part_key,
        part_value,
        part_out,
        part_in,
        part_down,
        part_attn_gain,
        part_mlp_gain,
        part_bias,
    ) = (
        lax.psum_scatter(grad_query, "fsdp", scatter_dimension=0, tiled=True),
        lax.psum_scatter(grad_key, "fsdp", scatter_dimension=0, tiled=True),
        lax.psum_scatter(grad_value, "fsdp", scatter_dimension=0, tiled=True),
        lax.psum_scatter(grad_out, "fsdp", scatter_dimension=0, tiled=True),
        lax.psum_scatter(grad_in, "fsdp", scatter_dimension=0, tiled=True),
        lax.psum_scatter(grad_down, "fsdp", scatter_dimension=0, tiled=True),
        lax.psum_scatter(grad_attn_gain, "fsdp", scatter_dimension=0, tiled=True),
        lax.psum_scatter(grad_mlp_gain, "fsdp", scatter_dimension=0, tiled=True),
        lax.psum_scatter(grad_bias_flat, "fsdp", scatter_dimension=0, tiled=True),
    )
    summed = (
        lax.psum(part_query.astype(jnp.bfloat16), "ctx").astype(jnp.float32),
        lax.psum(part_key.astype(jnp.bfloat16), "ctx").astype(jnp.float32),
        lax.psum(part_value.astype(jnp.bfloat16), "ctx").astype(jnp.float32),
        lax.psum(part_out.astype(jnp.bfloat16), "ctx").astype(jnp.float32),
        lax.psum(part_in.astype(jnp.bfloat16), "ctx").astype(jnp.float32),
        lax.psum(part_down.astype(jnp.bfloat16), "ctx").astype(jnp.float32),
        lax.psum(part_attn_gain.astype(jnp.bfloat16), "ctx").astype(jnp.float32),
        lax.psum(part_mlp_gain.astype(jnp.bfloat16), "ctx").astype(jnp.float32),
        lax.psum(part_bias.astype(jnp.bfloat16), "ctx").astype(jnp.float32),
    )
    output = result.astype(jnp.bfloat16).reshape(seq_count, row_count, width)
    return (
        output,
        grad_inputs,
        summed[0],
        summed[1],
        summed[2],
        summed[3],
        summed[4],
        summed[5],
        summed[6],
        summed[7],
        summed[8],
    )


MESH_ID = pl.DeviceIdType.MESH
BF = jnp.bfloat16
F32 = jnp.float32
WIDTH = 1024
TOKENS = 128
NT_DIMS = (((1,), (1,)), ((), ()))
TN_DIMS = (((0,), (0,)), ((), ()))


def dot_nn(left, right):
    return jnp.dot(left, right, preferred_element_type=F32)


def dot_nt(left, right):
    return lax.dot_general(left, right, NT_DIMS, preferred_element_type=F32)


def dot_tn(left, right):
    return lax.dot_general(left, right, TN_DIMS, preferred_element_type=F32)


def rows_at(start, count):
    return pl.ds(pl.multiple_of(start, count), count)


def remote(src, dst, send, recv, device):
    return pltpu.make_async_remote_copy(
        src_ref=src, dst_ref=dst, send_sem=send, recv_sem=recv, device_id=device, device_id_type=MESH_ID
    )


def fused_layer(
    x_in, cot_in, wq_in, wk_in, wv_in, wo_in, wi_in, wd_in, pack_in, bucket_in,
    out_ref, gin_ref, oqkv, oout, oin, odown, small_ref,
    XO, CO, GP, XB, COT, N1, NTB, GAL, WQKV, WOUT, WIN, WDOWN,
    QKV, PROB, BIAS, AT, ACT, GACT, GPRE, GATT, DQKV, DKACC, DVACC, BACC,
    SA, SG, SO, SN, RA, RG, RO, RN, HID, GH, NTS, GALS,
    DQ, DO, DI, DD, SIBQ, SIBO, SIBI, SIBD, ZQ, ZO, ZI, ZD, RZQ, RZO, RZI, RZD, FQ, FO, FI, FD,
    SMALL, RSMALL, PSMALL, RZSMALL,
    loc, gpx_s, gpx_r, gpz_s, gpz_r, xb_s, xb_r, co_s, co_r, nt_s, nt_r, ga_s, ga_r,
    a_s, a_r, g_s, g_r, o_s, o_r, n_s, n_r,
    wx_s, wx_r, wqz_s, wqz_r, wqb_s, wqb_r, wiz_s, wiz_r, wib_s, wib_r, wdz_s, wdz_r, wdb_s, wdb_r,
    woz_s, woz_r, wob_s, wob_r,
    sib_s, sib_r, zq_s, zq_r, zo_s, zo_r, zi_s, zi_r, zd_s, zd_r,
    fq_s, fq_r, fo_s, fo_r, fi_s, fi_r, fd_s, fd_r, sp_s, sp_r, sz_s, sz_r,
):
    c = lax.axis_index("ctx")
    f = lax.axis_index("fsdp")
    y, k = c // 2, lax.rem(c, 2)
    z, x = f // 2, lax.rem(f, 2)
    x1, y1, k1 = 1 - x, 1 - y, 1 - k
    f1 = 2 * z + x1
    q = 2 * x + y
    sib = (2 * y + k1, f)
    xdev = (c, f1)
    zs = [lax.rem(z + d, 4) for d in (1, 2, 3)]

    def zdev(target):
        return (c, 2 * target + x)

    plane = []
    for i in range(4):
        ci = lax.rem(c + i, 4)
        for j, xj in enumerate((x, x1)):
            if i or j:
                plane.append((ci, 2 * z + xj))

    barrier = pltpu.get_barrier_semaphore()
    for device in plane + [zdev(t) for t in zs]:
        pl.semaphore_signal(barrier, inc=1, device_id=device, device_id_type=MESH_ID)
    pl.semaphore_wait(barrier, 10)

    def recv(dst, sem):
        remote(dst, dst, sem, sem, sib).wait_recv()

    def sent(src, sem):
        remote(src, src, sem, sem, sib).wait_send()

    def gather_send(src, dst, send, got):
        mine = dst.at[rows_at(c * TOKENS, TOKENS)]

        @pl.when(k == x)
        def _():
            pltpu.make_async_copy(src, mine, got.at[c]).start()

        @pl.when(k != x)
        def _():
            remote(src, mine, send.at[0], got.at[c], sib).start()

        remote(src, mine, send.at[3], got.at[c], (2 * y1 + x, f1)).start()
        remote(src, mine, send.at[1], got.at[c], (2 * y + x, f1)).start()
        remote(src, mine, send.at[2], got.at[c], (2 * y1 + x, f)).start()

    def gather_sent(src, send):
        @pl.when(k != x)
        def _():
            sent(src, send.at[0])

        for i in (1, 2, 3):
            sent(src, send.at[i])

    def scatter_send(buf, dst, send, got, b):
        src = buf.at[rows_at(b * TOKENS, TOKENS)]
        here = (b == c) & (x == k)

        @pl.when(here)
        def _():
            pltpu.make_async_copy(src, dst.at[q], got.at[q]).start()

        @pl.when(jnp.logical_not(here))
        def _():
            remote(src, dst.at[q], send.at[b], got.at[q], (b, 2 * z + k)).start()

    def scatter_sent(buf, send):
        for b in range(4):

            @pl.when(jnp.logical_not((c == b) & (x == k)))
            def _():
                sent(buf.at[pl.ds(b * TOKENS, TOKENS)], send.at[b])

    def half(fb, kk):
        return rows_at(fb * 128 + kk * 64, 64)

    own_x = pltpu.make_async_copy(x_in.at[0], XO, loc.at[0])
    own_x.start()
    own_c = pltpu.make_async_copy(cot_in.at[0], CO, loc.at[1])
    own_c.start()
    own_pack = pltpu.make_async_copy(pack_in, GP.at[f], loc.at[2])
    own_pack.start()
    remote(pack_in, GP.at[f], gpx_s, gpx_r, xdev).start()
    proj = (wq_in, wk_in, wv_in)
    myrows = pl.ds(pl.multiple_of(128 * f, 128), 128)
    for w in range(3):
        for j in range(2):
            src = proj[w].at[:, pl.ds(pl.multiple_of(128 * (2 * (2 * y + j) + x), 128), 128)]
            pltpu.make_async_copy(src, WQKV.at[myrows, pl.ds(256 * w + 128 * j, 128)], loc.at[3]).start()
    for w in range(3):
        for j in range(2):
            src = proj[w].at[rows_at(64 * k, 64), pl.ds(pl.multiple_of(128 * (2 * (2 * y + j) + x1), 128), 128)]
            remote(src, WQKV.at[half(f, k), pl.ds(256 * w + 128 * j, 128)], wx_s.at[0], wx_r.at[0], xdev).start()
    gather_send(x_in.at[0], XB, xb_s, xb_r)
    pltpu.make_async_copy(WQKV.at[myrows], WQKV.at[myrows], loc.at[3]).wait()
    for t in zs:
        remote(WQKV.at[half(f, k)], WQKV.at[half(f, k)], wqz_s.at[0, t], wqz_r.at[f], zdev(t)).start()
    for j in range(4):
        src = wi_in.at[:, pl.ds(pl.multiple_of(512 * (2 * j + x) + 256 * y, 256), 256)]
        pltpu.make_async_copy(src, WIN.at[myrows, pl.ds(256 * j, 256)], loc.at[4]).start()
    pltpu.make_async_copy(
        wd_in.at[rows_at(256 * y, 256)], WDOWN.at[rows_at(256 * z, 256)], loc.at[5]
    ).start()

    @pl.when(z // 2 == y)
    def _():
        pltpu.make_async_copy(wo_in, WOUT.at[rows_at(128 * lax.rem(z, 2), 128)], loc.at[6]).start()

    own_pack.wait()
    recv(GP.at[f1], gpx_r)
    for t in zs:
        remote(GP.at[pl.ds(2 * z, 2)], GP.at[pl.ds(2 * z, 2)], gpz_s.at[t], gpz_r.at[z], zdev(t)).start()
    for t in zs:
        recv(GP.at[pl.ds(2 * t, 2)], gpz_r.at[t])

    def row_of(index):
        return jnp.concatenate([GP[g, index : index + 1, :] for g in range(8)], axis=1)

    lane = lax.broadcasted_iota(jnp.int32, (8, 128), 1)
    head_row = lax.broadcasted_iota(jnp.int32, (8, 128), 0)
    head_of = 8 * y + 4 * lax.div(head_row, 2) + 2 * x + lax.rem(head_row, 2)
    head_mask = (lax.rem(lane, 16) == head_of) & (head_row < 4)

    def bucket_hot(g):
        index = lax.broadcasted_iota(jnp.int32, (128, WIDTH), 0)
        wanted = jnp.where(index < 64, 4 * g + lax.div(index, 16), -1)
        return (bucket_in[0:1, :] == wanted)

    def add_bias(g, total):
        table = jnp.where(head_mask, jnp.broadcast_to(GP[g, 2:3, :], (8, 128)), 0.0).astype(BF)
        return total + dot_nn(table, bucket_hot(g).astype(BF))

    offsets = lax.fori_loop(0, 8, add_bias, jnp.zeros((8, WIDTH), F32))
    for h in range(4):
        spread = jnp.broadcast_to(offsets[h : h + 1, :], (128, WIDTH))
        BIAS[h] = pltpu.roll(spread, WIDTH - 127, 1, stride=1, stride_axis=0)
        BACC[h] = jnp.zeros((128, WIDTH), F32)

    recv(WQKV.at[half(f1, k)], wx_r.at[0])
    for t in zs:
        remote(WQKV.at[half(f1, k)], WQKV.at[half(f1, k)], wqz_s.at[1, t], wqz_r.at[f1], zdev(t)).start()
    remote(WQKV.at[half(f1, k)], WQKV.at[half(f1, k)], wqb_s.at[f1], wqb_r.at[f1], sib).start()

    gain_one = row_of(0)

    def norm_block(i, carry):
        b = lax.rem(2 * y + i, 4)
        recv(XB.at[rows_at(b * TOKENS, TOKENS)], xb_r.at[b])

        def chunk(r, inner):
            rows = rows_at(b * TOKENS + r * 32, 32)
            values = XB[rows, :].astype(F32)
            scale = lax.rsqrt(jnp.mean(values * values, axis=-1, keepdims=True) + EPS)
            N1[rows, :] = (values * scale * gain_one).astype(BF)
            return inner

        return lax.fori_loop(0, 4, chunk, carry)

    lax.fori_loop(0, 4, norm_block, 0)
    gather_send(cot_in.at[0], COT, co_s, co_r)
    for j in range(4):
        src = wi_in.at[rows_at(64 * k, 64), pl.ds(pl.multiple_of(512 * (2 * j + x1) + 256 * y, 256), 256)]
        remote(src, WIN.at[half(f, k), pl.ds(256 * j, 256)], wx_s.at[1], wx_r.at[1], xdev).start()

    for t in zs:
        for xx in (x, x1):
            piece = WQKV.at[half(2 * t + xx, k)]
            recv(piece, wqz_r.at[2 * t + xx])
            remote(piece, piece, wqb_s.at[2 * t + xx], wqb_r.at[2 * t + xx], sib).start()

    out_piece = WOUT.at[rows_at(128 * k, 128)]
    out_other = WOUT.at[rows_at(128 * k1, 128)]

    @pl.when(z // 2 == y)
    def _():
        pltpu.make_async_copy(wo_in, out_piece, loc.at[6]).wait()

    @pl.when(z == c)
    def _():
        for t in zs:
            remote(out_piece, out_piece, woz_s.at[t], woz_r, zdev(t)).start()

    pltpu.make_async_copy(WIN.at[myrows], WIN.at[myrows], loc.at[4]).wait()
    for t in zs:
        remote(WIN.at[half(f, k)], WIN.at[half(f, k)], wiz_s.at[0, t], wiz_r.at[f], zdev(t)).start()

    for t in zs:
        for xx in (x, x1):
            recv(WQKV.at[half(2 * t + xx, k1)], wqb_r.at[2 * t + xx])
    recv(WQKV.at[half(f1, k1)], wqb_r.at[f1])

    def project(n, carry):
        cols = rows_at(256 * n, 256)
        QKV[:, cols] = dot_nn(N1[...], WQKV[:, cols]).astype(BF)
        return carry

    lax.fori_loop(0, 3, project, 0)

    recv(WIN.at[half(f1, k)], wx_r.at[1])
    for t in zs:
        remote(WIN.at[half(f1, k)], WIN.at[half(f1, k)], wiz_s.at[1, t], wiz_r.at[f1], zdev(t)).start()
    remote(WIN.at[half(f1, k)], WIN.at[half(f1, k)], wib_s.at[f1], wib_r.at[f1], sib).start()

    @pl.when(z != c)
    def _():
        recv(out_piece, woz_r)
        remote(out_piece, out_piece, wob_s, wob_r, sib).start()

    @pl.when(z != 2 * y + k1)
    def _():
        recv(out_other, wob_r)

    low_lanes = lax.broadcasted_iota(jnp.int32, (TOKENS, 128), 1) < 64

    def pick(values, hh):
        keep = low_lanes if hh == 0 else jnp.logical_not(low_lanes)
        return jnp.where(keep, values, jnp.zeros_like(values))

    def attend(i, carry):
        b = lax.rem(2 * y1 + i, 4)
        rows = rows_at(b * TOKENS, TOKENS)
        window = rows_at(384 - 128 * b, 128)
        window = pl.ds(pl.multiple_of(384 - 128 * b, 128), 512)
        for j in range(2):
            outs = []
            for hh in range(2):
                h = 2 * j + hh
                query = pick(QKV[rows, 128 * j : 128 * j + 128], hh)
                scores = dot_nt(query, QKV[:, 256 + 128 * j : 384 + 128 * j]) + BIAS[h, :, window]
                weights = jnp.exp(scores - jnp.max(scores, axis=-1, keepdims=True))
                probs = weights * (1.0 / jnp.sum(weights, axis=-1, keepdims=True))
                PROB[h, rows, :] = probs
                outs.append(dot_nn(probs.astype(BF), QKV[:, 512 + 128 * j : 640 + 128 * j]))
            AT[rows, 128 * j : 128 * j + 128] = jnp.where(low_lanes, outs[0], outs[1]).astype(BF)
        SA[rows, :] = dot_nn(AT[rows, :], WOUT[...]).astype(BF)
        scatter_send(SA, RA, a_s, a_r, b)
        return carry

    lax.fori_loop(0, 4, attend, 0)

    down_half = rows_at(256 * z + 128 * k, 128)
    pltpu.make_async_copy(WDOWN.at[rows_at(256 * z, 256)], WDOWN.at[rows_at(256 * z, 256)], loc.at[5]).wait()
    for t in zs:
        remote(WDOWN.at[down_half], WDOWN.at[down_half], wdz_s.at[t], wdz_r.at[z], zdev(t)).start()

    own_x.wait()
    own_c.wait()
    gain_two = row_of(1)
    for s in range(4):
        recv(RA.at[s], a_r.at[s])

    def home_forward(r, carry):
        rows = rows_at(r * 32, 32)
        hidden = XO[rows, :].astype(F32)
        for s in range(4):
            hidden = hidden + RA[s, rows, :].astype(F32)
        HID[rows, :] = hidden
        scale = lax.rsqrt(jnp.mean(hidden * hidden, axis=-1, keepdims=True) + EPS)
        NTS[rows, :] = (hidden * scale * gain_two).astype(BF)
        return carry

    lax.fori_loop(0, 4, home_forward, 0)
    gather_send(NTS, NTB, nt_s, nt_r)

    for t in zs:
        for xx in (x, x1):
            piece = WIN.at[half(2 * t + xx, k)]
            recv(piece, wiz_r.at[2 * t + xx])
            remote(piece, piece, wib_s.at[2 * t + xx], wib_r.at[2 * t + xx], sib).start()
    for t in zs:
        piece = WDOWN.at[rows_at(256 * t + 128 * k, 128)]
        recv(piece, wdz_r.at[t])
        remote(piece, piece, wdb_s.at[t], wdb_r.at[t], sib).start()
    for t in zs:
        recv(WDOWN.at[rows_at(256 * t + 128 * k1, 128)], wdb_r.at[t])
        for xx in (x, x1):
            recv(WIN.at[half(2 * t + xx, k1)], wib_r.at[2 * t + xx])
    recv(WIN.at[half(f1, k1)], wib_r.at[f1])

    for b in range(4):
        recv(COT.at[pl.ds(b * TOKENS, TOKENS)], co_r.at[b])

    def back_act(n, carry):
        cols = rows_at(256 * n, 256)
        GACT[:, cols] = dot_nt(COT[...], WDOWN[cols, :])
        return carry

    lax.fori_loop(0, 4, back_act, 0)

    def feed(i, carry):
        yy = lax.rem(y + i, 2)
        rows = rows_at(256 * yy, 256)
        for b in (2 * yy, 2 * yy + 1):
            recv(NTB.at[rows_at(b * TOKENS, TOKENS)], nt_r.at[b])

        def hidden_units(n, inner):
            cols = rows_at(256 * n, 256)
            pre = dot_nn(NTB[rows, :], WIN[:, cols])
            cdf = 0.5 * (1.0 + lax.erf(pre * 0.7071067811865476))
            ACT[rows, cols] = (pre * cdf).astype(BF)
            slope = cdf + pre * jnp.exp(-0.5 * pre * pre) * 0.3989422804014327
            GPRE[rows, cols] = (GACT[rows, cols] * slope).astype(BF)
            return inner

        lax.fori_loop(0, 4, hidden_units, 0)

        def back_normed(n, inner):
            cols = rows_at(256 * n, 256)
            SG[rows, cols] = dot_nt(GPRE[rows, :], WIN[cols, :]).astype(BF)
            return inner

        lax.fori_loop(0, 4, back_normed, 0)
        scatter_send(SG, RG, g_s, g_r, 2 * yy)
        scatter_send(SG, RG, g_s, g_r, 2 * yy + 1)
        return carry

    lax.fori_loop(0, 2, feed, 0)

    def down_project(n, carry):
        cols = rows_at(256 * n, 256)
        SO[:, cols] = dot_nn(ACT[...], WDOWN[:, cols]).astype(BF)
        return carry

    lax.fori_loop(0, 4, down_project, 0)

    def grad_down(m, carry):
        tile = dot_tn(ACT[:, rows_at(256 * m, 256)], COT[...]).astype(BF)
        DD[0, m] = tile[0:128]
        DD[1, m] = tile[128:256]
        return carry

    lax.fori_loop(0, 4, grad_down, 0)
    remote(DD.at[k1], SIBD, sib_s.at[0], sib_r.at[0], sib).start()

    def grad_in(m, carry):
        tile = dot_tn(NTB[:, rows_at(256 * m, 256)], GPRE[...]).astype(BF)
        for part in range(2):
            DI[0, 2 * m + part] = tile[128 * part : 128 * part + 64]
            DI[1, 2 * m + part] = tile[128 * part + 64 : 128 * part + 128]
        return carry

    lax.fori_loop(0, 4, grad_in, 0)
    remote(DI.at[k1], SIBI, sib_s.at[1], sib_r.at[1], sib).start()
    recv(SIBD, sib_r.at[0])

    def join_down(m, carry):
        ZD[m] = (DD[k, m].astype(F32) + SIBD[m].astype(F32)).astype(BF)
        return carry

    lax.fori_loop(0, 4, join_down, 0)
    for t in zs:
        remote(ZD.at[t], RZD.at[z], zd_s.at[t], zd_r.at[z], zdev(t)).start()

    for s in range(4):
        recv(RG.at[s], g_r.at[s])

    def home_back(r, total):
        rows = rows_at(r * 32, 32)
        grad = RG[0, rows, :].astype(F32)
        for s in range(1, 4):
            grad = grad + RG[s, rows, :].astype(F32)
        hidden = HID[rows, :]
        scale = lax.rsqrt(jnp.mean(hidden * hidden, axis=-1, keepdims=True) + EPS)
        scaled = grad * gain_two
        inner = jnp.mean(scaled * hidden, axis=-1, keepdims=True)
        back = CO[rows, :].astype(F32) + scale * scaled - hidden * (scale * scale * scale * inner)
        GH[rows, :] = back
        GALS[rows, :] = back.astype(BF)
        return total + jnp.sum((grad * hidden * scale).reshape(4, 8, WIDTH), axis=0)

    mlp_gain_grad = lax.fori_loop(0, 4, home_back, jnp.zeros((8, WIDTH), F32))
    gather_send(GALS, GAL, ga_s, ga_r)
    for b in range(4):
        scatter_send(SO, RO, o_s, o_r, lax.rem(2 * y1 + b, 4))
    mlp_gain_grad = jnp.sum(mlp_gain_grad, axis=0, keepdims=True)
    for g in range(8):
        SMALL[g] = jnp.zeros((8, 128), F32)
        SMALL[g, 1:2, :] = mlp_gain_grad[:, 128 * g : 128 * g + 128]

    recv(SIBI, sib_r.at[1])

    def join_in(m, carry):
        ZI[m] = (DI[k, m].astype(F32) + SIBI[m].astype(F32)).astype(BF)
        return carry

    lax.fori_loop(0, 8, join_in, 0)
    for t in zs:
        remote(ZI.at[pl.ds(2 * t, 2)], RZI.at[z], zi_s.at[t], zi_r.at[z], zdev(t)).start()

    DKACC[...] = jnp.zeros_like(DKACC)
    DVACC[...] = jnp.zeros_like(DVACC)

    def attend_back(i, carry):
        b = lax.rem(2 * y + i, 4)
        rows = rows_at(b * TOKENS, TOKENS)
        window = pl.ds(pl.multiple_of(384 - 128 * b, 128), 512)
        recv(GAL.at[rows], ga_r.at[b])
        GATT[...] = dot_nt(GAL[rows, :], WOUT[...]).astype(BF)
        for j in range(2):
            pair = slice(128 * j, 128 * j + 128)
            keys = QKV[:, 256 + 128 * j : 384 + 128 * j]
            values = QKV[:, 512 + 128 * j : 640 + 128 * j]
            outs = []
            for hh in range(2):
                h = 2 * j + hh
                query = pick(QKV[rows, pair], hh)
                grad_att = pick(GATT[:, pair], hh)
                probs = PROB[h, rows, :]
                grad_probs = dot_nt(grad_att, values)
                inner = jnp.sum(probs * grad_probs, axis=-1, keepdims=True)
                grad_scores = (probs * (grad_probs - inner)).astype(BF)
                BACC[h, :, window] = BACC[h, :, window] + grad_scores.astype(F32)
                outs.append(dot_nn(grad_scores, keys))
                DKACC[:, pair] = DKACC[:, pair] + dot_tn(grad_scores, query)
                DVACC[:, pair] = DVACC[:, pair] + dot_tn(probs.astype(BF), grad_att)
            DQKV[rows, pair] = jnp.where(low_lanes, outs[0], outs[1]).astype(BF)
        return carry

    lax.fori_loop(0, 4, attend_back, 0)
    DQKV[:, 256:512] = DKACC[...].astype(BF)
    DQKV[:, 512:768] = DVACC[...].astype(BF)

    def back_project(i, carry):
        yy = lax.rem(y1 + i, 2)
        rows = rows_at(256 * yy, 256)
        SN[rows, :] = dot_nt(DQKV[rows, :], WQKV[...]).astype(BF)
        scatter_send(SN, RN, n_s, n_r, 2 * yy)
        scatter_send(SN, RN, n_s, n_r, 2 * yy + 1)
        return carry

    lax.fori_loop(0, 2, back_project, 0)

    def grad_proj(m, carry):
        tile = dot_tn(N1[:, rows_at(256 * m, 256)], DQKV[...]).astype(BF)
        for part in range(2):
            DQ[0, 2 * m + part] = tile[128 * part : 128 * part + 64]
            DQ[1, 2 * m + part] = tile[128 * part + 64 : 128 * part + 128]
        return carry

    lax.fori_loop(0, 4, grad_proj, 0)
    remote(DQ.at[k1], SIBQ, sib_s.at[2], sib_r.at[2], sib).start()

    def grad_out_rows(m, carry):
        DO[m] = dot_tn(AT[:, rows_at(128 * m, 128)], GAL[...]).astype(BF)
        return carry

    lax.fori_loop(0, 2, grad_out_rows, 0)
    remote(DO.at[k1], SIBO, sib_s.at[3], sib_r.at[3], sib).start()
    recv(SIBQ, sib_r.at[2])

    def join_proj(m, carry):
        ZQ[m] = (DQ[k, m].astype(F32) + SIBQ[m].astype(F32)).astype(BF)
        return carry

    lax.fori_loop(0, 8, join_proj, 0)
    for t in zs:
        remote(ZQ.at[pl.ds(2 * t, 2)], RZQ.at[z], zq_s.at[t], zq_r.at[z], zdev(t)).start()
    recv(SIBO, sib_r.at[3])
    ZO[...] = (DO[k].astype(F32) + SIBO[...].astype(F32)).astype(BF)

    @pl.when(z != c)
    def _():
        remote(ZO, RZO.at[z], zo_s, zo_r.at[z], zdev(c)).start()

    for t in zs:
        recv(RZD.at[t], zd_r.at[t])
    total = ZD[z].astype(F32)
    for t in zs:
        total = total + RZD[t].astype(F32)
    FD[...] = total.astype(BF)
    down_rows = odown.at[rows_at(128 * c, 128)]
    pltpu.make_async_copy(FD, down_rows, fd_r.at[c]).start()
    for i in range(1, 4):
        ci = lax.rem(c + i, 4)
        remote(FD, down_rows, fd_s.at[i], fd_r.at[c], (ci, f)).start()
    for t in zs:
        recv(RZI.at[t], zi_r.at[t])
    for xx in range(2):
        total = ZI[2 * z + xx].astype(F32)
        for t in zs:
            total = total + RZI[t, xx].astype(F32)
        for j in range(4):
            FI[xx, j] = total[:, 256 * j : 256 * j + 256].astype(BF)
    in_rows = oin.at[:, q, rows_at(64 * k, 64), :]
    pltpu.make_async_copy(FI.at[x], in_rows, fi_r.at[c, x]).start()
    for i in range(4):
        ci = lax.rem(c + i, 4)
        for j, xj in enumerate((x, x1)):
            if i or j:
                remote(FI.at[xj], in_rows, fi_s.at[i, j], fi_r.at[c, x], (ci, 2 * z + xj)).start()

    for s in range(4):
        recv(RO.at[s], o_r.at[s])

    def home_out(r, carry):
        rows = rows_at(r * 32, 32)
        result = HID[rows, :]
        for s in range(4):
            result = result + RO[s, rows, :].astype(F32)
        out_ref[0, rows, :] = result.astype(BF)
        return carry

    lax.fori_loop(0, 4, home_out, 0)
    for s in range(4):
        recv(RN.at[s], n_r.at[s])

    def home_inputs(r, total):
        rows = rows_at(r * 32, 32)
        grad = RN[0, rows, :].astype(F32)
        for s in range(1, 4):
            grad = grad + RN[s, rows, :].astype(F32)
        values = XO[rows, :].astype(F32)
        scale = lax.rsqrt(jnp.mean(values * values, axis=-1, keepdims=True) + EPS)
        scaled = grad * gain_one
        inner = jnp.mean(scaled * values, axis=-1, keepdims=True)
        back = GH[rows, :] + scale * scaled - values * (scale * scale * scale * inner)
        gin_ref[0, rows, :] = back.astype(BF)
        return total + jnp.sum((grad * values * scale).reshape(4, 8, WIDTH), axis=0)

    attn_gain_grad = lax.fori_loop(0, 4, home_inputs, jnp.zeros((8, WIDTH), F32))
    attn_gain_grad = jnp.sum(attn_gain_grad, axis=0, keepdims=True)

    head_sums = []
    for h in range(4):
        rest = BACC[h]
        count = 64
        while count >= 8:
            rest = pltpu.roll(rest[0:count, :], count, 1) + rest[count : 2 * count, :]
            count //= 2
        for bit in (1, 2, 4):
            shift_row = 7 - lax.broadcasted_iota(jnp.int32, (8, WIDTH), 0)
            rest = jnp.where(lax.rem(lax.div(shift_row, bit), 2) == 1, pltpu.roll(rest, bit, 1), rest)
        head_sums.append(jnp.sum(rest, axis=0, keepdims=True))
    head_sums = jnp.concatenate(head_sums + [jnp.zeros((4, WIDTH), F32)], axis=0)
    coarse = head_sums.astype(BF)
    split_sums = jnp.concatenate([coarse, (head_sums - coarse.astype(F32)).astype(BF)], axis=0)

    both_masks = jnp.concatenate([head_mask.astype(F32)] * 2, axis=0) > 0.5

    def bucket_sums(g, carry):
        sums = dot_nt(split_sums, bucket_hot(g).astype(BF))
        SMALL[g, 2:3, :] = jnp.sum(jnp.where(both_masks, sums, 0.0), axis=0, keepdims=True)
        return carry

    lax.fori_loop(0, 8, bucket_sums, 0)
    for g in range(8):
        SMALL[g, 0:1, :] = attn_gain_grad[:, 128 * g : 128 * g + 128]

    for i in range(4):
        ci = lax.rem(c + i, 4)
        for j, xj in enumerate((x, x1)):
            if i or j:
                remote(SMALL, RSMALL.at[2 * c + x], sp_s.at[i, j], sp_r.at[2 * c + x], (ci, 2 * z + xj)).start()

    for t in zs:
        recv(RZQ.at[t], zq_r.at[t])
    for xx in range(2):
        total = ZQ[2 * z + xx].astype(F32)
        for t in zs:
            total = total + RZQ[t, xx].astype(F32)
        FQ[xx] = total.astype(BF)
    proj_rows = oqkv.at[q, rows_at(64 * k, 64), :]
    pltpu.make_async_copy(FQ.at[x], proj_rows, fq_r.at[c, x]).start()
    for i in range(4):
        ci = lax.rem(c + i, 4)
        for j, xj in enumerate((x, x1)):
            if i or j:
                remote(FQ.at[xj], proj_rows, fq_s.at[i, j], fq_r.at[c, x], (ci, 2 * z + xj)).start()

    @pl.when(z == c)
    def _():
        for t in zs:
            recv(RZO.at[t], zo_r.at[t])
        total = ZO[...].astype(F32)
        for t in zs:
            total = total + RZO[t].astype(F32)
        FO[...] = total.astype(BF)
        pltpu.make_async_copy(FO, oout, fo_r).start()
        for i in range(1, 4):
            remote(FO, oout, fo_s.at[i], fo_r, (lax.rem(c + i, 4), f)).start()

    plane_sum = SMALL[...]
    for i in range(4):
        ci = lax.rem(c + i, 4)
        for j, xj in enumerate((x, x1)):
            if i or j:
                recv(RSMALL.at[2 * ci + xj], sp_r.at[2 * ci + xj])
                plane_sum = plane_sum + RSMALL[2 * ci + xj]
    PSMALL[...] = plane_sum
    for t in zs:
        remote(PSMALL.at[2 * t + x], RZSMALL.at[z], sz_s.at[t], sz_r.at[z], zdev(t)).start()
    total = PSMALL[f]
    for t in zs:
        recv(RZSMALL.at[t], sz_r.at[t])
        total = total + RZSMALL[t]
    small_ref[...] = total

    recv(oout, fo_r)
    for i in range(4):
        ci = lax.rem(c + i, 4)
        recv(odown.at[rows_at(128 * ci, 128)], fd_r.at[ci])
        for xj in (x, x1):
            qi = 2 * xj + ci // 2
            ki = lax.rem(ci, 2)
            recv(oin.at[:, qi, rows_at(64 * ki, 64), :], fi_r.at[ci, xj])
            recv(oqkv.at[qi, rows_at(64 * ki, 64), :], fq_r.at[ci, xj])

    sent(pack_in, gpx_s)
    gather_sent(x_in.at[0], xb_s)
    gather_sent(cot_in.at[0], co_s)
    gather_sent(NTS, nt_s)
    gather_sent(GALS, ga_s)
    scatter_sent(SA, a_s)
    scatter_sent(SG, g_s)
    scatter_sent(SO, o_s)
    scatter_sent(SN, n_s)
    sent(WQKV.at[half(f, k)], wx_s.at[0])
    sent(WIN.at[half(f, k)], wx_s.at[1])
    sent(WQKV.at[half(f1, k)], wqb_s.at[f1])
    sent(WIN.at[half(f1, k)], wib_s.at[f1])
    for t in zs:
        sent(GP.at[pl.ds(2 * z, 2)], gpz_s.at[t])
        for r, own in enumerate((f, f1)):
            sent(WQKV.at[half(own, k)], wqz_s.at[r, t])
            sent(WIN.at[half(own, k)], wiz_s.at[r, t])
        for xx in (x, x1):
            sent(WQKV.at[half(2 * t + xx, k)], wqb_s.at[2 * t + xx])
            sent(WIN.at[half(2 * t + xx, k)], wib_s.at[2 * t + xx])
        sent(WDOWN.at[down_half], wdz_s.at[t])
        sent(WDOWN.at[rows_at(256 * t + 128 * k, 128)], wdb_s.at[t])
        sent(ZD.at[t], zd_s.at[t])
        sent(ZI.at[pl.ds(2 * t, 2)], zi_s.at[t])
        sent(ZQ.at[pl.ds(2 * t, 2)], zq_s.at[t])
        sent(PSMALL.at[2 * t + x], sz_s.at[t])

    @pl.when(z == c)
    def _():
        for t in zs:
            sent(out_piece, woz_s.at[t])
        for i in range(1, 4):
            sent(FO, fo_s.at[i])

    @pl.when(z != c)
    def _():
        sent(out_piece, wob_s)
        sent(ZO, zo_s)

    sent(DD.at[k1], sib_s.at[0])
    sent(DI.at[k1], sib_s.at[1])
    sent(DQ.at[k1], sib_s.at[2])
    sent(DO.at[k1], sib_s.at[3])
    for i in range(1, 4):
        sent(FD, fd_s.at[i])
    for i in range(4):
        for j, xj in enumerate((x, x1)):
            if i or j:
                sent(SMALL, sp_s.at[i, j])
                sent(FI.at[xj], fi_s.at[i, j])
                sent(FQ.at[xj], fq_s.at[i, j])


def plane_shards(
    inputs, cotangent, w_query, w_key, w_value, w_out, w_in, w_down, gain_attn, gain_mlp, rel_bias, buckets
):
    pack = jnp.concatenate(
        [
            gain_attn.astype(F32)[None],
            gain_mlp.astype(F32)[None],
            jnp.pad(rel_bias.astype(F32), (0, 64))[None],
            jnp.zeros((5, 128), F32),
        ],
        axis=0,
    )
    bucket_row = jnp.pad(buckets, (0, 1))[None]
    vm = pltpu.VMEM
    dma = pltpu.SemaphoreType.DMA
    block = lambda kind: vm((TOKENS, WIDTH), kind)
    tokens = lambda width, kind: vm((512, width), kind)
    scratch = [
        block(BF), block(BF), vm((8, 8, 128), F32),
        tokens(1024, BF), tokens(1024, BF), tokens(1024, BF), tokens(1024, BF), tokens(1024, BF),
        vm((1024, 768), BF), vm((256, 1024), BF), vm((1024, 1024), BF), vm((1024, 1024), BF),
        tokens(768, BF), vm((4, 512, 512), F32), vm((4, 128, 1024), F32), tokens(256, BF),
        tokens(1024, BF), tokens(1024, F32), tokens(1024, BF),
        vm((128, 256), BF), tokens(768, BF), tokens(256, F32), tokens(256, F32), vm((4, 128, 1024), F32),
        tokens(1024, BF), tokens(1024, BF), tokens(1024, BF), tokens(1024, BF),
        vm((4, 128, 1024), BF), vm((4, 128, 1024), BF), vm((4, 128, 1024), BF), vm((4, 128, 1024), BF),
        block(F32), block(F32), block(BF), block(BF),
        vm((2, 8, 64, 768), BF), vm((2, 128, 1024), BF), vm((2, 8, 64, 1024), BF), vm((2, 4, 128, 1024), BF),
        vm((8, 64, 768), BF), vm((128, 1024), BF), vm((8, 64, 1024), BF), vm((4, 128, 1024), BF),
        vm((8, 64, 768), BF), vm((128, 1024), BF), vm((8, 64, 1024), BF), vm((4, 128, 1024), BF),
        vm((4, 2, 64, 768), BF), vm((4, 128, 1024), BF), vm((4, 2, 64, 1024), BF), vm((4, 128, 1024), BF),
        vm((2, 64, 768), BF), vm((128, 1024), BF), vm((2, 4, 64, 256), BF), vm((128, 1024), BF),
        vm((8, 8, 128), F32), vm((8, 8, 8, 128), F32), vm((8, 8, 128), F32), vm((4, 8, 128), F32),
        dma((7,)), dma, dma, dma((4,)), dma((4,)),
        dma((4,)), dma((4,)), dma((4,)), dma((4,)), dma((4,)), dma((4,)), dma((4,)), dma((4,)),
        dma((4,)), dma((4,)), dma((4,)), dma((4,)), dma((4,)), dma((4,)), dma((4,)), dma((4,)),
        dma((2,)), dma((2,)), dma((2, 4)), dma((8,)), dma((8,)), dma((8,)),
        dma((2, 4)), dma((8,)), dma((8,)), dma((8,)), dma((4,)), dma((4,)), dma((4,)), dma((4,)),
        dma((4,)), dma, dma, dma,
        dma((4,)), dma((4,)), dma((4,)), dma((4,)), dma, dma((4,)), dma((4,)), dma((4,)), dma((4,)), dma((4,)),
        dma((4, 2)), dma((4, 2)), dma((4,)), dma, dma((4, 2)), dma((4, 2)), dma((4,)), dma((4,)),
        dma((4, 2)), dma((8,)), dma((4,)), dma((4,)),
    ]
    anywhere = pl.BlockSpec(memory_space=pl.ANY)
    in_vmem = pl.BlockSpec(memory_space=pltpu.VMEM)
    shape = jax.ShapeDtypeStruct
    output, grad_inputs, proj, out, hidden, down, small = pl.pallas_call(
        fused_layer,
        out_shape=(
            shape((1, TOKENS, WIDTH), BF),
            shape((1, TOKENS, WIDTH), BF),
            shape((4, 128, 768), BF),
            shape((128, 1024), BF),
            shape((4, 4, 128, 256), BF),
            shape((512, 1024), BF),
            shape((8, 128), F32),
        ),
        in_specs=[anywhere] * 9 + [in_vmem],
        out_specs=(in_vmem, in_vmem, anywhere, anywhere, anywhere, anywhere, in_vmem),
        scratch_shapes=scratch,
        compiler_params=pltpu.CompilerParams(
            collective_id=0, has_side_effects=True, vmem_limit_bytes=63 << 20
        ),
        cost_estimate=pl.CostEstimate(flops=11 * 10**9, bytes_accessed=16 * 2**20, transcendentals=3 * 2**20),
    )(inputs, cotangent, w_query, w_key, w_value, w_out, w_in, w_down, pack, bucket_row)
    proj = proj.reshape(2, 2, 128, 3, 2, 128).transpose(3, 2, 1, 4, 0, 5).reshape(3, 128, 1024).astype(F32)
    hidden = hidden.transpose(2, 0, 1, 3).reshape(128, 4096).astype(F32)
    return (
        output, grad_inputs, proj[0], proj[1], proj[2], out.astype(F32), hidden, down.astype(F32),
        small[0], small[1], small[2, :64],
    )


def solution(mesh):
    placed = (
        P("fsdp", "ctx", None),
        P("fsdp", "ctx", None),
        P("fsdp", None),
        P("fsdp", None),
        P("fsdp", None),
        P("fsdp", None),
        P("fsdp", None),
        P("fsdp", None),
        P("fsdp"),
        P("fsdp"),
        P("fsdp"),
        P(),
    )
    by_planes = mesh.shape["ctx"] == 4 and mesh.shape["fsdp"] == 8
    return jax.shard_map(
        plane_shards if by_planes else shards,
        mesh=mesh,
        in_specs=placed,
        out_specs=(
            P("fsdp", "ctx", None),
            P("fsdp", "ctx", None),
            P("fsdp", None),
            P("fsdp", None),
            P("fsdp", None),
            P("fsdp", None),
            P("fsdp", None),
            P("fsdp", None),
            P("fsdp"),
            P("fsdp"),
            P("fsdp"),
        ),
        check_vma=False,
    )
```

```python
import jax
import jax.numpy as jnp
from jax import lax
from jax.experimental import pallas as pl
from jax.experimental.pallas import tpu as pltpu
from jax.sharding import PartitionSpec as P

HEADS = 16
HEAD = 64
BUCKETS = 32


EPS = 1e-06


def norm_rows(values, gain):
    return values * lax.rsqrt(jnp.mean(values * values, axis=-1, keepdims=True) + EPS) * gain


def smooth_gelu(values):
    return 0.5 * values * (1.0 + jax.scipy.special.erf(values * 0.7071067811865476))


def gelu_slope(values):
    return (
        0.5 * (1.0 + jax.scipy.special.erf(values * 0.7071067811865476))
        + values * jnp.exp(-0.5 * values * values) * 0.3989422804014327
    )


def bucket_offsets(buckets, first_query, query_count):
    seq_length = (buckets.shape[0] + 1) // 2
    key_place = jnp.arange(seq_length, dtype=jnp.int32)
    query_place = first_query + jnp.arange(query_count, dtype=jnp.int32)
    return key_place[None, :] - query_place[:, None] + (seq_length - 1)


def make_bias(flat_table, buckets, first_query, query_count):
    bias_table = flat_table.reshape(BUCKETS, HEADS)
    one_hot = (buckets[:, None] == jnp.arange(BUCKETS, dtype=jnp.int32)[None, :]).astype(
        flat_table.dtype
    )
    per_offset = jnp.dot(one_hot, bias_table, precision=lax.Precision.HIGHEST)
    offsets = bucket_offsets(buckets, first_query, query_count)
    return jnp.take(per_offset.T, offsets, axis=1)


def pair_table(buckets, first_query, query_count):
    offsets = bucket_offsets(buckets, first_query, query_count)
    pair_bucket = jnp.take(buckets, offsets.reshape(-1), axis=0)
    return (pair_bucket[:, None] == jnp.arange(BUCKETS, dtype=jnp.int32)[None, :]).astype(
        jnp.bfloat16
    )


def fetch_attention(w_query, w_key, w_value, w_out, gain_attn, rel_bias):
    return (
        lax.all_gather(w_query, "fsdp", axis=0, tiled=True),
        lax.all_gather(w_key, "fsdp", axis=0, tiled=True),
        lax.all_gather(w_value, "fsdp", axis=0, tiled=True),
        lax.all_gather(w_out, "fsdp", axis=0, tiled=True),
        lax.all_gather(gain_attn, "fsdp", axis=0, tiled=True),
        lax.all_gather(rel_bias, "fsdp", axis=0, tiled=True),
    )


def fetch_mlp(w_in, w_down, gain_mlp):
    return (
        lax.all_gather(w_in, "fsdp", axis=0, tiled=True),
        lax.all_gather(w_down, "fsdp", axis=0, tiled=True),
        lax.all_gather(gain_mlp, "fsdp", axis=0, tiled=True),
    )


def share_keys(key_rows, value_rows):
    return (
        lax.all_gather(key_rows, "ctx", axis=1, tiled=True),
        lax.all_gather(value_rows, "ctx", axis=1, tiled=True),
    )


def scores_of(query_part, key_part, bias_values):
    return (
        jnp.einsum("qhd,khd->hqk", query_part, key_part, preferred_element_type=jnp.float32)
        + bias_values
    )


def shards(
    inputs,
    cotangent,
    w_query,
    w_key,
    w_value,
    w_out,
    w_in,
    w_down,
    gain_attn,
    gain_mlp,
    rel_bias,
    buckets,
):
    seq_count, row_count, width = inputs.shape
    total_rows = seq_count * row_count
    first_query = lax.axis_index("ctx") * row_count
    query_w, key_w, value_w, out_w, attn_gain, bias_flat = fetch_attention(
        w_query, w_key, w_value, w_out, gain_attn, rel_bias
    )
    in_w, down_w, mlp_gain = fetch_mlp(w_in, w_down, gain_mlp)
    bias_values = make_bias(bias_flat.astype(jnp.float32), buckets, first_query, row_count)
    inputs_flat = inputs.astype(jnp.float32).reshape(total_rows, width)
    attn_scale = attn_gain.astype(jnp.float32)
    normed_one = norm_rows(inputs_flat, attn_scale).astype(jnp.bfloat16)
    query_rows = jnp.dot(normed_one, query_w, preferred_element_type=jnp.float32).astype(
        jnp.bfloat16
    )
    key_rows = (
        jnp.dot(normed_one, key_w, preferred_element_type=jnp.float32)
        .astype(jnp.bfloat16)
        .reshape(seq_count, row_count, width)
    )
    value_rows = (
        jnp.dot(normed_one, value_w, preferred_element_type=jnp.float32)
        .astype(jnp.bfloat16)
        .reshape(seq_count, row_count, width)
    )
    all_keys, all_values = share_keys(key_rows, value_rows)
    query_heads = query_rows.reshape(seq_count, row_count, HEADS, HEAD)
    seq_index = 0
    key_heads = all_keys[seq_index].reshape(-1, HEADS, HEAD)
    value_heads = all_values[seq_index].reshape(-1, HEADS, HEAD)
    scores = scores_of(query_heads[seq_index], key_heads, bias_values)
    top_score = jnp.max(scores, axis=-1, keepdims=True)
    weights_exp = jnp.exp(scores - top_score)
    totals = jnp.sum(weights_exp, axis=-1, keepdims=True)
    probs_low = (weights_exp / totals).astype(jnp.bfloat16)
    mixed = jnp.einsum("hqk,khd->qhd", probs_low, value_heads, preferred_element_type=jnp.float32)
    mixed_list = mixed.reshape(row_count, width)
    lse_list = [top_score + jnp.log(totals)]
    attended = mixed_list.astype(jnp.bfloat16)
    hidden_res = inputs_flat + jnp.dot(attended, out_w, preferred_element_type=jnp.float32)
    mlp_scale = mlp_gain.astype(jnp.float32)
    normed_two = norm_rows(hidden_res, mlp_scale).astype(jnp.bfloat16)
    pre_act = jnp.dot(normed_two, in_w, preferred_element_type=jnp.float32)
    activated = smooth_gelu(pre_act).astype(jnp.bfloat16)
    result = hidden_res + jnp.dot(activated, down_w, preferred_element_type=jnp.float32)
    in_w, down_w, mlp_gain = fetch_mlp(w_in, w_down, gain_mlp)
    query_w, key_w, value_w, out_w, attn_gain, bias_flat = fetch_attention(
        w_query, w_key, w_value, w_out, gain_attn, rel_bias
    )
    all_keys, all_values = share_keys(key_rows, value_rows)
    grad_rows = cotangent.reshape(total_rows, width)
    grad_down = jnp.einsum("nf,nd->fd", activated, grad_rows, preferred_element_type=jnp.float32)
    grad_act = jnp.einsum("nd,fd->nf", grad_rows, down_w, preferred_element_type=jnp.float32)
    grad_pre = (grad_act * gelu_slope(pre_act)).astype(jnp.bfloat16)
    grad_in = jnp.einsum("nd,nf->df", normed_two, grad_pre, preferred_element_type=jnp.float32)
    grad_normed_two = jnp.einsum("nf,df->nd", grad_pre, in_w, preferred_element_type=jnp.float32)
    back_hidden, grad_mlp_gain = jax.vjp(norm_rows, hidden_res, mlp_scale)[1](grad_normed_two)
    grad_hidden = grad_rows.astype(jnp.float32) + back_hidden
    grad_attn_low = grad_hidden.astype(jnp.bfloat16)
    grad_out = jnp.einsum("nd,ne->de", attended, grad_attn_low, preferred_element_type=jnp.float32)
    grad_attended = jnp.einsum(
        "ne,de->nd", grad_attn_low, out_w, preferred_element_type=jnp.float32
    ).astype(jnp.bfloat16)
    grad_heads = grad_attended.reshape(seq_count, row_count, HEADS, HEAD)
    pair_buckets = pair_table(buckets, first_query, row_count)
    seq_index = 0
    key_heads = all_keys[seq_index].reshape(-1, HEADS, HEAD)
    value_heads = all_values[seq_index].reshape(-1, HEADS, HEAD)
    scores = scores_of(query_heads[seq_index], key_heads, bias_values)
    probs = jnp.exp(scores - lse_list[seq_index])
    grad_probs = jnp.einsum(
        "qhd,khd->hqk", grad_heads[seq_index], value_heads, preferred_element_type=jnp.float32
    )
    row_inner = jnp.sum(probs * grad_probs, axis=-1, keepdims=True)
    grad_scores = (probs * (grad_probs - row_inner)).astype(jnp.bfloat16)
    bias_grad = jnp.dot(
        grad_scores.reshape(HEADS, -1), pair_buckets, preferred_element_type=jnp.float32
    )
    query_grads = jnp.einsum(
        "hqk,khd->qhd", grad_scores, key_heads, preferred_element_type=jnp.float32
    ).reshape(row_count, width)
    key_grads = [
        jnp.einsum(
            "hqk,qhd->khd", grad_scores, query_heads[seq_index], preferred_element_type=jnp.float32
        ).reshape(-1, width)
    ]
    value_grads = [
        jnp.einsum(
            "hqk,qhd->khd",
            probs.astype(jnp.bfloat16),
            grad_heads[seq_index],
            preferred_element_type=jnp.float32,
        ).reshape(-1, width)
    ]
    key_back, value_back = (
        lax.psum_scatter(
            jnp.stack(key_grads).astype(jnp.bfloat16), "ctx", scatter_dimension=1, tiled=True
        ).astype(jnp.float32),
        lax.psum_scatter(
            jnp.stack(value_grads).astype(jnp.bfloat16), "ctx", scatter_dimension=1, tiled=True
        ).astype(jnp.float32),
    )
    grad_query_rows = query_grads.astype(jnp.bfloat16)
    grad_key_rows = key_back.reshape(total_rows, width).astype(jnp.bfloat16)
    grad_value_rows = value_back.reshape(total_rows, width).astype(jnp.bfloat16)
    grad_query = jnp.einsum(
        "nd,ne->de", normed_one, grad_query_rows, preferred_element_type=jnp.float32
    )
    grad_key = jnp.einsum(
        "nd,ne->de", normed_one, grad_key_rows, preferred_element_type=jnp.float32
    )
    grad_value = jnp.einsum(
        "nd,ne->de", normed_one, grad_value_rows, preferred_element_type=jnp.float32
    )
    grad_normed_one = jnp.einsum(
        "ne,de->nd", grad_query_rows, query_w, preferred_element_type=jnp.float32
    )
    grad_normed_one = grad_normed_one + jnp.einsum(
        "ne,de->nd", grad_key_rows, key_w, preferred_element_type=jnp.float32
    )
    grad_normed_one = grad_normed_one + jnp.einsum(
        "ne,de->nd", grad_value_rows, value_w, preferred_element_type=jnp.float32
    )
    back_inputs, grad_attn_gain = jax.vjp(norm_rows, inputs_flat, attn_scale)[1](grad_normed_one)
    grad_inputs = (
        (grad_hidden + back_inputs).astype(jnp.bfloat16).reshape(seq_count, row_count, width)
    )
    grad_bias_flat = bias_grad.T.reshape(BUCKETS * HEADS)
    (
        part_query,
        part_key,
        part_value,
        part_out,
        part_in,
        part_down,
        part_attn_gain,
        part_mlp_gain,
        part_bias,
    ) = (
        lax.psum_scatter(grad_query, "fsdp", scatter_dimension=0, tiled=True),
        lax.psum_scatter(grad_key, "fsdp", scatter_dimension=0, tiled=True),
        lax.psum_scatter(grad_value, "fsdp", scatter_dimension=0, tiled=True),
        lax.psum_scatter(grad_out, "fsdp", scatter_dimension=0, tiled=True),
        lax.psum_scatter(grad_in, "fsdp", scatter_dimension=0, tiled=True),
        lax.psum_scatter(grad_down, "fsdp", scatter_dimension=0, tiled=True),
        lax.psum_scatter(grad_attn_gain, "fsdp", scatter_dimension=0, tiled=True),
        lax.psum_scatter(grad_mlp_gain, "fsdp", scatter_dimension=0, tiled=True),
        lax.psum_scatter(grad_bias_flat, "fsdp", scatter_dimension=0, tiled=True),
    )
    summed = (
        lax.psum(part_query.astype(jnp.bfloat16), "ctx").astype(jnp.float32),
        lax.psum(part_key.astype(jnp.bfloat16), "ctx").astype(jnp.float32),
        lax.psum(part_value.astype(jnp.bfloat16), "ctx").astype(jnp.float32),
        lax.psum(part_out.astype(jnp.bfloat16), "ctx").astype(jnp.float32),
        lax.psum(part_in.astype(jnp.bfloat16), "ctx").astype(jnp.float32),
        lax.psum(part_down.astype(jnp.bfloat16), "ctx").astype(jnp.float32),
        lax.psum(part_attn_gain.astype(jnp.bfloat16), "ctx").astype(jnp.float32),
        lax.psum(part_mlp_gain.astype(jnp.bfloat16), "ctx").astype(jnp.float32),
        lax.psum(part_bias.astype(jnp.bfloat16), "ctx").astype(jnp.float32),
    )
    output = result.astype(jnp.bfloat16).reshape(seq_count, row_count, width)
    return (
        output,
        grad_inputs,
        summed[0],
        summed[1],
        summed[2],
        summed[3],
        summed[4],
        summed[5],
        summed[6],
        summed[7],
        summed[8],
    )


MESH_ID = pl.DeviceIdType.MESH
BF = jnp.bfloat16
F32 = jnp.float32
WIDTH = 1024
TOKENS = 128
NT_DIMS = (((1,), (1,)), ((), ()))
TN_DIMS = (((0,), (0,)), ((), ()))


def dot_nn(left, right):
    return jnp.dot(left, right, preferred_element_type=F32)


def dot_nt(left, right):
    return lax.dot_general(left, right, NT_DIMS, preferred_element_type=F32)


def dot_tn(left, right):
    return lax.dot_general(left, right, TN_DIMS, preferred_element_type=F32)


def rows_at(start, count):
    return pl.ds(pl.multiple_of(start, count), count)


def remote(src, dst, send, recv, device):
    return pltpu.make_async_remote_copy(
        src_ref=src, dst_ref=dst, send_sem=send, recv_sem=recv, device_id=device, device_id_type=MESH_ID
    )


def fused_layer(
    x_in, cot_in, wq_in, wk_in, wv_in, wo_in, wi_in, wd_in, pack_in, bucket_in,
    out_ref, gin_ref, oqkv, oout, oin, odown, small_ref,
    XO, CO, GP, XB, COT, N1, NTB, GAL, WQKV, WOUT, WIN, WDOWN,
    QKV, PROB, PLOW, BIAS, AT, ACT, SLOPE, GPRE, GATT, DQKV, DS, BACC,
    SA, SG, SO, SN, RA, RG, RO, RN, HID, GH, NTS, GALS,
    DQ, DO, DI, DD, SIBQ, SIBO, SIBI, SIBD, ZQ, ZO, ZI, ZD, RZQ, RZO, REI, RED, RCI, RCD, FQ, FO, FI, FD,
    SMALL, RSMALL, PSMALL, RZSMALL,
    loc, gpx_s, gpx_r, gpz_s, gpz_r, xb_s, xb_r, co_s, co_r, nt_s, nt_r, ga_s, ga_r,
    a_s, a_r, g_s, g_r, o_s, o_r, n_s, n_r,
    wx_s, wx_r, wqz_s, wqf_s, wqz_r, wqb_s, wqb_r, wiz_s, wif_s, wiz_r, wib_s, wib_r,
    wdz_s, wdf_s, wdz_r, wdb_s, wdb_r, woz_s, woz_r, wob_s, wob_r,
    sib_s, sib_r, zq_s, zq_r, zv_s, zv_r, zo_s, zo_r, zi_s, zie_s, zi_r, zic_r, zd_s, zde_s, zd_r, zdc_r,
    fq_s, fqb_s, fq_r, fo_s, fo_r, fi_s, fib_s, fi_r, fd_s, fd_r, sp_s, sp_r, sz_s, sz_r,
):
    c = lax.axis_index("ctx")
    f = lax.axis_index("fsdp")
    y, k = c // 2, lax.rem(c, 2)
    z, x = f // 2, lax.rem(f, 2)
    x1, y1, k1 = 1 - x, 1 - y, 1 - k
    f1 = 2 * z + x1
    q = 2 * x + y
    sib = (2 * y + k1, f)
    xdev = (c, f1)
    zs = [lax.rem(z + d, 4) for d in (1, 2, 3)]
    near = z + 1 - 2 * lax.rem(z, 2)
    other = 2 - 2 * (z // 2)
    others = (other, other + 1)
    far = 2 - z // 2
    middle = (z == 1) | (z == 2)
    at_end = jnp.logical_not(middle)

    def zdev(target):
        return (c, 2 * target + x)

    plane = []
    for i in range(4):
        ci = lax.rem(c + i, 4)
        for j, xj in enumerate((x, x1)):
            if i or j:
                plane.append((ci, 2 * z + xj))

    barrier = pltpu.get_barrier_semaphore()
    for device in plane + [zdev(t) for t in zs]:
        pl.semaphore_signal(barrier, inc=1, device_id=device, device_id_type=MESH_ID)
    pl.semaphore_wait(barrier, 10)

    def recv(dst, sem):
        remote(dst, dst, sem, sem, sib).wait_recv()

    def sent(src, sem):
        remote(src, src, sem, sem, sib).wait_send()

    def block_half(buf, b, h):
        return buf.at[rows_at(b * TOKENS + 64 * h, 64)]

    def gather_send(src, dst, send, got):
        for h in range(2):
            half_src = src.at[pl.ds(64 * h, 64)]
            remote(half_src, block_half(dst, c, h), send.at[1, h], got.at[c, h], (2 * y + x, f1)).start()
        for h in (1, 0):
            half_src = src.at[pl.ds(64 * h, 64)]
            remote(half_src, block_half(dst, c, h), send.at[2, h], got.at[c, h], (2 * y1 + x, f)).start()
        for h in range(2):
            half_src = src.at[pl.ds(64 * h, 64)]

            @pl.when(k == x)
            def _():
                pltpu.make_async_copy(half_src, block_half(dst, c, h), got.at[c, h]).start()

            @pl.when(k != x)
            def _():
                remote(half_src, block_half(dst, c, h), send.at[0, h], got.at[c, h], sib).start()

    same = 1 - lax.rem(x + k, 2)
    pass_y = y + same * (1 - 2 * y)
    pass_to = (same * c + (1 - same) * (2 * y1 + k), same * f1 + (1 - same) * f)

    def gather_pass(dst, send, got):
        for i in range(2):
            piece = block_half(dst, 2 * pass_y + i, same)
            recv(piece, got.at[2 * pass_y + i, same])
            remote(piece, piece, send.at[3, i], got.at[2 * pass_y + i, same], pass_to).start()

    def gather_wait(dst, got, b):
        for h in range(2):

            @pl.when(jnp.logical_not((b // 2 == pass_y) & (same == h)))
            def _():
                recv(block_half(dst, b, h), got.at[b, h])

    def gather_sent(src, dst, send):
        for h in range(2):
            half_src = src.at[pl.ds(64 * h, 64)]
            sent(half_src, send.at[1, h])
            sent(half_src, send.at[2, h])
            sent(block_half(dst, 2 * pass_y + h, same), send.at[3, h])

            @pl.when(k != x)
            def _():
                sent(half_src, send.at[0, h])

    def scatter_send(buf, dst, send, got, b):
        src = buf.at[rows_at(b * TOKENS, TOKENS)]
        here = (b == c) & (x == k)

        @pl.when(here)
        def _():
            pltpu.make_async_copy(src, dst.at[q], got.at[q]).start()

        @pl.when(jnp.logical_not(here))
        def _():
            remote(src, dst.at[q], send.at[b], got.at[q], (b, 2 * z + k)).start()

    def scatter_sent(buf, send):
        for b in range(4):

            @pl.when(jnp.logical_not((c == b) & (x == k)))
            def _():
                sent(buf.at[pl.ds(b * TOKENS, TOKENS)], send.at[b])

    def half(fb, kk):
        return rows_at(fb * 128 + kk * 64, 64)

    def z_send(piece, send, got):
        remote(piece, piece, send.at[1], got, zdev(far)).start()
        remote(piece, piece, send.at[0], got, zdev(near)).start()

    def z_sent(piece, send):
        sent(piece, send.at[0])
        sent(piece, send.at[1])

    def take(piece, got, bsend, bgot):
        recv(piece, got)
        remote(piece, piece, bsend, bgot, sib).start()

    def pass_on(piece, send, got):
        remote(piece, piece, send, got, zdev(near)).start()

    def of_row(t, xx):
        return 2 * t + xx

    own_x = pltpu.make_async_copy(x_in.at[0], XO, loc.at[0])
    own_x.start()
    own_c = pltpu.make_async_copy(cot_in.at[0], CO, loc.at[1])
    own_c.start()
    own_pack = pltpu.make_async_copy(pack_in, GP.at[f], loc.at[2])
    own_pack.start()
    remote(pack_in, GP.at[f], gpx_s, gpx_r, xdev).start()
    proj = (wq_in, wk_in, wv_in)
    myrows = pl.ds(pl.multiple_of(128 * f, 128), 128)
    for w in range(3):
        for j in range(2):
            src = proj[w].at[:, pl.ds(pl.multiple_of(128 * (2 * (2 * y + j) + x), 128), 128)]
            pltpu.make_async_copy(src, WQKV.at[myrows, pl.ds(256 * w + 128 * j, 128)], loc.at[3]).start()
    for w in range(3):
        for j in range(2):
            src = proj[w].at[rows_at(64 * k, 64), pl.ds(pl.multiple_of(128 * (2 * (2 * y + j) + x1), 128), 128)]
            remote(src, WQKV.at[half(f, k), pl.ds(256 * w + 128 * j, 128)], wx_s.at[0], wx_r.at[0], xdev).start()
    gather_send(x_in.at[0], XB, xb_s, xb_r)
    for j in range(4):
        src = wi_in.at[rows_at(64 * k, 64), pl.ds(pl.multiple_of(512 * (2 * j + x1) + 256 * y, 256), 256)]
        remote(src, WIN.at[half(f, k), pl.ds(256 * j, 256)], wx_s.at[1], wx_r.at[1], xdev).start()
    out_piece = WOUT.at[rows_at(128 * k, 128)]
    out_other = WOUT.at[rows_at(128 * k1, 128)]

    pltpu.make_async_copy(WQKV.at[myrows], WQKV.at[myrows], loc.at[3]).wait()
    z_send(WQKV.at[half(f, k)], wqz_s.at[0], wqz_r.at[f])
    for j in range(4):
        src = wi_in.at[:, pl.ds(pl.multiple_of(512 * (2 * j + x) + 256 * y, 256), 256)]
        pltpu.make_async_copy(src, WIN.at[myrows, pl.ds(256 * j, 256)], loc.at[4]).start()
    pltpu.make_async_copy(
        wd_in.at[rows_at(256 * y, 256)], WDOWN.at[rows_at(256 * z, 256)], loc.at[5]
    ).start()

    @pl.when(z // 2 == y)
    def _():
        pltpu.make_async_copy(wo_in, WOUT.at[rows_at(128 * lax.rem(z, 2), 128)], loc.at[6]).start()

    own_pack.wait()
    recv(GP.at[f1], gpx_r)
    for t in zs:
        remote(GP.at[pl.ds(2 * z, 2)], GP.at[pl.ds(2 * z, 2)], gpz_s.at[t], gpz_r.at[z], zdev(t)).start()
    for t in zs:
        recv(GP.at[pl.ds(2 * t, 2)], gpz_r.at[t])

    def row_of(index):
        return jnp.concatenate([GP[g, index : index + 1, :] for g in range(8)], axis=1)

    lane = lax.broadcasted_iota(jnp.int32, (8, 128), 1)
    head_row = lax.broadcasted_iota(jnp.int32, (8, 128), 0)
    head_of = 8 * y + 4 * lax.div(head_row, 2) + 2 * x + lax.rem(head_row, 2)
    head_mask = (lax.rem(lane, 16) == head_of) & (head_row < 4)

    def bucket_hot(g):
        index = lax.broadcasted_iota(jnp.int32, (128, WIDTH), 0)
        wanted = jnp.where(index < 64, 4 * g + lax.div(index, 16), -1)
        return (bucket_in[0:1, :] == wanted)

    def add_bias(g, total):
        table = jnp.where(head_mask, jnp.broadcast_to(GP[g, 2:3, :], (8, 128)), 0.0).astype(BF)
        return total + dot_nn(table, bucket_hot(g).astype(BF))

    offsets = lax.fori_loop(0, 8, add_bias, jnp.zeros((8, WIDTH), F32))
    for h in range(4):
        spread = jnp.broadcast_to(offsets[h : h + 1, :], (128, WIDTH))
        BIAS[h] = pltpu.roll(spread, WIDTH - 127, 1, stride=1, stride_axis=0)
        BACC[h] = jnp.zeros((128, WIDTH), F32)

    recv(WQKV.at[half(f1, k)], wx_r.at[0])
    z_send(WQKV.at[half(f1, k)], wqz_s.at[1], wqz_r.at[f1])
    remote(WQKV.at[half(f1, k)], WQKV.at[half(f1, k)], wqb_s.at[f1], wqb_r.at[f1], sib).start()

    @pl.when(z == c)
    def _():
        remote(wo_in, out_piece, woz_s.at[1], woz_r, zdev(far)).start()
        remote(wo_in, out_piece, woz_s.at[0], woz_r, zdev(near)).start()

    gain_one = row_of(0)

    def norm_block(i, carry):
        b = lax.rem(2 * y + i, 4)
        gather_wait(XB, xb_r, b)

        def chunk(r, inner):
            rows = rows_at(b * TOKENS + r * 32, 32)
            values = XB[rows, :].astype(F32)
            scale = lax.rsqrt(jnp.mean(values * values, axis=-1, keepdims=True) + EPS)
            N1[rows, :] = (values * scale * gain_one).astype(BF)
            return inner

        return lax.fori_loop(0, 4, chunk, carry)

    gather_pass(XB, xb_s, xb_r)
    gather_send(cot_in.at[0], COT, co_s, co_r)
    lax.fori_loop(0, 4, norm_block, 0)

    for r, own in enumerate((f, f1)):
        z_sent(WQKV.at[half(own, k)], wqz_s.at[r])
    pltpu.make_async_copy(WIN.at[myrows], WIN.at[myrows], loc.at[4]).wait()
    z_send(WIN.at[half(f, k)], wiz_s.at[0], wiz_r.at[f])
    recv(WIN.at[half(f1, k)], wx_r.at[1])
    z_send(WIN.at[half(f1, k)], wiz_s.at[1], wiz_r.at[f1])
    remote(WIN.at[half(f1, k)], WIN.at[half(f1, k)], wib_s.at[f1], wib_r.at[f1], sib).start()
    for xx in (x, x1):
        g = of_row(near, xx)
        take(WQKV.at[half(g, k)], wqz_r.at[g], wqb_s.at[g], wqb_r.at[g])
    for i, xx in enumerate((x, x1)):
        for n in range(2):
            g = of_row(others[n], xx)
            piece = WQKV.at[half(g, k)]
            recv(piece, wqz_r.at[g])

            @pl.when(middle)
            def _():
                pass_on(piece, wqf_s.at[n, i], wqz_r.at[g])

            remote(piece, piece, wqb_s.at[g], wqb_r.at[g], sib).start()

    @pl.when(z != c)
    def _():
        recv(out_piece, woz_r)

        @pl.when(middle & (z // 2 != c // 2))
        def _():
            pass_on(out_piece, woz_s.at[0], woz_r)

        remote(out_piece, out_piece, wob_s, wob_r, sib).start()

    down_half = rows_at(256 * z + 128 * k, 128)
    pltpu.make_async_copy(WDOWN.at[rows_at(256 * z, 256)], WDOWN.at[rows_at(256 * z, 256)], loc.at[5]).wait()
    z_send(WDOWN.at[down_half], wdz_s, wdz_r.at[z])

    for t in zs:
        for xx in (x, x1):
            recv(WQKV.at[half(2 * t + xx, k1)], wqb_r.at[2 * t + xx])
    recv(WQKV.at[half(f1, k1)], wqb_r.at[f1])

    def project(n, carry):
        cols = rows_at(256 * n, 256)
        QKV[:, cols] = dot_nn(N1[...], WQKV[:, cols]).astype(BF)
        return carry

    lax.fori_loop(0, 3, project, 0)


    @pl.when(z // 2 == y)
    def _():
        pltpu.make_async_copy(wo_in, out_piece, loc.at[6]).wait()

    @pl.when(z != 2 * y + k1)
    def _():
        recv(out_other, wob_r)

    gather_pass(COT, co_s, co_r)

    low_lanes = lax.broadcasted_iota(jnp.int32, (TOKENS, 128), 1) < 64

    def pick(values, hh):
        keep = low_lanes if hh == 0 else jnp.logical_not(low_lanes)
        return jnp.where(keep, values, jnp.zeros_like(values))

    def attend(i, carry):
        b = lax.rem(2 * y1 + i, 4)
        rows = rows_at(b * TOKENS, TOKENS)
        window = rows_at(384 - 128 * b, 128)
        window = pl.ds(pl.multiple_of(384 - 128 * b, 128), 512)
        for j in range(2):
            outs = []
            for hh in range(2):
                h = 2 * j + hh
                query = pick(QKV[rows, 128 * j : 128 * j + 128], hh)
                scores = dot_nt(query, QKV[:, 256 + 128 * j : 384 + 128 * j]) + BIAS[h, :, window]
                weights = jnp.exp(scores - jnp.max(scores, axis=-1, keepdims=True))
                probs = weights * (1.0 / jnp.sum(weights, axis=-1, keepdims=True))
                PROB[h, rows, :] = probs
                low = probs.astype(BF)
                PLOW[h, rows, :] = low
                outs.append(dot_nn(low, QKV[:, 512 + 128 * j : 640 + 128 * j]))
            AT[rows, 128 * j : 128 * j + 128] = jnp.where(low_lanes, outs[0], outs[1]).astype(BF)
        SA[rows, :] = dot_nn(AT[rows, :], WOUT[...]).astype(BF)
        scatter_send(SA, RA, a_s, a_r, b)
        return carry

    lax.fori_loop(0, 4, attend, 0)

    for xx in (x, x1):
        g = of_row(near, xx)
        take(WIN.at[half(g, k)], wiz_r.at[g], wib_s.at[g], wib_r.at[g])

    @pl.when(middle)
    def _():
        for i, xx in enumerate((x, x1)):
            for n in range(2):
                g = of_row(others[n], xx)
                recv(WIN.at[half(g, k)], wiz_r.at[g])
                pass_on(WIN.at[half(g, k)], wif_s.at[n, i], wiz_r.at[g])
                remote(WIN.at[half(g, k)], WIN.at[half(g, k)], wib_s.at[g], wib_r.at[g], sib).start()

    own_x.wait()
    own_c.wait()
    gain_two = row_of(1)
    for s in range(4):
        recv(RA.at[s], a_r.at[s])

    def home_forward(r, carry):
        rows = rows_at(r * 32, 32)
        hidden = XO[rows, :].astype(F32)
        for s in range(4):
            hidden = hidden + RA[s, rows, :].astype(F32)
        HID[rows, :] = hidden
        scale = lax.rsqrt(jnp.mean(hidden * hidden, axis=-1, keepdims=True) + EPS)
        NTS[rows, :] = (hidden * scale * gain_two).astype(BF)
        return carry

    lax.fori_loop(0, 4, home_forward, 0)
    gather_send(NTS, NTB, nt_s, nt_r)

    def down_piece(t, kk):
        return WDOWN.at[rows_at(256 * t + 128 * kk, 128)]

    take(down_piece(near, k), wdz_r.at[near], wdb_s.at[near], wdb_r.at[near])

    @pl.when(middle)
    def _():
        for n in range(2):
            t = others[n]
            recv(down_piece(t, k), wdz_r.at[t])
            pass_on(down_piece(t, k), wdf_s.at[n], wdz_r.at[t])
            remote(down_piece(t, k), down_piece(t, k), wdb_s.at[t], wdb_r.at[t], sib).start()

    @pl.when(at_end)
    def _():
        for xx in (x, x1):
            for t in others:
                g = of_row(t, xx)
                take(WIN.at[half(g, k)], wiz_r.at[g], wib_s.at[g], wib_r.at[g])

    recv(WIN.at[half(f1, k1)], wib_r.at[f1])
    for t in zs:
        for xx in (x, x1):
            recv(WIN.at[half(2 * t + xx, k1)], wib_r.at[2 * t + xx])

    gather_pass(NTB, nt_s, nt_r)

    def feed(i, carry):
        yy = lax.rem(y + i, 2)
        rows = rows_at(256 * yy, 256)
        for b in (2 * yy, 2 * yy + 1):
            gather_wait(NTB, nt_r, b)

        def hidden_units(n, inner):
            cols = rows_at(256 * n, 256)
            pre = dot_nn(NTB[rows, :], WIN[:, cols])
            cdf = 0.5 * (1.0 + lax.erf(pre * 0.7071067811865476))
            ACT[rows, cols] = (pre * cdf).astype(BF)
            SLOPE[rows, cols] = cdf + pre * jnp.exp(-0.5 * pre * pre) * 0.3989422804014327
            return inner

        return lax.fori_loop(0, 4, hidden_units, carry)

    lax.fori_loop(0, 2, feed, 0)

    for b in range(4):
        gather_wait(COT, co_r, b)

    def grad_down(m, carry):
        tile = dot_tn(ACT[:, rows_at(256 * m, 256)], COT[...]).astype(BF)
        DD[0, m] = tile[0:128]
        DD[1, m] = tile[128:256]
        return carry

    lax.fori_loop(0, 4, grad_down, 0)
    remote(DD.at[k1], SIBD, sib_s.at[0], sib_r.at[0], sib).start()

    @pl.when(at_end)
    def _():
        for t in others:
            take(down_piece(t, k), wdz_r.at[t], wdb_s.at[t], wdb_r.at[t])

    for t in zs:
        recv(down_piece(t, k1), wdb_r.at[t])

    def z_reduce_send(terms, got, send, esend, recv_sem):
        @pl.when(at_end)
        def _():
            for n in range(2):
                t = others[n]
                remote(terms(t), got(t), esend.at[n], recv_sem.at[t], zdev(near)).start()

        remote(terms(near), got(near), send, recv_sem.at[near], zdev(near)).start()

    recv(SIBD, sib_r.at[0])

    def join_down(m, carry):
        ZD[m] = (DD[k, m].astype(F32) + SIBD[m].astype(F32)).astype(BF)
        return carry

    lax.fori_loop(0, 4, join_down, 0)
    z_reduce_send(lambda t: ZD.at[t], lambda t: RED.at[t], zd_s, zde_s, zd_r)

    def back_feed(i, carry):
        yy = lax.rem(y1 + i, 2)
        rows = rows_at(256 * yy, 256)

        def back_act(n, inner):
            cols = rows_at(256 * n, 256)
            GPRE[rows, cols] = (dot_nt(COT[rows, :], WDOWN[cols, :]) * SLOPE[rows, cols]).astype(BF)
            return inner

        lax.fori_loop(0, 4, back_act, 0)

        def back_normed(n, inner):
            cols = rows_at(256 * n, 256)
            SG[rows, cols] = dot_nt(GPRE[rows, :], WIN[cols, :]).astype(BF)
            return inner

        lax.fori_loop(0, 4, back_normed, 0)
        scatter_send(SG, RG, g_s, g_r, 2 * yy)
        scatter_send(SG, RG, g_s, g_r, 2 * yy + 1)
        return carry

    lax.fori_loop(0, 2, back_feed, 0)

    def grad_in(m, carry):
        tile = dot_tn(NTB[:, rows_at(256 * m, 256)], GPRE[...]).astype(BF)
        for part in range(2):
            DI[0, 2 * m + part] = tile[128 * part : 128 * part + 64]
            DI[1, 2 * m + part] = tile[128 * part + 64 : 128 * part + 128]
        return carry

    lax.fori_loop(0, 4, grad_in, 0)
    remote(DI.at[k1], SIBI, sib_s.at[1], sib_r.at[1], sib).start()

    def down_project(n, carry):
        cols = rows_at(256 * n, 256)
        SO[:, cols] = dot_nn(ACT[...], WDOWN[:, cols]).astype(BF)
        return carry

    lax.fori_loop(0, 4, down_project, 0)

    recv(SIBI, sib_r.at[1])

    def join_in(m, carry):
        ZI[m] = (DI[k, m].astype(F32) + SIBI[m].astype(F32)).astype(BF)
        return carry

    lax.fori_loop(0, 8, join_in, 0)
    z_reduce_send(
        lambda t: ZI.at[pl.ds(2 * t, 2)], lambda t: REI.at[pl.ds(2 * t, 2)], zi_s, zie_s, zi_r
    )

    @pl.when(middle)
    def _():
        for n in range(2):
            t = others[n]
            recv(RED.at[t], zd_r.at[t])
            ZD[t] = (ZD[t].astype(F32) + RED[t].astype(F32)).astype(BF)
            remote(ZD.at[t], RCD, zde_s.at[n], zdc_r, zdev(t)).start()

    for s in range(4):
        recv(RG.at[s], g_r.at[s])

    def home_back(r, total):
        rows = rows_at(r * 32, 32)
        grad = RG[0, rows, :].astype(F32)
        for s in range(1, 4):
            grad = grad + RG[s, rows, :].astype(F32)
        hidden = HID[rows, :]
        scale = lax.rsqrt(jnp.mean(hidden * hidden, axis=-1, keepdims=True) + EPS)
        scaled = grad * gain_two
        inner = jnp.mean(scaled * hidden, axis=-1, keepdims=True)
        back = CO[rows, :].astype(F32) + scale * scaled - hidden * (scale * scale * scale * inner)
        GH[rows, :] = back
        GALS[rows, :] = back.astype(BF)
        return total + jnp.sum((grad * hidden * scale).reshape(4, 8, WIDTH), axis=0)

    mlp_gain_grad = lax.fori_loop(0, 4, home_back, jnp.zeros((8, WIDTH), F32))
    gather_send(GALS, GAL, ga_s, ga_r)
    mlp_gain_grad = jnp.sum(mlp_gain_grad, axis=0, keepdims=True)
    for g in range(8):
        SMALL[1, g : g + 1, :] = mlp_gain_grad[:, 128 * g : 128 * g + 128]

    gather_pass(GAL, ga_s, ga_r)

    def back_out(i, carry):
        b = lax.rem(2 * y + i, 4)
        rows = rows_at(b * TOKENS, TOKENS)
        gather_wait(GAL, ga_r, b)
        GATT[rows, :] = dot_nt(GAL[rows, :], WOUT[...]).astype(BF)
        return carry

    lax.fori_loop(0, 4, back_out, 0)
    for i in range(4):
        scatter_send(SO, RO, o_s, o_r, lax.rem(2 * y1 + i, 4))
    all_low = lax.broadcasted_iota(jnp.int32, (512, 128), 1) < 64

    def pick_all(values, hh):
        keep = all_low if hh == 0 else jnp.logical_not(all_low)
        return jnp.where(keep, values, jnp.zeros_like(values))

    def grad_values(j, carry):
        grad_att = GATT[:, rows_at(128 * j, 128)]
        first = dot_tn(PLOW[2 * j], pick_all(grad_att, 0))
        second = dot_tn(PLOW[2 * j + 1], pick_all(grad_att, 1))
        DQKV[:, pl.ds(pl.multiple_of(512 + 128 * j, 128), 128)] = jnp.where(all_low, first, second).astype(BF)
        return carry

    lax.fori_loop(0, 2, grad_values, 0)

    def grad_proj(first, width):
        def step(m, carry):
            tile = dot_tn(N1[:, rows_at(256 * m, 256)], DQKV[:, first : first + width]).astype(BF)
            for part in range(2):
                DQ[0, 2 * m + part, :, first : first + width] = tile[128 * part : 128 * part + 64]
                DQ[1, 2 * m + part, :, first : first + width] = tile[128 * part + 64 : 128 * part + 128]
            return carry

        lax.fori_loop(0, 4, step, 0)

    def join_proj(first, width):
        def step(m, carry):
            total = DQ[k, m, :, first : first + width].astype(F32) + SIBQ[m, :, first : first + width].astype(F32)
            ZQ[m, :, first : first + width] = total.astype(BF)
            return carry

        lax.fori_loop(0, 8, step, 0)

    value_cols, other_cols = pl.ds(512, 256), pl.ds(0, 512)
    grad_proj(512, 256)
    remote(DQ.at[k1, :, :, value_cols], SIBQ.at[:, :, value_cols], sib_s.at[2], sib_r.at[2], sib).start()

    def grad_out_rows(m, carry):
        DO[m] = dot_tn(AT[:, rows_at(128 * m, 128)], GAL[...]).astype(BF)
        return carry

    lax.fori_loop(0, 2, grad_out_rows, 0)
    remote(DO.at[k1], SIBO, sib_s.at[3], sib_r.at[3], sib).start()

    def z_scatter(cols, send, got):
        for t in zs:
            remote(
                ZQ.at[pl.ds(2 * t, 2), :, cols], RZQ.at[z, :, :, cols], send.at[t], got.at[z], zdev(t)
            ).start()

    recv(SIBQ.at[:, :, value_cols], sib_r.at[2])
    join_proj(512, 256)
    z_scatter(value_cols, zv_s, zv_r)

    recv(SIBO, sib_r.at[3])
    ZO[...] = (DO[k].astype(F32) + SIBO[...].astype(F32)).astype(BF)

    out_near = z // 2 == c // 2

    @pl.when((z != c) & out_near)
    def _():
        remote(ZO, RZO.at[0], zo_s, zo_r.at[0], zdev(c)).start()

    @pl.when(jnp.logical_not(out_near) & at_end)
    def _():
        remote(ZO, RZO.at[0], zo_s, zo_r.at[0], zdev(near)).start()

    @pl.when(middle)
    def _():
        for n in range(2):
            t = others[n]
            recv(REI.at[pl.ds(2 * t, 2)], zi_r.at[t])
            for xx in range(2):
                ZI[2 * t + xx] = (ZI[2 * t + xx].astype(F32) + REI[2 * t + xx].astype(F32)).astype(BF)
            remote(ZI.at[pl.ds(2 * t, 2)], RCI, zie_s.at[n], zic_r, zdev(t)).start()

    @pl.when(jnp.logical_not(out_near) & middle)
    def _():
        recv(RZO.at[0], zo_r.at[0])
        ZO[...] = (ZO[...].astype(F32) + RZO[0].astype(F32)).astype(BF)
        remote(ZO, RZO.at[1], zo_s, zo_r.at[1], zdev(c)).start()

    def attend_back(i, carry):
        rows = rows_at(i * TOKENS, TOKENS)
        window = pl.ds(pl.multiple_of(384 - 128 * i, 128), 512)
        for j in range(2):
            pair = slice(128 * j, 128 * j + 128)
            keys = QKV[:, 256 + 128 * j : 384 + 128 * j]
            values = QKV[:, 512 + 128 * j : 640 + 128 * j]
            outs = []
            for hh in range(2):
                h = 2 * j + hh
                grad_att = pick(GATT[rows, pair], hh)
                probs = PROB[h, rows, :]
                grad_probs = dot_nt(grad_att, values)
                inner = jnp.sum(probs * grad_probs, axis=-1, keepdims=True)
                grad_scores = (probs * (grad_probs - inner)).astype(BF)
                DS[h, rows, :] = grad_scores
                BACC[h, :, window] = BACC[h, :, window] + grad_scores.astype(F32)
                outs.append(dot_nn(grad_scores, keys))
            DQKV[rows, pair] = jnp.where(low_lanes, outs[0], outs[1]).astype(BF)
        return carry

    lax.fori_loop(0, 4, attend_back, 0)

    def grad_keys(j, carry):
        query = QKV[:, rows_at(128 * j, 128)]
        first = dot_tn(DS[2 * j], pick_all(query, 0))
        second = dot_tn(DS[2 * j + 1], pick_all(query, 1))
        DQKV[:, pl.ds(pl.multiple_of(256 + 128 * j, 128), 128)] = jnp.where(all_low, first, second).astype(BF)
        return carry

    lax.fori_loop(0, 2, grad_keys, 0)

    grad_proj(0, 512)
    remote(DQ.at[k1, :, :, other_cols], SIBQ.at[:, :, other_cols], sib_s.at[4], sib_r.at[4], sib).start()
    def back_project(i, carry):
        yy = lax.rem(y1 + i, 2)
        rows = rows_at(256 * yy, 256)
        SN[rows, :] = dot_nt(DQKV[rows, :], WQKV[...]).astype(BF)
        scatter_send(SN, RN, n_s, n_r, 2 * yy)
        scatter_send(SN, RN, n_s, n_r, 2 * yy + 1)
        return carry

    lax.fori_loop(0, 2, back_project, 0)

    recv(SIBQ.at[:, :, other_cols], sib_r.at[4])
    join_proj(0, 512)
    z_scatter(other_cols, zq_s, zq_r)

    head_sums = []
    for h in range(4):
        rest = BACC[h]
        count = 64
        while count >= 8:
            rest = pltpu.roll(rest[0:count, :], count, 1) + rest[count : 2 * count, :]
            count //= 2
        for bit in (1, 2, 4):
            shift_row = 7 - lax.broadcasted_iota(jnp.int32, (8, WIDTH), 0)
            rest = jnp.where(lax.rem(lax.div(shift_row, bit), 2) == 1, pltpu.roll(rest, bit, 1), rest)
        head_sums.append(jnp.sum(rest, axis=0, keepdims=True))
    head_sums = jnp.concatenate(head_sums + [jnp.zeros((4, WIDTH), F32)], axis=0)
    coarse = head_sums.astype(BF)
    split_sums = jnp.concatenate([coarse, (head_sums - coarse.astype(F32)).astype(BF)], axis=0)
    both_masks = jnp.concatenate([head_mask.astype(F32)] * 2, axis=0) > 0.5

    def bucket_sums(g, carry):
        sums = dot_nt(split_sums, bucket_hot(g).astype(BF))
        SMALL[2, pl.ds(g, 1), :] = jnp.sum(jnp.where(both_masks, sums, 0.0), axis=0, keepdims=True)
        return carry

    lax.fori_loop(0, 8, bucket_sums, 0)

    recv(RED.at[z], zd_r.at[z])
    recv(RCD, zdc_r)
    FD[...] = (ZD[z].astype(F32) + RED[z].astype(F32) + RCD[...].astype(F32)).astype(BF)

    def down_rows(cc):
        return odown.at[rows_at(128 * cc, 128)]

    y_core = (2 * y1 + k, f)
    remote(FD, down_rows(c), fd_s.at[1], fd_r.at[c], y_core).start()
    remote(FD, down_rows(c), fd_s.at[0], fd_r.at[c], sib).start()
    pltpu.make_async_copy(FD, down_rows(c), fd_r.at[c]).start()

    def spread(final, place, send, bsend, got):
        remote(final.at[x1], place(q, k), send.at[2], got.at[q, k], (2 * y1 + k, f1)).start()
        remote(final.at[x1], place(q, k), send.at[1], got.at[q, k], (c, f1)).start()
        remote(final.at[x], place(q, k), send.at[0], got.at[q, k], y_core).start()
        remote(final.at[x], place(q, k), bsend.at[0], got.at[q, k], sib).start()
        pltpu.make_async_copy(final.at[x], place(q, k), got.at[q, k]).start()

    chips = (2 * x + y1, 2 * x1 + y, 2 * x1 + y1)

    def spread_on(place, bsend, got):
        for i in range(3):
            piece = place(chips[i], k)
            recv(piece, got.at[chips[i], k])
            remote(piece, piece, bsend.at[i + 1], got.at[chips[i], k], sib).start()

    def spread_done(final, place, send, bsend, got):
        recv(place(q, k), got.at[q, k])
        for qq in (q,) + chips:
            recv(place(qq, k1), got.at[qq, k1])
        sent(final.at[x1], send.at[2])
        sent(final.at[x1], send.at[1])
        sent(final.at[x], send.at[0])
        sent(final.at[x], bsend.at[0])
        for i in range(3):
            sent(place(chips[i], k), bsend.at[i + 1])

    def in_place(qq, kk):
        return oin.at[:, qq, rows_at(64 * kk, 64), :]

    def proj_place(qq, kk):
        return oqkv.at[qq, rows_at(64 * kk, 64), :]

    recv(REI.at[pl.ds(2 * z, 2)], zi_r.at[z])
    recv(RCI, zic_r)
    for xx in range(2):
        total = ZI[2 * z + xx].astype(F32) + REI[2 * z + xx].astype(F32) + RCI[xx].astype(F32)
        for j in range(4):
            FI[xx, j] = total[:, 256 * j : 256 * j + 256].astype(BF)
    spread(FI, in_place, fi_s, fib_s, fi_r)

    for s in range(4):
        recv(RO.at[s], o_r.at[s])

    def home_out(r, carry):
        rows = rows_at(r * 32, 32)
        result = HID[rows, :]
        for s in range(4):
            result = result + RO[s, rows, :].astype(F32)
        out_ref[0, rows, :] = result.astype(BF)
        return carry

    lax.fori_loop(0, 4, home_out, 0)
    for s in range(4):
        recv(RN.at[s], n_r.at[s])

    def home_inputs(r, total):
        rows = rows_at(r * 32, 32)
        grad = RN[0, rows, :].astype(F32)
        for s in range(1, 4):
            grad = grad + RN[s, rows, :].astype(F32)
        values = XO[rows, :].astype(F32)
        scale = lax.rsqrt(jnp.mean(values * values, axis=-1, keepdims=True) + EPS)
        scaled = grad * gain_one
        inner = jnp.mean(scaled * values, axis=-1, keepdims=True)
        back = GH[rows, :] + scale * scaled - values * (scale * scale * scale * inner)
        gin_ref[0, rows, :] = back.astype(BF)
        return total + jnp.sum((grad * values * scale).reshape(4, 8, WIDTH), axis=0)

    attn_gain_grad = lax.fori_loop(0, 4, home_inputs, jnp.zeros((8, WIDTH), F32))
    attn_gain_grad = jnp.sum(attn_gain_grad, axis=0, keepdims=True)
    for g in range(8):
        SMALL[0, g : g + 1, :] = attn_gain_grad[:, 128 * g : 128 * g + 128]

    for i in range(4):
        ci = lax.rem(c + i, 4)
        for j, xj in enumerate((x, x1)):
            if i or j:
                remote(SMALL, RSMALL.at[2 * c + x], sp_s.at[i, j], sp_r.at[2 * c + x], (ci, 2 * z + xj)).start()

    for t in zs:
        recv(RZQ.at[t, :, :, value_cols], zv_r.at[t])
        recv(RZQ.at[t, :, :, other_cols], zq_r.at[t])
    for xx in range(2):
        total = ZQ[2 * z + xx].astype(F32)
        for t in zs:
            total = total + RZQ[t, xx].astype(F32)
        FQ[xx] = total.astype(BF)
    spread(FQ, proj_place, fq_s, fqb_s, fq_r)

    @pl.when(z == c)
    def _():
        for s in range(2):
            recv(RZO.at[s], zo_r.at[s])
        FO[...] = (ZO[...].astype(F32) + RZO[0].astype(F32) + RZO[1].astype(F32)).astype(BF)
        pltpu.make_async_copy(FO, oout, fo_r).start()
        remote(FO, oout, fo_s.at[1], fo_r, y_core).start()
        remote(FO, oout, fo_s.at[0], fo_r, sib).start()

    plane_sum = SMALL[...]
    for i in range(4):
        ci = lax.rem(c + i, 4)
        for j, xj in enumerate((x, x1)):
            if i or j:
                recv(RSMALL.at[2 * ci + xj], sp_r.at[2 * ci + xj])
                plane_sum = plane_sum + RSMALL[2 * ci + xj]
    for t in range(4):
        for n in range(3):
            pair = plane_sum[n, 2 * t : 2 * t + 2, :]
            PSMALL[t, n : n + 1, :] = jnp.where(x == 0, pair[0:1], pair[1:2])
    for t in zs:
        remote(PSMALL.at[t], RZSMALL.at[z], sz_s.at[t], sz_r.at[z], zdev(t)).start()

    y_rows = down_rows(2 * y1 + k)
    recv(y_rows, fd_r.at[2 * y1 + k])
    remote(y_rows, y_rows, fd_s.at[2], fd_r.at[2 * y1 + k], sib).start()
    spread_on(in_place, fib_s, fi_r)
    spread_on(proj_place, fqb_s, fq_r)
    recv(oout, fo_r)
    out_on = (y != z // 2) & (k == lax.rem(z, 2))

    @pl.when(out_on)
    def _():
        remote(oout, oout, fo_s.at[0], fo_r, sib).start()

    total = PSMALL[z]
    for t in zs:
        recv(RZSMALL.at[t], sz_r.at[t])
        total = total + RZSMALL[t]
    small_ref[...] = total

    recv(down_rows(c), fd_r.at[c])
    recv(down_rows(2 * y + k1), fd_r.at[2 * y + k1])
    recv(down_rows(2 * y1 + k1), fd_r.at[2 * y1 + k1])
    spread_done(FI, in_place, fi_s, fib_s, fi_r)
    spread_done(FQ, proj_place, fq_s, fqb_s, fq_r)

    sent(pack_in, gpx_s)
    gather_sent(x_in.at[0], XB, xb_s)
    gather_sent(cot_in.at[0], COT, co_s)
    gather_sent(NTS, NTB, nt_s)
    gather_sent(GALS, GAL, ga_s)
    scatter_sent(SA, a_s)
    scatter_sent(SG, g_s)
    scatter_sent(SO, o_s)
    scatter_sent(SN, n_s)
    sent(WQKV.at[half(f, k)], wx_s.at[0])
    sent(WIN.at[half(f, k)], wx_s.at[1])
    for r, own in enumerate((f, f1)):
        z_sent(WIN.at[half(own, k)], wiz_s.at[r])
    z_sent(WDOWN.at[down_half], wdz_s)
    sent(WQKV.at[half(f1, k)], wqb_s.at[f1])
    sent(WIN.at[half(f1, k)], wib_s.at[f1])
    for t in zs:
        sent(GP.at[pl.ds(2 * z, 2)], gpz_s.at[t])
        for xx in (x, x1):
            sent(WQKV.at[half(2 * t + xx, k)], wqb_s.at[2 * t + xx])
            sent(WIN.at[half(2 * t + xx, k)], wib_s.at[2 * t + xx])
        sent(down_piece(t, k), wdb_s.at[t])
        sent(ZQ.at[pl.ds(2 * t, 2), :, value_cols], zv_s.at[t])
        sent(ZQ.at[pl.ds(2 * t, 2), :, other_cols], zq_s.at[t])
        sent(PSMALL.at[t], sz_s.at[t])
    sent(ZD.at[near], zd_s)
    sent(ZI.at[pl.ds(2 * near, 2)], zi_s)
    for n in range(2):
        sent(ZD.at[others[n]], zde_s.at[n])
        sent(ZI.at[pl.ds(2 * others[n], 2)], zie_s.at[n])

    @pl.when(middle)
    def _():
        for n in range(2):
            sent(down_piece(others[n], k), wdf_s.at[n])
            for i, xx in enumerate((x, x1)):
                g = of_row(others[n], xx)
                sent(WQKV.at[half(g, k)], wqf_s.at[n, i])
                sent(WIN.at[half(g, k)], wif_s.at[n, i])

    @pl.when(z == c)
    def _():
        z_sent(out_piece, woz_s)
        sent(FO, fo_s.at[0])
        sent(FO, fo_s.at[1])

    @pl.when(out_on)
    def _():
        sent(oout, fo_s.at[0])

    @pl.when(z != c)
    def _():
        sent(out_piece, wob_s)
        sent(ZO, zo_s)

        @pl.when(middle & (z // 2 != c // 2))
        def _():
            sent(out_piece, woz_s.at[0])

    sent(DD.at[k1], sib_s.at[0])
    sent(DI.at[k1], sib_s.at[1])
    sent(DQ.at[k1, :, :, value_cols], sib_s.at[2])
    sent(DO.at[k1], sib_s.at[3])
    sent(DQ.at[k1, :, :, other_cols], sib_s.at[4])
    for i in range(3):
        sent(FD, fd_s.at[i])
    for i in range(4):
        for j, xj in enumerate((x, x1)):
            if i or j:
                sent(SMALL, sp_s.at[i, j])


def plane_shards(
    inputs, cotangent, w_query, w_key, w_value, w_out, w_in, w_down, gain_attn, gain_mlp, rel_bias, buckets
):
    pack = jnp.concatenate(
        [
            gain_attn.astype(F32)[None],
            gain_mlp.astype(F32)[None],
            jnp.pad(rel_bias.astype(F32), (0, 64))[None],
            jnp.zeros((5, 128), F32),
        ],
        axis=0,
    )
    bucket_row = jnp.pad(buckets, (0, 1))[None]
    vm = pltpu.VMEM
    dma = pltpu.SemaphoreType.DMA
    block = lambda kind: vm((TOKENS, WIDTH), kind)
    tokens = lambda width, kind: vm((512, width), kind)
    scratch = [
        block(BF), block(BF), vm((8, 8, 128), F32),
        tokens(1024, BF), tokens(1024, BF), tokens(1024, BF), tokens(1024, BF), tokens(1024, BF),
        vm((1024, 768), BF), vm((256, 1024), BF), vm((1024, 1024), BF), vm((1024, 1024), BF),
        tokens(768, BF), vm((4, 512, 512), F32), vm((4, 512, 512), BF), vm((4, 128, 1024), F32),
        tokens(256, BF), tokens(1024, BF), tokens(1024, F32), tokens(1024, BF),
        tokens(256, BF), tokens(768, BF), vm((4, 512, 512), BF), vm((4, 128, 1024), F32),
        tokens(1024, BF), tokens(1024, BF), tokens(1024, BF), tokens(1024, BF),
        vm((4, 128, 1024), BF), vm((4, 128, 1024), BF), vm((4, 128, 1024), BF), vm((4, 128, 1024), BF),
        block(F32), block(F32), block(BF), block(BF),
        vm((2, 8, 64, 768), BF), vm((2, 128, 1024), BF), vm((2, 8, 64, 1024), BF), vm((2, 4, 128, 1024), BF),
        vm((8, 64, 768), BF), vm((128, 1024), BF), vm((8, 64, 1024), BF), vm((4, 128, 1024), BF),
        vm((8, 64, 768), BF), vm((128, 1024), BF), vm((8, 64, 1024), BF), vm((4, 128, 1024), BF),
        vm((4, 2, 64, 768), BF), vm((2, 128, 1024), BF), vm((8, 64, 1024), BF), vm((4, 128, 1024), BF),
        vm((2, 64, 1024), BF), vm((128, 1024), BF),
        vm((2, 64, 768), BF), vm((128, 1024), BF), vm((2, 4, 64, 256), BF), vm((128, 1024), BF),
        vm((3, 8, 128), F32), vm((8, 3, 8, 128), F32), vm((4, 8, 128), F32), vm((4, 8, 128), F32),
        dma((7,)), dma, dma, dma((4,)), dma((4,)),
        dma((4, 2)), dma((4, 2)), dma((4, 2)), dma((4, 2)), dma((4, 2)), dma((4, 2)), dma((4, 2)), dma((4, 2)),
        dma((4,)), dma((4,)), dma((4,)), dma((4,)), dma((4,)), dma((4,)), dma((4,)), dma((4,)),
        dma((2,)), dma((2,)), dma((2, 2)), dma((2, 2)), dma((8,)), dma((8,)), dma((8,)),
        dma((2, 2)), dma((2, 2)), dma((8,)), dma((8,)), dma((8,)),
        dma((2,)), dma((2,)), dma((4,)), dma((4,)), dma((4,)), dma((2,)), dma, dma, dma,
        dma((5,)), dma((5,)), dma((4,)), dma((4,)), dma((4,)), dma((4,)), dma, dma((2,)),
        dma, dma((2,)), dma((4,)), dma, dma, dma((2,)), dma((4,)), dma,
        dma((3,)), dma((4,)), dma((4, 2)), dma((2,)), dma, dma((3,)), dma((4,)), dma((4, 2)), dma((3,)), dma((4,)),
        dma((4, 2)), dma((8,)), dma((4,)), dma((4,)),
    ]
    anywhere = pl.BlockSpec(memory_space=pl.ANY)
    in_vmem = pl.BlockSpec(memory_space=pltpu.VMEM)
    shape = jax.ShapeDtypeStruct
    output, grad_inputs, proj, out, hidden, down, small = pl.pallas_call(
        fused_layer,
        out_shape=(
            shape((1, TOKENS, WIDTH), BF),
            shape((1, TOKENS, WIDTH), BF),
            shape((4, 128, 768), BF),
            shape((128, 1024), BF),
            shape((4, 4, 128, 256), BF),
            shape((512, 1024), BF),
            shape((8, 128), F32),
        ),
        in_specs=[anywhere] * 9 + [in_vmem],
        out_specs=(in_vmem, in_vmem, anywhere, anywhere, anywhere, anywhere, in_vmem),
        scratch_shapes=scratch,
        compiler_params=pltpu.CompilerParams(
            collective_id=0, has_side_effects=True, vmem_limit_bytes=63 << 20
        ),
        cost_estimate=pl.CostEstimate(flops=11 * 10**9, bytes_accessed=16 * 2**20, transcendentals=3 * 2**20),
    )(inputs, cotangent, w_query, w_key, w_value, w_out, w_in, w_down, pack, bucket_row)
    return finish(output, grad_inputs, proj, out, hidden, down, small)


def finish_kernel(
    output, grad_inputs, proj, out, hidden, down, small,
    o_output, o_inputs, o_query, o_key, o_value, o_out, o_in, o_down, o_attn, o_mlp, o_bias,
    b_output, b_inputs, b_proj, b_out, b_hidden, b_down, b_small, w_proj, w_out, w_in, w_down, got, left,
):
    moves = [
        pltpu.make_async_copy(proj, b_proj, got.at[0]),
        pltpu.make_async_copy(hidden, b_hidden, got.at[1]),
        pltpu.make_async_copy(down, b_down, got.at[2]),
        pltpu.make_async_copy(out, b_out, got.at[3]),
        pltpu.make_async_copy(small, b_small, got.at[4]),
        pltpu.make_async_copy(output, b_output, got.at[5]),
        pltpu.make_async_copy(grad_inputs, b_inputs, got.at[6]),
    ]
    for move in moves:
        move.start()
    sends = []

    def write(src, dst, slot):
        copy = pltpu.make_async_copy(src, dst, left.at[slot])
        copy.start()
        sends.append(copy)

    moves[0].wait()
    for w, place in enumerate((o_query, o_key, o_value)):
        for q in range(4):
            x, y = q // 2, q % 2
            for j in range(2):
                first = 512 * y + 256 * j + 128 * x
                w_proj[w, :, first : first + 128] = b_proj[q, :, 256 * w + 128 * j : 256 * w + 128 * j + 128].astype(F32)
        write(w_proj.at[w], place, w)
    moves[1].wait()
    for r in range(4):
        rows = slice(32 * r, 32 * r + 32)
        for z in range(4):
            for q in range(4):
                w_in[rows, 256 * (4 * z + q) : 256 * (4 * z + q) + 256] = b_hidden[z, q, rows, :].astype(F32)
        write(w_in.at[pl.ds(32 * r, 32)], o_in.at[pl.ds(32 * r, 32)], 3 + r)
    moves[2].wait()
    for r in range(4):
        rows = slice(128 * r, 128 * r + 128)
        w_down[rows, :] = b_down[rows, :].astype(F32)
        write(w_down.at[pl.ds(128 * r, 128)], o_down.at[pl.ds(128 * r, 128)], 7 + r)
    moves[3].wait()
    w_out[...] = b_out[...].astype(F32)
    write(w_out, o_out, 11)
    moves[4].wait()
    o_attn[...] = b_small[0:1, :]
    o_mlp[...] = b_small[1:2, :]
    o_bias[...] = b_small[2:3, 0:64]
    moves[5].wait()
    write(b_output, o_output, 12)
    moves[6].wait()
    write(b_inputs, o_inputs, 13)
    for copy in sends:
        copy.wait()


def finish(output, grad_inputs, proj, out, hidden, down, small):
    shape = jax.ShapeDtypeStruct
    vm = pltpu.VMEM
    anywhere = pl.BlockSpec(memory_space=pl.ANY)
    in_vmem = pl.BlockSpec(memory_space=pltpu.VMEM)
    results = pl.pallas_call(
        finish_kernel,
        out_shape=(
            shape(output.shape, BF),
            shape(grad_inputs.shape, BF),
            shape((128, 1024), F32),
            shape((128, 1024), F32),
            shape((128, 1024), F32),
            shape((128, 1024), F32),
            shape((128, 4096), F32),
            shape((512, 1024), F32),
            shape((1, 128), F32),
            shape((1, 128), F32),
            shape((1, 64), F32),
        ),
        in_specs=[anywhere] * 7,
        out_specs=(anywhere,) * 8 + (in_vmem,) * 3,
        scratch_shapes=[
            vm(output.shape, BF), vm(grad_inputs.shape, BF), vm(proj.shape, BF), vm(out.shape, BF), vm(hidden.shape, BF), vm(down.shape, BF), vm(small.shape, F32),
            vm((3, 128, 1024), F32), vm((128, 1024), F32), vm((128, 4096), F32), vm((512, 1024), F32),
            pltpu.SemaphoreType.DMA((7,)), pltpu.SemaphoreType.DMA((14,)),
        ],
        compiler_params=pltpu.CompilerParams(vmem_limit_bytes=63 << 20),
        cost_estimate=pl.CostEstimate(flops=0, bytes_accessed=10 * 2**20, transcendentals=0),
    )(output, grad_inputs, proj, out, hidden, down, small)
    return results[:8] + (results[8].reshape(128), results[9].reshape(128), results[10].reshape(64))


def solution(mesh):
    placed = (
        P("fsdp", "ctx", None),
        P("fsdp", "ctx", None),
        P("fsdp", None),
        P("fsdp", None),
        P("fsdp", None),
        P("fsdp", None),
        P("fsdp", None),
        P("fsdp", None),
        P("fsdp"),
        P("fsdp"),
        P("fsdp"),
        P(),
    )
    by_planes = mesh.shape["ctx"] == 4 and mesh.shape["fsdp"] == 8
    return jax.shard_map(
        plane_shards if by_planes else shards,
        mesh=mesh,
        in_specs=placed,
        out_specs=(
            P("fsdp", "ctx", None),
            P("fsdp", "ctx", None),
            P("fsdp", None),
            P("fsdp", None),
            P("fsdp", None),
            P("fsdp", None),
            P("fsdp", None),
            P("fsdp", None),
            P("fsdp"),
            P("fsdp"),
            P("fsdp"),
        ),
        check_vma=False,
    )
```

```python
import jax
import jax.numpy as jnp
from jax import lax
from jax.experimental import pallas as pl
from jax.experimental.pallas import tpu as pltpu
from jax.sharding import PartitionSpec as P

HEADS = 16
HEAD = 64
BUCKETS = 32


EPS = 1e-06


def norm_rows(values, gain):
    return values * lax.rsqrt(jnp.mean(values * values, axis=-1, keepdims=True) + EPS) * gain


def smooth_gelu(values):
    return 0.5 * values * (1.0 + jax.scipy.special.erf(values * 0.7071067811865476))


def gelu_slope(values):
    return (
        0.5 * (1.0 + jax.scipy.special.erf(values * 0.7071067811865476))
        + values * jnp.exp(-0.5 * values * values) * 0.3989422804014327
    )


def bucket_offsets(buckets, first_query, query_count):
    seq_length = (buckets.shape[0] + 1) // 2
    key_place = jnp.arange(seq_length, dtype=jnp.int32)
    query_place = first_query + jnp.arange(query_count, dtype=jnp.int32)
    return key_place[None, :] - query_place[:, None] + (seq_length - 1)


def make_bias(flat_table, buckets, first_query, query_count):
    bias_table = flat_table.reshape(BUCKETS, HEADS)
    one_hot = (buckets[:, None] == jnp.arange(BUCKETS, dtype=jnp.int32)[None, :]).astype(
        flat_table.dtype
    )
    per_offset = jnp.dot(one_hot, bias_table, precision=lax.Precision.HIGHEST)
    offsets = bucket_offsets(buckets, first_query, query_count)
    return jnp.take(per_offset.T, offsets, axis=1)


def pair_table(buckets, first_query, query_count):
    offsets = bucket_offsets(buckets, first_query, query_count)
    pair_bucket = jnp.take(buckets, offsets.reshape(-1), axis=0)
    return (pair_bucket[:, None] == jnp.arange(BUCKETS, dtype=jnp.int32)[None, :]).astype(
        jnp.bfloat16
    )


def fetch_attention(w_query, w_key, w_value, w_out, gain_attn, rel_bias):
    return (
        lax.all_gather(w_query, "fsdp", axis=0, tiled=True),
        lax.all_gather(w_key, "fsdp", axis=0, tiled=True),
        lax.all_gather(w_value, "fsdp", axis=0, tiled=True),
        lax.all_gather(w_out, "fsdp", axis=0, tiled=True),
        lax.all_gather(gain_attn, "fsdp", axis=0, tiled=True),
        lax.all_gather(rel_bias, "fsdp", axis=0, tiled=True),
    )


def fetch_mlp(w_in, w_down, gain_mlp):
    return (
        lax.all_gather(w_in, "fsdp", axis=0, tiled=True),
        lax.all_gather(w_down, "fsdp", axis=0, tiled=True),
        lax.all_gather(gain_mlp, "fsdp", axis=0, tiled=True),
    )


def share_keys(key_rows, value_rows):
    return (
        lax.all_gather(key_rows, "ctx", axis=1, tiled=True),
        lax.all_gather(value_rows, "ctx", axis=1, tiled=True),
    )


def scores_of(query_part, key_part, bias_values):
    return (
        jnp.einsum("qhd,khd->hqk", query_part, key_part, preferred_element_type=jnp.float32)
        + bias_values
    )


def shards(
    inputs,
    cotangent,
    w_query,
    w_key,
    w_value,
    w_out,
    w_in,
    w_down,
    gain_attn,
    gain_mlp,
    rel_bias,
    buckets,
):
    seq_count, row_count, width = inputs.shape
    total_rows = seq_count * row_count
    first_query = lax.axis_index("ctx") * row_count
    query_w, key_w, value_w, out_w, attn_gain, bias_flat = fetch_attention(
        w_query, w_key, w_value, w_out, gain_attn, rel_bias
    )
    in_w, down_w, mlp_gain = fetch_mlp(w_in, w_down, gain_mlp)
    bias_values = make_bias(bias_flat.astype(jnp.float32), buckets, first_query, row_count)
    inputs_flat = inputs.astype(jnp.float32).reshape(total_rows, width)
    attn_scale = attn_gain.astype(jnp.float32)
    normed_one = norm_rows(inputs_flat, attn_scale).astype(jnp.bfloat16)
    query_rows = jnp.dot(normed_one, query_w, preferred_element_type=jnp.float32).astype(
        jnp.bfloat16
    )
    key_rows = (
        jnp.dot(normed_one, key_w, preferred_element_type=jnp.float32)
        .astype(jnp.bfloat16)
        .reshape(seq_count, row_count, width)
    )
    value_rows = (
        jnp.dot(normed_one, value_w, preferred_element_type=jnp.float32)
        .astype(jnp.bfloat16)
        .reshape(seq_count, row_count, width)
    )
    all_keys, all_values = share_keys(key_rows, value_rows)
    query_heads = query_rows.reshape(seq_count, row_count, HEADS, HEAD)
    seq_index = 0
    key_heads = all_keys[seq_index].reshape(-1, HEADS, HEAD)
    value_heads = all_values[seq_index].reshape(-1, HEADS, HEAD)
    scores = scores_of(query_heads[seq_index], key_heads, bias_values)
    top_score = jnp.max(scores, axis=-1, keepdims=True)
    weights_exp = jnp.exp(scores - top_score)
    totals = jnp.sum(weights_exp, axis=-1, keepdims=True)
    probs_low = (weights_exp / totals).astype(jnp.bfloat16)
    mixed = jnp.einsum("hqk,khd->qhd", probs_low, value_heads, preferred_element_type=jnp.float32)
    mixed_list = mixed.reshape(row_count, width)
    lse_list = [top_score + jnp.log(totals)]
    attended = mixed_list.astype(jnp.bfloat16)
    hidden_res = inputs_flat + jnp.dot(attended, out_w, preferred_element_type=jnp.float32)
    mlp_scale = mlp_gain.astype(jnp.float32)
    normed_two = norm_rows(hidden_res, mlp_scale).astype(jnp.bfloat16)
    pre_act = jnp.dot(normed_two, in_w, preferred_element_type=jnp.float32)
    activated = smooth_gelu(pre_act).astype(jnp.bfloat16)
    result = hidden_res + jnp.dot(activated, down_w, preferred_element_type=jnp.float32)
    in_w, down_w, mlp_gain = fetch_mlp(w_in, w_down, gain_mlp)
    query_w, key_w, value_w, out_w, attn_gain, bias_flat = fetch_attention(
        w_query, w_key, w_value, w_out, gain_attn, rel_bias
    )
    all_keys, all_values = share_keys(key_rows, value_rows)
    grad_rows = cotangent.reshape(total_rows, width)
    grad_down = jnp.einsum("nf,nd->fd", activated, grad_rows, preferred_element_type=jnp.float32)
    grad_act = jnp.einsum("nd,fd->nf", grad_rows, down_w, preferred_element_type=jnp.float32)
    grad_pre = (grad_act * gelu_slope(pre_act)).astype(jnp.bfloat16)
    grad_in = jnp.einsum("nd,nf->df", normed_two, grad_pre, preferred_element_type=jnp.float32)
    grad_normed_two = jnp.einsum("nf,df->nd", grad_pre, in_w, preferred_element_type=jnp.float32)
    back_hidden, grad_mlp_gain = jax.vjp(norm_rows, hidden_res, mlp_scale)[1](grad_normed_two)
    grad_hidden = grad_rows.astype(jnp.float32) + back_hidden
    grad_attn_low = grad_hidden.astype(jnp.bfloat16)
    grad_out = jnp.einsum("nd,ne->de", attended, grad_attn_low, preferred_element_type=jnp.float32)
    grad_attended = jnp.einsum(
        "ne,de->nd", grad_attn_low, out_w, preferred_element_type=jnp.float32
    ).astype(jnp.bfloat16)
    grad_heads = grad_attended.reshape(seq_count, row_count, HEADS, HEAD)
    pair_buckets = pair_table(buckets, first_query, row_count)
    seq_index = 0
    key_heads = all_keys[seq_index].reshape(-1, HEADS, HEAD)
    value_heads = all_values[seq_index].reshape(-1, HEADS, HEAD)
    scores = scores_of(query_heads[seq_index], key_heads, bias_values)
    probs = jnp.exp(scores - lse_list[seq_index])
    grad_probs = jnp.einsum(
        "qhd,khd->hqk", grad_heads[seq_index], value_heads, preferred_element_type=jnp.float32
    )
    row_inner = jnp.sum(probs * grad_probs, axis=-1, keepdims=True)
    grad_scores = (probs * (grad_probs - row_inner)).astype(jnp.bfloat16)
    bias_grad = jnp.dot(
        grad_scores.reshape(HEADS, -1), pair_buckets, preferred_element_type=jnp.float32
    )
    query_grads = jnp.einsum(
        "hqk,khd->qhd", grad_scores, key_heads, preferred_element_type=jnp.float32
    ).reshape(row_count, width)
    key_grads = [
        jnp.einsum(
            "hqk,qhd->khd", grad_scores, query_heads[seq_index], preferred_element_type=jnp.float32
        ).reshape(-1, width)
    ]
    value_grads = [
        jnp.einsum(
            "hqk,qhd->khd",
            probs.astype(jnp.bfloat16),
            grad_heads[seq_index],
            preferred_element_type=jnp.float32,
        ).reshape(-1, width)
    ]
    key_back, value_back = (
        lax.psum_scatter(
            jnp.stack(key_grads).astype(jnp.bfloat16), "ctx", scatter_dimension=1, tiled=True
        ).astype(jnp.float32),
        lax.psum_scatter(
            jnp.stack(value_grads).astype(jnp.bfloat16), "ctx", scatter_dimension=1, tiled=True
        ).astype(jnp.float32),
    )
    grad_query_rows = query_grads.astype(jnp.bfloat16)
    grad_key_rows = key_back.reshape(total_rows, width).astype(jnp.bfloat16)
    grad_value_rows = value_back.reshape(total_rows, width).astype(jnp.bfloat16)
    grad_query = jnp.einsum(
        "nd,ne->de", normed_one, grad_query_rows, preferred_element_type=jnp.float32
    )
    grad_key = jnp.einsum(
        "nd,ne->de", normed_one, grad_key_rows, preferred_element_type=jnp.float32
    )
    grad_value = jnp.einsum(
        "nd,ne->de", normed_one, grad_value_rows, preferred_element_type=jnp.float32
    )
    grad_normed_one = jnp.einsum(
        "ne,de->nd", grad_query_rows, query_w, preferred_element_type=jnp.float32
    )
    grad_normed_one = grad_normed_one + jnp.einsum(
        "ne,de->nd", grad_key_rows, key_w, preferred_element_type=jnp.float32
    )
    grad_normed_one = grad_normed_one + jnp.einsum(
        "ne,de->nd", grad_value_rows, value_w, preferred_element_type=jnp.float32
    )
    back_inputs, grad_attn_gain = jax.vjp(norm_rows, inputs_flat, attn_scale)[1](grad_normed_one)
    grad_inputs = (
        (grad_hidden + back_inputs).astype(jnp.bfloat16).reshape(seq_count, row_count, width)
    )
    grad_bias_flat = bias_grad.T.reshape(BUCKETS * HEADS)
    (
        part_query,
        part_key,
        part_value,
        part_out,
        part_in,
        part_down,
        part_attn_gain,
        part_mlp_gain,
        part_bias,
    ) = (
        lax.psum_scatter(grad_query, "fsdp", scatter_dimension=0, tiled=True),
        lax.psum_scatter(grad_key, "fsdp", scatter_dimension=0, tiled=True),
        lax.psum_scatter(grad_value, "fsdp", scatter_dimension=0, tiled=True),
        lax.psum_scatter(grad_out, "fsdp", scatter_dimension=0, tiled=True),
        lax.psum_scatter(grad_in, "fsdp", scatter_dimension=0, tiled=True),
        lax.psum_scatter(grad_down, "fsdp", scatter_dimension=0, tiled=True),
        lax.psum_scatter(grad_attn_gain, "fsdp", scatter_dimension=0, tiled=True),
        lax.psum_scatter(grad_mlp_gain, "fsdp", scatter_dimension=0, tiled=True),
        lax.psum_scatter(grad_bias_flat, "fsdp", scatter_dimension=0, tiled=True),
    )
    summed = (
        lax.psum(part_query.astype(jnp.bfloat16), "ctx").astype(jnp.float32),
        lax.psum(part_key.astype(jnp.bfloat16), "ctx").astype(jnp.float32),
        lax.psum(part_value.astype(jnp.bfloat16), "ctx").astype(jnp.float32),
        lax.psum(part_out.astype(jnp.bfloat16), "ctx").astype(jnp.float32),
        lax.psum(part_in.astype(jnp.bfloat16), "ctx").astype(jnp.float32),
        lax.psum(part_down.astype(jnp.bfloat16), "ctx").astype(jnp.float32),
        lax.psum(part_attn_gain.astype(jnp.bfloat16), "ctx").astype(jnp.float32),
        lax.psum(part_mlp_gain.astype(jnp.bfloat16), "ctx").astype(jnp.float32),
        lax.psum(part_bias.astype(jnp.bfloat16), "ctx").astype(jnp.float32),
    )
    output = result.astype(jnp.bfloat16).reshape(seq_count, row_count, width)
    return (
        output,
        grad_inputs,
        summed[0],
        summed[1],
        summed[2],
        summed[3],
        summed[4],
        summed[5],
        summed[6],
        summed[7],
        summed[8],
    )


MESH_ID = pl.DeviceIdType.MESH
BF = jnp.bfloat16
F32 = jnp.float32
WIDTH = 1024
TOKENS = 128
NT_DIMS = (((1,), (1,)), ((), ()))
TN_DIMS = (((0,), (0,)), ((), ()))


def dot_nn(left, right):
    return jnp.dot(left, right, preferred_element_type=F32)


def dot_nt(left, right):
    return lax.dot_general(left, right, NT_DIMS, preferred_element_type=F32)


def dot_tn(left, right):
    return lax.dot_general(left, right, TN_DIMS, preferred_element_type=F32)


def rows_at(start, count):
    return pl.ds(pl.multiple_of(start, count), count)


def remote(src, dst, send, recv, device):
    return pltpu.make_async_remote_copy(
        src_ref=src, dst_ref=dst, send_sem=send, recv_sem=recv, device_id=device, device_id_type=MESH_ID
    )


def fused_layer(
    x_in, cot_in, wq_in, wk_in, wv_in, wo_in, wi_in, wd_in, pack_in, bucket_in,
    out_ref, gin_ref, oqkv, oout, oin, odown, small_ref,
    XO, CO, GP, XB, COT, N1, NTB, GAL, WQKV, WOUT, WIN, WDOWN,
    QKV, PROB, PLOW, BIAS, AT, ACT, SLOPE, GPRE, GATT, DQKV, DS, BACC,
    SA, SG, SO, SN, RA, RG, RO, RN, HID, GH, NTS, GALS,
    DQ, DO, DI, DD, SIBQ, SIBO, SIBI, SIBD, ZQ, ZO, ZI, ZD, RZQ, RZO, REI, RZD, RCI, FQ, FO, FI, FD,
    SMALL, RSMALL, PSMALL, RZSMALL,
    loc, gpx_s, gpx_r, gpz_s, gpz_r, xb_s, xb_r, xb_p, co_s, co_r, co_p, nt_s, nt_r, nt_p, ga_s, ga_r, ga_p,
    a_s, a_r, g_s, g_r, o_s, o_r, n_s, n_r,
    wx_s, wx_r, wqz_s, wqf_s, wqz_r, wqb_s, wqb_r, wiz_s, wif_s, wiz_r, wib_s, wib_r,
    wdz_s, wdf_s, wdz_r, wdb_s, wdb_r, woz_s, woz_r, wob_s, wob_r,
    sib_s, sib_r, zq_s, zq_r, zv_s, zv_r, zo_s, zo_r, zi_s, zie_s, zi_r, zic_r, zd_s, zd_r,
    fq_s, fqb_s, fq_r, fqb_r, fo_s, fo_r, fi_s, fib_s, fi_r, fib_r, fd_s, fd_r, sp_s, sp_r, sz_s, sz_r,
):
    c = lax.axis_index("ctx")
    f = lax.axis_index("fsdp")
    y, k = c // 2, lax.rem(c, 2)
    z, x = f // 2, lax.rem(f, 2)
    x1, y1, k1 = 1 - x, 1 - y, 1 - k
    f1 = 2 * z + x1
    q = 2 * x + y
    sib = (2 * y + k1, f)
    xdev = (c, f1)
    zs = [lax.rem(z + d, 4) for d in (1, 2, 3)]
    near = z + 1 - 2 * lax.rem(z, 2)
    other = 2 - 2 * (z // 2)
    others = (other, other + 1)
    far = 2 - z // 2
    middle = (z == 1) | (z == 2)
    at_end = jnp.logical_not(middle)

    def zdev(target):
        return (c, 2 * target + x)

    plane = []
    for i in range(4):
        ci = lax.rem(c + i, 4)
        for j, xj in enumerate((x, x1)):
            if i or j:
                plane.append((ci, 2 * z + xj))

    def recv(dst, sem):
        remote(dst, dst, sem, sem, sib).wait_recv()

    def sent(src, sem):
        remote(src, src, sem, sem, sib).wait_send()

    def block_half(buf, b, h):
        return buf.at[rows_at(b * TOKENS + 64 * h, 64)]

    def gather_send(src, dst, send, got, passed):
        halves = [src.at[pl.ds(64 * h, 64)] for h in range(2)]
        places = [block_half(dst, c, h) for h in range(2)]
        x_worker, y_worker = (2 * y + x, f1), (2 * y1 + x, f)
        remote(halves[0], places[0], send, passed.at[k], x_worker).start()
        remote(halves[1], places[1], send, passed.at[k], y_worker).start()
        remote(halves[1], places[1], send, got.at[c], x_worker).start()
        remote(halves[0], places[0], send, got.at[c], y_worker).start()
        whole = dst.at[rows_at(c * TOKENS, TOKENS)]

        @pl.when(k == x)
        def _():
            pltpu.make_async_copy(src, whole, got.at[c]).start()

        @pl.when(k != x)
        def _():
            remote(src, whole, send, got.at[c], sib).start()

    same = 1 - lax.rem(x + k, 2)
    pass_y = y + same * (1 - 2 * y)
    pass_to = (same * c + (1 - same) * (2 * y1 + k), same * f1 + (1 - same) * f)

    def gather_pass(dst, send, got, passed):
        for i in range(2):
            b = 2 * pass_y + i
            piece = block_half(dst, b, same)
            recv(piece, passed.at[i])
            remote(piece, piece, send, got.at[b], pass_to).start()

    def gather_wait(dst, got, b):
        @pl.when(b // 2 == pass_y)
        def _():
            recv(block_half(dst, b, 1 - same), got.at[b])

        @pl.when(b // 2 != pass_y)
        def _():
            recv(dst.at[rows_at(b * TOKENS, TOKENS)], got.at[b])

    def four_sent(buf, send):
        @pl.when(k == x)
        def _():
            sent(buf.at[pl.ds(0, 384)], send)

        @pl.when(k != x)
        def _():
            sent(buf, send)

    def scatter_send(buf, dst, send, got, b):
        src = buf.at[rows_at(b * TOKENS, TOKENS)]
        here = (b == c) & (x == k)

        @pl.when(here)
        def _():
            pltpu.make_async_copy(src, dst.at[q], got).start()

        @pl.when(jnp.logical_not(here))
        def _():
            remote(src, dst.at[q], send, got, (b, 2 * z + k)).start()

    def half(fb, kk):
        return rows_at(fb * 128 + kk * 64, 64)

    def z_send(piece, send, got):
        remote(piece, piece, send, got, zdev(far)).start()
        remote(piece, piece, send, got, zdev(near)).start()

    def take(piece, got, bsend, bgot):
        recv(piece, got)
        remote(piece, piece, bsend, bgot, sib).start()

    def pass_on(piece, send, got):
        remote(piece, piece, send, got, zdev(near)).start()

    def of_row(t, xx):
        return 2 * t + xx

    own_x = pltpu.make_async_copy(x_in.at[0], XO, loc.at[0])
    own_c = pltpu.make_async_copy(cot_in.at[0], CO, loc.at[1])
    own_pack = pltpu.make_async_copy(pack_in, GP.at[f], loc.at[2])
    proj = (wq_in, wk_in, wv_in)
    myrows = pl.ds(pl.multiple_of(128 * f, 128), 128)
    for w in range(3):
        for j in range(2):
            src = proj[w].at[:, pl.ds(pl.multiple_of(128 * (2 * (2 * y + j) + x), 128), 128)]
            pltpu.make_async_copy(src, WQKV.at[myrows, pl.ds(256 * w + 128 * j, 128)], loc.at[3]).start()
    own_pack.start()
    for j in range(4):
        src = wi_in.at[:, pl.ds(pl.multiple_of(512 * (2 * j + x) + 256 * y, 256), 256)]
        pltpu.make_async_copy(src, WIN.at[myrows, pl.ds(256 * j, 256)], loc.at[4]).start()
    pltpu.make_async_copy(
        wd_in.at[rows_at(256 * y, 256)], WDOWN.at[rows_at(256 * z, 256)], loc.at[5]
    ).start()

    @pl.when(z // 2 == y)
    def _():
        pltpu.make_async_copy(wo_in, WOUT.at[rows_at(128 * lax.rem(z, 2), 128)], loc.at[6]).start()

    own_x.start()
    own_c.start()

    barrier = pltpu.get_barrier_semaphore()
    for device in plane + [zdev(t) for t in zs]:
        pl.semaphore_signal(barrier, inc=1, device_id=device, device_id_type=MESH_ID)
    pl.semaphore_wait(barrier, 10)


    remote(pack_in, GP.at[f], gpx_s, gpx_r, xdev).start()
    for w in range(3):
        for j in range(2):
            src = proj[w].at[rows_at(64 * k, 64), pl.ds(pl.multiple_of(128 * (2 * (2 * y + j) + x1), 128), 128)]
            remote(src, WQKV.at[half(f, k), pl.ds(256 * w + 128 * j, 128)], wx_s.at[0], wx_r.at[0], xdev).start()
    pltpu.make_async_copy(WQKV.at[myrows], WQKV.at[myrows], loc.at[3]).wait()
    z_send(WQKV.at[half(f, k)], wqz_s, wqz_r.at[f])
    gather_send(x_in.at[0], XB, xb_s, xb_r, xb_p)
    for j in range(4):
        src = wi_in.at[rows_at(64 * k, 64), pl.ds(pl.multiple_of(512 * (2 * j + x1) + 256 * y, 256), 256)]
        remote(src, WIN.at[half(f, k), pl.ds(256 * j, 256)], wx_s.at[1], wx_r.at[1], xdev).start()
    out_piece = WOUT.at[rows_at(128 * k, 128)]
    out_other = WOUT.at[rows_at(128 * k1, 128)]

    own_pack.wait()
    recv(GP.at[f1], gpx_r)
    for t in zs:
        remote(GP.at[pl.ds(2 * z, 2)], GP.at[pl.ds(2 * z, 2)], gpz_s, gpz_r, zdev(t)).start()
    recv(WQKV.at[half(f1, k)], wx_r.at[0])
    z_send(WQKV.at[half(f1, k)], wqz_s, wqz_r.at[f1])
    remote(WQKV.at[half(f1, k)], WQKV.at[half(f1, k)], wqb_s, wqb_r, sib).start()

    @pl.when(z == c)
    def _():
        remote(wo_in, out_piece, woz_s, woz_r, zdev(far)).start()
        remote(wo_in, out_piece, woz_s, woz_r, zdev(near)).start()

    gather_pass(XB, xb_s, xb_r, xb_p)
    gather_send(cot_in.at[0], COT, co_s, co_r, co_p)

    def take_proj(xx):
        g = of_row(near, xx)
        take(WQKV.at[half(g, k)], wqz_r.at[g], wqb_s, wqb_r)
        for n in range(2):
            h = of_row(others[n], xx)
            piece = WQKV.at[half(h, k)]
            recv(piece, wqz_r.at[h])

            @pl.when(middle)
            def _():
                pass_on(piece, wqf_s, wqz_r.at[h])

            remote(piece, piece, wqb_s, wqb_r, sib).start()

    @pl.when(middle)
    def _():
        take_proj(x)

    recv(GP.at[pl.ds(0, 6)], gpz_r)

    def row_of(index):
        return jnp.concatenate([GP[g, index : index + 1, :] for g in range(8)], axis=1)

    lane = lax.broadcasted_iota(jnp.int32, (8, 128), 1)
    head_row = lax.broadcasted_iota(jnp.int32, (8, 128), 0)
    head_of = 8 * y + 4 * lax.div(head_row, 2) + 2 * x + lax.rem(head_row, 2)
    head_mask = (lax.rem(lane, 16) == head_of) & (head_row < 4)

    def bucket_hot(g):
        index = lax.broadcasted_iota(jnp.int32, (128, WIDTH), 0)
        wanted = jnp.where(index < 64, 4 * g + lax.div(index, 16), -1)
        return (bucket_in[0:1, :] == wanted)

    def add_bias(g, total):
        table = jnp.where(head_mask, jnp.broadcast_to(GP[g, 2:3, :], (8, 128)), 0.0).astype(BF)
        return total + dot_nn(table, bucket_hot(g).astype(BF))

    offsets = lax.fori_loop(0, 8, add_bias, jnp.zeros((8, WIDTH), F32))
    for h in range(4):
        spread = jnp.broadcast_to(offsets[h : h + 1, :], (128, WIDTH))
        BIAS[h] = pltpu.roll(spread, WIDTH - 127, 1, stride=1, stride_axis=0)
        BACC[h] = jnp.zeros((128, WIDTH), F32)

    gain_one = row_of(0)

    def norm_block(i, carry):
        b = lax.rem(2 * y + i, 4)
        gather_wait(XB, xb_r, b)

        def chunk(r, inner):
            rows = rows_at(b * TOKENS + r * 32, 32)
            values = XB[rows, :].astype(F32)
            scale = lax.rsqrt(jnp.mean(values * values, axis=-1, keepdims=True) + EPS)
            N1[rows, :] = (values * scale * gain_one).astype(BF)
            return inner

        return lax.fori_loop(0, 4, chunk, carry)

    lax.fori_loop(0, 4, norm_block, 0)

    sent(WQKV.at[pl.ds(0, 256)], wqz_s)
    pltpu.make_async_copy(WIN.at[myrows], WIN.at[myrows], loc.at[4]).wait()
    z_send(WIN.at[half(f, k)], wiz_s, wiz_r.at[f])
    recv(WIN.at[half(f1, k)], wx_r.at[1])
    z_send(WIN.at[half(f1, k)], wiz_s, wiz_r.at[f1])
    remote(WIN.at[half(f1, k)], WIN.at[half(f1, k)], wib_s, wib_r, sib).start()

    @pl.when(at_end)
    def _():
        take_proj(x)

    take_proj(x1)

    @pl.when(z != c)
    def _():
        recv(out_piece, woz_r)

        @pl.when(middle & (z // 2 != c // 2))
        def _():
            pass_on(out_piece, woz_s, woz_r)

        remote(out_piece, out_piece, wob_s, wob_r, sib).start()

    down_half = rows_at(256 * z + 128 * k, 128)
    pltpu.make_async_copy(WDOWN.at[rows_at(256 * z, 256)], WDOWN.at[rows_at(256 * z, 256)], loc.at[5]).wait()
    z_send(WDOWN.at[down_half], wdz_s, wdz_r.at[z])
    recv(WQKV.at[pl.ds(0, 448)], wqb_r)

    def project(n, carry):
        cols = rows_at(256 * n, 256)
        QKV[:, cols] = dot_nn(N1[...], WQKV[:, cols]).astype(BF)
        return carry

    lax.fori_loop(0, 3, project, 0)


    @pl.when(z // 2 == y)
    def _():
        pltpu.make_async_copy(wo_in, out_piece, loc.at[6]).wait()

    @pl.when(z != 2 * y + k1)
    def _():
        recv(out_other, wob_r)

    gather_pass(COT, co_s, co_r, co_p)

    low_lanes = lax.broadcasted_iota(jnp.int32, (TOKENS, 128), 1) < 64

    def pick(values, hh):
        keep = low_lanes if hh == 0 else jnp.logical_not(low_lanes)
        return jnp.where(keep, values, jnp.zeros_like(values))

    def attend(i, carry):
        b = lax.rem(2 * y1 + i, 4)
        rows = rows_at(b * TOKENS, TOKENS)
        window = rows_at(384 - 128 * b, 128)
        window = pl.ds(pl.multiple_of(384 - 128 * b, 128), 512)
        for j in range(2):
            outs = []
            for hh in range(2):
                h = 2 * j + hh
                query = pick(QKV[rows, 128 * j : 128 * j + 128], hh)
                scores = dot_nt(query, QKV[:, 256 + 128 * j : 384 + 128 * j]) + BIAS[h, :, window]
                weights = jnp.exp(scores - jnp.max(scores, axis=-1, keepdims=True))
                probs = weights * (1.0 / jnp.sum(weights, axis=-1, keepdims=True))
                PROB[h, rows, :] = probs
                low = probs.astype(BF)
                PLOW[h, rows, :] = low
                outs.append(dot_nn(low, QKV[:, 512 + 128 * j : 640 + 128 * j]))
            AT[rows, 128 * j : 128 * j + 128] = jnp.where(low_lanes, outs[0], outs[1]).astype(BF)
        SA[rows, :] = dot_nn(AT[rows, :], WOUT[...]).astype(BF)
        scatter_send(SA, RA, a_s, a_r, b)
        return carry

    lax.fori_loop(0, 4, attend, 0)

    for xx in (x, x1):
        g = of_row(near, xx)
        take(WIN.at[half(g, k)], wiz_r.at[g], wib_s, wib_r)

    @pl.when(middle)
    def _():
        for i, xx in enumerate((x, x1)):
            for n in range(2):
                g = of_row(others[n], xx)
                recv(WIN.at[half(g, k)], wiz_r.at[g])
                pass_on(WIN.at[half(g, k)], wif_s, wiz_r.at[g])
                remote(WIN.at[half(g, k)], WIN.at[half(g, k)], wib_s, wib_r, sib).start()

    own_x.wait()
    own_c.wait()
    gain_two = row_of(1)
    recv(RA, a_r)

    def home_forward(r, carry):
        rows = rows_at(r * 32, 32)
        hidden = XO[rows, :].astype(F32)
        for s in range(4):
            hidden = hidden + RA[s, rows, :].astype(F32)
        HID[rows, :] = hidden
        scale = lax.rsqrt(jnp.mean(hidden * hidden, axis=-1, keepdims=True) + EPS)
        NTS[rows, :] = (hidden * scale * gain_two).astype(BF)
        return carry

    lax.fori_loop(0, 4, home_forward, 0)
    gather_send(NTS, NTB, nt_s, nt_r, nt_p)

    def down_piece(t, kk):
        return WDOWN.at[rows_at(256 * t + 128 * kk, 128)]

    take(down_piece(near, k), wdz_r.at[near], wdb_s, wdb_r)

    @pl.when(middle)
    def _():
        for n in range(2):
            t = others[n]
            recv(down_piece(t, k), wdz_r.at[t])
            pass_on(down_piece(t, k), wdf_s, wdz_r.at[t])
            remote(down_piece(t, k), down_piece(t, k), wdb_s, wdb_r, sib).start()

    @pl.when(at_end)
    def _():
        for xx in (x, x1):
            for t in others:
                g = of_row(t, xx)
                take(WIN.at[half(g, k)], wiz_r.at[g], wib_s, wib_r)

    recv(WIN.at[pl.ds(0, 448)], wib_r)

    gather_pass(NTB, nt_s, nt_r, nt_p)

    def feed(i, carry):
        yy = lax.rem(y + i, 2)
        rows = rows_at(256 * yy, 256)
        for b in (2 * yy, 2 * yy + 1):
            gather_wait(NTB, nt_r, b)

        def hidden_units(n, inner):
            cols = rows_at(256 * n, 256)
            pre = dot_nn(NTB[rows, :], WIN[:, cols])
            cdf = 0.5 * (1.0 + lax.erf(pre * 0.7071067811865476))
            ACT[rows, cols] = (pre * cdf).astype(BF)
            SLOPE[rows, cols] = cdf + pre * jnp.exp(-0.5 * pre * pre) * 0.3989422804014327
            return inner

        return lax.fori_loop(0, 4, hidden_units, carry)

    lax.fori_loop(0, 2, feed, 0)

    for b in range(4):
        gather_wait(COT, co_r, b)

    def grad_down(m, carry):
        tile = dot_tn(ACT[:, rows_at(256 * m, 256)], COT[...]).astype(BF)
        DD[0, m] = tile[0:128]
        DD[1, m] = tile[128:256]
        return carry

    lax.fori_loop(0, 4, grad_down, 0)
    remote(DD.at[k1], SIBD, sib_s.at[0], sib_r.at[0], sib).start()

    @pl.when(at_end)
    def _():
        for t in others:
            take(down_piece(t, k), wdz_r.at[t], wdb_s, wdb_r)

    recv(WDOWN.at[pl.ds(0, 384)], wdb_r)

    recv(SIBD, sib_r.at[0])

    def join_down(m, carry):
        ZD[m] = (DD[k, m].astype(F32) + SIBD[m].astype(F32)).astype(BF)
        return carry

    lax.fori_loop(0, 4, join_down, 0)
    for t in zs:
        remote(ZD.at[t], RZD.at[z], zd_s, zd_r, zdev(t)).start()

    def back_feed(i, carry):
        yy = lax.rem(y1 + i, 2)
        rows = rows_at(256 * yy, 256)

        def back_act(n, inner):
            cols = rows_at(256 * n, 256)
            GPRE[rows, cols] = (dot_nt(COT[rows, :], WDOWN[cols, :]) * SLOPE[rows, cols]).astype(BF)
            return inner

        lax.fori_loop(0, 4, back_act, 0)

        def back_normed(n, inner):
            cols = rows_at(256 * n, 256)
            SG[rows, cols] = dot_nt(GPRE[rows, :], WIN[cols, :]).astype(BF)
            return inner

        lax.fori_loop(0, 4, back_normed, 0)
        scatter_send(SG, RG, g_s, g_r, 2 * yy)
        scatter_send(SG, RG, g_s, g_r, 2 * yy + 1)
        return carry

    lax.fori_loop(0, 2, back_feed, 0)

    def grad_in(m, carry):
        tile = dot_tn(NTB[:, rows_at(256 * m, 256)], GPRE[...]).astype(BF)
        for part in range(2):
            DI[0, 2 * m + part] = tile[128 * part : 128 * part + 64]
            DI[1, 2 * m + part] = tile[128 * part + 64 : 128 * part + 128]
        return carry

    lax.fori_loop(0, 4, grad_in, 0)
    remote(DI.at[k1], SIBI, sib_s.at[1], sib_r.at[1], sib).start()

    def down_project(n, carry):
        cols = rows_at(256 * n, 256)
        SO[:, cols] = dot_nn(ACT[...], WDOWN[:, cols]).astype(BF)
        return carry

    lax.fori_loop(0, 4, down_project, 0)

    recv(SIBI, sib_r.at[1])

    def join_in(m, carry):
        ZI[m] = (DI[k, m].astype(F32) + SIBI[m].astype(F32)).astype(BF)
        return carry

    lax.fori_loop(0, 8, join_in, 0)
    def in_rows(ref, t):
        return ref.at[pl.ds(2 * t, 2)]

    @pl.when(at_end)
    def _():
        for n in range(2):
            t = others[n]
            remote(in_rows(ZI, t), in_rows(REI, t), zie_s, zi_r.at[t], zdev(near)).start()

    recv(RG, g_r)

    def home_back(r, total):
        rows = rows_at(r * 32, 32)
        grad = RG[0, rows, :].astype(F32)
        for s in range(1, 4):
            grad = grad + RG[s, rows, :].astype(F32)
        hidden = HID[rows, :]
        scale = lax.rsqrt(jnp.mean(hidden * hidden, axis=-1, keepdims=True) + EPS)
        scaled = grad * gain_two
        inner = jnp.mean(scaled * hidden, axis=-1, keepdims=True)
        back = CO[rows, :].astype(F32) + scale * scaled - hidden * (scale * scale * scale * inner)
        GH[rows, :] = back
        GALS[rows, :] = back.astype(BF)
        return total + jnp.sum((grad * hidden * scale).reshape(4, 8, WIDTH), axis=0)

    mlp_gain_grad = lax.fori_loop(0, 4, home_back, jnp.zeros((8, WIDTH), F32))
    gather_send(GALS, GAL, ga_s, ga_r, ga_p)

    mlp_gain_grad = jnp.sum(mlp_gain_grad, axis=0, keepdims=True)
    for g in range(8):
        SMALL[1, g : g + 1, :] = mlp_gain_grad[:, 128 * g : 128 * g + 128]

    gather_pass(GAL, ga_s, ga_r, ga_p)

    def back_out(i, carry):
        b = lax.rem(2 * y + i, 4)
        rows = rows_at(b * TOKENS, TOKENS)
        gather_wait(GAL, ga_r, b)
        GATT[rows, :] = dot_nt(GAL[rows, :], WOUT[...]).astype(BF)
        return carry

    lax.fori_loop(0, 4, back_out, 0)
    for i in range(4):
        scatter_send(SO, RO, o_s, o_r, lax.rem(2 * y1 + i, 4))
    all_low = lax.broadcasted_iota(jnp.int32, (512, 128), 1) < 64

    def pick_all(values, hh):
        keep = all_low if hh == 0 else jnp.logical_not(all_low)
        return jnp.where(keep, values, jnp.zeros_like(values))

    def grad_values(j, carry):
        grad_att = GATT[:, rows_at(128 * j, 128)]
        first = dot_tn(PLOW[2 * j], pick_all(grad_att, 0))
        second = dot_tn(PLOW[2 * j + 1], pick_all(grad_att, 1))
        DQKV[:, pl.ds(pl.multiple_of(512 + 128 * j, 128), 128)] = jnp.where(all_low, first, second).astype(BF)
        return carry

    lax.fori_loop(0, 2, grad_values, 0)

    def grad_proj(first, width):
        def step(m, carry):
            tile = dot_tn(N1[:, rows_at(256 * m, 256)], DQKV[:, first : first + width]).astype(BF)
            for part in range(2):
                DQ[0, 2 * m + part, :, first : first + width] = tile[128 * part : 128 * part + 64]
                DQ[1, 2 * m + part, :, first : first + width] = tile[128 * part + 64 : 128 * part + 128]
            return carry

        lax.fori_loop(0, 4, step, 0)

    def join_proj(first, width):
        def step(m, carry):
            total = DQ[k, m, :, first : first + width].astype(F32) + SIBQ[m, :, first : first + width].astype(F32)
            ZQ[m, :, first : first + width] = total.astype(BF)
            return carry

        lax.fori_loop(0, 8, step, 0)

    value_cols, other_cols = pl.ds(512, 256), pl.ds(0, 512)
    grad_proj(512, 256)
    remote(DQ.at[k1, :, :, value_cols], SIBQ.at[:, :, value_cols], sib_s.at[2], sib_r.at[2], sib).start()

    def grad_out_rows(m, carry):
        DO[m] = dot_tn(AT[:, rows_at(128 * m, 128)], GAL[...]).astype(BF)
        return carry

    lax.fori_loop(0, 2, grad_out_rows, 0)
    remote(DO.at[k1], SIBO, sib_s.at[3], sib_r.at[3], sib).start()

    def z_scatter(cols, send, got):
        for t in zs:
            remote(
                ZQ.at[pl.ds(2 * t, 2), :, cols], RZQ.at[z, :, :, cols], send, got, zdev(t)
            ).start()

    recv(SIBQ.at[:, :, value_cols], sib_r.at[2])
    join_proj(512, 256)
    z_scatter(value_cols, zv_s, zv_r)

    recv(SIBO, sib_r.at[3])
    ZO[...] = (DO[k].astype(F32) + SIBO[...].astype(F32)).astype(BF)

    out_near = z // 2 == c // 2

    @pl.when((z != c) & out_near)
    def _():
        remote(ZO, RZO.at[0], zo_s, zo_r.at[0], zdev(c)).start()

    @pl.when(jnp.logical_not(out_near) & at_end)
    def _():
        remote(ZO, RZO.at[0], zo_s, zo_r.at[0], zdev(near)).start()

    remote(in_rows(ZI, near), in_rows(REI, near), zi_s, zi_r.at[near], zdev(near)).start()

    @pl.when(middle)
    def _():
        for n in range(2):
            t = others[n]
            recv(in_rows(REI, t), zi_r.at[t])
            for xx in range(2):
                ZI[2 * t + xx] = (ZI[2 * t + xx].astype(F32) + REI[2 * t + xx].astype(F32)).astype(BF)
            remote(in_rows(ZI, t), RCI, zie_s, zic_r, zdev(t)).start()

    def attend_back(i, carry):
        rows = rows_at(i * TOKENS, TOKENS)
        window = pl.ds(pl.multiple_of(384 - 128 * i, 128), 512)
        for j in range(2):
            pair = slice(128 * j, 128 * j + 128)
            keys = QKV[:, 256 + 128 * j : 384 + 128 * j]
            values = QKV[:, 512 + 128 * j : 640 + 128 * j]
            outs = []
            for hh in range(2):
                h = 2 * j + hh
                grad_att = pick(GATT[rows, pair], hh)
                probs = PROB[h, rows, :]
                grad_probs = dot_nt(grad_att, values)
                inner = jnp.sum(probs * grad_probs, axis=-1, keepdims=True)
                grad_scores = (probs * (grad_probs - inner)).astype(BF)
                DS[h, rows, :] = grad_scores
                BACC[h, :, window] = BACC[h, :, window] + grad_scores.astype(F32)
                outs.append(dot_nn(grad_scores, keys))
            DQKV[rows, pair] = jnp.where(low_lanes, outs[0], outs[1]).astype(BF)
        return carry

    lax.fori_loop(0, 4, attend_back, 0)

    def grad_keys(j, carry):
        query = QKV[:, rows_at(128 * j, 128)]
        first = dot_tn(DS[2 * j], pick_all(query, 0))
        second = dot_tn(DS[2 * j + 1], pick_all(query, 1))
        DQKV[:, pl.ds(pl.multiple_of(256 + 128 * j, 128), 128)] = jnp.where(all_low, first, second).astype(BF)
        return carry

    lax.fori_loop(0, 2, grad_keys, 0)

    grad_proj(0, 512)
    remote(DQ.at[k1, :, :, other_cols], SIBQ.at[:, :, other_cols], sib_s.at[4], sib_r.at[4], sib).start()
    def back_project(i, carry):
        yy = lax.rem(y1 + i, 2)
        rows = rows_at(256 * yy, 256)
        SN[rows, :] = dot_nt(DQKV[rows, :], WQKV[...]).astype(BF)
        scatter_send(SN, RN, n_s, n_r, 2 * yy)
        scatter_send(SN, RN, n_s, n_r, 2 * yy + 1)
        return carry

    lax.fori_loop(0, 2, back_project, 0)

    recv(SIBQ.at[:, :, other_cols], sib_r.at[4])
    join_proj(0, 512)
    z_scatter(other_cols, zq_s, zq_r)

    @pl.when(jnp.logical_not(out_near) & middle)
    def _():
        recv(RZO.at[0], zo_r.at[0])
        ZO[...] = (ZO[...].astype(F32) + RZO[0].astype(F32)).astype(BF)
        remote(ZO, RZO.at[1], zo_s, zo_r.at[1], zdev(c)).start()


    head_sums = []
    for h in range(4):
        rest = BACC[h]
        count = 64
        while count >= 8:
            rest = pltpu.roll(rest[0:count, :], count, 1) + rest[count : 2 * count, :]
            count //= 2
        for bit in (1, 2, 4):
            shift_row = 7 - lax.broadcasted_iota(jnp.int32, (8, WIDTH), 0)
            rest = jnp.where(lax.rem(lax.div(shift_row, bit), 2) == 1, pltpu.roll(rest, bit, 1), rest)
        head_sums.append(jnp.sum(rest, axis=0, keepdims=True))
    head_sums = jnp.concatenate(head_sums + [jnp.zeros((4, WIDTH), F32)], axis=0)
    coarse = head_sums.astype(BF)
    split_sums = jnp.concatenate([coarse, (head_sums - coarse.astype(F32)).astype(BF)], axis=0)
    both_masks = jnp.concatenate([head_mask.astype(F32)] * 2, axis=0) > 0.5

    def bucket_sums(g, carry):
        sums = dot_nt(split_sums, bucket_hot(g).astype(BF))
        SMALL[2, pl.ds(g, 1), :] = jnp.sum(jnp.where(both_masks, sums, 0.0), axis=0, keepdims=True)
        return carry

    lax.fori_loop(0, 8, bucket_sums, 0)

    recv(RZD.at[pl.ds(0, 3)], zd_r)
    total = ZD[z].astype(F32)
    for t in zs:
        total = total + RZD[t].astype(F32)
    FD[...] = total.astype(BF)

    def down_rows(cc):
        return odown.at[rows_at(128 * cc, 128)]

    y_core = (2 * y1 + k, f)
    four_sent(SN, n_s)
    remote(FD, down_rows(c), fd_s, fd_r.at[1], y_core).start()
    remote(FD, down_rows(c), fd_s, fd_r.at[2], sib).start()
    pltpu.make_async_copy(FD, down_rows(c), fd_r.at[0]).start()

    def spread(final, place, send, bsend, got, bgot):
        remote(final.at[x1], place(q, k), send, got.at[3], (2 * y1 + k, f1)).start()
        remote(final.at[x1], place(q, k), send, got.at[2], (c, f1)).start()
        remote(final.at[x], place(q, k), send, got.at[1], y_core).start()
        remote(final.at[x], place(q, k), bsend, bgot, sib).start()
        pltpu.make_async_copy(final.at[x], place(q, k), got.at[0]).start()

    chips = (2 * x + y1, 2 * x1 + y, 2 * x1 + y1)

    def spread_on(place, bsend, got, bgot):
        for i in range(3):
            piece = place(chips[i], k)
            recv(piece, got.at[i + 1])
            remote(piece, piece, bsend, bgot, sib).start()

    def in_place(qq, kk):
        return oin.at[:, qq, rows_at(64 * kk, 64), :]

    def proj_place(qq, kk):
        return oqkv.at[qq, rows_at(64 * kk, 64), :]

    recv(RO, o_r)

    def home_out(r, carry):
        rows = rows_at(r * 32, 32)
        result = HID[rows, :]
        for s in range(4):
            result = result + RO[s, rows, :].astype(F32)
        out_ref[0, rows, :] = result.astype(BF)
        return carry

    lax.fori_loop(0, 4, home_out, 0)
    recv(RN, n_r)

    def home_inputs(r, total):
        rows = rows_at(r * 32, 32)
        grad = RN[0, rows, :].astype(F32)
        for s in range(1, 4):
            grad = grad + RN[s, rows, :].astype(F32)
        values = XO[rows, :].astype(F32)
        scale = lax.rsqrt(jnp.mean(values * values, axis=-1, keepdims=True) + EPS)
        scaled = grad * gain_one
        inner = jnp.mean(scaled * values, axis=-1, keepdims=True)
        back = GH[rows, :] + scale * scaled - values * (scale * scale * scale * inner)
        gin_ref[0, rows, :] = back.astype(BF)
        return total + jnp.sum((grad * values * scale).reshape(4, 8, WIDTH), axis=0)

    attn_gain_grad = lax.fori_loop(0, 4, home_inputs, jnp.zeros((8, WIDTH), F32))
    attn_gain_grad = jnp.sum(attn_gain_grad, axis=0, keepdims=True)
    for g in range(8):
        SMALL[0, g : g + 1, :] = attn_gain_grad[:, 128 * g : 128 * g + 128]

    for i in range(4):
        ci = lax.rem(c + i, 4)
        for j, xj in enumerate((x, x1)):
            if i or j:
                remote(SMALL, RSMALL.at[2 * c + x], sp_s, sp_r, (ci, 2 * z + xj)).start()

    recv(in_rows(REI, z), zi_r.at[z])
    recv(RCI, zic_r)
    for xx in range(2):
        total = ZI[2 * z + xx].astype(F32) + REI[2 * z + xx].astype(F32) + RCI[xx].astype(F32)
        for j in range(4):
            FI[xx, j] = total[:, 256 * j : 256 * j + 256].astype(BF)
    spread(FI, in_place, fi_s, fib_s, fi_r, fib_r)

    recv(RZQ.at[pl.ds(0, 3), :, :, value_cols], zv_r)
    recv(RZQ.at[pl.ds(0, 3), :, :, other_cols], zq_r)
    for xx in range(2):
        total = ZQ[2 * z + xx].astype(F32)
        for t in zs:
            total = total + RZQ[t, xx].astype(F32)
        FQ[xx] = total.astype(BF)
    spread(FQ, proj_place, fq_s, fqb_s, fq_r, fqb_r)

    @pl.when(z == c)
    def _():
        for s in range(2):
            recv(RZO.at[s], zo_r.at[s])
        FO[...] = (ZO[...].astype(F32) + RZO[0].astype(F32) + RZO[1].astype(F32)).astype(BF)
        pltpu.make_async_copy(FO, oout, fo_r).start()
        remote(FO, oout, fo_s, fo_r, y_core).start()
        remote(FO, oout, fo_s, fo_r, sib).start()

    recv(RSMALL.at[pl.ds(0, 7)], sp_r)
    plane_sum = SMALL[...]
    for i in range(4):
        ci = lax.rem(c + i, 4)
        for j, xj in enumerate((x, x1)):
            if i or j:
                plane_sum = plane_sum + RSMALL[2 * ci + xj]
    for t in range(4):
        for n in range(3):
            pair = plane_sum[n, 2 * t : 2 * t + 2, :]
            PSMALL[t, n : n + 1, :] = jnp.where(x == 0, pair[0:1], pair[1:2])
    for t in zs:
        remote(PSMALL.at[t], RZSMALL.at[z], sz_s, sz_r, zdev(t)).start()

    y_rows = down_rows(2 * y1 + k)
    recv(y_rows, fd_r.at[1])
    remote(y_rows, y_rows, fd_s, fd_r.at[2], sib).start()
    spread_on(in_place, fib_s, fi_r, fib_r)
    spread_on(proj_place, fqb_s, fq_r, fqb_r)
    recv(oout, fo_r)
    out_on = (y != z // 2) & (k == lax.rem(z, 2))

    @pl.when(out_on)
    def _():
        remote(oout, oout, fo_s, fo_r, sib).start()

    recv(RZSMALL.at[pl.ds(0, 3)], sz_r)
    total = PSMALL[z]
    for t in zs:
        total = total + RZSMALL[t]
    small_ref[...] = total

    recv(down_rows(c), fd_r.at[0])
    recv(odown.at[pl.ds(0, 256)], fd_r.at[2])
    recv(in_place(q, k), fi_r.at[0])
    recv(oin.at[:, :, rows_at(64 * k1, 64), :], fib_r)
    recv(proj_place(q, k), fq_r.at[0])
    recv(oqkv.at[:, rows_at(64 * k1, 64), :], fqb_r)

    sent(pack_in, gpx_s)
    four_sent(XB, xb_s)
    four_sent(COT, co_s)
    four_sent(NTB, nt_s)
    four_sent(GAL, ga_s)
    four_sent(SA, a_s)
    four_sent(SG, g_s)
    four_sent(SO, o_s)
    sent(WQKV.at[half(f, k)], wx_s.at[0])
    sent(WIN.at[half(f, k)], wx_s.at[1])
    sent(WIN.at[pl.ds(0, 256)], wiz_s)
    sent(WDOWN.at[pl.ds(0, 256)], wdz_s)
    sent(WQKV.at[pl.ds(0, 448)], wqb_s)
    sent(WIN.at[pl.ds(0, 448)], wib_s)
    sent(WDOWN.at[pl.ds(0, 384)], wdb_s)
    sent(GP.at[pl.ds(0, 6)], gpz_s)
    sent(ZQ.at[pl.ds(0, 6), :, value_cols], zv_s)
    sent(ZQ.at[pl.ds(0, 6), :, other_cols], zq_s)
    sent(ZD.at[pl.ds(0, 3)], zd_s)
    sent(PSMALL.at[pl.ds(0, 3)], sz_s)
    sent(in_rows(ZI, near), zi_s)
    sent(ZI.at[pl.ds(0, 4)], zie_s)

    @pl.when(middle)
    def _():
        sent(WDOWN.at[pl.ds(0, 256)], wdf_s)
        sent(WQKV.at[pl.ds(0, 256)], wqf_s)
        sent(WIN.at[pl.ds(0, 256)], wif_s)

    @pl.when(z == c)
    def _():
        sent(WOUT, woz_s)
        sent(odown.at[pl.ds(0, 256)], fo_s)

    @pl.when(out_on)
    def _():
        sent(oout, fo_s)

    @pl.when(z != c)
    def _():
        sent(out_piece, wob_s)
        sent(ZO, zo_s)

        @pl.when(middle & (z // 2 != c // 2))
        def _():
            sent(out_piece, woz_s)

    sent(DD.at[k1], sib_s.at[0])
    sent(DI.at[k1], sib_s.at[1])
    sent(DQ.at[k1, :, :, value_cols], sib_s.at[2])
    sent(DO.at[k1], sib_s.at[3])
    sent(DQ.at[k1, :, :, other_cols], sib_s.at[4])
    sent(odown.at[pl.ds(0, 384)], fd_s)
    sent(oin.at[:, pl.ds(0, 3), pl.ds(0, 64), :], fi_s)
    sent(oqkv.at[pl.ds(0, 3), pl.ds(0, 64), :], fq_s)
    sent(oin.at[:, :, rows_at(64 * k, 64), :], fib_s)
    sent(oqkv.at[:, rows_at(64 * k, 64), :], fqb_s)
    sent(RSMALL.at[pl.ds(0, 7)], sp_s)


def plane_shards(
    inputs, cotangent, w_query, w_key, w_value, w_out, w_in, w_down, gain_attn, gain_mlp, rel_bias, buckets
):
    pack = jnp.concatenate(
        [
            gain_attn.astype(F32)[None],
            gain_mlp.astype(F32)[None],
            jnp.pad(rel_bias.astype(F32), (0, 64))[None],
            jnp.zeros((5, 128), F32),
        ],
        axis=0,
    )
    bucket_row = jnp.pad(buckets, (0, 1))[None]
    vm = pltpu.VMEM
    dma = pltpu.SemaphoreType.DMA
    block = lambda kind: vm((TOKENS, WIDTH), kind)
    tokens = lambda width, kind: vm((512, width), kind)
    scratch = [
        block(BF), block(BF), vm((8, 8, 128), F32),
        tokens(1024, BF), tokens(1024, BF), tokens(1024, BF), tokens(1024, BF), tokens(1024, BF),
        vm((1024, 768), BF), vm((256, 1024), BF), vm((1024, 1024), BF), vm((1024, 1024), BF),
        tokens(768, BF), vm((4, 512, 512), F32), vm((4, 512, 512), BF), vm((4, 128, 1024), F32),
        tokens(256, BF), tokens(1024, BF), tokens(1024, F32), tokens(1024, BF),
        tokens(256, BF), tokens(768, BF), vm((4, 512, 512), BF), vm((4, 128, 1024), F32),
        tokens(1024, BF), tokens(1024, BF), tokens(1024, BF), tokens(1024, BF),
        vm((4, 128, 1024), BF), vm((4, 128, 1024), BF), vm((4, 128, 1024), BF), vm((4, 128, 1024), BF),
        block(F32), block(F32), block(BF), block(BF),
        vm((2, 8, 64, 768), BF), vm((2, 128, 1024), BF), vm((2, 8, 64, 1024), BF), vm((2, 4, 128, 1024), BF),
        vm((8, 64, 768), BF), vm((128, 1024), BF), vm((8, 64, 1024), BF), vm((4, 128, 1024), BF),
        vm((8, 64, 768), BF), vm((128, 1024), BF), vm((8, 64, 1024), BF), vm((4, 128, 1024), BF),
        vm((4, 2, 64, 768), BF), vm((2, 128, 1024), BF), vm((8, 64, 1024), BF), vm((4, 128, 1024), BF),
        vm((2, 64, 1024), BF),
        vm((2, 64, 768), BF), vm((128, 1024), BF), vm((2, 4, 64, 256), BF), vm((128, 1024), BF),
        vm((3, 8, 128), F32), vm((8, 3, 8, 128), F32), vm((4, 8, 128), F32), vm((4, 8, 128), F32),
        dma((7,)), dma, dma, dma, dma, dma, dma((4,)), dma((2,)), dma, dma((4,)), dma((2,)), dma, dma((4,)), dma((2,)), dma, dma((4,)), dma((2,)),
        dma, dma, dma, dma, dma, dma, dma, dma,
        dma((2,)), dma((2,)), dma, dma, dma((8,)), dma, dma, dma, dma, dma((8,)), dma, dma,
        dma, dma, dma((4,)), dma, dma, dma, dma, dma, dma,
        dma((5,)), dma((5,)), dma, dma, dma, dma, dma, dma((2,)), dma, dma, dma((4,)), dma, dma, dma,
        dma, dma, dma((4,)), dma, dma, dma, dma, dma, dma((4,)), dma, dma, dma((3,)), dma, dma, dma, dma,
    ]
    anywhere = pl.BlockSpec(memory_space=pl.ANY)
    in_vmem = pl.BlockSpec(memory_space=pltpu.VMEM)
    shape = jax.ShapeDtypeStruct
    output, grad_inputs, proj, out, hidden, down, small = pl.pallas_call(
        fused_layer,
        out_shape=(
            shape((1, TOKENS, WIDTH), BF),
            shape((1, TOKENS, WIDTH), BF),
            shape((4, 128, 768), BF),
            shape((128, 1024), BF),
            shape((4, 4, 128, 256), BF),
            shape((512, 1024), BF),
            shape((8, 128), F32),
        ),
        in_specs=[anywhere] * 9 + [in_vmem],
        out_specs=(in_vmem, in_vmem, anywhere, anywhere, anywhere, anywhere, in_vmem),
        scratch_shapes=scratch,
        compiler_params=pltpu.CompilerParams(
            collective_id=0, has_side_effects=True, vmem_limit_bytes=63 << 20
        ),
        cost_estimate=pl.CostEstimate(flops=11 * 10**9, bytes_accessed=16 * 2**20, transcendentals=3 * 2**20),
    )(inputs, cotangent, w_query, w_key, w_value, w_out, w_in, w_down, pack, bucket_row)
    return finish(output, grad_inputs, proj, out, hidden, down, small)


def finish_kernel(
    output, grad_inputs, proj, out, hidden, down, small,
    o_output, o_inputs, o_query, o_key, o_value, o_out, o_in, o_down, o_attn, o_mlp, o_bias,
    b_output, b_inputs, b_proj, b_out, b_hidden, b_down, b_small, w_proj, w_out, w_in, w_down, got, left,
):
    moves = [
        pltpu.make_async_copy(proj, b_proj, got.at[0]),
        pltpu.make_async_copy(hidden, b_hidden, got.at[1]),
        pltpu.make_async_copy(down, b_down, got.at[2]),
        pltpu.make_async_copy(out, b_out, got.at[3]),
        pltpu.make_async_copy(small, b_small, got.at[4]),
        pltpu.make_async_copy(output, b_output, got.at[5]),
        pltpu.make_async_copy(grad_inputs, b_inputs, got.at[6]),
    ]
    for move in moves:
        move.start()
    sends = []

    def write(src, dst, slot):
        copy = pltpu.make_async_copy(src, dst, left.at[slot])
        copy.start()
        sends.append(copy)

    moves[0].wait()
    for w, place in enumerate((o_query, o_key, o_value)):
        for q in range(4):
            x, y = q // 2, q % 2
            for j in range(2):
                first = 512 * y + 256 * j + 128 * x
                w_proj[w, :, first : first + 128] = b_proj[q, :, 256 * w + 128 * j : 256 * w + 128 * j + 128].astype(F32)
        write(w_proj.at[w], place, w)
    moves[1].wait()
    for r in range(4):
        rows = slice(32 * r, 32 * r + 32)
        for z in range(4):
            for q in range(4):
                w_in[rows, 256 * (4 * z + q) : 256 * (4 * z + q) + 256] = b_hidden[z, q, rows, :].astype(F32)
        write(w_in.at[pl.ds(32 * r, 32)], o_in.at[pl.ds(32 * r, 32)], 3 + r)
    moves[2].wait()
    for r in range(4):
        rows = slice(128 * r, 128 * r + 128)
        w_down[rows, :] = b_down[rows, :].astype(F32)
        write(w_down.at[pl.ds(128 * r, 128)], o_down.at[pl.ds(128 * r, 128)], 7 + r)
    moves[3].wait()
    w_out[...] = b_out[...].astype(F32)
    write(w_out, o_out, 11)
    moves[4].wait()
    o_attn[...] = b_small[0:1, :]
    o_mlp[...] = b_small[1:2, :]
    o_bias[...] = b_small[2:3, 0:64]
    moves[5].wait()
    write(b_output, o_output, 12)
    moves[6].wait()
    write(b_inputs, o_inputs, 13)
    for copy in sends:
        copy.wait()


def finish(output, grad_inputs, proj, out, hidden, down, small):
    shape = jax.ShapeDtypeStruct
    vm = pltpu.VMEM
    anywhere = pl.BlockSpec(memory_space=pl.ANY)
    in_vmem = pl.BlockSpec(memory_space=pltpu.VMEM)
    results = pl.pallas_call(
        finish_kernel,
        out_shape=(
            shape(output.shape, BF),
            shape(grad_inputs.shape, BF),
            shape((128, 1024), F32),
            shape((128, 1024), F32),
            shape((128, 1024), F32),
            shape((128, 1024), F32),
            shape((128, 4096), F32),
            shape((512, 1024), F32),
            shape((1, 128), F32),
            shape((1, 128), F32),
            shape((1, 64), F32),
        ),
        in_specs=[anywhere] * 7,
        out_specs=(anywhere,) * 8 + (in_vmem,) * 3,
        scratch_shapes=[
            vm(output.shape, BF), vm(grad_inputs.shape, BF), vm(proj.shape, BF), vm(out.shape, BF), vm(hidden.shape, BF), vm(down.shape, BF), vm(small.shape, F32),
            vm((3, 128, 1024), F32), vm((128, 1024), F32), vm((128, 4096), F32), vm((512, 1024), F32),
            pltpu.SemaphoreType.DMA((7,)), pltpu.SemaphoreType.DMA((14,)),
        ],
        compiler_params=pltpu.CompilerParams(vmem_limit_bytes=63 << 20),
        cost_estimate=pl.CostEstimate(flops=0, bytes_accessed=10 * 2**20, transcendentals=0),
    )(output, grad_inputs, proj, out, hidden, down, small)
    return results[:8] + (results[8].reshape(128), results[9].reshape(128), results[10].reshape(64))


def solution(mesh):
    placed = (
        P("fsdp", "ctx", None),
        P("fsdp", "ctx", None),
        P("fsdp", None),
        P("fsdp", None),
        P("fsdp", None),
        P("fsdp", None),
        P("fsdp", None),
        P("fsdp", None),
        P("fsdp"),
        P("fsdp"),
        P("fsdp"),
        P(),
    )
    by_planes = mesh.shape["ctx"] == 4 and mesh.shape["fsdp"] == 8
    return jax.shard_map(
        plane_shards if by_planes else shards,
        mesh=mesh,
        in_specs=placed,
        out_specs=(
            P("fsdp", "ctx", None),
            P("fsdp", "ctx", None),
            P("fsdp", None),
            P("fsdp", None),
            P("fsdp", None),
            P("fsdp", None),
            P("fsdp", None),
            P("fsdp", None),
            P("fsdp"),
            P("fsdp"),
            P("fsdp"),
        ),
        check_vma=False,
    )
```

```python
import jax
import jax.numpy as jnp
from jax import lax
from jax.experimental import pallas as pl
from jax.experimental.pallas import tpu as pltpu
from jax.sharding import PartitionSpec as P

HEADS = 16
HEAD = 64
BUCKETS = 32


EPS = 1e-06


def norm_rows(values, gain):
    return values * lax.rsqrt(jnp.mean(values * values, axis=-1, keepdims=True) + EPS) * gain


def smooth_gelu(values):
    return 0.5 * values * (1.0 + jax.scipy.special.erf(values * 0.7071067811865476))


def gelu_slope(values):
    return (
        0.5 * (1.0 + jax.scipy.special.erf(values * 0.7071067811865476))
        + values * jnp.exp(-0.5 * values * values) * 0.3989422804014327
    )


def bucket_offsets(buckets, first_query, query_count):
    seq_length = (buckets.shape[0] + 1) // 2
    key_place = jnp.arange(seq_length, dtype=jnp.int32)
    query_place = first_query + jnp.arange(query_count, dtype=jnp.int32)
    return key_place[None, :] - query_place[:, None] + (seq_length - 1)


def make_bias(flat_table, buckets, first_query, query_count):
    bias_table = flat_table.reshape(BUCKETS, HEADS)
    one_hot = (buckets[:, None] == jnp.arange(BUCKETS, dtype=jnp.int32)[None, :]).astype(
        flat_table.dtype
    )
    per_offset = jnp.dot(one_hot, bias_table, precision=lax.Precision.HIGHEST)
    offsets = bucket_offsets(buckets, first_query, query_count)
    return jnp.take(per_offset.T, offsets, axis=1)


def pair_table(buckets, first_query, query_count):
    offsets = bucket_offsets(buckets, first_query, query_count)
    pair_bucket = jnp.take(buckets, offsets.reshape(-1), axis=0)
    return (pair_bucket[:, None] == jnp.arange(BUCKETS, dtype=jnp.int32)[None, :]).astype(
        jnp.bfloat16
    )


def fetch_attention(w_query, w_key, w_value, w_out, gain_attn, rel_bias):
    return (
        lax.all_gather(w_query, "fsdp", axis=0, tiled=True),
        lax.all_gather(w_key, "fsdp", axis=0, tiled=True),
        lax.all_gather(w_value, "fsdp", axis=0, tiled=True),
        lax.all_gather(w_out, "fsdp", axis=0, tiled=True),
        lax.all_gather(gain_attn, "fsdp", axis=0, tiled=True),
        lax.all_gather(rel_bias, "fsdp", axis=0, tiled=True),
    )


def fetch_mlp(w_in, w_down, gain_mlp):
    return (
        lax.all_gather(w_in, "fsdp", axis=0, tiled=True),
        lax.all_gather(w_down, "fsdp", axis=0, tiled=True),
        lax.all_gather(gain_mlp, "fsdp", axis=0, tiled=True),
    )


def share_keys(key_rows, value_rows):
    return (
        lax.all_gather(key_rows, "ctx", axis=1, tiled=True),
        lax.all_gather(value_rows, "ctx", axis=1, tiled=True),
    )


def scores_of(query_part, key_part, bias_values):
    return (
        jnp.einsum("qhd,khd->hqk", query_part, key_part, preferred_element_type=jnp.float32)
        + bias_values
    )


def shards(
    inputs,
    cotangent,
    w_query,
    w_key,
    w_value,
    w_out,
    w_in,
    w_down,
    gain_attn,
    gain_mlp,
    rel_bias,
    buckets,
):
    seq_count, row_count, width = inputs.shape
    total_rows = seq_count * row_count
    first_query = lax.axis_index("ctx") * row_count
    query_w, key_w, value_w, out_w, attn_gain, bias_flat = fetch_attention(
        w_query, w_key, w_value, w_out, gain_attn, rel_bias
    )
    in_w, down_w, mlp_gain = fetch_mlp(w_in, w_down, gain_mlp)
    bias_values = make_bias(bias_flat.astype(jnp.float32), buckets, first_query, row_count)
    inputs_flat = inputs.astype(jnp.float32).reshape(total_rows, width)
    attn_scale = attn_gain.astype(jnp.float32)
    normed_one = norm_rows(inputs_flat, attn_scale).astype(jnp.bfloat16)
    query_rows = jnp.dot(normed_one, query_w, preferred_element_type=jnp.float32).astype(
        jnp.bfloat16
    )
    key_rows = (
        jnp.dot(normed_one, key_w, preferred_element_type=jnp.float32)
        .astype(jnp.bfloat16)
        .reshape(seq_count, row_count, width)
    )
    value_rows = (
        jnp.dot(normed_one, value_w, preferred_element_type=jnp.float32)
        .astype(jnp.bfloat16)
        .reshape(seq_count, row_count, width)
    )
    all_keys, all_values = share_keys(key_rows, value_rows)
    query_heads = query_rows.reshape(seq_count, row_count, HEADS, HEAD)
    seq_index = 0
    key_heads = all_keys[seq_index].reshape(-1, HEADS, HEAD)
    value_heads = all_values[seq_index].reshape(-1, HEADS, HEAD)
    scores = scores_of(query_heads[seq_index], key_heads, bias_values)
    top_score = jnp.max(scores, axis=-1, keepdims=True)
    weights_exp = jnp.exp(scores - top_score)
    totals = jnp.sum(weights_exp, axis=-1, keepdims=True)
    probs_low = (weights_exp / totals).astype(jnp.bfloat16)
    mixed = jnp.einsum("hqk,khd->qhd", probs_low, value_heads, preferred_element_type=jnp.float32)
    mixed_list = mixed.reshape(row_count, width)
    lse_list = [top_score + jnp.log(totals)]
    attended = mixed_list.astype(jnp.bfloat16)
    hidden_res = inputs_flat + jnp.dot(attended, out_w, preferred_element_type=jnp.float32)
    mlp_scale = mlp_gain.astype(jnp.float32)
    normed_two = norm_rows(hidden_res, mlp_scale).astype(jnp.bfloat16)
    pre_act = jnp.dot(normed_two, in_w, preferred_element_type=jnp.float32)
    activated = smooth_gelu(pre_act).astype(jnp.bfloat16)
    result = hidden_res + jnp.dot(activated, down_w, preferred_element_type=jnp.float32)
    in_w, down_w, mlp_gain = fetch_mlp(w_in, w_down, gain_mlp)
    query_w, key_w, value_w, out_w, attn_gain, bias_flat = fetch_attention(
        w_query, w_key, w_value, w_out, gain_attn, rel_bias
    )
    all_keys, all_values = share_keys(key_rows, value_rows)
    grad_rows = cotangent.reshape(total_rows, width)
    grad_down = jnp.einsum("nf,nd->fd", activated, grad_rows, preferred_element_type=jnp.float32)
    grad_act = jnp.einsum("nd,fd->nf", grad_rows, down_w, preferred_element_type=jnp.float32)
    grad_pre = (grad_act * gelu_slope(pre_act)).astype(jnp.bfloat16)
    grad_in = jnp.einsum("nd,nf->df", normed_two, grad_pre, preferred_element_type=jnp.float32)
    grad_normed_two = jnp.einsum("nf,df->nd", grad_pre, in_w, preferred_element_type=jnp.float32)
    back_hidden, grad_mlp_gain = jax.vjp(norm_rows, hidden_res, mlp_scale)[1](grad_normed_two)
    grad_hidden = grad_rows.astype(jnp.float32) + back_hidden
    grad_attn_low = grad_hidden.astype(jnp.bfloat16)
    grad_out = jnp.einsum("nd,ne->de", attended, grad_attn_low, preferred_element_type=jnp.float32)
    grad_attended = jnp.einsum(
        "ne,de->nd", grad_attn_low, out_w, preferred_element_type=jnp.float32
    ).astype(jnp.bfloat16)
    grad_heads = grad_attended.reshape(seq_count, row_count, HEADS, HEAD)
    pair_buckets = pair_table(buckets, first_query, row_count)
    seq_index = 0
    key_heads = all_keys[seq_index].reshape(-1, HEADS, HEAD)
    value_heads = all_values[seq_index].reshape(-1, HEADS, HEAD)
    scores = scores_of(query_heads[seq_index], key_heads, bias_values)
    probs = jnp.exp(scores - lse_list[seq_index])
    grad_probs = jnp.einsum(
        "qhd,khd->hqk", grad_heads[seq_index], value_heads, preferred_element_type=jnp.float32
    )
    row_inner = jnp.sum(probs * grad_probs, axis=-1, keepdims=True)
    grad_scores = (probs * (grad_probs - row_inner)).astype(jnp.bfloat16)
    bias_grad = jnp.dot(
        grad_scores.reshape(HEADS, -1), pair_buckets, preferred_element_type=jnp.float32
    )
    query_grads = jnp.einsum(
        "hqk,khd->qhd", grad_scores, key_heads, preferred_element_type=jnp.float32
    ).reshape(row_count, width)
    key_grads = [
        jnp.einsum(
            "hqk,qhd->khd", grad_scores, query_heads[seq_index], preferred_element_type=jnp.float32
        ).reshape(-1, width)
    ]
    value_grads = [
        jnp.einsum(
            "hqk,qhd->khd",
            probs.astype(jnp.bfloat16),
            grad_heads[seq_index],
            preferred_element_type=jnp.float32,
        ).reshape(-1, width)
    ]
    key_back, value_back = (
        lax.psum_scatter(
            jnp.stack(key_grads).astype(jnp.bfloat16), "ctx", scatter_dimension=1, tiled=True
        ).astype(jnp.float32),
        lax.psum_scatter(
            jnp.stack(value_grads).astype(jnp.bfloat16), "ctx", scatter_dimension=1, tiled=True
        ).astype(jnp.float32),
    )
    grad_query_rows = query_grads.astype(jnp.bfloat16)
    grad_key_rows = key_back.reshape(total_rows, width).astype(jnp.bfloat16)
    grad_value_rows = value_back.reshape(total_rows, width).astype(jnp.bfloat16)
    grad_query = jnp.einsum(
        "nd,ne->de", normed_one, grad_query_rows, preferred_element_type=jnp.float32
    )
    grad_key = jnp.einsum(
        "nd,ne->de", normed_one, grad_key_rows, preferred_element_type=jnp.float32
    )
    grad_value = jnp.einsum(
        "nd,ne->de", normed_one, grad_value_rows, preferred_element_type=jnp.float32
    )
    grad_normed_one = jnp.einsum(
        "ne,de->nd", grad_query_rows, query_w, preferred_element_type=jnp.float32
    )
    grad_normed_one = grad_normed_one + jnp.einsum(
        "ne,de->nd", grad_key_rows, key_w, preferred_element_type=jnp.float32
    )
    grad_normed_one = grad_normed_one + jnp.einsum(
        "ne,de->nd", grad_value_rows, value_w, preferred_element_type=jnp.float32
    )
    back_inputs, grad_attn_gain = jax.vjp(norm_rows, inputs_flat, attn_scale)[1](grad_normed_one)
    grad_inputs = (
        (grad_hidden + back_inputs).astype(jnp.bfloat16).reshape(seq_count, row_count, width)
    )
    grad_bias_flat = bias_grad.T.reshape(BUCKETS * HEADS)
    (
        part_query,
        part_key,
        part_value,
        part_out,
        part_in,
        part_down,
        part_attn_gain,
        part_mlp_gain,
        part_bias,
    ) = (
        lax.psum_scatter(grad_query, "fsdp", scatter_dimension=0, tiled=True),
        lax.psum_scatter(grad_key, "fsdp", scatter_dimension=0, tiled=True),
        lax.psum_scatter(grad_value, "fsdp", scatter_dimension=0, tiled=True),
        lax.psum_scatter(grad_out, "fsdp", scatter_dimension=0, tiled=True),
        lax.psum_scatter(grad_in, "fsdp", scatter_dimension=0, tiled=True),
        lax.psum_scatter(grad_down, "fsdp", scatter_dimension=0, tiled=True),
        lax.psum_scatter(grad_attn_gain, "fsdp", scatter_dimension=0, tiled=True),
        lax.psum_scatter(grad_mlp_gain, "fsdp", scatter_dimension=0, tiled=True),
        lax.psum_scatter(grad_bias_flat, "fsdp", scatter_dimension=0, tiled=True),
    )
    summed = (
        lax.psum(part_query.astype(jnp.bfloat16), "ctx").astype(jnp.float32),
        lax.psum(part_key.astype(jnp.bfloat16), "ctx").astype(jnp.float32),
        lax.psum(part_value.astype(jnp.bfloat16), "ctx").astype(jnp.float32),
        lax.psum(part_out.astype(jnp.bfloat16), "ctx").astype(jnp.float32),
        lax.psum(part_in.astype(jnp.bfloat16), "ctx").astype(jnp.float32),
        lax.psum(part_down.astype(jnp.bfloat16), "ctx").astype(jnp.float32),
        lax.psum(part_attn_gain.astype(jnp.bfloat16), "ctx").astype(jnp.float32),
        lax.psum(part_mlp_gain.astype(jnp.bfloat16), "ctx").astype(jnp.float32),
        lax.psum(part_bias.astype(jnp.bfloat16), "ctx").astype(jnp.float32),
    )
    output = result.astype(jnp.bfloat16).reshape(seq_count, row_count, width)
    return (
        output,
        grad_inputs,
        summed[0],
        summed[1],
        summed[2],
        summed[3],
        summed[4],
        summed[5],
        summed[6],
        summed[7],
        summed[8],
    )


MESH_ID = pl.DeviceIdType.MESH
BF = jnp.bfloat16
F32 = jnp.float32
WIDTH = 1024
TOKENS = 128
NT_DIMS = (((1,), (1,)), ((), ()))
TN_DIMS = (((0,), (0,)), ((), ()))


def dot_nn(left, right):
    return jnp.dot(left, right, preferred_element_type=F32)


def dot_nt(left, right):
    return lax.dot_general(left, right, NT_DIMS, preferred_element_type=F32)


def dot_tn(left, right):
    return lax.dot_general(left, right, TN_DIMS, preferred_element_type=F32)


def rows_at(start, count):
    return pl.ds(pl.multiple_of(start, count), count)


def remote(src, dst, send, recv, device):
    return pltpu.make_async_remote_copy(
        src_ref=src, dst_ref=dst, send_sem=send, recv_sem=recv, device_id=device, device_id_type=MESH_ID
    )


def fused_layer(
    x_in, cot_in, wq_in, wk_in, wv_in, wo_in, wi_in, wd_in, attn_in, mlp_in, table_in, bucket_in,
    out_ref, gin_ref, oqkv, oout, oin, odown, small_ref,
    XO, CO, PACK, BUCKET, STAGE, ACROSS, GP, XB, COT, N1, NTB, GAL, WQKV, WOUT, WIN, WDOWN,
    QKV, PROB, PLOW, BIAS, AT, ACT, SLOPE, GPRE, GATT, DQKV, DS, BACC,
    SA, SG, SO, SN, RA, RG, RO, RN, HID, GH, NTS, GALS,
    DQ, DO, DI, DD, SIBQ, SIBO, SIBI, SIBD, ZQ, ZO, ZI, ZD, REQ, REO, REI, RED, RCQ, RCO, RCI, RCD, FQ, FO, FI, FD,
    SMALL, RSMALL, PSMALL, RZSMALL,
    loc, gp_s, gp_r, xb_s, xb_r, xb_p, co_s, co_r, co_p, nt_s, nt_r, nt_p, ga_s, ga_r, ga_p,
    a_s, a_r, g_s, g_r, o_s, o_r, n_s, n_r,
    wx_s, wx_r, wqz_s, wqf_s, wqz_r, wqb_s, wqb_r, wiz_s, wif_s, wiz_r, wib_s, wib_r,
    wdz_s, wdf_s, wdz_r, wdb_s, wdb_r, woz_s, woz_r, wob_s, wob_r,
    sib_s, sib_r, sibd_r, zq_s, zqe_s, zq_r, zqc_r, zv_s, zve_s, zv_r, zvc_r, zo_s, zoe_s, zo_r, zoc_r,
    zi_s, zie_s, zi_r, zic_r, zd_s, zde_s, zd_r, zdc_r,
    fq_s, fqb_s, fq_r, fqb_r, fo_s, fo_r, fi_s, fib_s, fi_r, fib_r, fd_s, fd_r, sp_s, sp_r, sz_s, sz_r,
):
    c = lax.axis_index("ctx")
    f = lax.axis_index("fsdp")
    y, k = c // 2, lax.rem(c, 2)
    z, x = f // 2, lax.rem(f, 2)
    x1, y1, k1 = 1 - x, 1 - y, 1 - k
    f1 = 2 * z + x1
    q = 2 * x + y
    sib = (2 * y + k1, f)
    xdev = (c, f1)
    zs = [lax.rem(z + d, 4) for d in (1, 2, 3)]
    near = z + 1 - 2 * lax.rem(z, 2)
    other = 2 - 2 * (z // 2)
    others = (other, other + 1)
    far = 2 - z // 2
    middle = (z == 1) | (z == 2)
    at_end = jnp.logical_not(middle)

    def zdev(target):
        return (c, 2 * target + x)

    plane = []
    for i in range(4):
        ci = lax.rem(c + i, 4)
        for j, xj in enumerate((x, x1)):
            if i or j:
                plane.append((ci, 2 * z + xj))

    def recv(dst, sem):
        remote(dst, dst, sem, sem, sib).wait_recv()

    def sent(src, sem):
        remote(src, src, sem, sem, sib).wait_send()

    def block_half(buf, b, h):
        return buf.at[rows_at(b * TOKENS + 64 * h, 64)]

    def gather_send(src, dst, send, got, passed):
        halves = [src.at[pl.ds(64 * h, 64)] for h in range(2)]
        places = [block_half(dst, c, h) for h in range(2)]
        x_worker, y_worker = (2 * y + x, f1), (2 * y1 + x, f)
        remote(halves[0], places[0], send, passed.at[k], x_worker).start()
        remote(halves[1], places[1], send, passed.at[k], y_worker).start()
        remote(halves[1], places[1], send, got.at[c], x_worker).start()
        remote(halves[0], places[0], send, got.at[c], y_worker).start()
        whole = dst.at[rows_at(c * TOKENS, TOKENS)]

        @pl.when(k == x)
        def _():
            pltpu.make_async_copy(src, whole, got.at[c]).start()

        @pl.when(k != x)
        def _():
            remote(src, whole, send, got.at[c], sib).start()

    same = 1 - lax.rem(x + k, 2)
    pass_y = y + same * (1 - 2 * y)
    pass_to = (same * c + (1 - same) * (2 * y1 + k), same * f1 + (1 - same) * f)

    def gather_pass(dst, send, got, passed):
        for i in range(2):
            b = 2 * pass_y + i
            piece = block_half(dst, b, same)
            recv(piece, passed.at[i])
            remote(piece, piece, send, got.at[b], pass_to).start()

    def gather_wait(dst, got, b):
        @pl.when(b // 2 == pass_y)
        def _():
            recv(block_half(dst, b, 1 - same), got.at[b])

        @pl.when(b // 2 != pass_y)
        def _():
            recv(dst.at[rows_at(b * TOKENS, TOKENS)], got.at[b])

    def four_sent(buf, send):
        @pl.when(k == x)
        def _():
            sent(buf.at[pl.ds(0, 384)], send)

        @pl.when(k != x)
        def _():
            sent(buf, send)

    def scatter_send(buf, dst, send, got, b):
        src = buf.at[rows_at(b * TOKENS, TOKENS)]
        here = (b == c) & (x == k)

        @pl.when(here)
        def _():
            pltpu.make_async_copy(src, dst.at[q], got).start()

        @pl.when(jnp.logical_not(here))
        def _():
            remote(src, dst.at[q], send, got, (b, 2 * z + k)).start()

    def half(fb, kk):
        return rows_at(fb * 128 + kk * 64, 64)

    def z_far(piece, send, got, src=None):
        remote(piece if src is None else src, piece, send, got, zdev(far)).start()

    def z_near(piece, send, got, src=None):
        remote(piece if src is None else src, piece, send, got, zdev(near)).start()

    def z_send(piece, send, got):
        z_far(piece, send, got)
        z_near(piece, send, got)

    def down_of(ref, t):
        return ref.at[t]

    def in_of(ref, t):
        return ref.at[pl.ds(2 * t, 2)]

    def value_of(ref, t):
        return ref.at[pl.ds(2 * t, 2), :, value_cols]

    def other_of(ref, t):
        return ref.at[pl.ds(2 * t, 2), :, other_cols]

    value_cols, other_cols = pl.ds(512, 256), pl.ds(0, 512)

    def reduce_others(of, terms, got, send, sem):
        @pl.when(at_end)
        def _():
            for t in others:
                remote(of(terms, t), of(got, t), send, sem.at[t], zdev(near)).start()

    def reduce_near(of, terms, got, send, sem):
        remote(of(terms, near), of(got, near), send, sem.at[near], zdev(near)).start()

    def reduce_middle(of, terms, got, final, send, sem, final_sem):
        @pl.when(middle)
        def _():
            for t in others:
                recv(of(got, t), sem.at[t])
                mine = of(terms, t)
                mine[...] = (mine[...].astype(F32) + of(got, t)[...].astype(F32)).astype(BF)
                remote(mine, final, send, final_sem, zdev(t)).start()

    def take(piece, got, bsend, bgot):
        recv(piece, got)
        remote(piece, piece, bsend, bgot, sib).start()

    def pass_on(piece, send, got):
        remote(piece, piece, send, got, zdev(near)).start()

    def of_row(t, xx):
        return 2 * t + xx

    own_x = pltpu.make_async_copy(x_in.at[0], XO, loc.at[0])
    own_c = pltpu.make_async_copy(cot_in.at[0], CO, loc.at[1])
    myrows = pl.ds(pl.multiple_of(128 * f, 128), 128)
    for w, proj in enumerate((wq_in, wk_in, wv_in)):
        pltpu.make_async_copy(proj, STAGE.at[w], loc.at[3]).start()
    for j in range(4):
        src = wi_in.at[:, pl.ds(pl.multiple_of(512 * (2 * j + x) + 256 * y, 256), 256)]
        pltpu.make_async_copy(src, WIN.at[myrows, pl.ds(256 * j, 256)], loc.at[4]).start()
    pltpu.make_async_copy(
        wd_in.at[rows_at(256 * y, 256)], WDOWN.at[rows_at(256 * z, 256)], loc.at[5]
    ).start()

    pltpu.make_async_copy(wo_in.at[rows_at(64 * y, 64)], WOUT.at[rows_at(64 * z, 64)], loc.at[6]).start()
    own_x.start()
    own_c.start()

    barrier = pltpu.get_barrier_semaphore()
    across = [(c, 2 * t + x1) for t in zs]
    for device in plane + [zdev(t) for t in zs] + across:
        pl.semaphore_signal(barrier, inc=1, device_id=device, device_id_type=MESH_ID)


    PACK[...] = jnp.zeros((8, 128), F32)
    PACK[0:1, :] = attn_in[...].astype(F32)
    PACK[1:2, :] = mlp_in[...].astype(F32)
    PACK[2:3, 0:64] = table_in[...].astype(F32)
    BUCKET[...] = jnp.full((1, WIDTH), -1, jnp.int32)
    BUCKET[0:1, 0 : WIDTH - 1] = bucket_in[...]
    GP[f] = PACK[...]

    pltpu.make_async_copy(STAGE, STAGE, loc.at[3]).wait()

    def pack_heads(dst, dst_rows, src_rows, xx, count):
        low = lax.broadcasted_iota(jnp.int32, (count, 128), 1) < 64
        for w in range(3):
            for j in range(2):
                first, second = [
                    STAGE[w, src_rows, pl.ds(pl.multiple_of(128 * (4 * j + 2 * n + xx), 128), 128)].astype(F32)
                    for n in range(2)
                ]
                left = jnp.where(y == 0, first, pltpu.roll(first, 64, 1))
                right = jnp.where(y == 0, pltpu.roll(second, 64, 1), second)
                dst[dst_rows, 256 * w + 128 * j : 256 * w + 128 * j + 128] = jnp.where(low, left, right).astype(BF)

    pack_heads(ACROSS, slice(0, 64), rows_at(64 * k, 64), x1, 64)
    pack_heads(WQKV, myrows, slice(0, 128), x, 128)
    pl.semaphore_wait(barrier, 13)
    for device in [xdev] + [zdev(t) for t in zs] + across:
        remote(PACK, GP.at[f], gp_s, gp_r, device).start()
    remote(ACROSS, WQKV.at[half(f, k)], wx_s.at[0], wx_r.at[0], xdev).start()
    z_send(WQKV.at[half(f, k)], wqz_s, wqz_r.at[f])
    gather_send(x_in.at[0], XB, xb_s, xb_r, xb_p)
    for j in range(4):
        src = wi_in.at[rows_at(64 * k, 64), pl.ds(pl.multiple_of(512 * (2 * j + x1) + 256 * y, 256), 256)]
        remote(src, WIN.at[half(f, k), pl.ds(256 * j, 256)], wx_s.at[1], wx_r.at[1], xdev).start()

    recv(WQKV.at[half(f1, k)], wx_r.at[0])
    z_send(WQKV.at[half(f1, k)], wqz_s, wqz_r.at[f1])
    remote(WQKV.at[half(f1, k)], WQKV.at[half(f1, k)], wqb_s, wqb_r, sib).start()
    down_half = rows_at(256 * z + 128 * k, 128)
    pltpu.make_async_copy(WIN.at[myrows], WIN.at[myrows], loc.at[4]).wait()

    def out_piece(t):
        return WOUT.at[rows_at(64 * t + 32 * k, 32)]

    out_own = wo_in.at[rows_at(64 * y + 32 * k, 32)]
    z_far(out_piece(z), woz_s, woz_r.at[z], out_own)

    @pl.when(at_end)
    def _():
        z_near(out_piece(z), woz_s, woz_r.at[z], out_own)

    z_far(WIN.at[half(f, k)], wiz_s, wiz_r.at[f])

    @pl.when(at_end)
    def _():
        z_near(WIN.at[half(f, k)], wiz_s, wiz_r.at[f])

    def take_proj(xx):
        for n in range(2):
            h = of_row(others[n], xx)
            piece = WQKV.at[half(h, k)]
            recv(piece, wqz_r.at[h])

            @pl.when(middle)
            def _():
                pass_on(piece, wqf_s, wqz_r.at[h])

            remote(piece, piece, wqb_s, wqb_r, sib).start()

    def take_near(xx):
        g = of_row(near, xx)
        take(WQKV.at[half(g, k)], wqz_r.at[g], wqb_s, wqb_r)

    @pl.when(middle)
    def _():
        take_proj(x)

    gather_pass(XB, xb_s, xb_r, xb_p)
    gather_send(cot_in.at[0], COT, co_s, co_r, co_p)
    take_near(x)

    @pl.when(middle)
    def _():
        take_proj(x1)
        take_near(x1)

        z_near(out_piece(z), woz_s, woz_r.at[z], out_own)

    recv(GP.at[pl.ds(0, 7)], gp_r)

    def row_of(index):
        return jnp.concatenate([GP[g, index : index + 1, :] for g in range(8)], axis=1)

    lane = lax.broadcasted_iota(jnp.int32, (8, 128), 1)
    head_row = lax.broadcasted_iota(jnp.int32, (8, 128), 0)
    head_of = 4 * head_row + 2 * x + y
    head_mask = (lax.rem(lane, 16) == head_of) & (head_row < 4)

    def bucket_hot(g):
        index = lax.broadcasted_iota(jnp.int32, (128, WIDTH), 0)
        wanted = jnp.where(index < 64, 4 * g + lax.div(index, 16), -1)
        return (BUCKET[0:1, :] == wanted)

    def add_bias(g, total):
        table = jnp.where(head_mask, jnp.broadcast_to(GP[g, 2:3, :], (8, 128)), 0.0).astype(BF)
        return total + dot_nn(table, bucket_hot(g).astype(BF))

    offsets = lax.fori_loop(0, 8, add_bias, jnp.zeros((8, WIDTH), F32))
    for h in range(4):
        spread = jnp.broadcast_to(offsets[h : h + 1, :], (128, WIDTH))
        BIAS[h] = pltpu.roll(spread, WIDTH - 127, 1, stride=1, stride_axis=0)
        BACC[h] = jnp.zeros((128, WIDTH), F32)

    gain_one = row_of(0)

    def norm_block(i, carry):
        b = lax.rem(2 * y + i, 4)
        gather_wait(XB, xb_r, b)

        def chunk(r, inner):
            rows = rows_at(b * TOKENS + r * 32, 32)
            values = XB[rows, :].astype(F32)
            scale = lax.rsqrt(jnp.mean(values * values, axis=-1, keepdims=True) + EPS)
            N1[rows, :] = (values * scale * gain_one).astype(BF)
            return inner

        return lax.fori_loop(0, 4, chunk, carry)

    lax.fori_loop(0, 4, norm_block, 0)

    @pl.when(middle)
    def _():
        for t in others:
            recv(out_piece(t), woz_r.at[t])
            pass_on(out_piece(t), woz_s, woz_r.at[t])
            remote(out_piece(t), out_piece(t), wob_s, wob_r, sib).start()

        z_near(WIN.at[half(f, k)], wiz_s, wiz_r.at[f])

    recv(WIN.at[half(f1, k)], wx_r.at[1])
    z_far(WIN.at[half(f1, k)], wiz_s, wiz_r.at[f1])
    remote(WIN.at[half(f1, k)], WIN.at[half(f1, k)], wib_s, wib_r, sib).start()
    pltpu.make_async_copy(WDOWN.at[rows_at(256 * z, 256)], WDOWN.at[rows_at(256 * z, 256)], loc.at[5]).wait()
    z_far(WDOWN.at[down_half], wdz_s, wdz_r.at[z])

    z_near(WIN.at[half(f1, k)], wiz_s, wiz_r.at[f1])

    @pl.when(at_end)
    def _():
        z_near(WDOWN.at[down_half], wdz_s, wdz_r.at[z])
        take_near(x1)
        take_proj(x)
        take_proj(x1)

    recv(WQKV.at[pl.ds(0, 448)], wqb_r)

    def project(n, carry):
        cols = rows_at(256 * n, 256)
        QKV[:, cols] = dot_nn(N1[...], WQKV[:, cols]).astype(BF)
        return carry

    lax.fori_loop(0, 3, project, 0)


    gather_pass(COT, co_s, co_r, co_p)

    @pl.when(middle)
    def _():
        z_near(WDOWN.at[down_half], wdz_s, wdz_r.at[z])

    low_lanes = lax.broadcasted_iota(jnp.int32, (TOKENS, 128), 1) < 64

    def pick(values, hh):
        keep = low_lanes if hh == 0 else jnp.logical_not(low_lanes)
        return jnp.where(keep, values, jnp.zeros_like(values))

    def attend(i, carry):
        b = lax.rem(2 * y1 + i, 4)
        rows = rows_at(b * TOKENS, TOKENS)
        window = rows_at(384 - 128 * b, 128)
        window = pl.ds(pl.multiple_of(384 - 128 * b, 128), 512)
        for j in range(2):
            outs = []
            for hh in range(2):
                h = 2 * j + hh
                query = pick(QKV[rows, 128 * j : 128 * j + 128], hh)
                scores = dot_nt(query, QKV[:, 256 + 128 * j : 384 + 128 * j]) + BIAS[h, :, window]
                weights = jnp.exp(scores - jnp.max(scores, axis=-1, keepdims=True))
                probs = weights * (1.0 / jnp.sum(weights, axis=-1, keepdims=True))
                PROB[h, rows, :] = probs
                low = probs.astype(BF)
                PLOW[h, rows, :] = low
                outs.append(dot_nn(low, QKV[:, 512 + 128 * j : 640 + 128 * j]))
            AT[rows, 128 * j : 128 * j + 128] = jnp.where(low_lanes, outs[0], outs[1]).astype(BF)

        @pl.when(i == 0)
        def _():
            take(out_piece(near), woz_r.at[near], wob_s, wob_r)

            @pl.when(at_end)
            def _():
                for t in others:
                    take(out_piece(t), woz_r.at[t], wob_s, wob_r)

            pltpu.make_async_copy(WOUT.at[rows_at(64 * z, 64)], WOUT.at[rows_at(64 * z, 64)], loc.at[6]).wait()
            recv(WOUT.at[pl.ds(0, 96)], wob_r)

        SA[rows, :] = dot_nn(AT[rows, :], WOUT[...]).astype(BF)
        scatter_send(SA, RA, a_s, a_r, b)
        return carry

    lax.fori_loop(0, 4, attend, 0)

    for xx in (x, x1):
        g = of_row(near, xx)
        take(WIN.at[half(g, k)], wiz_r.at[g], wib_s, wib_r)

    @pl.when(middle)
    def _():
        for i, xx in enumerate((x, x1)):
            for n in range(2):
                g = of_row(others[n], xx)
                recv(WIN.at[half(g, k)], wiz_r.at[g])
                pass_on(WIN.at[half(g, k)], wif_s, wiz_r.at[g])
                remote(WIN.at[half(g, k)], WIN.at[half(g, k)], wib_s, wib_r, sib).start()

    own_x.wait()
    own_c.wait()
    gain_two = row_of(1)
    recv(RA, a_r)

    def home_forward(r, carry):
        rows = rows_at(r * 32, 32)
        hidden = XO[rows, :].astype(F32)
        for s in range(4):
            hidden = hidden + RA[s, rows, :].astype(F32)
        HID[rows, :] = hidden
        scale = lax.rsqrt(jnp.mean(hidden * hidden, axis=-1, keepdims=True) + EPS)
        NTS[rows, :] = (hidden * scale * gain_two).astype(BF)
        return carry

    lax.fori_loop(0, 4, home_forward, 0)
    gather_send(NTS, NTB, nt_s, nt_r, nt_p)

    def down_piece(t, kk):
        return WDOWN.at[rows_at(256 * t + 128 * kk, 128)]

    take(down_piece(near, k), wdz_r.at[near], wdb_s, wdb_r)

    @pl.when(middle)
    def _():
        for n in range(2):
            t = others[n]
            recv(down_piece(t, k), wdz_r.at[t])
            pass_on(down_piece(t, k), wdf_s, wdz_r.at[t])
            remote(down_piece(t, k), down_piece(t, k), wdb_s, wdb_r, sib).start()

    @pl.when(at_end)
    def _():
        for xx in (x, x1):
            for t in others:
                g = of_row(t, xx)
                take(WIN.at[half(g, k)], wiz_r.at[g], wib_s, wib_r)

    recv(WIN.at[pl.ds(0, 448)], wib_r)

    gather_pass(NTB, nt_s, nt_r, nt_p)

    def feed(i, carry):
        yy = lax.rem(y + i, 2)
        rows = rows_at(256 * yy, 256)
        for b in (2 * yy, 2 * yy + 1):
            gather_wait(NTB, nt_r, b)

        def hidden_units(n, inner):
            cols = rows_at(256 * n, 256)
            pre = dot_nn(NTB[rows, :], WIN[:, cols])
            cdf = 0.5 * (1.0 + lax.erf(pre * 0.7071067811865476))
            ACT[rows, cols] = (pre * cdf).astype(BF)
            SLOPE[rows, cols] = cdf + pre * jnp.exp(-0.5 * pre * pre) * 0.3989422804014327
            return inner

        return lax.fori_loop(0, 4, hidden_units, carry)

    lax.fori_loop(0, 2, feed, 0)

    for b in range(4):
        gather_wait(COT, co_r, b)

    order = (other, other + 1, near, z)

    def grad_down(i, carry):
        m = jnp.where(i < 2, other + i, jnp.where(i == 2, near, z))
        tile = dot_tn(ACT[:, rows_at(256 * m, 256)], COT[...]).astype(BF)
        DD[0, m] = tile[0:128]
        DD[1, m] = tile[128:256]
        remote(DD.at[k1, m], SIBD.at[m], sib_s.at[0], sibd_r.at[i], sib).start()
        return carry

    lax.fori_loop(0, 4, grad_down, 0)

    def join_down(i, carry):
        m = jnp.where(i < 2, other + i, jnp.where(i == 2, near, z))
        recv(SIBD.at[m], sibd_r.at[i])
        ZD[m] = (DD[k, m].astype(F32) + SIBD[m].astype(F32)).astype(BF)

        @pl.when(at_end & (i < 2))
        def _():
            remote(ZD.at[m], RED.at[m], zde_s, zd_r.at[m], zdev(near)).start()

        @pl.when(middle & (i == 2))
        def _():
            remote(ZD.at[m], RED.at[m], zd_s, zd_r.at[m], zdev(near)).start()

        return carry

    lax.fori_loop(0, 4, join_down, 0)

    @pl.when(at_end)
    def _():
        for t in others:
            take(down_piece(t, k), wdz_r.at[t], wdb_s, wdb_r)

    recv(WDOWN.at[pl.ds(0, 384)], wdb_r)

    def back_feed(i, carry):
        yy = lax.rem(y1 + i, 2)
        rows = rows_at(256 * yy, 256)

        def back_act(n, inner):
            cols = rows_at(256 * n, 256)
            GPRE[rows, cols] = (dot_nt(COT[rows, :], WDOWN[cols, :]) * SLOPE[rows, cols]).astype(BF)
            return inner

        lax.fori_loop(0, 4, back_act, 0)

        def back_normed(n, inner):
            cols = rows_at(256 * n, 256)
            SG[rows, cols] = dot_nt(GPRE[rows, :], WIN[cols, :]).astype(BF)
            return inner

        lax.fori_loop(0, 4, back_normed, 0)
        scatter_send(SG, RG, g_s, g_r, 2 * yy)
        scatter_send(SG, RG, g_s, g_r, 2 * yy + 1)
        return carry

    lax.fori_loop(0, 2, back_feed, 0)

    def grad_in(m, carry):
        tile = dot_tn(NTB[:, rows_at(256 * m, 256)], GPRE[...]).astype(BF)
        for part in range(2):
            DI[0, 2 * m + part] = tile[128 * part : 128 * part + 64]
            DI[1, 2 * m + part] = tile[128 * part + 64 : 128 * part + 128]
        return carry

    lax.fori_loop(0, 4, grad_in, 0)
    remote(DI.at[k1], SIBI, sib_s.at[1], sib_r.at[1], sib).start()

    def down_project(n, carry):
        cols = rows_at(256 * n, 256)
        SO[:, cols] = dot_nn(ACT[...], WDOWN[:, cols]).astype(BF)
        return carry

    lax.fori_loop(0, 4, down_project, 0)

    recv(SIBI, sib_r.at[1])

    def join_in(m, carry):
        ZI[m] = (DI[k, m].astype(F32) + SIBI[m].astype(F32)).astype(BF)
        return carry

    lax.fori_loop(0, 8, join_in, 0)
    reduce_others(in_of, ZI, REI, zie_s, zi_r)

    recv(RG, g_r)

    def home_back(r, total):
        rows = rows_at(r * 32, 32)
        grad = RG[0, rows, :].astype(F32)
        for s in range(1, 4):
            grad = grad + RG[s, rows, :].astype(F32)
        hidden = HID[rows, :]
        scale = lax.rsqrt(jnp.mean(hidden * hidden, axis=-1, keepdims=True) + EPS)
        scaled = grad * gain_two
        inner = jnp.mean(scaled * hidden, axis=-1, keepdims=True)
        back = CO[rows, :].astype(F32) + scale * scaled - hidden * (scale * scale * scale * inner)
        GH[rows, :] = back
        GALS[rows, :] = back.astype(BF)
        return total + jnp.sum((grad * hidden * scale).reshape(4, 8, WIDTH), axis=0)

    mlp_gain_grad = lax.fori_loop(0, 4, home_back, jnp.zeros((8, WIDTH), F32))
    gather_send(GALS, GAL, ga_s, ga_r, ga_p)
    reduce_middle(down_of, ZD, RED, RCD, zde_s, zd_r, zdc_r)

    mlp_gain_grad = jnp.sum(mlp_gain_grad, axis=0, keepdims=True)
    for g in range(8):
        SMALL[1, g : g + 1, :] = mlp_gain_grad[:, 128 * g : 128 * g + 128]

    gather_pass(GAL, ga_s, ga_r, ga_p)

    def back_out(i, carry):
        b = lax.rem(2 * y + i, 4)
        rows = rows_at(b * TOKENS, TOKENS)
        gather_wait(GAL, ga_r, b)
        GATT[rows, :] = dot_nt(GAL[rows, :], WOUT[...]).astype(BF)
        return carry

    lax.fori_loop(0, 4, back_out, 0)
    for i in range(4):
        scatter_send(SO, RO, o_s, o_r, lax.rem(2 * y1 + i, 4))
    all_low = lax.broadcasted_iota(jnp.int32, (512, 128), 1) < 64

    def pick_all(values, hh):
        keep = all_low if hh == 0 else jnp.logical_not(all_low)
        return jnp.where(keep, values, jnp.zeros_like(values))

    def grad_values(j, carry):
        grad_att = GATT[:, rows_at(128 * j, 128)]
        first = dot_tn(PLOW[2 * j], pick_all(grad_att, 0))
        second = dot_tn(PLOW[2 * j + 1], pick_all(grad_att, 1))
        DQKV[:, pl.ds(pl.multiple_of(512 + 128 * j, 128), 128)] = jnp.where(all_low, first, second).astype(BF)
        return carry

    lax.fori_loop(0, 2, grad_values, 0)

    def grad_proj(first, width):
        def step(m, carry):
            tile = dot_tn(N1[:, rows_at(256 * m, 256)], DQKV[:, first : first + width]).astype(BF)
            for part in range(2):
                DQ[0, 2 * m + part, :, first : first + width] = tile[128 * part : 128 * part + 64]
                DQ[1, 2 * m + part, :, first : first + width] = tile[128 * part + 64 : 128 * part + 128]
            return carry

        lax.fori_loop(0, 4, step, 0)

    def join_proj(first, width):
        def step(m, carry):
            total = DQ[k, m, :, first : first + width].astype(F32) + SIBQ[m, :, first : first + width].astype(F32)
            ZQ[m, :, first : first + width] = total.astype(BF)
            return carry

        lax.fori_loop(0, 8, step, 0)

    grad_proj(512, 256)
    remote(DQ.at[k1, :, :, value_cols], SIBQ.at[:, :, value_cols], sib_s.at[2], sib_r.at[2], sib).start()

    def grad_out_rows(m, carry):
        tile = dot_tn(AT[:, rows_at(128 * m, 128)], GAL[...]).astype(BF)
        for n in range(2):
            for kk in range(2):
                DO[kk, 2 * m + n] = tile[64 * n + 32 * kk : 64 * n + 32 * kk + 32]
        return carry

    lax.fori_loop(0, 2, grad_out_rows, 0)
    remote(DO.at[k1], SIBO, sib_s.at[3], sib_r.at[3], sib).start()

    recv(SIBQ.at[:, :, value_cols], sib_r.at[2])
    join_proj(512, 256)
    reduce_others(value_of, ZQ, REQ, zve_s, zv_r)

    recv(SIBO, sib_r.at[3])
    ZO[...] = (DO[k].astype(F32) + SIBO[...].astype(F32)).astype(BF)

    reduce_others(down_of, ZO, REO, zoe_s, zo_r)

    @pl.when(middle)
    def _():
        reduce_near(in_of, ZI, REI, zi_s, zi_r)
        reduce_near(value_of, ZQ, REQ, zv_s, zv_r)
        reduce_near(down_of, ZO, REO, zo_s, zo_r)

    reduce_middle(in_of, ZI, REI, RCI, zie_s, zi_r, zic_r)

    def attend_back(i, carry):
        rows = rows_at(i * TOKENS, TOKENS)
        window = pl.ds(pl.multiple_of(384 - 128 * i, 128), 512)
        for j in range(2):
            pair = slice(128 * j, 128 * j + 128)
            keys = QKV[:, 256 + 128 * j : 384 + 128 * j]
            values = QKV[:, 512 + 128 * j : 640 + 128 * j]
            outs = []
            for hh in range(2):
                h = 2 * j + hh
                grad_att = pick(GATT[rows, pair], hh)
                probs = PROB[h, rows, :]
                grad_probs = dot_nt(grad_att, values)
                inner = jnp.sum(probs * grad_probs, axis=-1, keepdims=True)
                grad_scores = (probs * (grad_probs - inner)).astype(BF)
                DS[h, rows, :] = grad_scores
                BACC[h, :, window] = BACC[h, :, window] + grad_scores.astype(F32)
                outs.append(dot_nn(grad_scores, keys))
            DQKV[rows, pair] = jnp.where(low_lanes, outs[0], outs[1]).astype(BF)
        return carry

    lax.fori_loop(0, 4, attend_back, 0)

    def grad_keys(j, carry):
        query = QKV[:, rows_at(128 * j, 128)]
        first = dot_tn(DS[2 * j], pick_all(query, 0))
        second = dot_tn(DS[2 * j + 1], pick_all(query, 1))
        DQKV[:, pl.ds(pl.multiple_of(256 + 128 * j, 128), 128)] = jnp.where(all_low, first, second).astype(BF)
        return carry

    lax.fori_loop(0, 2, grad_keys, 0)

    @pl.when(at_end)
    def _():
        reduce_near(down_of, ZD, RED, zd_s, zd_r)

    reduce_middle(value_of, ZQ, REQ, RCQ.at[:, :, value_cols], zve_s, zv_r, zvc_r)
    reduce_middle(down_of, ZO, REO, RCO, zoe_s, zo_r, zoc_r)
    grad_proj(0, 512)
    remote(DQ.at[k1, :, :, other_cols], SIBQ.at[:, :, other_cols], sib_s.at[4], sib_r.at[4], sib).start()
    def back_project(i, carry):
        yy = lax.rem(y1 + i, 2)
        rows = rows_at(256 * yy, 256)
        SN[rows, :] = dot_nt(DQKV[rows, :], WQKV[...]).astype(BF)
        scatter_send(SN, RN, n_s, n_r, 2 * yy)
        scatter_send(SN, RN, n_s, n_r, 2 * yy + 1)
        return carry

    lax.fori_loop(0, 2, back_project, 0)

    recv(SIBQ.at[:, :, other_cols], sib_r.at[4])
    join_proj(0, 512)
    reduce_others(other_of, ZQ, REQ, zqe_s, zq_r)

    @pl.when(at_end)
    def _():
        reduce_near(in_of, ZI, REI, zi_s, zi_r)
        reduce_near(value_of, ZQ, REQ, zv_s, zv_r)
        reduce_near(down_of, ZO, REO, zo_s, zo_r)

    reduce_near(other_of, ZQ, REQ, zq_s, zq_r)

    head_sums = []
    for h in range(4):
        rest = BACC[h]
        count = 64
        while count >= 8:
            rest = pltpu.roll(rest[0:count, :], count, 1) + rest[count : 2 * count, :]
            count //= 2
        for bit in (1, 2, 4):
            shift_row = 7 - lax.broadcasted_iota(jnp.int32, (8, WIDTH), 0)
            rest = jnp.where(lax.rem(lax.div(shift_row, bit), 2) == 1, pltpu.roll(rest, bit, 1), rest)
        head_sums.append(jnp.sum(rest, axis=0, keepdims=True))
    head_sums = jnp.concatenate(head_sums + [jnp.zeros((4, WIDTH), F32)], axis=0)
    coarse = head_sums.astype(BF)
    split_sums = jnp.concatenate([coarse, (head_sums - coarse.astype(F32)).astype(BF)], axis=0)
    both_masks = jnp.concatenate([head_mask.astype(F32)] * 2, axis=0) > 0.5

    def bucket_sums(g, carry):
        sums = dot_nt(split_sums, bucket_hot(g).astype(BF))
        SMALL[2, pl.ds(g, 1), :] = jnp.sum(jnp.where(both_masks, sums, 0.0), axis=0, keepdims=True)
        return carry

    lax.fori_loop(0, 8, bucket_sums, 0)

    reduce_middle(other_of, ZQ, REQ, RCQ.at[:, :, other_cols], zqe_s, zq_r, zqc_r)
    recv(RED.at[z], zd_r.at[z])
    recv(RCD, zdc_r)
    FD[...] = (ZD[z].astype(F32) + RED[z].astype(F32) + RCD[...].astype(F32)).astype(BF)

    def down_rows(cc):
        return odown.at[rows_at(128 * cc, 128)]

    y_core = (2 * y1 + k, f)
    remote(FD, down_rows(c), fd_s, fd_r.at[1], y_core).start()
    remote(FD, down_rows(c), fd_s, fd_r.at[2], sib).start()
    pltpu.make_async_copy(FD, down_rows(c), fd_r.at[0]).start()

    def spread(final, place, send, bsend, got, bgot):
        remote(final.at[x1], place(q, k), send, got.at[3], (2 * y1 + k, f1)).start()
        remote(final.at[x1], place(q, k), send, got.at[2], (c, f1)).start()
        remote(final.at[x], place(q, k), send, got.at[1], y_core).start()
        remote(final.at[x], place(q, k), bsend, bgot, sib).start()
        pltpu.make_async_copy(final.at[x], place(q, k), got.at[0]).start()

    chips = (2 * x + y1, 2 * x1 + y, 2 * x1 + y1)

    def spread_on(place, bsend, got, bgot):
        for i in range(3):
            piece = place(chips[i], k)
            recv(piece, got.at[i + 1])
            remote(piece, piece, bsend, bgot, sib).start()

    def in_place(qq, kk):
        return oin.at[:, qq, rows_at(64 * kk, 64), :]

    def proj_place(qq, kk):
        return oqkv.at[qq, rows_at(64 * kk, 64), :]

    recv(RO, o_r)

    def home_out(r, carry):
        rows = rows_at(r * 32, 32)
        result = HID[rows, :]
        for s in range(4):
            result = result + RO[s, rows, :].astype(F32)
        out_ref[0, rows, :] = result.astype(BF)
        return carry

    lax.fori_loop(0, 4, home_out, 0)
    recv(RN, n_r)

    def home_inputs(r, total):
        rows = rows_at(r * 32, 32)
        grad = RN[0, rows, :].astype(F32)
        for s in range(1, 4):
            grad = grad + RN[s, rows, :].astype(F32)
        values = XO[rows, :].astype(F32)
        scale = lax.rsqrt(jnp.mean(values * values, axis=-1, keepdims=True) + EPS)
        scaled = grad * gain_one
        inner = jnp.mean(scaled * values, axis=-1, keepdims=True)
        back = GH[rows, :] + scale * scaled - values * (scale * scale * scale * inner)
        gin_ref[0, rows, :] = back.astype(BF)
        return total + jnp.sum((grad * values * scale).reshape(4, 8, WIDTH), axis=0)

    attn_gain_grad = lax.fori_loop(0, 4, home_inputs, jnp.zeros((8, WIDTH), F32))
    attn_gain_grad = jnp.sum(attn_gain_grad, axis=0, keepdims=True)
    for g in range(8):
        SMALL[0, g : g + 1, :] = attn_gain_grad[:, 128 * g : 128 * g + 128]

    for i in range(4):
        ci = lax.rem(c + i, 4)
        for j, xj in enumerate((x, x1)):
            if i or j:
                remote(SMALL, RSMALL.at[2 * c + x], sp_s, sp_r, (ci, 2 * z + xj)).start()

    recv(in_of(REI, z), zi_r.at[z])
    recv(RCI, zic_r)
    for xx in range(2):
        total = ZI[2 * z + xx].astype(F32) + REI[2 * z + xx].astype(F32) + RCI[xx].astype(F32)
        for j in range(4):
            FI[xx, j] = total[:, 256 * j : 256 * j + 256].astype(BF)
    spread(FI, in_place, fi_s, fib_s, fi_r, fib_r)

    recv(value_of(REQ, z), zv_r.at[z])
    recv(other_of(REQ, z), zq_r.at[z])
    recv(RCQ.at[:, :, value_cols], zvc_r)
    recv(RCQ.at[:, :, other_cols], zqc_r)
    for xx in range(2):
        total = ZQ[2 * z + xx].astype(F32) + REQ[2 * z + xx].astype(F32) + RCQ[xx].astype(F32)
        FQ[xx] = total.astype(BF)
    spread(FQ, proj_place, fq_s, fqb_s, fq_r, fqb_r)

    recv(REO.at[z], zo_r.at[z])
    recv(RCO, zoc_r)
    FO[...] = (ZO[z].astype(F32) + REO[z].astype(F32) + RCO[...].astype(F32)).astype(BF)

    def out_rows(cc):
        return oout.at[rows_at(32 * cc, 32)]

    remote(FO, out_rows(c), fo_s, fo_r.at[1], y_core).start()
    remote(FO, out_rows(c), fo_s, fo_r.at[2], sib).start()
    pltpu.make_async_copy(FO, out_rows(c), fo_r.at[0]).start()

    y_rows = down_rows(2 * y1 + k)
    recv(y_rows, fd_r.at[1])
    remote(y_rows, y_rows, fd_s, fd_r.at[2], sib).start()
    spread_on(in_place, fib_s, fi_r, fib_r)
    recv(RSMALL.at[pl.ds(0, 7)], sp_r)
    plane_sum = SMALL[...]
    for i in range(4):
        ci = lax.rem(c + i, 4)
        for j, xj in enumerate((x, x1)):
            if i or j:
                plane_sum = plane_sum + RSMALL[2 * ci + xj]
    for t in range(4):
        for n in range(3):
            pair = plane_sum[n, 2 * t : 2 * t + 2, :]
            PSMALL[t, n : n + 1, :] = jnp.where(x == 0, pair[0:1], pair[1:2])
    for t in zs:
        remote(PSMALL.at[t], RZSMALL.at[z], sz_s, sz_r, zdev(t)).start()

    spread_on(proj_place, fqb_s, fq_r, fqb_r)
    y_out = out_rows(2 * y1 + k)
    recv(y_out, fo_r.at[1])
    remote(y_out, y_out, fo_s, fo_r.at[2], sib).start()
    recv(RZSMALL.at[pl.ds(0, 3)], sz_r)
    total = PSMALL[z]
    for t in zs:
        total = total + RZSMALL[t]
    small_ref[...] = total

    recv(down_rows(c), fd_r.at[0])
    recv(odown.at[pl.ds(0, 256)], fd_r.at[2])
    recv(out_rows(c), fo_r.at[0])
    recv(oout.at[pl.ds(0, 64)], fo_r.at[2])
    recv(in_place(q, k), fi_r.at[0])
    recv(oin.at[:, :, rows_at(64 * k1, 64), :], fib_r)
    recv(proj_place(q, k), fq_r.at[0])
    recv(oqkv.at[:, rows_at(64 * k1, 64), :], fqb_r)

    sent(GP.at[pl.ds(0, 7)], gp_s)
    four_sent(XB, xb_s)
    four_sent(COT, co_s)
    four_sent(NTB, nt_s)
    four_sent(GAL, ga_s)
    four_sent(SA, a_s)
    four_sent(SG, g_s)
    four_sent(SO, o_s)
    four_sent(SN, n_s)
    sent(WQKV.at[pl.ds(0, 256)], wqz_s)
    sent(WQKV.at[half(f, k)], wx_s.at[0])
    sent(WIN.at[half(f, k)], wx_s.at[1])
    sent(WIN.at[pl.ds(0, 256)], wiz_s)
    sent(WDOWN.at[pl.ds(0, 256)], wdz_s)
    sent(WQKV.at[pl.ds(0, 448)], wqb_s)
    sent(WIN.at[pl.ds(0, 448)], wib_s)
    sent(WDOWN.at[pl.ds(0, 384)], wdb_s)
    sent(value_of(ZQ, near), zv_s)
    sent(other_of(ZQ, near), zq_s)
    sent(ZQ.at[pl.ds(0, 4), :, value_cols], zve_s)
    sent(ZQ.at[pl.ds(0, 4), :, other_cols], zqe_s)
    sent(down_of(ZD, near), zd_s)
    sent(ZD.at[pl.ds(0, 2)], zde_s)
    sent(PSMALL.at[pl.ds(0, 3)], sz_s)
    sent(in_of(ZI, near), zi_s)
    sent(ZI.at[pl.ds(0, 4)], zie_s)

    @pl.when(middle)
    def _():
        sent(WDOWN.at[pl.ds(0, 256)], wdf_s)
        sent(WQKV.at[pl.ds(0, 256)], wqf_s)
        sent(WIN.at[pl.ds(0, 256)], wif_s)

    @pl.when(middle)
    def _():
        sent(WOUT.at[pl.ds(0, 128)], woz_s)

    @pl.when(at_end)
    def _():
        sent(WOUT.at[pl.ds(0, 64)], woz_s)

    sent(WOUT.at[pl.ds(0, 96)], wob_s)
    sent(ZO.at[near], zo_s)
    sent(ZO.at[pl.ds(0, 2)], zoe_s)
    sent(oout.at[pl.ds(0, 96)], fo_s)
    sent(DD.at[k1], sib_s.at[0])
    sent(DI.at[k1], sib_s.at[1])
    sent(DQ.at[k1, :, :, value_cols], sib_s.at[2])
    sent(DO.at[k1], sib_s.at[3])
    sent(DQ.at[k1, :, :, other_cols], sib_s.at[4])
    sent(odown.at[pl.ds(0, 384)], fd_s)
    sent(oin.at[:, pl.ds(0, 3), pl.ds(0, 64), :], fi_s)
    sent(oqkv.at[pl.ds(0, 3), pl.ds(0, 64), :], fq_s)
    sent(oin.at[:, :, rows_at(64 * k, 64), :], fib_s)
    sent(oqkv.at[:, rows_at(64 * k, 64), :], fqb_s)
    sent(RSMALL.at[pl.ds(0, 7)], sp_s)


def plane_shards(
    inputs, cotangent, w_query, w_key, w_value, w_out, w_in, w_down, gain_attn, gain_mlp, rel_bias, buckets
):
    vm = pltpu.VMEM
    dma = pltpu.SemaphoreType.DMA
    block = lambda kind: vm((TOKENS, WIDTH), kind)
    tokens = lambda width, kind: vm((512, width), kind)
    scratch = [
        block(BF), block(BF), vm((8, 128), F32), vm((1, 1024), jnp.int32),
        vm((3, 128, 1024), BF), vm((64, 768), BF), vm((8, 8, 128), F32),
        tokens(1024, BF), tokens(1024, BF), tokens(1024, BF), tokens(1024, BF), tokens(1024, BF),
        vm((1024, 768), BF), vm((256, 1024), BF), vm((1024, 1024), BF), vm((1024, 1024), BF),
        tokens(768, BF), vm((4, 512, 512), F32), vm((4, 512, 512), BF), vm((4, 128, 1024), F32),
        tokens(256, BF), tokens(1024, BF), tokens(1024, F32), tokens(1024, BF),
        tokens(256, BF), tokens(768, BF), vm((4, 512, 512), BF), vm((4, 128, 1024), F32),
        tokens(1024, BF), tokens(1024, BF), tokens(1024, BF), tokens(1024, BF),
        vm((4, 128, 1024), BF), vm((4, 128, 1024), BF), vm((4, 128, 1024), BF), vm((4, 128, 1024), BF),
        block(F32), block(F32), block(BF), block(BF),
        vm((2, 8, 64, 768), BF), vm((2, 4, 32, 1024), BF), vm((2, 8, 64, 1024), BF), vm((2, 4, 128, 1024), BF),
        vm((8, 64, 768), BF), vm((4, 32, 1024), BF), vm((8, 64, 1024), BF), vm((4, 128, 1024), BF),
        vm((8, 64, 768), BF), vm((4, 32, 1024), BF), vm((8, 64, 1024), BF), vm((4, 128, 1024), BF),
        vm((8, 64, 768), BF), vm((4, 32, 1024), BF), vm((8, 64, 1024), BF), vm((4, 128, 1024), BF),
        vm((2, 64, 768), BF), vm((32, 1024), BF), vm((2, 64, 1024), BF), vm((128, 1024), BF),
        vm((2, 64, 768), BF), vm((32, 1024), BF), vm((2, 4, 64, 256), BF), vm((128, 1024), BF),
        vm((3, 8, 128), F32), vm((8, 3, 8, 128), F32), vm((4, 8, 128), F32), vm((4, 8, 128), F32),
        dma((7,)), dma, dma, dma, dma((4,)), dma((2,)), dma, dma((4,)), dma((2,)), dma, dma((4,)), dma((2,)), dma, dma((4,)), dma((2,)),
        dma, dma, dma, dma, dma, dma, dma, dma,
        dma((2,)), dma((2,)), dma, dma, dma((8,)), dma, dma, dma, dma, dma((8,)), dma, dma,
        dma, dma, dma((4,)), dma, dma, dma, dma((4,)), dma, dma,
        dma((5,)), dma((5,)), dma((4,)), dma, dma, dma((4,)), dma, dma, dma, dma((4,)), dma, dma, dma, dma((4,)), dma,
        dma, dma, dma((4,)), dma, dma, dma, dma((4,)), dma,
        dma, dma, dma((4,)), dma, dma, dma((3,)), dma, dma, dma((4,)), dma, dma, dma((3,)), dma, dma, dma, dma,
    ]
    anywhere = pl.BlockSpec(memory_space=pl.ANY)
    in_vmem = pl.BlockSpec(memory_space=pltpu.VMEM)
    shape = jax.ShapeDtypeStruct
    output, grad_inputs, proj, out, hidden, down, small = pl.pallas_call(
        fused_layer,
        out_shape=(
            shape((1, TOKENS, WIDTH), BF),
            shape((1, TOKENS, WIDTH), BF),
            shape((4, 128, 768), BF),
            shape((128, 1024), BF),
            shape((4, 4, 128, 256), BF),
            shape((512, 1024), BF),
            shape((8, 128), F32),
        ),
        in_specs=[anywhere] * 8 + [in_vmem] * 4,
        out_specs=(in_vmem, in_vmem, anywhere, anywhere, anywhere, anywhere, in_vmem),
        scratch_shapes=scratch,
        compiler_params=pltpu.CompilerParams(
            collective_id=0, has_side_effects=True, vmem_limit_bytes=63 << 20
        ),
        cost_estimate=pl.CostEstimate(flops=11 * 10**9, bytes_accessed=16 * 2**20, transcendentals=3 * 2**20),
    )(inputs, cotangent, w_query, w_key, w_value, w_out, w_in, w_down, gain_attn[None], gain_mlp[None], rel_bias[None], buckets[None])
    return finish(output, grad_inputs, proj, out, hidden, down, small)


def finish_kernel(
    output, grad_inputs, proj, out, hidden, down, small,
    o_output, o_inputs, o_query, o_key, o_value, o_out, o_in, o_down, o_attn, o_mlp, o_bias,
    b_output, b_inputs, b_proj, b_out, b_hidden, b_down, b_small, w_proj, w_out, w_in, w_down, got, left,
):
    moves = [
        pltpu.make_async_copy(proj, b_proj, got.at[0]),
        pltpu.make_async_copy(hidden, b_hidden, got.at[1]),
        pltpu.make_async_copy(down, b_down, got.at[2]),
        pltpu.make_async_copy(out, b_out, got.at[3]),
        pltpu.make_async_copy(small, b_small, got.at[4]),
        pltpu.make_async_copy(output, b_output, got.at[5]),
        pltpu.make_async_copy(grad_inputs, b_inputs, got.at[6]),
    ]
    for move in moves:
        move.start()
    sends = []

    def write(src, dst, slot):
        copy = pltpu.make_async_copy(src, dst, left.at[slot])
        copy.start()
        sends.append(copy)

    moves[0].wait()
    for w, place in enumerate((o_query, o_key, o_value)):
        for shard in range(8):
            z, x = shard // 2, shard % 2
            lanes = slice(256 * w + 64 * z, 256 * w + 64 * z + 64)
            parts = [b_proj[2 * x + y, :, lanes].astype(F32) for y in range(2)]
            w_proj[w, :, 128 * shard : 128 * shard + 128] = jnp.concatenate(parts, axis=1)
        write(w_proj.at[w], place, w)
    moves[1].wait()
    for r in range(4):
        rows = slice(32 * r, 32 * r + 32)
        for z in range(4):
            for q in range(4):
                w_in[rows, 256 * (4 * z + q) : 256 * (4 * z + q) + 256] = b_hidden[z, q, rows, :].astype(F32)
        write(w_in.at[pl.ds(32 * r, 32)], o_in.at[pl.ds(32 * r, 32)], 3 + r)
    moves[2].wait()
    for r in range(4):
        rows = slice(128 * r, 128 * r + 128)
        w_down[rows, :] = b_down[rows, :].astype(F32)
        write(w_down.at[pl.ds(128 * r, 128)], o_down.at[pl.ds(128 * r, 128)], 7 + r)
    moves[3].wait()
    w_out[...] = b_out[...].astype(F32)
    write(w_out, o_out, 11)
    moves[4].wait()
    o_attn[...] = b_small[0:1, :]
    o_mlp[...] = b_small[1:2, :]
    o_bias[...] = b_small[2:3, 0:64]
    moves[5].wait()
    write(b_output, o_output, 12)
    moves[6].wait()
    write(b_inputs, o_inputs, 13)
    for copy in sends:
        copy.wait()


def finish(output, grad_inputs, proj, out, hidden, down, small):
    shape = jax.ShapeDtypeStruct
    vm = pltpu.VMEM
    anywhere = pl.BlockSpec(memory_space=pl.ANY)
    in_vmem = pl.BlockSpec(memory_space=pltpu.VMEM)
    results = pl.pallas_call(
        finish_kernel,
        out_shape=(
            shape(output.shape, BF),
            shape(grad_inputs.shape, BF),
            shape((128, 1024), F32),
            shape((128, 1024), F32),
            shape((128, 1024), F32),
            shape((128, 1024), F32),
            shape((128, 4096), F32),
            shape((512, 1024), F32),
            shape((1, 128), F32),
            shape((1, 128), F32),
            shape((1, 64), F32),
        ),
        in_specs=[anywhere] * 7,
        out_specs=(anywhere,) * 8 + (in_vmem,) * 3,
        scratch_shapes=[
            vm(output.shape, BF), vm(grad_inputs.shape, BF), vm(proj.shape, BF), vm(out.shape, BF), vm(hidden.shape, BF), vm(down.shape, BF), vm(small.shape, F32),
            vm((3, 128, 1024), F32), vm((128, 1024), F32), vm((128, 4096), F32), vm((512, 1024), F32),
            pltpu.SemaphoreType.DMA((7,)), pltpu.SemaphoreType.DMA((14,)),
        ],
        compiler_params=pltpu.CompilerParams(vmem_limit_bytes=63 << 20),
        cost_estimate=pl.CostEstimate(flops=0, bytes_accessed=10 * 2**20, transcendentals=0),
    )(output, grad_inputs, proj, out, hidden, down, small)
    return results[:8] + (results[8].reshape(128), results[9].reshape(128), results[10].reshape(64))


def solution(mesh):
    placed = (
        P("fsdp", "ctx", None),
        P("fsdp", "ctx", None),
        P("fsdp", None),
        P("fsdp", None),
        P("fsdp", None),
        P("fsdp", None),
        P("fsdp", None),
        P("fsdp", None),
        P("fsdp"),
        P("fsdp"),
        P("fsdp"),
        P(),
    )
    by_planes = mesh.shape["ctx"] == 4 and mesh.shape["fsdp"] == 8
    return jax.shard_map(
        plane_shards if by_planes else shards,
        mesh=mesh,
        in_specs=placed,
        out_specs=(
            P("fsdp", "ctx", None),
            P("fsdp", "ctx", None),
            P("fsdp", None),
            P("fsdp", None),
            P("fsdp", None),
            P("fsdp", None),
            P("fsdp", None),
            P("fsdp", None),
            P("fsdp"),
            P("fsdp"),
            P("fsdp"),
        ),
        check_vma=False,
    )
```

```python
import jax
import jax.numpy as jnp
from jax import lax
from jax.experimental import pallas as pl
from jax.experimental.pallas import tpu as pltpu
from jax.sharding import PartitionSpec as P

HEADS = 16
HEAD = 64
BUCKETS = 32


EPS = 1e-06


def norm_rows(values, gain):
    return values * lax.rsqrt(jnp.mean(values * values, axis=-1, keepdims=True) + EPS) * gain


def smooth_gelu(values):
    return 0.5 * values * (1.0 + jax.scipy.special.erf(values * 0.7071067811865476))


def gelu_slope(values):
    return (
        0.5 * (1.0 + jax.scipy.special.erf(values * 0.7071067811865476))
        + values * jnp.exp(-0.5 * values * values) * 0.3989422804014327
    )


def bucket_offsets(buckets, first_query, query_count):
    seq_length = (buckets.shape[0] + 1) // 2
    key_place = jnp.arange(seq_length, dtype=jnp.int32)
    query_place = first_query + jnp.arange(query_count, dtype=jnp.int32)
    return key_place[None, :] - query_place[:, None] + (seq_length - 1)


def make_bias(flat_table, buckets, first_query, query_count):
    bias_table = flat_table.reshape(BUCKETS, HEADS)
    one_hot = (buckets[:, None] == jnp.arange(BUCKETS, dtype=jnp.int32)[None, :]).astype(
        flat_table.dtype
    )
    per_offset = jnp.dot(one_hot, bias_table, precision=lax.Precision.HIGHEST)
    offsets = bucket_offsets(buckets, first_query, query_count)
    return jnp.take(per_offset.T, offsets, axis=1)


def pair_table(buckets, first_query, query_count):
    offsets = bucket_offsets(buckets, first_query, query_count)
    pair_bucket = jnp.take(buckets, offsets.reshape(-1), axis=0)
    return (pair_bucket[:, None] == jnp.arange(BUCKETS, dtype=jnp.int32)[None, :]).astype(
        jnp.bfloat16
    )


def fetch_attention(w_query, w_key, w_value, w_out, gain_attn, rel_bias):
    return (
        lax.all_gather(w_query, "fsdp", axis=0, tiled=True),
        lax.all_gather(w_key, "fsdp", axis=0, tiled=True),
        lax.all_gather(w_value, "fsdp", axis=0, tiled=True),
        lax.all_gather(w_out, "fsdp", axis=0, tiled=True),
        lax.all_gather(gain_attn, "fsdp", axis=0, tiled=True),
        lax.all_gather(rel_bias, "fsdp", axis=0, tiled=True),
    )


def fetch_mlp(w_in, w_down, gain_mlp):
    return (
        lax.all_gather(w_in, "fsdp", axis=0, tiled=True),
        lax.all_gather(w_down, "fsdp", axis=0, tiled=True),
        lax.all_gather(gain_mlp, "fsdp", axis=0, tiled=True),
    )


def share_keys(key_rows, value_rows):
    return (
        lax.all_gather(key_rows, "ctx", axis=1, tiled=True),
        lax.all_gather(value_rows, "ctx", axis=1, tiled=True),
    )


def scores_of(query_part, key_part, bias_values):
    return (
        jnp.einsum("qhd,khd->hqk", query_part, key_part, preferred_element_type=jnp.float32)
        + bias_values
    )


def shards(
    inputs,
    cotangent,
    w_query,
    w_key,
    w_value,
    w_out,
    w_in,
    w_down,
    gain_attn,
    gain_mlp,
    rel_bias,
    buckets,
):
    seq_count, row_count, width = inputs.shape
    total_rows = seq_count * row_count
    first_query = lax.axis_index("ctx") * row_count
    query_w, key_w, value_w, out_w, attn_gain, bias_flat = fetch_attention(
        w_query, w_key, w_value, w_out, gain_attn, rel_bias
    )
    in_w, down_w, mlp_gain = fetch_mlp(w_in, w_down, gain_mlp)
    bias_values = make_bias(bias_flat.astype(jnp.float32), buckets, first_query, row_count)
    inputs_flat = inputs.astype(jnp.float32).reshape(total_rows, width)
    attn_scale = attn_gain.astype(jnp.float32)
    normed_one = norm_rows(inputs_flat, attn_scale).astype(jnp.bfloat16)
    query_rows = jnp.dot(normed_one, query_w, preferred_element_type=jnp.float32).astype(
        jnp.bfloat16
    )
    key_rows = (
        jnp.dot(normed_one, key_w, preferred_element_type=jnp.float32)
        .astype(jnp.bfloat16)
        .reshape(seq_count, row_count, width)
    )
    value_rows = (
        jnp.dot(normed_one, value_w, preferred_element_type=jnp.float32)
        .astype(jnp.bfloat16)
        .reshape(seq_count, row_count, width)
    )
    all_keys, all_values = share_keys(key_rows, value_rows)
    query_heads = query_rows.reshape(seq_count, row_count, HEADS, HEAD)
    seq_index = 0
    key_heads = all_keys[seq_index].reshape(-1, HEADS, HEAD)
    value_heads = all_values[seq_index].reshape(-1, HEADS, HEAD)
    scores = scores_of(query_heads[seq_index], key_heads, bias_values)
    top_score = jnp.max(scores, axis=-1, keepdims=True)
    weights_exp = jnp.exp(scores - top_score)
    totals = jnp.sum(weights_exp, axis=-1, keepdims=True)
    probs_low = (weights_exp / totals).astype(jnp.bfloat16)
    mixed = jnp.einsum("hqk,khd->qhd", probs_low, value_heads, preferred_element_type=jnp.float32)
    mixed_list = mixed.reshape(row_count, width)
    lse_list = [top_score + jnp.log(totals)]
    attended = mixed_list.astype(jnp.bfloat16)
    hidden_res = inputs_flat + jnp.dot(attended, out_w, preferred_element_type=jnp.float32)
    mlp_scale = mlp_gain.astype(jnp.float32)
    normed_two = norm_rows(hidden_res, mlp_scale).astype(jnp.bfloat16)
    pre_act = jnp.dot(normed_two, in_w, preferred_element_type=jnp.float32)
    activated = smooth_gelu(pre_act).astype(jnp.bfloat16)
    result = hidden_res + jnp.dot(activated, down_w, preferred_element_type=jnp.float32)
    in_w, down_w, mlp_gain = fetch_mlp(w_in, w_down, gain_mlp)
    query_w, key_w, value_w, out_w, attn_gain, bias_flat = fetch_attention(
        w_query, w_key, w_value, w_out, gain_attn, rel_bias
    )
    all_keys, all_values = share_keys(key_rows, value_rows)
    grad_rows = cotangent.reshape(total_rows, width)
    grad_down = jnp.einsum("nf,nd->fd", activated, grad_rows, preferred_element_type=jnp.float32)
    grad_act = jnp.einsum("nd,fd->nf", grad_rows, down_w, preferred_element_type=jnp.float32)
    grad_pre = (grad_act * gelu_slope(pre_act)).astype(jnp.bfloat16)
    grad_in = jnp.einsum("nd,nf->df", normed_two, grad_pre, preferred_element_type=jnp.float32)
    grad_normed_two = jnp.einsum("nf,df->nd", grad_pre, in_w, preferred_element_type=jnp.float32)
    back_hidden, grad_mlp_gain = jax.vjp(norm_rows, hidden_res, mlp_scale)[1](grad_normed_two)
    grad_hidden = grad_rows.astype(jnp.float32) + back_hidden
    grad_attn_low = grad_hidden.astype(jnp.bfloat16)
    grad_out = jnp.einsum("nd,ne->de", attended, grad_attn_low, preferred_element_type=jnp.float32)
    grad_attended = jnp.einsum(
        "ne,de->nd", grad_attn_low, out_w, preferred_element_type=jnp.float32
    ).astype(jnp.bfloat16)
    grad_heads = grad_attended.reshape(seq_count, row_count, HEADS, HEAD)
    pair_buckets = pair_table(buckets, first_query, row_count)
    seq_index = 0
    key_heads = all_keys[seq_index].reshape(-1, HEADS, HEAD)
    value_heads = all_values[seq_index].reshape(-1, HEADS, HEAD)
    scores = scores_of(query_heads[seq_index], key_heads, bias_values)
    probs = jnp.exp(scores - lse_list[seq_index])
    grad_probs = jnp.einsum(
        "qhd,khd->hqk", grad_heads[seq_index], value_heads, preferred_element_type=jnp.float32
    )
    row_inner = jnp.sum(probs * grad_probs, axis=-1, keepdims=True)
    grad_scores = (probs * (grad_probs - row_inner)).astype(jnp.bfloat16)
    bias_grad = jnp.dot(
        grad_scores.reshape(HEADS, -1), pair_buckets, preferred_element_type=jnp.float32
    )
    query_grads = jnp.einsum(
        "hqk,khd->qhd", grad_scores, key_heads, preferred_element_type=jnp.float32
    ).reshape(row_count, width)
    key_grads = [
        jnp.einsum(
            "hqk,qhd->khd", grad_scores, query_heads[seq_index], preferred_element_type=jnp.float32
        ).reshape(-1, width)
    ]
    value_grads = [
        jnp.einsum(
            "hqk,qhd->khd",
            probs.astype(jnp.bfloat16),
            grad_heads[seq_index],
            preferred_element_type=jnp.float32,
        ).reshape(-1, width)
    ]
    key_back, value_back = (
        lax.psum_scatter(
            jnp.stack(key_grads).astype(jnp.bfloat16), "ctx", scatter_dimension=1, tiled=True
        ).astype(jnp.float32),
        lax.psum_scatter(
            jnp.stack(value_grads).astype(jnp.bfloat16), "ctx", scatter_dimension=1, tiled=True
        ).astype(jnp.float32),
    )
    grad_query_rows = query_grads.astype(jnp.bfloat16)
    grad_key_rows = key_back.reshape(total_rows, width).astype(jnp.bfloat16)
    grad_value_rows = value_back.reshape(total_rows, width).astype(jnp.bfloat16)
    grad_query = jnp.einsum(
        "nd,ne->de", normed_one, grad_query_rows, preferred_element_type=jnp.float32
    )
    grad_key = jnp.einsum(
        "nd,ne->de", normed_one, grad_key_rows, preferred_element_type=jnp.float32
    )
    grad_value = jnp.einsum(
        "nd,ne->de", normed_one, grad_value_rows, preferred_element_type=jnp.float32
    )
    grad_normed_one = jnp.einsum(
        "ne,de->nd", grad_query_rows, query_w, preferred_element_type=jnp.float32
    )
    grad_normed_one = grad_normed_one + jnp.einsum(
        "ne,de->nd", grad_key_rows, key_w, preferred_element_type=jnp.float32
    )
    grad_normed_one = grad_normed_one + jnp.einsum(
        "ne,de->nd", grad_value_rows, value_w, preferred_element_type=jnp.float32
    )
    back_inputs, grad_attn_gain = jax.vjp(norm_rows, inputs_flat, attn_scale)[1](grad_normed_one)
    grad_inputs = (
        (grad_hidden + back_inputs).astype(jnp.bfloat16).reshape(seq_count, row_count, width)
    )
    grad_bias_flat = bias_grad.T.reshape(BUCKETS * HEADS)
    (
        part_query,
        part_key,
        part_value,
        part_out,
        part_in,
        part_down,
        part_attn_gain,
        part_mlp_gain,
        part_bias,
    ) = (
        lax.psum_scatter(grad_query, "fsdp", scatter_dimension=0, tiled=True),
        lax.psum_scatter(grad_key, "fsdp", scatter_dimension=0, tiled=True),
        lax.psum_scatter(grad_value, "fsdp", scatter_dimension=0, tiled=True),
        lax.psum_scatter(grad_out, "fsdp", scatter_dimension=0, tiled=True),
        lax.psum_scatter(grad_in, "fsdp", scatter_dimension=0, tiled=True),
        lax.psum_scatter(grad_down, "fsdp", scatter_dimension=0, tiled=True),
        lax.psum_scatter(grad_attn_gain, "fsdp", scatter_dimension=0, tiled=True),
        lax.psum_scatter(grad_mlp_gain, "fsdp", scatter_dimension=0, tiled=True),
        lax.psum_scatter(grad_bias_flat, "fsdp", scatter_dimension=0, tiled=True),
    )
    summed = (
        lax.psum(part_query.astype(jnp.bfloat16), "ctx").astype(jnp.float32),
        lax.psum(part_key.astype(jnp.bfloat16), "ctx").astype(jnp.float32),
        lax.psum(part_value.astype(jnp.bfloat16), "ctx").astype(jnp.float32),
        lax.psum(part_out.astype(jnp.bfloat16), "ctx").astype(jnp.float32),
        lax.psum(part_in.astype(jnp.bfloat16), "ctx").astype(jnp.float32),
        lax.psum(part_down.astype(jnp.bfloat16), "ctx").astype(jnp.float32),
        lax.psum(part_attn_gain.astype(jnp.bfloat16), "ctx").astype(jnp.float32),
        lax.psum(part_mlp_gain.astype(jnp.bfloat16), "ctx").astype(jnp.float32),
        lax.psum(part_bias.astype(jnp.bfloat16), "ctx").astype(jnp.float32),
    )
    output = result.astype(jnp.bfloat16).reshape(seq_count, row_count, width)
    return (
        output,
        grad_inputs,
        summed[0],
        summed[1],
        summed[2],
        summed[3],
        summed[4],
        summed[5],
        summed[6],
        summed[7],
        summed[8],
    )


MESH_ID = pl.DeviceIdType.MESH
BF = jnp.bfloat16
F32 = jnp.float32
WIDTH = 1024
TOKENS = 128
NT_DIMS = (((1,), (1,)), ((), ()))
TN_DIMS = (((0,), (0,)), ((), ()))


def dot_nn(left, right):
    return jnp.dot(left, right, preferred_element_type=F32)


def dot_nt(left, right):
    return lax.dot_general(left, right, NT_DIMS, preferred_element_type=F32)


def dot_tn(left, right):
    return lax.dot_general(left, right, TN_DIMS, preferred_element_type=F32)


def rows_at(start, count):
    return pl.ds(start if isinstance(start, int) else pl.multiple_of(start, count), count)


def remote(src, dst, send, recv, device):
    return pltpu.make_async_remote_copy(
        src_ref=src, dst_ref=dst, send_sem=send, recv_sem=recv, device_id=device, device_id_type=MESH_ID
    )


def steps(count, body, carry):
    for i in range(count):
        carry = body(i, carry)
    return carry


def fused_layer(
    x_in, cot_in, wq_in, wk_in, wv_in, wo_in, wi_in, wd_in, attn_in, mlp_in, table_in, bucket_in,
    out_ref, gin_ref, oqkv, oout, oin, odown, small_ref,
    XO, CO, PACK, BUCKET, STAGE, ACROSS, GP, XB, COT, N1, NTB, GAL, WQKV, WOUT, WIN, WDOWN,
    QKV, PROB, PLOW, BIAS, AT, ACT, SLOPE, GPRE, GATT, DQKV, DS, BACC,
    SA, SG, SO, SN, RA, RG, RO, RN, XA, XG, XS, XN, HID, GH, NTS, GALS,
    DQ, DO, DI, DD, SIBQ, SIBO, SIBI, SIBD, ZQ, ZO, ZI, ZD, REQ, REO, REI, RED, RCQ, RCO, RCI, RCD, FQ, FO, FI, FD,
    SMALL, RSMALL, PSMALL, RZSMALL,
    loc, gp_s, gp_r, xb_s, xb_r, xb_p, co_s, co_r, co_p, nt_s, nt_r, nt_p, ga_s, ga_r, ga_p,
    a_s, a_r, a_x, g_s, g_r, g_x, o_s, o_r, o_x, n_s, n_r, n_x,
    wx_s, wx_r, wqz_s, wqf_s, wqz_r, wqb_s, wqb_r, wiz_s, wif_s, wiz_r, wib_s, wib_r,
    wdz_s, wdf_s, wdz_r, wdb_s, wdb_r, woz_s, woz_r, wob_s, wob_r,
    sib_s, sib_r, sibd_r, zq_s, zqe_s, zq_r, zqc_r, zv_s, zve_s, zv_r, zvc_r, zo_s, zoe_s, zo_r, zoc_r,
    zi_s, zie_s, zi_r, zic_r, zd_s, zde_s, zd_r, zdc_r,
    fq_s, fqb_s, fq_r, fqb_r, fv_s, fvb_s, fv_r, fvb_r, fo_s, fo_r, fi_s, fib_s, fi_r, fib_r, fd_s, fd_r, sp_s, sp_r, sz_s, sz_r,
):
    c = lax.axis_index("ctx")
    f = lax.axis_index("fsdp")
    y, k = c // 2, lax.rem(c, 2)
    z, x = f // 2, lax.rem(f, 2)
    x1, y1, k1 = 1 - x, 1 - y, 1 - k
    f1 = 2 * z + x1
    q = 2 * x + y
    sib = (2 * y + k1, f)
    xdev = (c, f1)
    zs = [lax.rem(z + d, 4) for d in (1, 2, 3)]
    near = z + 1 - 2 * lax.rem(z, 2)
    other = 2 - 2 * (z // 2)
    others = (other, other + 1)
    far = 2 - z // 2
    middle = (z == 1) | (z == 2)
    at_end = jnp.logical_not(middle)

    def zdev(target):
        return (c, 2 * target + x)

    plane = []
    for i in range(4):
        ci = lax.rem(c + i, 4)
        for j, xj in enumerate((x, x1)):
            if i or j:
                plane.append((ci, 2 * z + xj))

    def recv(dst, sem):
        remote(dst, dst, sem, sem, sib).wait_recv()

    def sent(src, sem):
        remote(src, src, sem, sem, sib).wait_send()

    def block_half(buf, b, h):
        return buf.at[rows_at(b * TOKENS + 64 * h, 64)]

    def gather_send(src, dst, send, got, passed):
        halves = [src.at[pl.ds(64 * h, 64)] for h in range(2)]
        places = [block_half(dst, c, h) for h in range(2)]
        x_worker, y_worker = (2 * y + x, f1), (2 * y1 + x, f)
        remote(halves[0], places[0], send, passed.at[k], x_worker).start()
        remote(halves[1], places[1], send, passed.at[k], y_worker).start()
        remote(halves[1], places[1], send, got.at[c], x_worker).start()
        remote(halves[0], places[0], send, got.at[c], y_worker).start()
        whole = dst.at[rows_at(c * TOKENS, TOKENS)]

        @pl.when(k == x)
        def _():
            pltpu.make_async_copy(src, whole, got.at[c]).start()

        @pl.when(k != x)
        def _():
            remote(src, whole, send, got.at[c], sib).start()

    same = 1 - lax.rem(x + k, 2)
    pass_y = y + same * (1 - 2 * y)
    pass_to = (same * c + (1 - same) * (2 * y1 + k), same * f1 + (1 - same) * f)

    def gather_pass(dst, send, got, passed):
        for i in range(2):
            b = 2 * pass_y + i
            piece = block_half(dst, b, same)
            recv(piece, passed.at[i])
            remote(piece, piece, send, got.at[b], pass_to).start()

    def gather_wait(dst, got, b):
        @pl.when(b // 2 == pass_y)
        def _():
            recv(block_half(dst, b, 1 - same), got.at[b])

        @pl.when(b // 2 != pass_y)
        def _():
            recv(dst.at[rows_at(b * TOKENS, TOKENS)], got.at[b])

    def four_sent(buf, send):
        @pl.when(k == x)
        def _():
            sent(buf.at[pl.ds(0, 384)], send)

        @pl.when(k != x)
        def _():
            sent(buf, send)

    first_pair = 1 - pass_y

    def scatter_first(buf, dst, send, got, cross, cross_got, i):
        b = 2 * first_pair + i

        @pl.when(k != x)
        def _():
            remote(block_half(buf, b, 0), cross.at[i], send, cross_got.at[i], (2 * y1 + k, f)).start()
            remote(block_half(buf, b, 1), cross.at[i], send, cross_got.at[i], (c, f1)).start()

        whole = buf.at[rows_at(b * TOKENS, TOKENS)]

        @pl.when((k == x) & (i == k))
        def _():
            pltpu.make_async_copy(whole, dst.at[0], got).start()

        @pl.when((k == x) & (i != k))
        def _():
            remote(whole, dst.at[0], send, got, sib).start()

    def scatter_half(buf, dst, send, got, i, h):
        b = 2 * pass_y + i
        place = dst.at[1 + same, rows_at(64 * h, 64)]
        remote(block_half(buf, b, h), place, send, got, (b, 2 * z + k)).start()

    def scatter_second(buf, dst, send, got, i):
        scatter_half(buf, dst, send, got, i, 1 - same)

    def scatter_sums(buf, dst, send, got, cross, cross_got):
        for i in range(2):
            recv(cross.at[i], cross_got.at[i])
            rows = rows_at((2 * pass_y + i) * TOKENS + 64 * same, 64)
            buf[rows, :] = (buf[rows, :].astype(F32) + cross[i].astype(F32)).astype(BF)
            scatter_half(buf, dst, send, got, i, same)

    def half(fb, kk):
        return rows_at(fb * 128 + kk * 64, 64)

    def z_far(piece, send, got, src=None):
        remote(piece if src is None else src, piece, send, got, zdev(far)).start()

    def z_near(piece, send, got, src=None):
        remote(piece if src is None else src, piece, send, got, zdev(near)).start()

    def z_send(piece, send, got):
        z_far(piece, send, got)
        z_near(piece, send, got)

    def down_of(ref, t):
        return ref.at[t]

    def in_of(ref, t):
        return ref.at[pl.ds(2 * t, 2)]

    def value_of(ref, t):
        return ref.at[pl.ds(2 * t, 2), :, value_cols]

    def other_of(ref, t):
        return ref.at[pl.ds(2 * t, 2), :, other_cols]

    value_cols, other_cols = pl.ds(512, 256), pl.ds(0, 512)

    def reduce_others(of, terms, got, send, sem):
        @pl.when(at_end)
        def _():
            for t in others:
                remote(of(terms, t), of(got, t), send, sem.at[t], zdev(near)).start()

    def reduce_near(of, terms, got, send, sem):
        remote(of(terms, near), of(got, near), send, sem.at[near], zdev(near)).start()

    def reduce_middle(of, terms, got, final, send, sem, final_sem):
        @pl.when(middle)
        def _():
            for t in others:
                recv(of(got, t), sem.at[t])
                mine = of(terms, t)
                mine[...] = (mine[...].astype(F32) + of(got, t)[...].astype(F32)).astype(BF)
                remote(mine, final, send, final_sem, zdev(t)).start()

    def take(piece, got, bsend, bgot):
        recv(piece, got)
        remote(piece, piece, bsend, bgot, sib).start()

    def pass_on(piece, send, got):
        remote(piece, piece, send, got, zdev(near)).start()

    def of_row(t, xx):
        return 2 * t + xx

    own_x = pltpu.make_async_copy(x_in.at[0], XO, loc.at[0])
    own_c = pltpu.make_async_copy(cot_in.at[0], CO, loc.at[1])
    myrows = pl.ds(pl.multiple_of(128 * f, 128), 128)
    for w, proj in enumerate((wq_in, wk_in, wv_in)):
        pltpu.make_async_copy(proj, STAGE.at[w], loc.at[3]).start()
    for j in range(4):
        src = wi_in.at[:, pl.ds(pl.multiple_of(512 * (2 * j + x) + 256 * y, 256), 256)]
        pltpu.make_async_copy(src, WIN.at[myrows, pl.ds(256 * j, 256)], loc.at[4]).start()
    pltpu.make_async_copy(
        wd_in.at[rows_at(256 * y, 256)], WDOWN.at[rows_at(256 * z, 256)], loc.at[5]
    ).start()

    pltpu.make_async_copy(wo_in.at[rows_at(64 * y, 64)], WOUT.at[rows_at(64 * z, 64)], loc.at[6]).start()
    own_x.start()
    own_c.start()

    barrier = pltpu.get_barrier_semaphore()
    across = [(c, 2 * t + x1) for t in zs]
    for device in plane + [zdev(t) for t in zs] + across:
        pl.semaphore_signal(barrier, inc=1, device_id=device, device_id_type=MESH_ID)


    PACK[...] = jnp.zeros((8, 128), F32)
    PACK[0:1, :] = attn_in[...].astype(F32)
    PACK[1:2, :] = mlp_in[...].astype(F32)
    PACK[2:3, 0:64] = table_in[...].astype(F32)
    BUCKET[...] = jnp.full((1, WIDTH), -1, jnp.int32)
    BUCKET[0:1, 0 : WIDTH - 1] = bucket_in[...]
    GP[f] = PACK[...]

    pltpu.make_async_copy(STAGE, STAGE, loc.at[3]).wait()

    def pack_heads(dst, dst_rows, src_rows, xx, count):
        low = lax.broadcasted_iota(jnp.int32, (count, 128), 1) < 64
        for w in range(3):
            for j in range(2):
                first, second = [
                    STAGE[w, src_rows, pl.ds(pl.multiple_of(128 * (4 * j + 2 * n + xx), 128), 128)].astype(F32)
                    for n in range(2)
                ]
                left = jnp.where(y == 0, first, pltpu.roll(first, 64, 1))
                right = jnp.where(y == 0, pltpu.roll(second, 64, 1), second)
                dst[dst_rows, 256 * w + 128 * j : 256 * w + 128 * j + 128] = jnp.where(low, left, right).astype(BF)

    pack_heads(ACROSS, slice(0, 64), rows_at(64 * k, 64), x1, 64)
    pack_heads(WQKV, myrows, slice(0, 128), x, 128)
    pl.semaphore_wait(barrier, 13)
    for device in [xdev] + [zdev(t) for t in zs] + across:
        remote(PACK, GP.at[f], gp_s, gp_r, device).start()
    remote(ACROSS, WQKV.at[half(f, k)], wx_s.at[0], wx_r.at[0], xdev).start()
    z_send(WQKV.at[half(f, k)], wqz_s, wqz_r.at[f])
    gather_send(x_in.at[0], XB, xb_s, xb_r, xb_p)
    for j in range(4):
        src = wi_in.at[rows_at(64 * k, 64), pl.ds(pl.multiple_of(512 * (2 * j + x1) + 256 * y, 256), 256)]
        remote(src, WIN.at[half(f, k), pl.ds(256 * j, 256)], wx_s.at[1], wx_r.at[1], xdev).start()

    recv(WQKV.at[half(f1, k)], wx_r.at[0])
    z_send(WQKV.at[half(f1, k)], wqz_s, wqz_r.at[f1])
    remote(WQKV.at[half(f1, k)], WQKV.at[half(f1, k)], wqb_s, wqb_r, sib).start()
    down_half = rows_at(256 * z + 128 * k, 128)
    pltpu.make_async_copy(WIN.at[myrows], WIN.at[myrows], loc.at[4]).wait()

    def out_piece(t):
        return WOUT.at[rows_at(64 * t + 32 * k, 32)]

    out_own = wo_in.at[rows_at(64 * y + 32 * k, 32)]
    z_far(out_piece(z), woz_s, woz_r.at[z], out_own)

    @pl.when(at_end)
    def _():
        z_near(out_piece(z), woz_s, woz_r.at[z], out_own)

    z_far(WIN.at[half(f, k)], wiz_s, wiz_r.at[f])

    @pl.when(at_end)
    def _():
        z_near(WIN.at[half(f, k)], wiz_s, wiz_r.at[f])

    def take_proj(xx):
        for n in range(2):
            h = of_row(others[n], xx)
            piece = WQKV.at[half(h, k)]
            recv(piece, wqz_r.at[h])

            @pl.when(middle)
            def _():
                pass_on(piece, wqf_s, wqz_r.at[h])

            remote(piece, piece, wqb_s, wqb_r, sib).start()

    def take_near(xx):
        g = of_row(near, xx)
        take(WQKV.at[half(g, k)], wqz_r.at[g], wqb_s, wqb_r)

    @pl.when(middle)
    def _():
        take_proj(x)

    gather_pass(XB, xb_s, xb_r, xb_p)
    gather_send(cot_in.at[0], COT, co_s, co_r, co_p)
    take_near(x)

    @pl.when(middle)
    def _():
        take_proj(x1)
        take_near(x1)

        z_near(out_piece(z), woz_s, woz_r.at[z], out_own)

    recv(GP.at[pl.ds(0, 7)], gp_r)

    def row_of(index):
        return jnp.concatenate([GP[g, index : index + 1, :] for g in range(8)], axis=1)

    lane = lax.broadcasted_iota(jnp.int32, (8, 128), 1)
    head_row = lax.broadcasted_iota(jnp.int32, (8, 128), 0)
    head_of = 4 * head_row + 2 * x + y
    head_mask = (lax.rem(lane, 16) == head_of) & (head_row < 4)

    def bucket_hot(g):
        index = lax.broadcasted_iota(jnp.int32, (128, WIDTH), 0)
        wanted = jnp.where(index < 64, 4 * g + lax.div(index, 16), -1)
        return (BUCKET[0:1, :] == wanted)

    def add_bias(g, total):
        table = jnp.where(head_mask, jnp.broadcast_to(GP[g, 2:3, :], (8, 128)), 0.0).astype(BF)
        return total + dot_nn(table, bucket_hot(g).astype(BF))

    offsets = lax.fori_loop(0, 8, add_bias, jnp.zeros((8, WIDTH), F32))
    for h in range(4):
        spread = jnp.broadcast_to(offsets[h : h + 1, :], (128, WIDTH))
        BIAS[h] = pltpu.roll(spread, WIDTH - 127, 1, stride=1, stride_axis=0)
        BACC[h] = jnp.zeros((128, WIDTH), F32)

    gain_one = row_of(0)

    def norm_block(i, carry):
        b = lax.rem(2 * y + i, 4)
        gather_wait(XB, xb_r, b)

        def chunk(r, inner):
            rows = rows_at(b * TOKENS + r * 32, 32)
            values = XB[rows, :].astype(F32)
            scale = lax.rsqrt(jnp.mean(values * values, axis=-1, keepdims=True) + EPS)
            N1[rows, :] = (values * scale * gain_one).astype(BF)
            return inner

        return steps(4, chunk, carry)

    lax.fori_loop(0, 4, norm_block, 0)

    @pl.when(middle)
    def _():
        for t in others:
            recv(out_piece(t), woz_r.at[t])
            pass_on(out_piece(t), woz_s, woz_r.at[t])
            remote(out_piece(t), out_piece(t), wob_s, wob_r, sib).start()

        z_near(WIN.at[half(f, k)], wiz_s, wiz_r.at[f])

    recv(WIN.at[half(f1, k)], wx_r.at[1])
    z_far(WIN.at[half(f1, k)], wiz_s, wiz_r.at[f1])
    remote(WIN.at[half(f1, k)], WIN.at[half(f1, k)], wib_s, wib_r, sib).start()
    pltpu.make_async_copy(WDOWN.at[rows_at(256 * z, 256)], WDOWN.at[rows_at(256 * z, 256)], loc.at[5]).wait()
    z_far(WDOWN.at[down_half], wdz_s, wdz_r.at[z])

    z_near(WIN.at[half(f1, k)], wiz_s, wiz_r.at[f1])

    @pl.when(at_end)
    def _():
        z_near(WDOWN.at[down_half], wdz_s, wdz_r.at[z])
        take_near(x1)
        take_proj(x)
        take_proj(x1)

    recv(WQKV.at[pl.ds(0, 448)], wqb_r)

    def project(n, carry):
        cols = rows_at(256 * n, 256)
        QKV[:, cols] = dot_nn(N1[...], WQKV[:, cols]).astype(BF)
        return carry

    steps(3, project, 0)


    gather_pass(COT, co_s, co_r, co_p)

    @pl.when(middle)
    def _():
        z_near(WDOWN.at[down_half], wdz_s, wdz_r.at[z])

    low_lanes = lax.broadcasted_iota(jnp.int32, (TOKENS, 128), 1) < 64

    def pick(values, hh):
        keep = low_lanes if hh == 0 else jnp.logical_not(low_lanes)
        return jnp.where(keep, values, jnp.zeros_like(values))

    def attend(i, carry):
        b = lax.rem(2 * first_pair + i, 4)
        rows = rows_at(b * TOKENS, TOKENS)
        window = pl.ds(pl.multiple_of(384 - 128 * b, 128), 512)
        for j in range(2):
            outs = []
            for hh in range(2):
                h = 2 * j + hh
                query = pick(QKV[rows, 128 * j : 128 * j + 128], hh)
                scores = dot_nt(query, QKV[:, 256 + 128 * j : 384 + 128 * j]) + BIAS[h, :, window]
                weights = jnp.exp(scores - jnp.max(scores, axis=-1, keepdims=True))
                probs = weights * (1.0 / jnp.sum(weights, axis=-1, keepdims=True))
                PROB[h, rows, :] = probs
                low = probs.astype(BF)
                PLOW[h, rows, :] = low
                outs.append(dot_nn(low, QKV[:, 512 + 128 * j : 640 + 128 * j]))
            AT[rows, 128 * j : 128 * j + 128] = jnp.where(low_lanes, outs[0], outs[1]).astype(BF)

        @pl.when(i == 0)
        def _():
            take(out_piece(near), woz_r.at[near], wob_s, wob_r)

            @pl.when(at_end)
            def _():
                for t in others:
                    take(out_piece(t), woz_r.at[t], wob_s, wob_r)

            pltpu.make_async_copy(WOUT.at[rows_at(64 * z, 64)], WOUT.at[rows_at(64 * z, 64)], loc.at[6]).wait()
            recv(WOUT.at[pl.ds(0, 96)], wob_r)

        SA[rows, :] = dot_nn(AT[rows, :], WOUT[...]).astype(BF)

        @pl.when(i < 2)
        def _():
            scatter_first(SA, RA, a_s, a_r, XA, a_x, i)

        @pl.when(i >= 2)
        def _():
            scatter_second(SA, RA, a_s, a_r, i - 2)

        return carry

    lax.fori_loop(0, 4, attend, 0)
    scatter_sums(SA, RA, a_s, a_r, XA, a_x)

    for xx in (x, x1):
        g = of_row(near, xx)
        take(WIN.at[half(g, k)], wiz_r.at[g], wib_s, wib_r)

    @pl.when(middle)
    def _():
        for i, xx in enumerate((x, x1)):
            for n in range(2):
                g = of_row(others[n], xx)
                recv(WIN.at[half(g, k)], wiz_r.at[g])
                pass_on(WIN.at[half(g, k)], wif_s, wiz_r.at[g])
                remote(WIN.at[half(g, k)], WIN.at[half(g, k)], wib_s, wib_r, sib).start()

    own_x.wait()
    own_c.wait()
    gain_two = row_of(1)
    recv(RA, a_r)

    def home_forward(r, carry):
        rows = rows_at(r * 32, 32)
        hidden = XO[rows, :].astype(F32)
        for s in range(3):
            hidden = hidden + RA[s, rows, :].astype(F32)
        HID[rows, :] = hidden
        scale = lax.rsqrt(jnp.mean(hidden * hidden, axis=-1, keepdims=True) + EPS)
        NTS[rows, :] = (hidden * scale * gain_two).astype(BF)
        return carry

    steps(4, home_forward, 0)
    gather_send(NTS, NTB, nt_s, nt_r, nt_p)

    def down_piece(t, kk):
        return WDOWN.at[rows_at(256 * t + 128 * kk, 128)]

    take(down_piece(near, k), wdz_r.at[near], wdb_s, wdb_r)

    @pl.when(middle)
    def _():
        for n in range(2):
            t = others[n]
            recv(down_piece(t, k), wdz_r.at[t])
            pass_on(down_piece(t, k), wdf_s, wdz_r.at[t])
            remote(down_piece(t, k), down_piece(t, k), wdb_s, wdb_r, sib).start()

    @pl.when(at_end)
    def _():
        for xx in (x, x1):
            for t in others:
                g = of_row(t, xx)
                take(WIN.at[half(g, k)], wiz_r.at[g], wib_s, wib_r)

    recv(WIN.at[pl.ds(0, 448)], wib_r)

    gather_pass(NTB, nt_s, nt_r, nt_p)

    def feed(i, carry):
        yy = lax.rem(y + i, 2)
        rows = rows_at(256 * yy, 256)
        for b in (2 * yy, 2 * yy + 1):
            gather_wait(NTB, nt_r, b)

        def hidden_units(n, inner):
            cols = rows_at(256 * n, 256)
            pre = dot_nn(NTB[rows, :], WIN[:, cols])
            cdf = 0.5 * (1.0 + lax.erf(pre * 0.7071067811865476))
            ACT[rows, cols] = (pre * cdf).astype(BF)
            SLOPE[rows, cols] = cdf + pre * jnp.exp(-0.5 * pre * pre) * 0.3989422804014327
            return inner

        return steps(4, hidden_units, carry)

    lax.fori_loop(0, 2, feed, 0)

    for b in range(4):
        gather_wait(COT, co_r, b)

    order = (other, other + 1, near, z)

    def grad_down(i, carry):
        m = jnp.where(i < 2, other + i, jnp.where(i == 2, near, z))
        tile = dot_tn(ACT[:, rows_at(256 * m, 256)], COT[...]).astype(BF)
        DD[0, m] = tile[0:128]
        DD[1, m] = tile[128:256]
        remote(DD.at[k1, m], SIBD.at[m], sib_s.at[0], sibd_r.at[i], sib).start()
        return carry

    steps(4, grad_down, 0)

    def join_down(i, carry):
        m = jnp.where(i < 2, other + i, jnp.where(i == 2, near, z))
        recv(SIBD.at[m], sibd_r.at[i])
        ZD[m] = (DD[k, m].astype(F32) + SIBD[m].astype(F32)).astype(BF)

        @pl.when(at_end & (i < 2))
        def _():
            remote(ZD.at[m], RED.at[m], zde_s, zd_r.at[m], zdev(near)).start()

        @pl.when(middle & (i == 2))
        def _():
            remote(ZD.at[m], RED.at[m], zd_s, zd_r.at[m], zdev(near)).start()

        return carry

    steps(4, join_down, 0)

    @pl.when(at_end)
    def _():
        for t in others:
            take(down_piece(t, k), wdz_r.at[t], wdb_s, wdb_r)

    recv(WDOWN.at[pl.ds(0, 384)], wdb_r)

    def back_feed(i, carry):
        yy = lax.rem(first_pair + i, 2)
        rows = rows_at(256 * yy, 256)

        def back_act(n, inner):
            cols = rows_at(256 * n, 256)
            GPRE[rows, cols] = (dot_nt(COT[rows, :], WDOWN[cols, :]) * SLOPE[rows, cols]).astype(BF)
            return inner

        steps(4, back_act, 0)

        def back_normed(n, inner):
            cols = rows_at(256 * n, 256)
            SG[rows, cols] = dot_nt(GPRE[rows, :], WIN[cols, :]).astype(BF)
            return inner

        steps(4, back_normed, 0)

        @pl.when(i == 0)
        def _():
            for n in range(2):
                scatter_first(SG, RG, g_s, g_r, XG, g_x, n)

        @pl.when(i == 1)
        def _():
            for n in range(2):
                scatter_second(SG, RG, g_s, g_r, n)

        return carry

    lax.fori_loop(0, 2, back_feed, 0)

    def grad_in(m, carry):
        tile = dot_tn(NTB[:, rows_at(256 * m, 256)], GPRE[...]).astype(BF)
        for part in range(2):
            DI[0, 2 * m + part] = tile[128 * part : 128 * part + 64]
            DI[1, 2 * m + part] = tile[128 * part + 64 : 128 * part + 128]
        return carry

    steps(4, grad_in, 0)
    scatter_sums(SG, RG, g_s, g_r, XG, g_x)
    remote(DI.at[k1], SIBI, sib_s.at[1], sib_r.at[1], sib).start()

    def down_project(n, carry):
        cols = rows_at(256 * n, 256)
        SO[:, cols] = dot_nn(ACT[...], WDOWN[:, cols]).astype(BF)
        return carry

    steps(4, down_project, 0)

    recv(SIBI, sib_r.at[1])

    def join_in(m, carry):
        ZI[m] = (DI[k, m].astype(F32) + SIBI[m].astype(F32)).astype(BF)
        return carry

    steps(8, join_in, 0)
    reduce_others(in_of, ZI, REI, zie_s, zi_r)

    @pl.when(at_end)
    def _():
        reduce_near(down_of, ZD, RED, zd_s, zd_r)

    reduce_near(in_of, ZI, REI, zi_s, zi_r)

    recv(RG, g_r)

    def home_back(r, total):
        rows = rows_at(r * 32, 32)
        grad = RG[0, rows, :].astype(F32)
        for s in range(1, 3):
            grad = grad + RG[s, rows, :].astype(F32)
        hidden = HID[rows, :]
        scale = lax.rsqrt(jnp.mean(hidden * hidden, axis=-1, keepdims=True) + EPS)
        scaled = grad * gain_two
        inner = jnp.mean(scaled * hidden, axis=-1, keepdims=True)
        back = CO[rows, :].astype(F32) + scale * scaled - hidden * (scale * scale * scale * inner)
        GH[rows, :] = back
        GALS[rows, :] = back.astype(BF)
        return total + jnp.sum((grad * hidden * scale).reshape(4, 8, WIDTH), axis=0)

    mlp_gain_grad = steps(4, home_back, jnp.zeros((8, WIDTH), F32))
    gather_send(GALS, GAL, ga_s, ga_r, ga_p)
    reduce_middle(down_of, ZD, RED, RCD, zde_s, zd_r, zdc_r)

    mlp_gain_grad = jnp.sum(mlp_gain_grad, axis=0, keepdims=True)
    for g in range(8):
        SMALL[1, g : g + 1, :] = mlp_gain_grad[:, 128 * g : 128 * g + 128]

    gather_pass(GAL, ga_s, ga_r, ga_p)
    for i in range(2):
        scatter_first(SO, RO, o_s, o_r, XS, o_x, i)
        scatter_second(SO, RO, o_s, o_r, i)

    all_low = lax.broadcasted_iota(jnp.int32, (512, 128), 1) < 64

    def pick_all(values, hh):
        keep = all_low if hh == 0 else jnp.logical_not(all_low)
        return jnp.where(keep, values, jnp.zeros_like(values))

    def attend_back(i, carry):
        b = lax.rem(2 * y + i, 4)
        rows = rows_at(b * TOKENS, TOKENS)
        gather_wait(GAL, ga_r, b)

        @pl.when(i == 2)
        def _():
            reduce_middle(in_of, ZI, REI, RCI, zie_s, zi_r, zic_r)

        GATT[rows, :] = dot_nt(GAL[rows, :], WOUT[...]).astype(BF)
        for j in range(2):
            pair = slice(128 * j, 128 * j + 128)
            keys = QKV[:, 256 + 128 * j : 384 + 128 * j]
            values = QKV[:, 512 + 128 * j : 640 + 128 * j]
            outs = []
            for hh in range(2):
                h = 2 * j + hh
                grad_att = pick(GATT[rows, pair], hh)
                probs = PROB[h, rows, :]
                grad_probs = dot_nt(grad_att, values)
                inner = jnp.sum(probs * grad_probs, axis=-1, keepdims=True)
                grad_scores = (probs * (grad_probs - inner)).astype(BF)
                DS[h, rows, :] = grad_scores
                outs.append(dot_nn(grad_scores, keys))
            DQKV[rows, pair] = jnp.where(low_lanes, outs[0], outs[1]).astype(BF)
        return carry

    lax.fori_loop(0, 4, attend_back, 0)
    scatter_sums(SO, RO, o_s, o_r, XS, o_x)

    def grad_keys(j, carry):
        query = QKV[:, rows_at(128 * j, 128)]
        first = dot_tn(DS[2 * j], pick_all(query, 0))
        second = dot_tn(DS[2 * j + 1], pick_all(query, 1))
        DQKV[:, pl.ds(pl.multiple_of(256 + 128 * j, 128), 128)] = jnp.where(all_low, first, second).astype(BF)
        return carry

    steps(2, grad_keys, 0)

    def grad_values(j, carry):
        grad_att = GATT[:, rows_at(128 * j, 128)]
        first = dot_tn(PLOW[2 * j], pick_all(grad_att, 0))
        second = dot_tn(PLOW[2 * j + 1], pick_all(grad_att, 1))
        DQKV[:, pl.ds(pl.multiple_of(512 + 128 * j, 128), 128)] = jnp.where(all_low, first, second).astype(BF)
        return carry

    steps(2, grad_values, 0)

    def grad_proj(first, width):
        def step(m, carry):
            tile = dot_tn(N1[:, rows_at(256 * m, 256)], DQKV[:, first : first + width]).astype(BF)
            for part in range(2):
                DQ[0, 2 * m + part, :, first : first + width] = tile[128 * part : 128 * part + 64]
                DQ[1, 2 * m + part, :, first : first + width] = tile[128 * part + 64 : 128 * part + 128]
            return carry

        steps(4, step, 0)

    def join_proj(first, width):
        def step(m, carry):
            total = DQ[k, m, :, first : first + width].astype(F32) + SIBQ[m, :, first : first + width].astype(F32)
            ZQ[m, :, first : first + width] = total.astype(BF)
            return carry

        steps(8, step, 0)

    grad_proj(0, 512)
    remote(DQ.at[k1, :, :, other_cols], SIBQ.at[:, :, other_cols], sib_s.at[4], sib_r.at[4], sib).start()
    grad_proj(512, 256)
    remote(DQ.at[k1, :, :, value_cols], SIBQ.at[:, :, value_cols], sib_s.at[2], sib_r.at[2], sib).start()

    def back_project(i, carry):
        yy = lax.rem(first_pair + i, 2)
        rows = rows_at(256 * yy, 256)
        SN[rows, :] = dot_nt(DQKV[rows, :], WQKV[...]).astype(BF)

        @pl.when(i == 0)
        def _():
            for n in range(2):
                scatter_first(SN, RN, n_s, n_r, XN, n_x, n)

        @pl.when(i == 1)
        def _():
            for n in range(2):
                scatter_second(SN, RN, n_s, n_r, n)

        return carry

    lax.fori_loop(0, 2, back_project, 0)

    recv(SIBQ.at[:, :, other_cols], sib_r.at[4])
    join_proj(0, 512)
    reduce_others(other_of, ZQ, REQ, zqe_s, zq_r)

    def grad_out_rows(m, carry):
        tile = dot_tn(AT[:, rows_at(128 * m, 128)], GAL[...]).astype(BF)
        for n in range(2):
            for kk in range(2):
                DO[kk, 2 * m + n] = tile[64 * n + 32 * kk : 64 * n + 32 * kk + 32]
        return carry

    steps(2, grad_out_rows, 0)
    remote(DO.at[k1], SIBO, sib_s.at[3], sib_r.at[3], sib).start()
    scatter_sums(SN, RN, n_s, n_r, XN, n_x)
    recv(SIBQ.at[:, :, value_cols], sib_r.at[2])
    join_proj(512, 256)
    reduce_others(value_of, ZQ, REQ, zve_s, zv_r)
    recv(SIBO, sib_r.at[3])
    ZO[...] = (DO[k].astype(F32) + SIBO[...].astype(F32)).astype(BF)
    reduce_others(down_of, ZO, REO, zoe_s, zo_r)
    reduce_near(other_of, ZQ, REQ, zq_s, zq_r)
    reduce_near(value_of, ZQ, REQ, zv_s, zv_r)
    reduce_near(down_of, ZO, REO, zo_s, zo_r)

    def place_scores(i, carry):
        rows = rows_at(i * TOKENS, TOKENS)
        window = pl.ds(pl.multiple_of(384 - 128 * i, 128), 512)
        for h in range(4):
            BACC[h, :, window] = BACC[h, :, window] + DS[h, rows, :].astype(F32)
        return carry

    lax.fori_loop(0, 4, place_scores, 0)
    head_sums = []
    for h in range(4):
        rest = BACC[h]
        count = 64
        while count >= 8:
            rest = pltpu.roll(rest[0:count, :], count, 1) + rest[count : 2 * count, :]
            count //= 2
        for bit in (1, 2, 4):
            shift_row = 7 - lax.broadcasted_iota(jnp.int32, (8, WIDTH), 0)
            rest = jnp.where(lax.rem(lax.div(shift_row, bit), 2) == 1, pltpu.roll(rest, bit, 1), rest)
        head_sums.append(jnp.sum(rest, axis=0, keepdims=True))
    head_sums = jnp.concatenate(head_sums + [jnp.zeros((4, WIDTH), F32)], axis=0)
    coarse = head_sums.astype(BF)
    split_sums = jnp.concatenate([coarse, (head_sums - coarse.astype(F32)).astype(BF)], axis=0)
    both_masks = jnp.concatenate([head_mask.astype(F32)] * 2, axis=0) > 0.5

    def bucket_sums(g, carry):
        sums = dot_nt(split_sums, bucket_hot(g).astype(BF))
        SMALL[2, pl.ds(g, 1), :] = jnp.sum(jnp.where(both_masks, sums, 0.0), axis=0, keepdims=True)
        return carry

    lax.fori_loop(0, 8, bucket_sums, 0)

    recv(RED.at[z], zd_r.at[z])
    recv(RCD, zdc_r)
    FD[...] = (ZD[z].astype(F32) + RED[z].astype(F32) + RCD[...].astype(F32)).astype(BF)

    def down_rows(cc):
        return odown.at[rows_at(128 * cc, 128)]

    y_core = (2 * y1 + k, f)
    remote(FD, down_rows(c), fd_s, fd_r.at[1], y_core).start()
    remote(FD, down_rows(c), fd_s, fd_r.at[2], sib).start()
    pltpu.make_async_copy(FD, down_rows(c), fd_r.at[0]).start()

    def spread(final, place, send, bsend, got, bgot):
        remote(final.at[x1], place(q, k), send, got.at[3], (2 * y1 + k, f1)).start()
        remote(final.at[x1], place(q, k), send, got.at[2], (c, f1)).start()
        remote(final.at[x], place(q, k), send, got.at[1], y_core).start()
        remote(final.at[x], place(q, k), bsend, bgot, sib).start()
        pltpu.make_async_copy(final.at[x], place(q, k), got.at[0]).start()

    chips = (2 * x + y1, 2 * x1 + y, 2 * x1 + y1)

    def spread_on(place, bsend, got, bgot):
        for i in range(3):
            piece = place(chips[i], k)
            recv(piece, got.at[i + 1])
            remote(piece, piece, bsend, bgot, sib).start()

    def in_place(qq, kk):
        return oin.at[:, qq, rows_at(64 * kk, 64), :]

    recv(RO, o_r)

    def home_out(r, carry):
        rows = rows_at(r * 32, 32)
        result = HID[rows, :]
        for s in range(3):
            result = result + RO[s, rows, :].astype(F32)
        out_ref[0, rows, :] = result.astype(BF)
        return carry

    steps(4, home_out, 0)
    recv(RN, n_r)

    def home_inputs(r, total):
        rows = rows_at(r * 32, 32)
        grad = RN[0, rows, :].astype(F32)
        for s in range(1, 3):
            grad = grad + RN[s, rows, :].astype(F32)
        values = XO[rows, :].astype(F32)
        scale = lax.rsqrt(jnp.mean(values * values, axis=-1, keepdims=True) + EPS)
        scaled = grad * gain_one
        inner = jnp.mean(scaled * values, axis=-1, keepdims=True)
        back = GH[rows, :] + scale * scaled - values * (scale * scale * scale * inner)
        gin_ref[0, rows, :] = back.astype(BF)
        return total + jnp.sum((grad * values * scale).reshape(4, 8, WIDTH), axis=0)

    attn_gain_grad = steps(4, home_inputs, jnp.zeros((8, WIDTH), F32))
    attn_gain_grad = jnp.sum(attn_gain_grad, axis=0, keepdims=True)
    for g in range(8):
        SMALL[0, g : g + 1, :] = attn_gain_grad[:, 128 * g : 128 * g + 128]

    for i in range(4):
        ci = lax.rem(c + i, 4)
        for j, xj in enumerate((x, x1)):
            if i or j:
                remote(SMALL, RSMALL.at[2 * c + x], sp_s, sp_r, (ci, 2 * z + xj)).start()

    recv(in_of(REI, z), zi_r.at[z])
    recv(RCI, zic_r)
    for xx in range(2):
        total = ZI[2 * z + xx].astype(F32) + REI[2 * z + xx].astype(F32) + RCI[xx].astype(F32)
        for j in range(4):
            FI[xx, j] = total[:, 256 * j : 256 * j + 256].astype(BF)
    spread(FI, in_place, fi_s, fib_s, fi_r, fib_r)

    reduce_middle(other_of, ZQ, REQ, RCQ.at[:, :, other_cols], zqe_s, zq_r, zqc_r)
    reduce_middle(value_of, ZQ, REQ, RCQ.at[:, :, value_cols], zve_s, zv_r, zvc_r)
    reduce_middle(down_of, ZO, REO, RCO, zoe_s, zo_r, zoc_r)

    def final_proj(of, cols, first, width, sem, final_sem):
        recv(of(REQ, z), sem.at[z])
        recv(RCQ.at[:, :, cols], final_sem)
        for xx in range(2):
            total = ZQ[2 * z + xx, :, first : first + width].astype(F32)
            total = total + REQ[2 * z + xx, :, first : first + width].astype(F32)
            total = total + RCQ[xx, :, first : first + width].astype(F32)
            FQ[xx, :, first : first + width] = total.astype(BF)

    def other_place(qq, kk):
        return oqkv.at[qq, rows_at(64 * kk, 64), other_cols]

    def value_place(qq, kk):
        return oqkv.at[qq, rows_at(64 * kk, 64), value_cols]

    def out_rows(cc):
        return oout.at[rows_at(32 * cc, 32)]

    y_rows = down_rows(2 * y1 + k)
    recv(y_rows, fd_r.at[1])
    remote(y_rows, y_rows, fd_s, fd_r.at[2], sib).start()
    recv(RSMALL.at[pl.ds(0, 7)], sp_r)
    plane_sum = SMALL[...]
    for i in range(4):
        ci = lax.rem(c + i, 4)
        for j, xj in enumerate((x, x1)):
            if i or j:
                plane_sum = plane_sum + RSMALL[2 * ci + xj]
    for t in range(4):
        for n in range(3):
            pair = plane_sum[n, 2 * t : 2 * t + 2, :]
            PSMALL[t, n : n + 1, :] = jnp.where(x == 0, pair[0:1], pair[1:2])
    for t in zs:
        remote(PSMALL.at[t], RZSMALL.at[z], sz_s, sz_r, zdev(t)).start()

    final_proj(other_of, other_cols, 0, 512, zq_r, zqc_r)
    spread(FQ.at[:, :, other_cols], other_place, fq_s, fqb_s, fq_r, fqb_r)
    final_proj(value_of, value_cols, 512, 256, zv_r, zvc_r)
    spread(FQ.at[:, :, value_cols], value_place, fv_s, fvb_s, fv_r, fvb_r)
    spread_on(in_place, fib_s, fi_r, fib_r)
    recv(REO.at[z], zo_r.at[z])
    recv(RCO, zoc_r)
    FO[...] = (ZO[z].astype(F32) + REO[z].astype(F32) + RCO[...].astype(F32)).astype(BF)
    remote(FO, out_rows(c), fo_s, fo_r.at[1], y_core).start()
    remote(FO, out_rows(c), fo_s, fo_r.at[2], sib).start()
    pltpu.make_async_copy(FO, out_rows(c), fo_r.at[0]).start()
    spread_on(other_place, fqb_s, fq_r, fqb_r)
    spread_on(value_place, fvb_s, fv_r, fvb_r)
    y_out = out_rows(2 * y1 + k)
    recv(y_out, fo_r.at[1])
    remote(y_out, y_out, fo_s, fo_r.at[2], sib).start()
    recv(RZSMALL.at[pl.ds(0, 3)], sz_r)
    total = PSMALL[z]
    for t in zs:
        total = total + RZSMALL[t]
    small_ref[...] = total

    recv(down_rows(c), fd_r.at[0])
    recv(odown.at[pl.ds(0, 256)], fd_r.at[2])
    recv(out_rows(c), fo_r.at[0])
    recv(oout.at[pl.ds(0, 64)], fo_r.at[2])
    recv(in_place(q, k), fi_r.at[0])
    recv(oin.at[:, :, rows_at(64 * k1, 64), :], fib_r)
    recv(other_place(q, k), fq_r.at[0])
    recv(oqkv.at[:, rows_at(64 * k1, 64), other_cols], fqb_r)
    recv(value_place(q, k), fv_r.at[0])
    recv(oqkv.at[:, rows_at(64 * k1, 64), value_cols], fvb_r)

    sent(GP.at[pl.ds(0, 7)], gp_s)
    four_sent(XB, xb_s)
    four_sent(COT, co_s)
    four_sent(NTB, nt_s)
    four_sent(GAL, ga_s)
    four_sent(SA, a_s)
    four_sent(SG, g_s)
    four_sent(SO, o_s)
    four_sent(SN, n_s)
    sent(WQKV.at[pl.ds(0, 256)], wqz_s)
    sent(WQKV.at[half(f, k)], wx_s.at[0])
    sent(WIN.at[half(f, k)], wx_s.at[1])
    sent(WIN.at[pl.ds(0, 256)], wiz_s)
    sent(WDOWN.at[pl.ds(0, 256)], wdz_s)
    sent(WQKV.at[pl.ds(0, 448)], wqb_s)
    sent(WIN.at[pl.ds(0, 448)], wib_s)
    sent(WDOWN.at[pl.ds(0, 384)], wdb_s)
    sent(value_of(ZQ, near), zv_s)
    sent(other_of(ZQ, near), zq_s)
    sent(ZQ.at[pl.ds(0, 4), :, value_cols], zve_s)
    sent(ZQ.at[pl.ds(0, 4), :, other_cols], zqe_s)
    sent(down_of(ZD, near), zd_s)
    sent(ZD.at[pl.ds(0, 2)], zde_s)
    sent(PSMALL.at[pl.ds(0, 3)], sz_s)
    sent(in_of(ZI, near), zi_s)
    sent(ZI.at[pl.ds(0, 4)], zie_s)

    @pl.when(middle)
    def _():
        sent(WDOWN.at[pl.ds(0, 256)], wdf_s)
        sent(WQKV.at[pl.ds(0, 256)], wqf_s)
        sent(WIN.at[pl.ds(0, 256)], wif_s)

    @pl.when(middle)
    def _():
        sent(WOUT.at[pl.ds(0, 128)], woz_s)

    @pl.when(at_end)
    def _():
        sent(WOUT.at[pl.ds(0, 64)], woz_s)

    sent(WOUT.at[pl.ds(0, 96)], wob_s)
    sent(ZO.at[near], zo_s)
    sent(ZO.at[pl.ds(0, 2)], zoe_s)
    sent(oout.at[pl.ds(0, 96)], fo_s)
    sent(DD.at[k1], sib_s.at[0])
    sent(DI.at[k1], sib_s.at[1])
    sent(DQ.at[k1, :, :, value_cols], sib_s.at[2])
    sent(DO.at[k1], sib_s.at[3])
    sent(DQ.at[k1, :, :, other_cols], sib_s.at[4])
    sent(odown.at[pl.ds(0, 384)], fd_s)
    sent(oin.at[:, pl.ds(0, 3), pl.ds(0, 64), :], fi_s)
    sent(oqkv.at[pl.ds(0, 3), pl.ds(0, 64), other_cols], fq_s)
    sent(oqkv.at[pl.ds(0, 3), pl.ds(0, 64), value_cols], fv_s)
    sent(oin.at[:, :, rows_at(64 * k, 64), :], fib_s)
    sent(oqkv.at[:, rows_at(64 * k, 64), other_cols], fqb_s)
    sent(oqkv.at[:, rows_at(64 * k, 64), value_cols], fvb_s)
    sent(RSMALL.at[pl.ds(0, 7)], sp_s)


def plane_shards(
    inputs, cotangent, w_query, w_key, w_value, w_out, w_in, w_down, gain_attn, gain_mlp, rel_bias, buckets
):
    vm = pltpu.VMEM
    dma = pltpu.SemaphoreType.DMA
    block = lambda kind: vm((TOKENS, WIDTH), kind)
    tokens = lambda width, kind: vm((512, width), kind)
    scratch = [
        block(BF), block(BF), vm((8, 128), F32), vm((1, 1024), jnp.int32),
        vm((3, 128, 1024), BF), vm((64, 768), BF), vm((8, 8, 128), F32),
        tokens(1024, BF), tokens(1024, BF), tokens(1024, BF), tokens(1024, BF), tokens(1024, BF),
        vm((1024, 768), BF), vm((256, 1024), BF), vm((1024, 1024), BF), vm((1024, 1024), BF),
        tokens(768, BF), vm((4, 512, 512), F32), vm((4, 512, 512), BF), vm((4, 128, 1024), F32),
        tokens(256, BF), tokens(1024, BF), tokens(1024, F32), tokens(1024, BF),
        tokens(256, BF), tokens(768, BF), vm((4, 512, 512), BF), vm((4, 128, 1024), F32),
        tokens(1024, BF), tokens(1024, BF), tokens(1024, BF), tokens(1024, BF),
        vm((3, 128, 1024), BF), vm((3, 128, 1024), BF), vm((3, 128, 1024), BF), vm((3, 128, 1024), BF),
        vm((2, 64, 1024), BF), vm((2, 64, 1024), BF), vm((2, 64, 1024), BF), vm((2, 64, 1024), BF),
        block(F32), block(F32), block(BF), block(BF),
        vm((2, 8, 64, 768), BF), vm((2, 4, 32, 1024), BF), vm((2, 8, 64, 1024), BF), vm((2, 4, 128, 1024), BF),
        vm((8, 64, 768), BF), vm((4, 32, 1024), BF), vm((8, 64, 1024), BF), vm((4, 128, 1024), BF),
        vm((8, 64, 768), BF), vm((4, 32, 1024), BF), vm((8, 64, 1024), BF), vm((4, 128, 1024), BF),
        vm((8, 64, 768), BF), vm((4, 32, 1024), BF), vm((8, 64, 1024), BF), vm((4, 128, 1024), BF),
        vm((2, 64, 768), BF), vm((32, 1024), BF), vm((2, 64, 1024), BF), vm((128, 1024), BF),
        vm((2, 64, 768), BF), vm((32, 1024), BF), vm((2, 4, 64, 256), BF), vm((128, 1024), BF),
        vm((3, 8, 128), F32), vm((8, 3, 8, 128), F32), vm((4, 8, 128), F32), vm((4, 8, 128), F32),
        dma((7,)), dma, dma, dma, dma((4,)), dma((2,)), dma, dma((4,)), dma((2,)), dma, dma((4,)), dma((2,)), dma, dma((4,)), dma((2,)),
        dma, dma, dma((2,)), dma, dma, dma((2,)), dma, dma, dma((2,)), dma, dma, dma((2,)),
        dma((2,)), dma((2,)), dma, dma, dma((8,)), dma, dma, dma, dma, dma((8,)), dma, dma,
        dma, dma, dma((4,)), dma, dma, dma, dma((4,)), dma, dma,
        dma((5,)), dma((5,)), dma((4,)), dma, dma, dma((4,)), dma, dma, dma, dma((4,)), dma, dma, dma, dma((4,)), dma,
        dma, dma, dma((4,)), dma, dma, dma, dma((4,)), dma,
        dma, dma, dma((4,)), dma, dma, dma, dma((4,)), dma, dma, dma((3,)), dma, dma, dma((4,)), dma, dma, dma((3,)), dma, dma, dma, dma,
    ]
    anywhere = pl.BlockSpec(memory_space=pl.ANY)
    in_vmem = pl.BlockSpec(memory_space=pltpu.VMEM)
    shape = jax.ShapeDtypeStruct
    output, grad_inputs, proj, out, hidden, down, small = pl.pallas_call(
        fused_layer,
        out_shape=(
            shape((1, TOKENS, WIDTH), BF),
            shape((1, TOKENS, WIDTH), BF),
            shape((4, 128, 768), BF),
            shape((128, 1024), BF),
            shape((4, 4, 128, 256), BF),
            shape((512, 1024), BF),
            shape((8, 128), F32),
        ),
        in_specs=[anywhere] * 8 + [in_vmem] * 4,
        out_specs=(in_vmem, in_vmem, anywhere, anywhere, anywhere, anywhere, in_vmem),
        scratch_shapes=scratch,
        compiler_params=pltpu.CompilerParams(
            collective_id=0, has_side_effects=True, vmem_limit_bytes=63 << 20
        ),
        cost_estimate=pl.CostEstimate(flops=11 * 10**9, bytes_accessed=16 * 2**20, transcendentals=3 * 2**20),
    )(inputs, cotangent, w_query, w_key, w_value, w_out, w_in, w_down, gain_attn[None], gain_mlp[None], rel_bias[None], buckets[None])
    return finish(output, grad_inputs, proj, out, hidden, down, small)


def finish_kernel(
    output, grad_inputs, proj, out, hidden, down, small,
    o_output, o_inputs, o_query, o_key, o_value, o_out, o_in, o_down, o_attn, o_mlp, o_bias,
    b_output, b_inputs, b_proj, b_out, b_hidden, b_down, b_small, w_proj, w_out, w_in, w_down, got, left,
):
    moves = [
        pltpu.make_async_copy(proj, b_proj, got.at[0]),
        pltpu.make_async_copy(hidden, b_hidden, got.at[1]),
        pltpu.make_async_copy(down, b_down, got.at[2]),
        pltpu.make_async_copy(out, b_out, got.at[3]),
        pltpu.make_async_copy(small, b_small, got.at[4]),
        pltpu.make_async_copy(output, b_output, got.at[5]),
        pltpu.make_async_copy(grad_inputs, b_inputs, got.at[6]),
    ]
    for move in moves:
        move.start()
    sends = []

    def write(src, dst, slot):
        copy = pltpu.make_async_copy(src, dst, left.at[slot])
        copy.start()
        sends.append(copy)

    moves[0].wait()
    for w, place in enumerate((o_query, o_key, o_value)):
        for shard in range(8):
            z, x = shard // 2, shard % 2
            lanes = slice(256 * w + 64 * z, 256 * w + 64 * z + 64)
            parts = [b_proj[2 * x + y, :, lanes].astype(F32) for y in range(2)]
            w_proj[w, :, 128 * shard : 128 * shard + 128] = jnp.concatenate(parts, axis=1)
        write(w_proj.at[w], place, w)
    moves[1].wait()
    for r in range(4):
        rows = slice(32 * r, 32 * r + 32)
        for z in range(4):
            for q in range(4):
                w_in[rows, 256 * (4 * z + q) : 256 * (4 * z + q) + 256] = b_hidden[z, q, rows, :].astype(F32)
        write(w_in.at[pl.ds(32 * r, 32)], o_in.at[pl.ds(32 * r, 32)], 3 + r)
    moves[2].wait()
    for r in range(4):
        rows = slice(128 * r, 128 * r + 128)
        w_down[rows, :] = b_down[rows, :].astype(F32)
        write(w_down.at[pl.ds(128 * r, 128)], o_down.at[pl.ds(128 * r, 128)], 7 + r)
    moves[3].wait()
    w_out[...] = b_out[...].astype(F32)
    write(w_out, o_out, 11)
    moves[4].wait()
    o_attn[...] = b_small[0:1, :]
    o_mlp[...] = b_small[1:2, :]
    o_bias[...] = b_small[2:3, 0:64]
    moves[5].wait()
    write(b_output, o_output, 12)
    moves[6].wait()
    write(b_inputs, o_inputs, 13)
    for copy in sends:
        copy.wait()


def finish(output, grad_inputs, proj, out, hidden, down, small):
    shape = jax.ShapeDtypeStruct
    vm = pltpu.VMEM
    anywhere = pl.BlockSpec(memory_space=pl.ANY)
    in_vmem = pl.BlockSpec(memory_space=pltpu.VMEM)
    results = pl.pallas_call(
        finish_kernel,
        out_shape=(
            shape(output.shape, BF),
            shape(grad_inputs.shape, BF),
            shape((128, 1024), F32),
            shape((128, 1024), F32),
            shape((128, 1024), F32),
            shape((128, 1024), F32),
            shape((128, 4096), F32),
            shape((512, 1024), F32),
            shape((1, 128), F32),
            shape((1, 128), F32),
            shape((1, 64), F32),
        ),
        in_specs=[anywhere] * 7,
        out_specs=(anywhere,) * 8 + (in_vmem,) * 3,
        scratch_shapes=[
            vm(output.shape, BF), vm(grad_inputs.shape, BF), vm(proj.shape, BF), vm(out.shape, BF), vm(hidden.shape, BF), vm(down.shape, BF), vm(small.shape, F32),
            vm((3, 128, 1024), F32), vm((128, 1024), F32), vm((128, 4096), F32), vm((512, 1024), F32),
            pltpu.SemaphoreType.DMA((7,)), pltpu.SemaphoreType.DMA((14,)),
        ],
        compiler_params=pltpu.CompilerParams(vmem_limit_bytes=63 << 20),
        cost_estimate=pl.CostEstimate(flops=0, bytes_accessed=10 * 2**20, transcendentals=0),
    )(output, grad_inputs, proj, out, hidden, down, small)
    return results[:8] + (results[8].reshape(128), results[9].reshape(128), results[10].reshape(64))


def solution(mesh):
    placed = (
        P("fsdp", "ctx", None),
        P("fsdp", "ctx", None),
        P("fsdp", None),
        P("fsdp", None),
        P("fsdp", None),
        P("fsdp", None),
        P("fsdp", None),
        P("fsdp", None),
        P("fsdp"),
        P("fsdp"),
        P("fsdp"),
        P(),
    )
    by_planes = mesh.shape["ctx"] == 4 and mesh.shape["fsdp"] == 8
    return jax.shard_map(
        plane_shards if by_planes else shards,
        mesh=mesh,
        in_specs=placed,
        out_specs=(
            P("fsdp", "ctx", None),
            P("fsdp", "ctx", None),
            P("fsdp", None),
            P("fsdp", None),
            P("fsdp", None),
            P("fsdp", None),
            P("fsdp", None),
            P("fsdp", None),
            P("fsdp"),
            P("fsdp"),
            P("fsdp"),
        ),
        check_vma=False,
    )
```

```python
import jax
import jax.numpy as jnp
from jax import lax
from jax.experimental import pallas as pl
from jax.experimental.pallas import tpu as pltpu
from jax.sharding import PartitionSpec as P

HEADS = 16
HEAD = 64
BUCKETS = 32


EPS = 1e-06


def norm_rows(values, gain):
    return values * lax.rsqrt(jnp.mean(values * values, axis=-1, keepdims=True) + EPS) * gain


def smooth_gelu(values):
    return 0.5 * values * (1.0 + jax.scipy.special.erf(values * 0.7071067811865476))


def gelu_slope(values):
    return (
        0.5 * (1.0 + jax.scipy.special.erf(values * 0.7071067811865476))
        + values * jnp.exp(-0.5 * values * values) * 0.3989422804014327
    )


def bucket_offsets(buckets, first_query, query_count):
    seq_length = (buckets.shape[0] + 1) // 2
    key_place = jnp.arange(seq_length, dtype=jnp.int32)
    query_place = first_query + jnp.arange(query_count, dtype=jnp.int32)
    return key_place[None, :] - query_place[:, None] + (seq_length - 1)


def make_bias(flat_table, buckets, first_query, query_count):
    bias_table = flat_table.reshape(BUCKETS, HEADS)
    one_hot = (buckets[:, None] == jnp.arange(BUCKETS, dtype=jnp.int32)[None, :]).astype(
        flat_table.dtype
    )
    per_offset = jnp.dot(one_hot, bias_table, precision=lax.Precision.HIGHEST)
    offsets = bucket_offsets(buckets, first_query, query_count)
    return jnp.take(per_offset.T, offsets, axis=1)


def pair_table(buckets, first_query, query_count):
    offsets = bucket_offsets(buckets, first_query, query_count)
    pair_bucket = jnp.take(buckets, offsets.reshape(-1), axis=0)
    return (pair_bucket[:, None] == jnp.arange(BUCKETS, dtype=jnp.int32)[None, :]).astype(
        jnp.bfloat16
    )


def fetch_attention(w_query, w_key, w_value, w_out, gain_attn, rel_bias):
    return (
        lax.all_gather(w_query, "fsdp", axis=0, tiled=True),
        lax.all_gather(w_key, "fsdp", axis=0, tiled=True),
        lax.all_gather(w_value, "fsdp", axis=0, tiled=True),
        lax.all_gather(w_out, "fsdp", axis=0, tiled=True),
        lax.all_gather(gain_attn, "fsdp", axis=0, tiled=True),
        lax.all_gather(rel_bias, "fsdp", axis=0, tiled=True),
    )


def fetch_mlp(w_in, w_down, gain_mlp):
    return (
        lax.all_gather(w_in, "fsdp", axis=0, tiled=True),
        lax.all_gather(w_down, "fsdp", axis=0, tiled=True),
        lax.all_gather(gain_mlp, "fsdp", axis=0, tiled=True),
    )


def share_keys(key_rows, value_rows):
    return (
        lax.all_gather(key_rows, "ctx", axis=1, tiled=True),
        lax.all_gather(value_rows, "ctx", axis=1, tiled=True),
    )


def scores_of(query_part, key_part, bias_values):
    return (
        jnp.einsum("qhd,khd->hqk", query_part, key_part, preferred_element_type=jnp.float32)
        + bias_values
    )


def shards(
    inputs,
    cotangent,
    w_query,
    w_key,
    w_value,
    w_out,
    w_in,
    w_down,
    gain_attn,
    gain_mlp,
    rel_bias,
    buckets,
):
    seq_count, row_count, width = inputs.shape
    total_rows = seq_count * row_count
    first_query = lax.axis_index("ctx") * row_count
    query_w, key_w, value_w, out_w, attn_gain, bias_flat = fetch_attention(
        w_query, w_key, w_value, w_out, gain_attn, rel_bias
    )
    in_w, down_w, mlp_gain = fetch_mlp(w_in, w_down, gain_mlp)
    bias_values = make_bias(bias_flat.astype(jnp.float32), buckets, first_query, row_count)
    inputs_flat = inputs.astype(jnp.float32).reshape(total_rows, width)
    attn_scale = attn_gain.astype(jnp.float32)
    normed_one = norm_rows(inputs_flat, attn_scale).astype(jnp.bfloat16)
    query_rows = jnp.dot(normed_one, query_w, preferred_element_type=jnp.float32).astype(
        jnp.bfloat16
    )
    key_rows = (
        jnp.dot(normed_one, key_w, preferred_element_type=jnp.float32)
        .astype(jnp.bfloat16)
        .reshape(seq_count, row_count, width)
    )
    value_rows = (
        jnp.dot(normed_one, value_w, preferred_element_type=jnp.float32)
        .astype(jnp.bfloat16)
        .reshape(seq_count, row_count, width)
    )
    all_keys, all_values = share_keys(key_rows, value_rows)
    query_heads = query_rows.reshape(seq_count, row_count, HEADS, HEAD)
    seq_index = 0
    key_heads = all_keys[seq_index].reshape(-1, HEADS, HEAD)
    value_heads = all_values[seq_index].reshape(-1, HEADS, HEAD)
    scores = scores_of(query_heads[seq_index], key_heads, bias_values)
    top_score = jnp.max(scores, axis=-1, keepdims=True)
    weights_exp = jnp.exp(scores - top_score)
    totals = jnp.sum(weights_exp, axis=-1, keepdims=True)
    probs_low = (weights_exp / totals).astype(jnp.bfloat16)
    mixed = jnp.einsum("hqk,khd->qhd", probs_low, value_heads, preferred_element_type=jnp.float32)
    mixed_list = mixed.reshape(row_count, width)
    lse_list = [top_score + jnp.log(totals)]
    attended = mixed_list.astype(jnp.bfloat16)
    hidden_res = inputs_flat + jnp.dot(attended, out_w, preferred_element_type=jnp.float32)
    mlp_scale = mlp_gain.astype(jnp.float32)
    normed_two = norm_rows(hidden_res, mlp_scale).astype(jnp.bfloat16)
    pre_act = jnp.dot(normed_two, in_w, preferred_element_type=jnp.float32)
    activated = smooth_gelu(pre_act).astype(jnp.bfloat16)
    result = hidden_res + jnp.dot(activated, down_w, preferred_element_type=jnp.float32)
    in_w, down_w, mlp_gain = fetch_mlp(w_in, w_down, gain_mlp)
    query_w, key_w, value_w, out_w, attn_gain, bias_flat = fetch_attention(
        w_query, w_key, w_value, w_out, gain_attn, rel_bias
    )
    all_keys, all_values = share_keys(key_rows, value_rows)
    grad_rows = cotangent.reshape(total_rows, width)
    grad_down = jnp.einsum("nf,nd->fd", activated, grad_rows, preferred_element_type=jnp.float32)
    grad_act = jnp.einsum("nd,fd->nf", grad_rows, down_w, preferred_element_type=jnp.float32)
    grad_pre = (grad_act * gelu_slope(pre_act)).astype(jnp.bfloat16)
    grad_in = jnp.einsum("nd,nf->df", normed_two, grad_pre, preferred_element_type=jnp.float32)
    grad_normed_two = jnp.einsum("nf,df->nd", grad_pre, in_w, preferred_element_type=jnp.float32)
    back_hidden, grad_mlp_gain = jax.vjp(norm_rows, hidden_res, mlp_scale)[1](grad_normed_two)
    grad_hidden = grad_rows.astype(jnp.float32) + back_hidden
    grad_attn_low = grad_hidden.astype(jnp.bfloat16)
    grad_out = jnp.einsum("nd,ne->de", attended, grad_attn_low, preferred_element_type=jnp.float32)
    grad_attended = jnp.einsum(
        "ne,de->nd", grad_attn_low, out_w, preferred_element_type=jnp.float32
    ).astype(jnp.bfloat16)
    grad_heads = grad_attended.reshape(seq_count, row_count, HEADS, HEAD)
    pair_buckets = pair_table(buckets, first_query, row_count)
    seq_index = 0
    key_heads = all_keys[seq_index].reshape(-1, HEADS, HEAD)
    value_heads = all_values[seq_index].reshape(-1, HEADS, HEAD)
    scores = scores_of(query_heads[seq_index], key_heads, bias_values)
    probs = jnp.exp(scores - lse_list[seq_index])
    grad_probs = jnp.einsum(
        "qhd,khd->hqk", grad_heads[seq_index], value_heads, preferred_element_type=jnp.float32
    )
    row_inner = jnp.sum(probs * grad_probs, axis=-1, keepdims=True)
    grad_scores = (probs * (grad_probs - row_inner)).astype(jnp.bfloat16)
    bias_grad = jnp.dot(
        grad_scores.reshape(HEADS, -1), pair_buckets, preferred_element_type=jnp.float32
    )
    query_grads = jnp.einsum(
        "hqk,khd->qhd", grad_scores, key_heads, preferred_element_type=jnp.float32
    ).reshape(row_count, width)
    key_grads = [
        jnp.einsum(
            "hqk,qhd->khd", grad_scores, query_heads[seq_index], preferred_element_type=jnp.float32
        ).reshape(-1, width)
    ]
    value_grads = [
        jnp.einsum(
            "hqk,qhd->khd",
            probs.astype(jnp.bfloat16),
            grad_heads[seq_index],
            preferred_element_type=jnp.float32,
        ).reshape(-1, width)
    ]
    key_back, value_back = (
        lax.psum_scatter(
            jnp.stack(key_grads).astype(jnp.bfloat16), "ctx", scatter_dimension=1, tiled=True
        ).astype(jnp.float32),
        lax.psum_scatter(
            jnp.stack(value_grads).astype(jnp.bfloat16), "ctx", scatter_dimension=1, tiled=True
        ).astype(jnp.float32),
    )
    grad_query_rows = query_grads.astype(jnp.bfloat16)
    grad_key_rows = key_back.reshape(total_rows, width).astype(jnp.bfloat16)
    grad_value_rows = value_back.reshape(total_rows, width).astype(jnp.bfloat16)
    grad_query = jnp.einsum(
        "nd,ne->de", normed_one, grad_query_rows, preferred_element_type=jnp.float32
    )
    grad_key = jnp.einsum(
        "nd,ne->de", normed_one, grad_key_rows, preferred_element_type=jnp.float32
    )
    grad_value = jnp.einsum(
        "nd,ne->de", normed_one, grad_value_rows, preferred_element_type=jnp.float32
    )
    grad_normed_one = jnp.einsum(
        "ne,de->nd", grad_query_rows, query_w, preferred_element_type=jnp.float32
    )
    grad_normed_one = grad_normed_one + jnp.einsum(
        "ne,de->nd", grad_key_rows, key_w, preferred_element_type=jnp.float32
    )
    grad_normed_one = grad_normed_one + jnp.einsum(
        "ne,de->nd", grad_value_rows, value_w, preferred_element_type=jnp.float32
    )
    back_inputs, grad_attn_gain = jax.vjp(norm_rows, inputs_flat, attn_scale)[1](grad_normed_one)
    grad_inputs = (
        (grad_hidden + back_inputs).astype(jnp.bfloat16).reshape(seq_count, row_count, width)
    )
    grad_bias_flat = bias_grad.T.reshape(BUCKETS * HEADS)
    (
        part_query,
        part_key,
        part_value,
        part_out,
        part_in,
        part_down,
        part_attn_gain,
        part_mlp_gain,
        part_bias,
    ) = (
        lax.psum_scatter(grad_query, "fsdp", scatter_dimension=0, tiled=True),
        lax.psum_scatter(grad_key, "fsdp", scatter_dimension=0, tiled=True),
        lax.psum_scatter(grad_value, "fsdp", scatter_dimension=0, tiled=True),
        lax.psum_scatter(grad_out, "fsdp", scatter_dimension=0, tiled=True),
        lax.psum_scatter(grad_in, "fsdp", scatter_dimension=0, tiled=True),
        lax.psum_scatter(grad_down, "fsdp", scatter_dimension=0, tiled=True),
        lax.psum_scatter(grad_attn_gain, "fsdp", scatter_dimension=0, tiled=True),
        lax.psum_scatter(grad_mlp_gain, "fsdp", scatter_dimension=0, tiled=True),
        lax.psum_scatter(grad_bias_flat, "fsdp", scatter_dimension=0, tiled=True),
    )
    summed = (
        lax.psum(part_query.astype(jnp.bfloat16), "ctx").astype(jnp.float32),
        lax.psum(part_key.astype(jnp.bfloat16), "ctx").astype(jnp.float32),
        lax.psum(part_value.astype(jnp.bfloat16), "ctx").astype(jnp.float32),
        lax.psum(part_out.astype(jnp.bfloat16), "ctx").astype(jnp.float32),
        lax.psum(part_in.astype(jnp.bfloat16), "ctx").astype(jnp.float32),
        lax.psum(part_down.astype(jnp.bfloat16), "ctx").astype(jnp.float32),
        lax.psum(part_attn_gain.astype(jnp.bfloat16), "ctx").astype(jnp.float32),
        lax.psum(part_mlp_gain.astype(jnp.bfloat16), "ctx").astype(jnp.float32),
        lax.psum(part_bias.astype(jnp.bfloat16), "ctx").astype(jnp.float32),
    )
    output = result.astype(jnp.bfloat16).reshape(seq_count, row_count, width)
    return (
        output,
        grad_inputs,
        summed[0],
        summed[1],
        summed[2],
        summed[3],
        summed[4],
        summed[5],
        summed[6],
        summed[7],
        summed[8],
    )


MESH_ID = pl.DeviceIdType.MESH
BF = jnp.bfloat16
F32 = jnp.float32
WIDTH = 1024
TOKENS = 128
NT_DIMS = (((1,), (1,)), ((), ()))
TN_DIMS = (((0,), (0,)), ((), ()))


def dot_nn(left, right):
    return jnp.dot(left, right, preferred_element_type=F32)


def dot_nt(left, right):
    return lax.dot_general(left, right, NT_DIMS, preferred_element_type=F32)


def dot_tn(left, right):
    return lax.dot_general(left, right, TN_DIMS, preferred_element_type=F32)


def rows_at(start, count):
    return pl.ds(start if isinstance(start, int) else pl.multiple_of(start, count), count)


def remote(src, dst, send, recv, device):
    return pltpu.make_async_remote_copy(
        src_ref=src, dst_ref=dst, send_sem=send, recv_sem=recv, device_id=device, device_id_type=MESH_ID
    )


def steps(count, body, carry):
    for i in range(count):
        carry = body(i, carry)
    return carry


def fused_layer(
    x_in, cot_in, wq_in, wk_in, wv_in, wo_in, wi_in, wd_in, attn_in, mlp_in, table_in, bucket_in,
    out_ref, gin_ref, oqkv, oout, oin, odown, small_ref,
    XO, CO, PACK, BUCKET, STAGE, ACROSS, GP, XB, COT, N1, NTB, GAL, WQKV, WOUT, WIN, WDOWN,
    QKV, PROB, PLOW, BIAS, AT, ACT, SLOPE, GPRE, GATT, DQKV, DS, BACC,
    SA, SG, SO, SN, RA, RG, RO, RN, XA, XG, XS, XN, HID, GH, NTS, GALS,
    DQ, DO, DI, DD, SIBQ, SIBO, SIBI, SIBD, ZQ, ZO, ZI, ZD, REQ, REO, REI, RED, RCQ, RCO, RCI, RCD, FQ, FO, FI, FD,
    SMALL, RSMALL, PSMALL, RZSMALL,
    loc, gp_s, gp_r, xb_s, xb_r, xb_p, co_s, co_r, co_p, nt_s, nt_r, nt_p, ga_s, ga_r, ga_p,
    a_s, a_r, a_x, g_s, g_r, g_x, o_s, o_r, o_x, n_s, n_r, n_x,
    wx_s, wx_r, wqz_s, wqf_s, wqz_r, wqb_s, wqb_r, wiz_s, wif_s, wiz_r, wib_s, wib_r,
    wdz_s, wdf_s, wdz_r, wdb_s, wdb_r, woz_s, woz_r, wob_s, wob_r,
    sib_s, sib_r, sibd_r, zq_s, zqe_s, zq_r, zqc_r, zv_s, zve_s, zv_r, zvc_r, zo_s, zoe_s, zo_r, zoc_r,
    zi_s, zie_s, zi_r, zic_r, zd_s, zde_s, zd_r, zdc_r,
    fq_s, fqb_s, fq_r, fqb_r, fv_s, fvb_s, fv_r, fvb_r, fo_s, fo_r, fi_s, fib_s, fi_r, fib_r, fd_s, fd_r, sp_s, sp_r, sz_s, sz_r,
):
    c = lax.axis_index("ctx")
    f = lax.axis_index("fsdp")
    y, k = c // 2, lax.rem(c, 2)
    z, x = f // 2, lax.rem(f, 2)
    x1, y1, k1 = 1 - x, 1 - y, 1 - k
    f1 = 2 * z + x1
    q = 2 * x + y
    sib = (2 * y + k1, f)
    xdev = (c, f1)
    zs = [lax.rem(z + d, 4) for d in (1, 2, 3)]
    near = z + 1 - 2 * lax.rem(z, 2)
    other = 2 - 2 * (z // 2)
    others = (other, other + 1)
    far = 2 - z // 2
    middle = (z == 1) | (z == 2)
    at_end = jnp.logical_not(middle)

    def zdev(target):
        return (c, 2 * target + x)

    plane = []
    for i in range(4):
        ci = lax.rem(c + i, 4)
        for j, xj in enumerate((x, x1)):
            if i or j:
                plane.append((ci, 2 * z + xj))

    def recv(dst, sem):
        remote(dst, dst, sem, sem, sib).wait_recv()

    def sent(src, sem):
        remote(src, src, sem, sem, sib).wait_send()

    def block_half(buf, b, h):
        return buf.at[rows_at(b * TOKENS + 64 * h, 64)]

    def gather_send(src, dst, send, got, passed):
        halves = [src.at[pl.ds(64 * h, 64)] for h in range(2)]
        places = [block_half(dst, c, h) for h in range(2)]
        x_worker, y_worker = (2 * y + x, f1), (2 * y1 + x, f)
        remote(halves[0], places[0], send, passed.at[k], x_worker).start()
        remote(halves[1], places[1], send, passed.at[k], y_worker).start()
        remote(halves[1], places[1], send, got.at[c], x_worker).start()
        remote(halves[0], places[0], send, got.at[c], y_worker).start()
        whole = dst.at[rows_at(c * TOKENS, TOKENS)]

        @pl.when(k == x)
        def _():
            pltpu.make_async_copy(src, whole, got.at[c]).start()

        @pl.when(k != x)
        def _():
            remote(src, whole, send, got.at[c], sib).start()

    same = 1 - lax.rem(x + k, 2)
    pass_y = y + same * (1 - 2 * y)
    pass_to = (same * c + (1 - same) * (2 * y1 + k), same * f1 + (1 - same) * f)

    def gather_pass(dst, send, got, passed):
        for i in range(2):
            b = 2 * pass_y + i
            piece = block_half(dst, b, same)
            recv(piece, passed.at[i])
            remote(piece, piece, send, got.at[b], pass_to).start()

    def gather_wait(dst, got, b):
        @pl.when(b // 2 == pass_y)
        def _():
            recv(block_half(dst, b, 1 - same), got.at[b])

        @pl.when(b // 2 != pass_y)
        def _():
            recv(dst.at[rows_at(b * TOKENS, TOKENS)], got.at[b])

    def four_sent(buf, send):
        @pl.when(k == x)
        def _():
            sent(buf.at[pl.ds(0, 384)], send)

        @pl.when(k != x)
        def _():
            sent(buf, send)

    first_pair = 1 - pass_y

    def scatter_first(buf, dst, send, got, cross, cross_got, i):
        b = 2 * first_pair + i

        @pl.when(k != x)
        def _():
            remote(block_half(buf, b, 0), cross.at[i], send, cross_got.at[i], (2 * y1 + k, f)).start()
            remote(block_half(buf, b, 1), cross.at[i], send, cross_got.at[i], (c, f1)).start()

        whole = buf.at[rows_at(b * TOKENS, TOKENS)]

        @pl.when((k == x) & (i == k))
        def _():
            pltpu.make_async_copy(whole, dst.at[0], got).start()

        @pl.when((k == x) & (i != k))
        def _():
            remote(whole, dst.at[0], send, got, sib).start()

    def scatter_half(buf, dst, send, got, i, h):
        b = 2 * pass_y + i
        place = dst.at[1 + same, rows_at(64 * h, 64)]
        remote(block_half(buf, b, h), place, send, got, (b, 2 * z + k)).start()

    def scatter_second(buf, dst, send, got, i):
        scatter_half(buf, dst, send, got, i, 1 - same)

    def scatter_sums(buf, dst, send, got, cross, cross_got):
        for i in range(2):
            recv(cross.at[i], cross_got.at[i])
            rows = rows_at((2 * pass_y + i) * TOKENS + 64 * same, 64)
            buf[rows, :] = (buf[rows, :].astype(F32) + cross[i].astype(F32)).astype(BF)
            scatter_half(buf, dst, send, got, i, same)

    def half(fb, kk):
        return rows_at(fb * 128 + kk * 64, 64)

    def z_far(piece, send, got, src=None):
        remote(piece if src is None else src, piece, send, got, zdev(far)).start()

    def z_near(piece, send, got, src=None):
        remote(piece if src is None else src, piece, send, got, zdev(near)).start()

    def z_send(piece, send, got):
        z_far(piece, send, got)
        z_near(piece, send, got)

    def down_of(ref, t):
        return ref.at[t]

    def in_of(ref, t):
        return ref.at[pl.ds(2 * t, 2)]

    def value_of(ref, t):
        return ref.at[pl.ds(2 * t, 2), :, value_cols]

    def other_of(ref, t):
        return ref.at[pl.ds(2 * t, 2), :, other_cols]

    value_cols, other_cols = pl.ds(512, 256), pl.ds(0, 512)

    def reduce_others(of, terms, got, send, sem):
        @pl.when(at_end)
        def _():
            for t in others:
                remote(of(terms, t), of(got, t), send, sem.at[t], zdev(near)).start()

    def reduce_near(of, terms, got, send, sem):
        remote(of(terms, near), of(got, near), send, sem.at[near], zdev(near)).start()

    def reduce_middle(of, terms, got, final, send, sem, final_sem):
        @pl.when(middle)
        def _():
            for t in others:
                recv(of(got, t), sem.at[t])
                mine = of(terms, t)
                mine[...] = (mine[...].astype(F32) + of(got, t)[...].astype(F32)).astype(BF)
                remote(mine, final, send, final_sem, zdev(t)).start()

    def take(piece, got, bsend, bgot):
        recv(piece, got)
        remote(piece, piece, bsend, bgot, sib).start()

    def pass_on(piece, send, got):
        remote(piece, piece, send, got, zdev(near)).start()

    def of_row(t, xx):
        return 2 * t + xx

    own_x = pltpu.make_async_copy(x_in.at[0], XO, loc.at[0])
    own_c = pltpu.make_async_copy(cot_in.at[0], CO, loc.at[1])
    myrows = pl.ds(pl.multiple_of(128 * f, 128), 128)
    for w, proj in enumerate((wq_in, wk_in, wv_in)):
        pltpu.make_async_copy(proj, STAGE.at[w], loc.at[3]).start()
    for j in range(4):
        src = wi_in.at[:, pl.ds(pl.multiple_of(512 * (2 * j + x) + 256 * y, 256), 256)]
        pltpu.make_async_copy(src, WIN.at[myrows, pl.ds(256 * j, 256)], loc.at[4]).start()
    pltpu.make_async_copy(
        wd_in.at[rows_at(256 * y, 256)], WDOWN.at[rows_at(256 * z, 256)], loc.at[5]
    ).start()

    pltpu.make_async_copy(wo_in.at[rows_at(64 * y, 64)], WOUT.at[rows_at(64 * z, 64)], loc.at[6]).start()
    own_x.start()
    own_c.start()

    barrier = pltpu.get_barrier_semaphore()
    across = [(c, 2 * t + x1) for t in zs]
    for device in plane + [zdev(t) for t in zs] + across:
        pl.semaphore_signal(barrier, inc=1, device_id=device, device_id_type=MESH_ID)


    PACK[...] = jnp.zeros((8, 128), F32)
    PACK[0:1, :] = attn_in[...].astype(F32)
    PACK[1:2, :] = mlp_in[...].astype(F32)
    PACK[2:3, 0:64] = table_in[...].astype(F32)
    BUCKET[...] = jnp.full((1, WIDTH), -1, jnp.int32)
    BUCKET[0:1, 0 : WIDTH - 1] = bucket_in[...]
    GP[f] = PACK[...]

    pltpu.make_async_copy(STAGE, STAGE, loc.at[3]).wait()

    def pack_heads(dst, dst_rows, src_rows, xx, count):
        low = lax.broadcasted_iota(jnp.int32, (count, 128), 1) < 64
        for w in range(3):
            for j in range(2):
                first, second = [
                    STAGE[w, src_rows, pl.ds(pl.multiple_of(128 * (4 * j + 2 * n + xx), 128), 128)].astype(F32)
                    for n in range(2)
                ]
                left = jnp.where(y == 0, first, pltpu.roll(first, 64, 1))
                right = jnp.where(y == 0, pltpu.roll(second, 64, 1), second)
                dst[dst_rows, 256 * w + 128 * j : 256 * w + 128 * j + 128] = jnp.where(low, left, right).astype(BF)

    pack_heads(ACROSS, slice(0, 64), rows_at(64 * k, 64), x1, 64)
    pack_heads(WQKV, myrows, slice(0, 128), x, 128)
    pl.semaphore_wait(barrier, 13)
    for device in [xdev] + [zdev(t) for t in zs] + across:
        remote(PACK, GP.at[f], gp_s, gp_r, device).start()
    remote(ACROSS, WQKV.at[half(f, k)], wx_s.at[0], wx_r.at[0], xdev).start()
    z_send(WQKV.at[half(f, k)], wqz_s, wqz_r.at[f])
    gather_send(x_in.at[0], XB, xb_s, xb_r, xb_p)
    for j in range(4):
        src = wi_in.at[rows_at(64 * k, 64), pl.ds(pl.multiple_of(512 * (2 * j + x1) + 256 * y, 256), 256)]
        remote(src, WIN.at[half(f, k), pl.ds(256 * j, 256)], wx_s.at[1], wx_r.at[1], xdev).start()

    recv(WQKV.at[half(f1, k)], wx_r.at[0])
    z_send(WQKV.at[half(f1, k)], wqz_s, wqz_r.at[f1])
    remote(WQKV.at[half(f1, k)], WQKV.at[half(f1, k)], wqb_s, wqb_r, sib).start()
    down_half = rows_at(256 * z + 128 * k, 128)
    pltpu.make_async_copy(WIN.at[myrows], WIN.at[myrows], loc.at[4]).wait()

    def out_piece(t):
        return WOUT.at[rows_at(64 * t + 32 * k, 32)]

    out_own = wo_in.at[rows_at(64 * y + 32 * k, 32)]
    z_far(out_piece(z), woz_s, woz_r.at[z], out_own)

    @pl.when(at_end)
    def _():
        z_near(out_piece(z), woz_s, woz_r.at[z], out_own)

    z_far(WIN.at[half(f, k)], wiz_s, wiz_r.at[f])

    @pl.when(at_end)
    def _():
        z_near(WIN.at[half(f, k)], wiz_s, wiz_r.at[f])

    def take_proj(xx):
        for n in range(2):
            h = of_row(others[n], xx)
            piece = WQKV.at[half(h, k)]
            recv(piece, wqz_r.at[h])

            @pl.when(middle)
            def _():
                pass_on(piece, wqf_s, wqz_r.at[h])

            remote(piece, piece, wqb_s, wqb_r, sib).start()

    def take_near(xx):
        g = of_row(near, xx)
        take(WQKV.at[half(g, k)], wqz_r.at[g], wqb_s, wqb_r)

    @pl.when(middle)
    def _():
        take_proj(x)

    gather_pass(XB, xb_s, xb_r, xb_p)
    gather_send(cot_in.at[0], COT, co_s, co_r, co_p)
    take_near(x)

    @pl.when(middle)
    def _():
        take_proj(x1)
        take_near(x1)

        z_near(out_piece(z), woz_s, woz_r.at[z], out_own)

    recv(GP.at[pl.ds(0, 7)], gp_r)

    def row_of(index):
        return jnp.concatenate([GP[g, index : index + 1, :] for g in range(8)], axis=1)

    lane = lax.broadcasted_iota(jnp.int32, (8, 128), 1)
    head_row = lax.broadcasted_iota(jnp.int32, (8, 128), 0)
    head_of = 4 * head_row + 2 * x + y
    head_mask = (lax.rem(lane, 16) == head_of) & (head_row < 4)

    def bucket_hot(g):
        index = lax.broadcasted_iota(jnp.int32, (128, WIDTH), 0)
        wanted = jnp.where(index < 64, 4 * g + lax.div(index, 16), -1)
        return (BUCKET[0:1, :] == wanted)

    def add_bias(g, total):
        table = jnp.where(head_mask, jnp.broadcast_to(GP[g, 2:3, :], (8, 128)), 0.0).astype(BF)
        return total + dot_nn(table, bucket_hot(g).astype(BF))

    offsets = steps(8, add_bias, jnp.zeros((8, WIDTH), F32))
    for h in range(4):
        spread = jnp.broadcast_to(offsets[h : h + 1, :], (128, WIDTH))
        BIAS[h] = pltpu.roll(spread, WIDTH - 127, 1, stride=1, stride_axis=0)
        BACC[h] = jnp.zeros((128, WIDTH), F32)

    gain_one = row_of(0)

    def norm_block(i, carry):
        b = lax.rem(2 * y + i, 4)
        gather_wait(XB, xb_r, b)

        def chunk(r, inner):
            rows = rows_at(b * TOKENS + r * 32, 32)
            values = XB[rows, :].astype(F32)
            scale = lax.rsqrt(jnp.mean(values * values, axis=-1, keepdims=True) + EPS)
            N1[rows, :] = (values * scale * gain_one).astype(BF)
            return inner

        return steps(4, chunk, carry)

    steps(4, norm_block, 0)

    @pl.when(middle)
    def _():
        for t in others:
            recv(out_piece(t), woz_r.at[t])
            pass_on(out_piece(t), woz_s, woz_r.at[t])
            remote(out_piece(t), out_piece(t), wob_s, wob_r, sib).start()

        z_near(WIN.at[half(f, k)], wiz_s, wiz_r.at[f])

    recv(WIN.at[half(f1, k)], wx_r.at[1])
    z_far(WIN.at[half(f1, k)], wiz_s, wiz_r.at[f1])
    remote(WIN.at[half(f1, k)], WIN.at[half(f1, k)], wib_s, wib_r, sib).start()
    pltpu.make_async_copy(WDOWN.at[rows_at(256 * z, 256)], WDOWN.at[rows_at(256 * z, 256)], loc.at[5]).wait()
    z_far(WDOWN.at[down_half], wdz_s, wdz_r.at[z])

    z_near(WIN.at[half(f1, k)], wiz_s, wiz_r.at[f1])

    @pl.when(at_end)
    def _():
        z_near(WDOWN.at[down_half], wdz_s, wdz_r.at[z])
        take_near(x1)
        take_proj(x)
        take_proj(x1)

    recv(WQKV.at[pl.ds(0, 448)], wqb_r)

    def project(n, carry):
        cols = rows_at(256 * n, 256)
        QKV[:, cols] = dot_nn(N1[...], WQKV[:, cols]).astype(BF)
        return carry

    steps(3, project, 0)


    gather_pass(COT, co_s, co_r, co_p)

    @pl.when(middle)
    def _():
        z_near(WDOWN.at[down_half], wdz_s, wdz_r.at[z])

    low_lanes = lax.broadcasted_iota(jnp.int32, (TOKENS, 128), 1) < 64

    def pick(values, hh):
        keep = low_lanes if hh == 0 else jnp.logical_not(low_lanes)
        return jnp.where(keep, values, jnp.zeros_like(values))

    def attend(i, carry):
        b = lax.rem(2 * first_pair + i, 4)
        rows = rows_at(b * TOKENS, TOKENS)
        window = pl.ds(pl.multiple_of(384 - 128 * b, 128), 512)
        for j in range(2):
            outs = []
            for hh in range(2):
                h = 2 * j + hh
                query = pick(QKV[rows, 128 * j : 128 * j + 128], hh)
                scores = dot_nt(query, QKV[:, 256 + 128 * j : 384 + 128 * j]) + BIAS[h, :, window]
                weights = jnp.exp(scores - jnp.max(scores, axis=-1, keepdims=True))
                probs = weights * (1.0 / jnp.sum(weights, axis=-1, keepdims=True))
                PROB[h, rows, :] = probs
                low = probs.astype(BF)
                PLOW[h, rows, :] = low
                outs.append(dot_nn(low, QKV[:, 512 + 128 * j : 640 + 128 * j]))
            AT[rows, 128 * j : 128 * j + 128] = jnp.where(low_lanes, outs[0], outs[1]).astype(BF)

        @pl.when(i == 0)
        def _():
            take(out_piece(near), woz_r.at[near], wob_s, wob_r)

            @pl.when(at_end)
            def _():
                for t in others:
                    take(out_piece(t), woz_r.at[t], wob_s, wob_r)

            pltpu.make_async_copy(WOUT.at[rows_at(64 * z, 64)], WOUT.at[rows_at(64 * z, 64)], loc.at[6]).wait()
            recv(WOUT.at[pl.ds(0, 96)], wob_r)

        SA[rows, :] = dot_nn(AT[rows, :], WOUT[...]).astype(BF)

        @pl.when(i < 2)
        def _():
            scatter_first(SA, RA, a_s, a_r, XA, a_x, i)

        @pl.when(i >= 2)
        def _():
            scatter_second(SA, RA, a_s, a_r, i - 2)

        return carry

    lax.fori_loop(0, 4, attend, 0)
    scatter_sums(SA, RA, a_s, a_r, XA, a_x)

    for xx in (x, x1):
        g = of_row(near, xx)
        take(WIN.at[half(g, k)], wiz_r.at[g], wib_s, wib_r)

    @pl.when(middle)
    def _():
        for i, xx in enumerate((x, x1)):
            for n in range(2):
                g = of_row(others[n], xx)
                recv(WIN.at[half(g, k)], wiz_r.at[g])
                pass_on(WIN.at[half(g, k)], wif_s, wiz_r.at[g])
                remote(WIN.at[half(g, k)], WIN.at[half(g, k)], wib_s, wib_r, sib).start()

    own_x.wait()
    own_c.wait()
    gain_two = row_of(1)
    recv(RA, a_r)

    def home_forward(r, carry):
        rows = rows_at(r * 32, 32)
        hidden = XO[rows, :].astype(F32)
        for s in range(3):
            hidden = hidden + RA[s, rows, :].astype(F32)
        HID[rows, :] = hidden
        scale = lax.rsqrt(jnp.mean(hidden * hidden, axis=-1, keepdims=True) + EPS)
        NTS[rows, :] = (hidden * scale * gain_two).astype(BF)
        return carry

    steps(4, home_forward, 0)
    gather_send(NTS, NTB, nt_s, nt_r, nt_p)

    def down_piece(t, kk):
        return WDOWN.at[rows_at(256 * t + 128 * kk, 128)]

    take(down_piece(near, k), wdz_r.at[near], wdb_s, wdb_r)

    @pl.when(middle)
    def _():
        for n in range(2):
            t = others[n]
            recv(down_piece(t, k), wdz_r.at[t])
            pass_on(down_piece(t, k), wdf_s, wdz_r.at[t])
            remote(down_piece(t, k), down_piece(t, k), wdb_s, wdb_r, sib).start()

    @pl.when(at_end)
    def _():
        for xx in (x, x1):
            for t in others:
                g = of_row(t, xx)
                take(WIN.at[half(g, k)], wiz_r.at[g], wib_s, wib_r)

    recv(WIN.at[pl.ds(0, 448)], wib_r)

    gather_pass(NTB, nt_s, nt_r, nt_p)

    def feed(i, carry):
        yy = lax.rem(y + i, 2)
        rows = rows_at(256 * yy, 256)
        for b in (2 * yy, 2 * yy + 1):
            gather_wait(NTB, nt_r, b)

        def hidden_units(n, inner):
            cols = rows_at(256 * n, 256)
            pre = dot_nn(NTB[rows, :], WIN[:, cols])
            cdf = 0.5 * (1.0 + lax.erf(pre * 0.7071067811865476))
            ACT[rows, cols] = (pre * cdf).astype(BF)
            SLOPE[rows, cols] = cdf + pre * jnp.exp(-0.5 * pre * pre) * 0.3989422804014327
            return inner

        return steps(4, hidden_units, carry)

    lax.fori_loop(0, 2, feed, 0)

    for b in range(4):
        gather_wait(COT, co_r, b)

    order = (other, other + 1, near, z)

    def grad_down(i, carry):
        m = jnp.where(i < 2, other + i, jnp.where(i == 2, near, z))
        tile = dot_tn(ACT[:, rows_at(256 * m, 256)], COT[...]).astype(BF)
        DD[0, m] = tile[0:128]
        DD[1, m] = tile[128:256]
        remote(DD.at[k1, m], SIBD.at[m], sib_s.at[0], sibd_r.at[i], sib).start()
        return carry

    steps(4, grad_down, 0)

    def join_down(i, carry):
        m = jnp.where(i < 2, other + i, jnp.where(i == 2, near, z))
        recv(SIBD.at[m], sibd_r.at[i])
        ZD[m] = (DD[k, m].astype(F32) + SIBD[m].astype(F32)).astype(BF)

        @pl.when(at_end & (i < 2))
        def _():
            remote(ZD.at[m], RED.at[m], zde_s, zd_r.at[m], zdev(near)).start()

        @pl.when(middle & (i == 2))
        def _():
            remote(ZD.at[m], RED.at[m], zd_s, zd_r.at[m], zdev(near)).start()

        return carry

    steps(4, join_down, 0)

    @pl.when(at_end)
    def _():
        for t in others:
            take(down_piece(t, k), wdz_r.at[t], wdb_s, wdb_r)

    recv(WDOWN.at[pl.ds(0, 384)], wdb_r)

    def back_feed(i, carry):
        yy = lax.rem(first_pair + i, 2)
        rows = rows_at(256 * yy, 256)

        def back_act(n, inner):
            cols = rows_at(256 * n, 256)
            GPRE[rows, cols] = (dot_nt(COT[rows, :], WDOWN[cols, :]) * SLOPE[rows, cols]).astype(BF)
            return inner

        steps(4, back_act, 0)

        def back_normed(n, inner):
            cols = rows_at(256 * n, 256)
            SG[rows, cols] = dot_nt(GPRE[rows, :], WIN[cols, :]).astype(BF)
            return inner

        steps(4, back_normed, 0)

        @pl.when(i == 0)
        def _():
            for n in range(2):
                scatter_first(SG, RG, g_s, g_r, XG, g_x, n)

        @pl.when(i == 1)
        def _():
            for n in range(2):
                scatter_second(SG, RG, g_s, g_r, n)

        return carry

    lax.fori_loop(0, 2, back_feed, 0)

    def grad_in(m, carry):
        tile = dot_tn(NTB[:, rows_at(256 * m, 256)], GPRE[...]).astype(BF)
        for part in range(2):
            DI[0, 2 * m + part] = tile[128 * part : 128 * part + 64]
            DI[1, 2 * m + part] = tile[128 * part + 64 : 128 * part + 128]
        return carry

    steps(4, grad_in, 0)
    scatter_sums(SG, RG, g_s, g_r, XG, g_x)
    remote(DI.at[k1], SIBI, sib_s.at[1], sib_r.at[1], sib).start()

    def down_project(n, carry):
        cols = rows_at(256 * n, 256)
        SO[:, cols] = dot_nn(ACT[...], WDOWN[:, cols]).astype(BF)
        return carry

    steps(4, down_project, 0)
    for i in range(2):
        scatter_first(SO, RO, o_s, o_r, XS, o_x, i)


    recv(SIBI, sib_r.at[1])

    def join_in(m, carry):
        ZI[m] = (DI[k, m].astype(F32) + SIBI[m].astype(F32)).astype(BF)
        return carry

    steps(8, join_in, 0)
    reduce_others(in_of, ZI, REI, zie_s, zi_r)

    @pl.when(at_end)
    def _():
        reduce_near(down_of, ZD, RED, zd_s, zd_r)

    reduce_near(in_of, ZI, REI, zi_s, zi_r)

    recv(RG, g_r)

    def home_back(r, total):
        rows = rows_at(r * 32, 32)
        grad = RG[0, rows, :].astype(F32)
        for s in range(1, 3):
            grad = grad + RG[s, rows, :].astype(F32)
        hidden = HID[rows, :]
        scale = lax.rsqrt(jnp.mean(hidden * hidden, axis=-1, keepdims=True) + EPS)
        scaled = grad * gain_two
        inner = jnp.mean(scaled * hidden, axis=-1, keepdims=True)
        back = CO[rows, :].astype(F32) + scale * scaled - hidden * (scale * scale * scale * inner)
        GH[rows, :] = back
        GALS[rows, :] = back.astype(BF)
        return total + jnp.sum((grad * hidden * scale).reshape(4, 8, WIDTH), axis=0)

    mlp_gain_grad = steps(4, home_back, jnp.zeros((8, WIDTH), F32))
    gather_send(GALS, GAL, ga_s, ga_r, ga_p)
    reduce_middle(down_of, ZD, RED, RCD, zde_s, zd_r, zdc_r)

    mlp_gain_grad = jnp.sum(mlp_gain_grad, axis=0, keepdims=True)
    for g in range(8):
        SMALL[1, g : g + 1, :] = mlp_gain_grad[:, 128 * g : 128 * g + 128]

    gather_pass(GAL, ga_s, ga_r, ga_p)
    for i in range(2):
        scatter_second(SO, RO, o_s, o_r, i)

    scatter_sums(SO, RO, o_s, o_r, XS, o_x)

    all_low = lax.broadcasted_iota(jnp.int32, (512, 128), 1) < 64

    def pick_all(values, hh):
        keep = all_low if hh == 0 else jnp.logical_not(all_low)
        return jnp.where(keep, values, jnp.zeros_like(values))

    def attend_back(i, carry):
        b = lax.rem(2 * y + i, 4)
        rows = rows_at(b * TOKENS, TOKENS)
        gather_wait(GAL, ga_r, b)

        @pl.when(i == 2)
        def _():
            reduce_middle(in_of, ZI, REI, RCI, zie_s, zi_r, zic_r)

        GATT[rows, :] = dot_nt(GAL[rows, :], WOUT[...]).astype(BF)
        for j in range(2):
            pair = slice(128 * j, 128 * j + 128)
            keys = QKV[:, 256 + 128 * j : 384 + 128 * j]
            values = QKV[:, 512 + 128 * j : 640 + 128 * j]
            outs = []
            for hh in range(2):
                h = 2 * j + hh
                grad_att = pick(GATT[rows, pair], hh)
                probs = PROB[h, rows, :]
                grad_probs = dot_nt(grad_att, values)
                inner = jnp.sum(probs * grad_probs, axis=-1, keepdims=True)
                grad_scores = (probs * (grad_probs - inner)).astype(BF)
                DS[h, rows, :] = grad_scores
                outs.append(dot_nn(grad_scores, keys))
            DQKV[rows, pair] = jnp.where(low_lanes, outs[0], outs[1]).astype(BF)
        return carry

    lax.fori_loop(0, 4, attend_back, 0)

    def grad_keys(j, carry):
        query = QKV[:, rows_at(128 * j, 128)]
        first = dot_tn(DS[2 * j], pick_all(query, 0))
        second = dot_tn(DS[2 * j + 1], pick_all(query, 1))
        DQKV[:, pl.ds(pl.multiple_of(256 + 128 * j, 128), 128)] = jnp.where(all_low, first, second).astype(BF)
        return carry

    steps(2, grad_keys, 0)

    def grad_values(j, carry):
        grad_att = GATT[:, rows_at(128 * j, 128)]
        first = dot_tn(PLOW[2 * j], pick_all(grad_att, 0))
        second = dot_tn(PLOW[2 * j + 1], pick_all(grad_att, 1))
        DQKV[:, pl.ds(pl.multiple_of(512 + 128 * j, 128), 128)] = jnp.where(all_low, first, second).astype(BF)
        return carry

    steps(2, grad_values, 0)

    def grad_proj(first, width):
        def step(m, carry):
            tile = dot_tn(N1[:, rows_at(256 * m, 256)], DQKV[:, first : first + width]).astype(BF)
            for part in range(2):
                DQ[0, 2 * m + part, :, first : first + width] = tile[128 * part : 128 * part + 64]
                DQ[1, 2 * m + part, :, first : first + width] = tile[128 * part + 64 : 128 * part + 128]
            return carry

        steps(4, step, 0)

    def join_proj(first, width):
        def step(m, carry):
            total = DQ[k, m, :, first : first + width].astype(F32) + SIBQ[m, :, first : first + width].astype(F32)
            ZQ[m, :, first : first + width] = total.astype(BF)
            return carry

        steps(8, step, 0)

    def back_project(i, carry):
        yy = lax.rem(first_pair + i, 2)
        rows = rows_at(256 * yy, 256)
        SN[rows, :] = dot_nt(DQKV[rows, :], WQKV[...]).astype(BF)

        @pl.when(i == 0)
        def _():
            for n in range(2):
                scatter_first(SN, RN, n_s, n_r, XN, n_x, n)

        @pl.when(i == 1)
        def _():
            for n in range(2):
                scatter_second(SN, RN, n_s, n_r, n)

        return carry

    lax.fori_loop(0, 2, back_project, 0)

    grad_proj(0, 512)
    remote(DQ.at[k1, :, :, other_cols], SIBQ.at[:, :, other_cols], sib_s.at[4], sib_r.at[4], sib).start()
    grad_proj(512, 256)
    remote(DQ.at[k1, :, :, value_cols], SIBQ.at[:, :, value_cols], sib_s.at[2], sib_r.at[2], sib).start()


    recv(SIBQ.at[:, :, other_cols], sib_r.at[4])
    join_proj(0, 512)
    reduce_others(other_of, ZQ, REQ, zqe_s, zq_r)

    def grad_out_rows(m, carry):
        tile = dot_tn(AT[:, rows_at(128 * m, 128)], GAL[...]).astype(BF)
        for n in range(2):
            for kk in range(2):
                DO[kk, 2 * m + n] = tile[64 * n + 32 * kk : 64 * n + 32 * kk + 32]
        return carry

    steps(2, grad_out_rows, 0)
    remote(DO.at[k1], SIBO, sib_s.at[3], sib_r.at[3], sib).start()
    scatter_sums(SN, RN, n_s, n_r, XN, n_x)
    recv(SIBQ.at[:, :, value_cols], sib_r.at[2])
    join_proj(512, 256)
    reduce_others(value_of, ZQ, REQ, zve_s, zv_r)
    recv(SIBO, sib_r.at[3])
    ZO[...] = (DO[k].astype(F32) + SIBO[...].astype(F32)).astype(BF)
    reduce_others(down_of, ZO, REO, zoe_s, zo_r)
    reduce_near(other_of, ZQ, REQ, zq_s, zq_r)
    reduce_near(value_of, ZQ, REQ, zv_s, zv_r)
    reduce_near(down_of, ZO, REO, zo_s, zo_r)

    def place_scores(i, carry):
        rows = rows_at(i * TOKENS, TOKENS)
        window = pl.ds(pl.multiple_of(384 - 128 * i, 128), 512)
        for h in range(4):
            BACC[h, :, window] = BACC[h, :, window] + DS[h, rows, :].astype(F32)
        return carry

    steps(4, place_scores, 0)
    head_sums = []
    for h in range(4):
        rest = BACC[h]
        count = 64
        while count >= 8:
            rest = pltpu.roll(rest[0:count, :], count, 1) + rest[count : 2 * count, :]
            count //= 2
        for bit in (1, 2, 4):
            shift_row = 7 - lax.broadcasted_iota(jnp.int32, (8, WIDTH), 0)
            rest = jnp.where(lax.rem(lax.div(shift_row, bit), 2) == 1, pltpu.roll(rest, bit, 1), rest)
        head_sums.append(jnp.sum(rest, axis=0, keepdims=True))
    head_sums = jnp.concatenate(head_sums + [jnp.zeros((4, WIDTH), F32)], axis=0)
    coarse = head_sums.astype(BF)
    split_sums = jnp.concatenate([coarse, (head_sums - coarse.astype(F32)).astype(BF)], axis=0)
    both_masks = jnp.concatenate([head_mask.astype(F32)] * 2, axis=0) > 0.5

    def bucket_sums(g, carry):
        sums = dot_nt(split_sums, bucket_hot(g).astype(BF))
        SMALL[2, pl.ds(g, 1), :] = jnp.sum(jnp.where(both_masks, sums, 0.0), axis=0, keepdims=True)
        return carry

    steps(8, bucket_sums, 0)

    recv(RED.at[z], zd_r.at[z])
    recv(RCD, zdc_r)
    FD[...] = (ZD[z].astype(F32) + RED[z].astype(F32) + RCD[...].astype(F32)).astype(BF)

    def down_rows(cc):
        return odown.at[rows_at(128 * cc, 128)]

    y_core = (2 * y1 + k, f)
    remote(FD, down_rows(c), fd_s, fd_r.at[1], y_core).start()
    remote(FD, down_rows(c), fd_s, fd_r.at[2], sib).start()
    pltpu.make_async_copy(FD, down_rows(c), fd_r.at[0]).start()

    def spread(final, place, send, bsend, got, bgot):
        remote(final.at[x1], place(q, k), send, got.at[3], (2 * y1 + k, f1)).start()
        remote(final.at[x1], place(q, k), send, got.at[2], (c, f1)).start()
        remote(final.at[x], place(q, k), send, got.at[1], y_core).start()
        remote(final.at[x], place(q, k), bsend, bgot, sib).start()
        pltpu.make_async_copy(final.at[x], place(q, k), got.at[0]).start()

    chips = (2 * x + y1, 2 * x1 + y, 2 * x1 + y1)

    def spread_on(place, bsend, got, bgot):
        for i in range(3):
            piece = place(chips[i], k)
            recv(piece, got.at[i + 1])
            remote(piece, piece, bsend, bgot, sib).start()

    def in_place(qq, kk):
        return oin.at[:, qq, rows_at(64 * kk, 64), :]

    recv(RO, o_r)

    def home_out(r, carry):
        rows = rows_at(r * 32, 32)
        result = HID[rows, :]
        for s in range(3):
            result = result + RO[s, rows, :].astype(F32)
        out_ref[0, rows, :] = result.astype(BF)
        return carry

    steps(4, home_out, 0)
    recv(RN, n_r)

    def home_inputs(r, total):
        rows = rows_at(r * 32, 32)
        grad = RN[0, rows, :].astype(F32)
        for s in range(1, 3):
            grad = grad + RN[s, rows, :].astype(F32)
        values = XO[rows, :].astype(F32)
        scale = lax.rsqrt(jnp.mean(values * values, axis=-1, keepdims=True) + EPS)
        scaled = grad * gain_one
        inner = jnp.mean(scaled * values, axis=-1, keepdims=True)
        back = GH[rows, :] + scale * scaled - values * (scale * scale * scale * inner)
        gin_ref[0, rows, :] = back.astype(BF)
        return total + jnp.sum((grad * values * scale).reshape(4, 8, WIDTH), axis=0)

    attn_gain_grad = steps(4, home_inputs, jnp.zeros((8, WIDTH), F32))
    attn_gain_grad = jnp.sum(attn_gain_grad, axis=0, keepdims=True)
    for g in range(8):
        SMALL[0, g : g + 1, :] = attn_gain_grad[:, 128 * g : 128 * g + 128]

    for i in range(4):
        ci = lax.rem(c + i, 4)
        for j, xj in enumerate((x, x1)):
            if i or j:
                remote(SMALL, RSMALL.at[2 * c + x], sp_s, sp_r, (ci, 2 * z + xj)).start()

    recv(in_of(REI, z), zi_r.at[z])
    recv(RCI, zic_r)
    for xx in range(2):
        total = ZI[2 * z + xx].astype(F32) + REI[2 * z + xx].astype(F32) + RCI[xx].astype(F32)
        for j in range(4):
            FI[xx, j] = total[:, 256 * j : 256 * j + 256].astype(BF)
    spread(FI, in_place, fi_s, fib_s, fi_r, fib_r)

    reduce_middle(other_of, ZQ, REQ, RCQ.at[:, :, other_cols], zqe_s, zq_r, zqc_r)
    reduce_middle(value_of, ZQ, REQ, RCQ.at[:, :, value_cols], zve_s, zv_r, zvc_r)
    reduce_middle(down_of, ZO, REO, RCO, zoe_s, zo_r, zoc_r)

    def final_proj(of, cols, first, width, sem, final_sem):
        recv(of(REQ, z), sem.at[z])
        recv(RCQ.at[:, :, cols], final_sem)
        for xx in range(2):
            total = ZQ[2 * z + xx, :, first : first + width].astype(F32)
            total = total + REQ[2 * z + xx, :, first : first + width].astype(F32)
            total = total + RCQ[xx, :, first : first + width].astype(F32)
            FQ[xx, :, first : first + width] = total.astype(BF)

    def other_place(qq, kk):
        return oqkv.at[qq, rows_at(64 * kk, 64), other_cols]

    def value_place(qq, kk):
        return oqkv.at[qq, rows_at(64 * kk, 64), value_cols]

    def out_rows(cc):
        return oout.at[rows_at(32 * cc, 32)]

    y_rows = down_rows(2 * y1 + k)
    recv(y_rows, fd_r.at[1])
    remote(y_rows, y_rows, fd_s, fd_r.at[2], sib).start()
    recv(RSMALL.at[pl.ds(0, 7)], sp_r)
    plane_sum = SMALL[...]
    for i in range(4):
        ci = lax.rem(c + i, 4)
        for j, xj in enumerate((x, x1)):
            if i or j:
                plane_sum = plane_sum + RSMALL[2 * ci + xj]
    for t in range(4):
        for n in range(3):
            pair = plane_sum[n, 2 * t : 2 * t + 2, :]
            PSMALL[t, n : n + 1, :] = jnp.where(x == 0, pair[0:1], pair[1:2])
    for t in zs:
        remote(PSMALL.at[t], RZSMALL.at[z], sz_s, sz_r, zdev(t)).start()

    final_proj(other_of, other_cols, 0, 512, zq_r, zqc_r)
    spread(FQ.at[:, :, other_cols], other_place, fq_s, fqb_s, fq_r, fqb_r)
    final_proj(value_of, value_cols, 512, 256, zv_r, zvc_r)
    spread(FQ.at[:, :, value_cols], value_place, fv_s, fvb_s, fv_r, fvb_r)
    spread_on(in_place, fib_s, fi_r, fib_r)
    recv(REO.at[z], zo_r.at[z])
    recv(RCO, zoc_r)
    FO[...] = (ZO[z].astype(F32) + REO[z].astype(F32) + RCO[...].astype(F32)).astype(BF)
    remote(FO, out_rows(c), fo_s, fo_r.at[1], y_core).start()
    remote(FO, out_rows(c), fo_s, fo_r.at[2], sib).start()
    pltpu.make_async_copy(FO, out_rows(c), fo_r.at[0]).start()
    spread_on(other_place, fqb_s, fq_r, fqb_r)
    spread_on(value_place, fvb_s, fv_r, fvb_r)
    y_out = out_rows(2 * y1 + k)
    recv(y_out, fo_r.at[1])
    remote(y_out, y_out, fo_s, fo_r.at[2], sib).start()
    recv(RZSMALL.at[pl.ds(0, 3)], sz_r)
    total = PSMALL[z]
    for t in zs:
        total = total + RZSMALL[t]
    small_ref[...] = total

    recv(down_rows(c), fd_r.at[0])
    recv(odown.at[pl.ds(0, 256)], fd_r.at[2])
    recv(out_rows(c), fo_r.at[0])
    recv(oout.at[pl.ds(0, 64)], fo_r.at[2])
    recv(in_place(q, k), fi_r.at[0])
    recv(oin.at[:, :, rows_at(64 * k1, 64), :], fib_r)
    recv(other_place(q, k), fq_r.at[0])
    recv(oqkv.at[:, rows_at(64 * k1, 64), other_cols], fqb_r)
    recv(value_place(q, k), fv_r.at[0])
    recv(oqkv.at[:, rows_at(64 * k1, 64), value_cols], fvb_r)

    sent(GP.at[pl.ds(0, 7)], gp_s)
    four_sent(XB, xb_s)
    four_sent(COT, co_s)
    four_sent(NTB, nt_s)
    four_sent(GAL, ga_s)
    four_sent(SA, a_s)
    four_sent(SG, g_s)
    four_sent(SO, o_s)
    four_sent(SN, n_s)
    sent(WQKV.at[pl.ds(0, 256)], wqz_s)
    sent(WQKV.at[half(f, k)], wx_s.at[0])
    sent(WIN.at[half(f, k)], wx_s.at[1])
    sent(WIN.at[pl.ds(0, 256)], wiz_s)
    sent(WDOWN.at[pl.ds(0, 256)], wdz_s)
    sent(WQKV.at[pl.ds(0, 448)], wqb_s)
    sent(WIN.at[pl.ds(0, 448)], wib_s)
    sent(WDOWN.at[pl.ds(0, 384)], wdb_s)
    sent(value_of(ZQ, near), zv_s)
    sent(other_of(ZQ, near), zq_s)
    sent(ZQ.at[pl.ds(0, 4), :, value_cols], zve_s)
    sent(ZQ.at[pl.ds(0, 4), :, other_cols], zqe_s)
    sent(down_of(ZD, near), zd_s)
    sent(ZD.at[pl.ds(0, 2)], zde_s)
    sent(PSMALL.at[pl.ds(0, 3)], sz_s)
    sent(in_of(ZI, near), zi_s)
    sent(ZI.at[pl.ds(0, 4)], zie_s)

    @pl.when(middle)
    def _():
        sent(WDOWN.at[pl.ds(0, 256)], wdf_s)
        sent(WQKV.at[pl.ds(0, 256)], wqf_s)
        sent(WIN.at[pl.ds(0, 256)], wif_s)

    @pl.when(middle)
    def _():
        sent(WOUT.at[pl.ds(0, 128)], woz_s)

    @pl.when(at_end)
    def _():
        sent(WOUT.at[pl.ds(0, 64)], woz_s)

    sent(WOUT.at[pl.ds(0, 96)], wob_s)
    sent(ZO.at[near], zo_s)
    sent(ZO.at[pl.ds(0, 2)], zoe_s)
    sent(oout.at[pl.ds(0, 96)], fo_s)
    sent(DD.at[k1], sib_s.at[0])
    sent(DI.at[k1], sib_s.at[1])
    sent(DQ.at[k1, :, :, value_cols], sib_s.at[2])
    sent(DO.at[k1], sib_s.at[3])
    sent(DQ.at[k1, :, :, other_cols], sib_s.at[4])
    sent(odown.at[pl.ds(0, 384)], fd_s)
    sent(oin.at[:, pl.ds(0, 3), pl.ds(0, 64), :], fi_s)
    sent(oqkv.at[pl.ds(0, 3), pl.ds(0, 64), other_cols], fq_s)
    sent(oqkv.at[pl.ds(0, 3), pl.ds(0, 64), value_cols], fv_s)
    sent(oin.at[:, :, rows_at(64 * k, 64), :], fib_s)
    sent(oqkv.at[:, rows_at(64 * k, 64), other_cols], fqb_s)
    sent(oqkv.at[:, rows_at(64 * k, 64), value_cols], fvb_s)
    sent(RSMALL.at[pl.ds(0, 7)], sp_s)


def plane_shards(
    inputs, cotangent, w_query, w_key, w_value, w_out, w_in, w_down, gain_attn, gain_mlp, rel_bias, buckets
):
    vm = pltpu.VMEM
    dma = pltpu.SemaphoreType.DMA
    block = lambda kind: vm((TOKENS, WIDTH), kind)
    tokens = lambda width, kind: vm((512, width), kind)
    scratch = [
        block(BF), block(BF), vm((8, 128), F32), vm((1, 1024), jnp.int32),
        vm((3, 128, 1024), BF), vm((64, 768), BF), vm((8, 8, 128), F32),
        tokens(1024, BF), tokens(1024, BF), tokens(1024, BF), tokens(1024, BF), tokens(1024, BF),
        vm((1024, 768), BF), vm((256, 1024), BF), vm((1024, 1024), BF), vm((1024, 1024), BF),
        tokens(768, BF), vm((4, 512, 512), F32), vm((4, 512, 512), BF), vm((4, 128, 1024), F32),
        tokens(256, BF), tokens(1024, BF), tokens(1024, F32), tokens(1024, BF),
        tokens(256, BF), tokens(768, BF), vm((4, 512, 512), BF), vm((4, 128, 1024), F32),
        tokens(1024, BF), tokens(1024, BF), tokens(1024, BF), tokens(1024, BF),
        vm((3, 128, 1024), BF), vm((3, 128, 1024), BF), vm((3, 128, 1024), BF), vm((3, 128, 1024), BF),
        vm((2, 64, 1024), BF), vm((2, 64, 1024), BF), vm((2, 64, 1024), BF), vm((2, 64, 1024), BF),
        block(F32), block(F32), block(BF), block(BF),
        vm((2, 8, 64, 768), BF), vm((2, 4, 32, 1024), BF), vm((2, 8, 64, 1024), BF), vm((2, 4, 128, 1024), BF),
        vm((8, 64, 768), BF), vm((4, 32, 1024), BF), vm((8, 64, 1024), BF), vm((4, 128, 1024), BF),
        vm((8, 64, 768), BF), vm((4, 32, 1024), BF), vm((8, 64, 1024), BF), vm((4, 128, 1024), BF),
        vm((8, 64, 768), BF), vm((4, 32, 1024), BF), vm((8, 64, 1024), BF), vm((4, 128, 1024), BF),
        vm((2, 64, 768), BF), vm((32, 1024), BF), vm((2, 64, 1024), BF), vm((128, 1024), BF),
        vm((2, 64, 768), BF), vm((32, 1024), BF), vm((2, 4, 64, 256), BF), vm((128, 1024), BF),
        vm((3, 8, 128), F32), vm((8, 3, 8, 128), F32), vm((4, 8, 128), F32), vm((4, 8, 128), F32),
        dma((7,)), dma, dma, dma, dma((4,)), dma((2,)), dma, dma((4,)), dma((2,)), dma, dma((4,)), dma((2,)), dma, dma((4,)), dma((2,)),
        dma, dma, dma((2,)), dma, dma, dma((2,)), dma, dma, dma((2,)), dma, dma, dma((2,)),
        dma((2,)), dma((2,)), dma, dma, dma((8,)), dma, dma, dma, dma, dma((8,)), dma, dma,
        dma, dma, dma((4,)), dma, dma, dma, dma((4,)), dma, dma,
        dma((5,)), dma((5,)), dma((4,)), dma, dma, dma((4,)), dma, dma, dma, dma((4,)), dma, dma, dma, dma((4,)), dma,
        dma, dma, dma((4,)), dma, dma, dma, dma((4,)), dma,
        dma, dma, dma((4,)), dma, dma, dma, dma((4,)), dma, dma, dma((3,)), dma, dma, dma((4,)), dma, dma, dma((3,)), dma, dma, dma, dma,
    ]
    anywhere = pl.BlockSpec(memory_space=pl.ANY)
    in_vmem = pl.BlockSpec(memory_space=pltpu.VMEM)
    shape = jax.ShapeDtypeStruct
    output, grad_inputs, proj, out, hidden, down, small = pl.pallas_call(
        fused_layer,
        out_shape=(
            shape((1, TOKENS, WIDTH), BF),
            shape((1, TOKENS, WIDTH), BF),
            shape((4, 128, 768), BF),
            shape((128, 1024), BF),
            shape((4, 4, 128, 256), BF),
            shape((512, 1024), BF),
            shape((8, 128), F32),
        ),
        in_specs=[anywhere] * 8 + [in_vmem] * 4,
        out_specs=(in_vmem, in_vmem, anywhere, anywhere, anywhere, anywhere, in_vmem),
        scratch_shapes=scratch,
        compiler_params=pltpu.CompilerParams(
            collective_id=0, has_side_effects=True, vmem_limit_bytes=63 << 20
        ),
        cost_estimate=pl.CostEstimate(flops=11 * 10**9, bytes_accessed=16 * 2**20, transcendentals=3 * 2**20),
    )(inputs, cotangent, w_query, w_key, w_value, w_out, w_in, w_down, gain_attn[None], gain_mlp[None], rel_bias[None], buckets[None])
    return finish(output, grad_inputs, proj, out, hidden, down, small)


def finish_kernel(
    output, grad_inputs, proj, out, hidden, down, small,
    o_output, o_inputs, o_query, o_key, o_value, o_out, o_in, o_down, o_attn, o_mlp, o_bias,
    b_output, b_inputs, b_proj, b_out, b_hidden, b_down, b_small, w_proj, w_out, w_in, w_down, got, left,
):
    moves = [
        pltpu.make_async_copy(proj, b_proj, got.at[0]),
        pltpu.make_async_copy(hidden, b_hidden, got.at[1]),
        pltpu.make_async_copy(down, b_down, got.at[2]),
        pltpu.make_async_copy(out, b_out, got.at[3]),
        pltpu.make_async_copy(small, b_small, got.at[4]),
        pltpu.make_async_copy(output, b_output, got.at[5]),
        pltpu.make_async_copy(grad_inputs, b_inputs, got.at[6]),
    ]
    for move in moves:
        move.start()
    sends = []

    def write(src, dst, slot):
        copy = pltpu.make_async_copy(src, dst, left.at[slot])
        copy.start()
        sends.append(copy)

    moves[0].wait()
    for w, place in enumerate((o_query, o_key, o_value)):
        for shard in range(8):
            z, x = shard // 2, shard % 2
            lanes = slice(256 * w + 64 * z, 256 * w + 64 * z + 64)
            parts = [b_proj[2 * x + y, :, lanes].astype(F32) for y in range(2)]
            w_proj[w, :, 128 * shard : 128 * shard + 128] = jnp.concatenate(parts, axis=1)
        write(w_proj.at[w], place, w)
    moves[1].wait()
    for r in range(4):
        rows = slice(32 * r, 32 * r + 32)
        for z in range(4):
            for q in range(4):
                w_in[rows, 256 * (4 * z + q) : 256 * (4 * z + q) + 256] = b_hidden[z, q, rows, :].astype(F32)
        write(w_in.at[pl.ds(32 * r, 32)], o_in.at[pl.ds(32 * r, 32)], 3 + r)
    moves[2].wait()
    for r in range(4):
        rows = slice(128 * r, 128 * r + 128)
        w_down[rows, :] = b_down[rows, :].astype(F32)
        write(w_down.at[pl.ds(128 * r, 128)], o_down.at[pl.ds(128 * r, 128)], 7 + r)
    moves[3].wait()
    w_out[...] = b_out[...].astype(F32)
    write(w_out, o_out, 11)
    moves[4].wait()
    o_attn[...] = b_small[0:1, :]
    o_mlp[...] = b_small[1:2, :]
    o_bias[...] = b_small[2:3, 0:64]
    moves[5].wait()
    write(b_output, o_output, 12)
    moves[6].wait()
    write(b_inputs, o_inputs, 13)
    for copy in sends:
        copy.wait()


def finish(output, grad_inputs, proj, out, hidden, down, small):
    shape = jax.ShapeDtypeStruct
    vm = pltpu.VMEM
    anywhere = pl.BlockSpec(memory_space=pl.ANY)
    in_vmem = pl.BlockSpec(memory_space=pltpu.VMEM)
    results = pl.pallas_call(
        finish_kernel,
        out_shape=(
            shape(output.shape, BF),
            shape(grad_inputs.shape, BF),
            shape((128, 1024), F32),
            shape((128, 1024), F32),
            shape((128, 1024), F32),
            shape((128, 1024), F32),
            shape((128, 4096), F32),
            shape((512, 1024), F32),
            shape((1, 128), F32),
            shape((1, 128), F32),
            shape((1, 64), F32),
        ),
        in_specs=[anywhere] * 7,
        out_specs=(anywhere,) * 8 + (in_vmem,) * 3,
        scratch_shapes=[
            vm(output.shape, BF), vm(grad_inputs.shape, BF), vm(proj.shape, BF), vm(out.shape, BF), vm(hidden.shape, BF), vm(down.shape, BF), vm(small.shape, F32),
            vm((3, 128, 1024), F32), vm((128, 1024), F32), vm((128, 4096), F32), vm((512, 1024), F32),
            pltpu.SemaphoreType.DMA((7,)), pltpu.SemaphoreType.DMA((14,)),
        ],
        compiler_params=pltpu.CompilerParams(vmem_limit_bytes=63 << 20),
        cost_estimate=pl.CostEstimate(flops=0, bytes_accessed=10 * 2**20, transcendentals=0),
    )(output, grad_inputs, proj, out, hidden, down, small)
    return results[:8] + (results[8].reshape(128), results[9].reshape(128), results[10].reshape(64))


def solution(mesh):
    placed = (
        P("fsdp", "ctx", None),
        P("fsdp", "ctx", None),
        P("fsdp", None),
        P("fsdp", None),
        P("fsdp", None),
        P("fsdp", None),
        P("fsdp", None),
        P("fsdp", None),
        P("fsdp"),
        P("fsdp"),
        P("fsdp"),
        P(),
    )
    by_planes = mesh.shape["ctx"] == 4 and mesh.shape["fsdp"] == 8
    return jax.shard_map(
        plane_shards if by_planes else shards,
        mesh=mesh,
        in_specs=placed,
        out_specs=(
            P("fsdp", "ctx", None),
            P("fsdp", "ctx", None),
            P("fsdp", None),
            P("fsdp", None),
            P("fsdp", None),
            P("fsdp", None),
            P("fsdp", None),
            P("fsdp", None),
            P("fsdp"),
            P("fsdp"),
            P("fsdp"),
        ),
        check_vma=False,
    )
```

```python
import jax
import jax.numpy as jnp
from jax import lax
from jax.experimental import pallas as pl
from jax.experimental.pallas import tpu as pltpu
from jax.sharding import PartitionSpec as P

HEADS = 16
HEAD = 64
BUCKETS = 32


EPS = 1e-06


def norm_rows(values, gain):
    return values * lax.rsqrt(jnp.mean(values * values, axis=-1, keepdims=True) + EPS) * gain


def smooth_gelu(values):
    return 0.5 * values * (1.0 + jax.scipy.special.erf(values * 0.7071067811865476))


def gelu_slope(values):
    return (
        0.5 * (1.0 + jax.scipy.special.erf(values * 0.7071067811865476))
        + values * jnp.exp(-0.5 * values * values) * 0.3989422804014327
    )


def bucket_offsets(buckets, first_query, query_count):
    seq_length = (buckets.shape[0] + 1) // 2
    key_place = jnp.arange(seq_length, dtype=jnp.int32)
    query_place = first_query + jnp.arange(query_count, dtype=jnp.int32)
    return key_place[None, :] - query_place[:, None] + (seq_length - 1)


def make_bias(flat_table, buckets, first_query, query_count):
    bias_table = flat_table.reshape(BUCKETS, HEADS)
    one_hot = (buckets[:, None] == jnp.arange(BUCKETS, dtype=jnp.int32)[None, :]).astype(
        flat_table.dtype
    )
    per_offset = jnp.dot(one_hot, bias_table, precision=lax.Precision.HIGHEST)
    offsets = bucket_offsets(buckets, first_query, query_count)
    return jnp.take(per_offset.T, offsets, axis=1)


def pair_table(buckets, first_query, query_count):
    offsets = bucket_offsets(buckets, first_query, query_count)
    pair_bucket = jnp.take(buckets, offsets.reshape(-1), axis=0)
    return (pair_bucket[:, None] == jnp.arange(BUCKETS, dtype=jnp.int32)[None, :]).astype(
        jnp.bfloat16
    )


def fetch_attention(w_query, w_key, w_value, w_out, gain_attn, rel_bias):
    return (
        lax.all_gather(w_query, "fsdp", axis=0, tiled=True),
        lax.all_gather(w_key, "fsdp", axis=0, tiled=True),
        lax.all_gather(w_value, "fsdp", axis=0, tiled=True),
        lax.all_gather(w_out, "fsdp", axis=0, tiled=True),
        lax.all_gather(gain_attn, "fsdp", axis=0, tiled=True),
        lax.all_gather(rel_bias, "fsdp", axis=0, tiled=True),
    )


def fetch_mlp(w_in, w_down, gain_mlp):
    return (
        lax.all_gather(w_in, "fsdp", axis=0, tiled=True),
        lax.all_gather(w_down, "fsdp", axis=0, tiled=True),
        lax.all_gather(gain_mlp, "fsdp", axis=0, tiled=True),
    )


def share_keys(key_rows, value_rows):
    return (
        lax.all_gather(key_rows, "ctx", axis=1, tiled=True),
        lax.all_gather(value_rows, "ctx", axis=1, tiled=True),
    )


def scores_of(query_part, key_part, bias_values):
    return (
        jnp.einsum("qhd,khd->hqk", query_part, key_part, preferred_element_type=jnp.float32)
        + bias_values
    )


def shards(
    inputs,
    cotangent,
    w_query,
    w_key,
    w_value,
    w_out,
    w_in,
    w_down,
    gain_attn,
    gain_mlp,
    rel_bias,
    buckets,
):
    seq_count, row_count, width = inputs.shape
    total_rows = seq_count * row_count
    first_query = lax.axis_index("ctx") * row_count
    query_w, key_w, value_w, out_w, attn_gain, bias_flat = fetch_attention(
        w_query, w_key, w_value, w_out, gain_attn, rel_bias
    )
    in_w, down_w, mlp_gain = fetch_mlp(w_in, w_down, gain_mlp)
    bias_values = make_bias(bias_flat.astype(jnp.float32), buckets, first_query, row_count)
    inputs_flat = inputs.astype(jnp.float32).reshape(total_rows, width)
    attn_scale = attn_gain.astype(jnp.float32)
    normed_one = norm_rows(inputs_flat, attn_scale).astype(jnp.bfloat16)
    query_rows = jnp.dot(normed_one, query_w, preferred_element_type=jnp.float32).astype(
        jnp.bfloat16
    )
    key_rows = (
        jnp.dot(normed_one, key_w, preferred_element_type=jnp.float32)
        .astype(jnp.bfloat16)
        .reshape(seq_count, row_count, width)
    )
    value_rows = (
        jnp.dot(normed_one, value_w, preferred_element_type=jnp.float32)
        .astype(jnp.bfloat16)
        .reshape(seq_count, row_count, width)
    )
    all_keys, all_values = share_keys(key_rows, value_rows)
    query_heads = query_rows.reshape(seq_count, row_count, HEADS, HEAD)
    seq_index = 0
    key_heads = all_keys[seq_index].reshape(-1, HEADS, HEAD)
    value_heads = all_values[seq_index].reshape(-1, HEADS, HEAD)
    scores = scores_of(query_heads[seq_index], key_heads, bias_values)
    top_score = jnp.max(scores, axis=-1, keepdims=True)
    weights_exp = jnp.exp(scores - top_score)
    totals = jnp.sum(weights_exp, axis=-1, keepdims=True)
    probs_low = (weights_exp / totals).astype(jnp.bfloat16)
    mixed = jnp.einsum("hqk,khd->qhd", probs_low, value_heads, preferred_element_type=jnp.float32)
    mixed_list = mixed.reshape(row_count, width)
    lse_list = [top_score + jnp.log(totals)]
    attended = mixed_list.astype(jnp.bfloat16)
    hidden_res = inputs_flat + jnp.dot(attended, out_w, preferred_element_type=jnp.float32)
    mlp_scale = mlp_gain.astype(jnp.float32)
    normed_two = norm_rows(hidden_res, mlp_scale).astype(jnp.bfloat16)
    pre_act = jnp.dot(normed_two, in_w, preferred_element_type=jnp.float32)
    activated = smooth_gelu(pre_act).astype(jnp.bfloat16)
    result = hidden_res + jnp.dot(activated, down_w, preferred_element_type=jnp.float32)
    in_w, down_w, mlp_gain = fetch_mlp(w_in, w_down, gain_mlp)
    query_w, key_w, value_w, out_w, attn_gain, bias_flat = fetch_attention(
        w_query, w_key, w_value, w_out, gain_attn, rel_bias
    )
    all_keys, all_values = share_keys(key_rows, value_rows)
    grad_rows = cotangent.reshape(total_rows, width)
    grad_down = jnp.einsum("nf,nd->fd", activated, grad_rows, preferred_element_type=jnp.float32)
    grad_act = jnp.einsum("nd,fd->nf", grad_rows, down_w, preferred_element_type=jnp.float32)
    grad_pre = (grad_act * gelu_slope(pre_act)).astype(jnp.bfloat16)
    grad_in = jnp.einsum("nd,nf->df", normed_two, grad_pre, preferred_element_type=jnp.float32)
    grad_normed_two = jnp.einsum("nf,df->nd", grad_pre, in_w, preferred_element_type=jnp.float32)
    back_hidden, grad_mlp_gain = jax.vjp(norm_rows, hidden_res, mlp_scale)[1](grad_normed_two)
    grad_hidden = grad_rows.astype(jnp.float32) + back_hidden
    grad_attn_low = grad_hidden.astype(jnp.bfloat16)
    grad_out = jnp.einsum("nd,ne->de", attended, grad_attn_low, preferred_element_type=jnp.float32)
    grad_attended = jnp.einsum(
        "ne,de->nd", grad_attn_low, out_w, preferred_element_type=jnp.float32
    ).astype(jnp.bfloat16)
    grad_heads = grad_attended.reshape(seq_count, row_count, HEADS, HEAD)
    pair_buckets = pair_table(buckets, first_query, row_count)
    seq_index = 0
    key_heads = all_keys[seq_index].reshape(-1, HEADS, HEAD)
    value_heads = all_values[seq_index].reshape(-1, HEADS, HEAD)
    scores = scores_of(query_heads[seq_index], key_heads, bias_values)
    probs = jnp.exp(scores - lse_list[seq_index])
    grad_probs = jnp.einsum(
        "qhd,khd->hqk", grad_heads[seq_index], value_heads, preferred_element_type=jnp.float32
    )
    row_inner = jnp.sum(probs * grad_probs, axis=-1, keepdims=True)
    grad_scores = (probs * (grad_probs - row_inner)).astype(jnp.bfloat16)
    bias_grad = jnp.dot(
        grad_scores.reshape(HEADS, -1), pair_buckets, preferred_element_type=jnp.float32
    )
    query_grads = jnp.einsum(
        "hqk,khd->qhd", grad_scores, key_heads, preferred_element_type=jnp.float32
    ).reshape(row_count, width)
    key_grads = [
        jnp.einsum(
            "hqk,qhd->khd", grad_scores, query_heads[seq_index], preferred_element_type=jnp.float32
        ).reshape(-1, width)
    ]
    value_grads = [
        jnp.einsum(
            "hqk,qhd->khd",
            probs.astype(jnp.bfloat16),
            grad_heads[seq_index],
            preferred_element_type=jnp.float32,
        ).reshape(-1, width)
    ]
    key_back, value_back = (
        lax.psum_scatter(
            jnp.stack(key_grads).astype(jnp.bfloat16), "ctx", scatter_dimension=1, tiled=True
        ).astype(jnp.float32),
        lax.psum_scatter(
            jnp.stack(value_grads).astype(jnp.bfloat16), "ctx", scatter_dimension=1, tiled=True
        ).astype(jnp.float32),
    )
    grad_query_rows = query_grads.astype(jnp.bfloat16)
    grad_key_rows = key_back.reshape(total_rows, width).astype(jnp.bfloat16)
    grad_value_rows = value_back.reshape(total_rows, width).astype(jnp.bfloat16)
    grad_query = jnp.einsum(
        "nd,ne->de", normed_one, grad_query_rows, preferred_element_type=jnp.float32
    )
    grad_key = jnp.einsum(
        "nd,ne->de", normed_one, grad_key_rows, preferred_element_type=jnp.float32
    )
    grad_value = jnp.einsum(
        "nd,ne->de", normed_one, grad_value_rows, preferred_element_type=jnp.float32
    )
    grad_normed_one = jnp.einsum(
        "ne,de->nd", grad_query_rows, query_w, preferred_element_type=jnp.float32
    )
    grad_normed_one = grad_normed_one + jnp.einsum(
        "ne,de->nd", grad_key_rows, key_w, preferred_element_type=jnp.float32
    )
    grad_normed_one = grad_normed_one + jnp.einsum(
        "ne,de->nd", grad_value_rows, value_w, preferred_element_type=jnp.float32
    )
    back_inputs, grad_attn_gain = jax.vjp(norm_rows, inputs_flat, attn_scale)[1](grad_normed_one)
    grad_inputs = (
        (grad_hidden + back_inputs).astype(jnp.bfloat16).reshape(seq_count, row_count, width)
    )
    grad_bias_flat = bias_grad.T.reshape(BUCKETS * HEADS)
    (
        part_query,
        part_key,
        part_value,
        part_out,
        part_in,
        part_down,
        part_attn_gain,
        part_mlp_gain,
        part_bias,
    ) = (
        lax.psum_scatter(grad_query, "fsdp", scatter_dimension=0, tiled=True),
        lax.psum_scatter(grad_key, "fsdp", scatter_dimension=0, tiled=True),
        lax.psum_scatter(grad_value, "fsdp", scatter_dimension=0, tiled=True),
        lax.psum_scatter(grad_out, "fsdp", scatter_dimension=0, tiled=True),
        lax.psum_scatter(grad_in, "fsdp", scatter_dimension=0, tiled=True),
        lax.psum_scatter(grad_down, "fsdp", scatter_dimension=0, tiled=True),
        lax.psum_scatter(grad_attn_gain, "fsdp", scatter_dimension=0, tiled=True),
        lax.psum_scatter(grad_mlp_gain, "fsdp", scatter_dimension=0, tiled=True),
        lax.psum_scatter(grad_bias_flat, "fsdp", scatter_dimension=0, tiled=True),
    )
    summed = (
        lax.psum(part_query.astype(jnp.bfloat16), "ctx").astype(jnp.float32),
        lax.psum(part_key.astype(jnp.bfloat16), "ctx").astype(jnp.float32),
        lax.psum(part_value.astype(jnp.bfloat16), "ctx").astype(jnp.float32),
        lax.psum(part_out.astype(jnp.bfloat16), "ctx").astype(jnp.float32),
        lax.psum(part_in.astype(jnp.bfloat16), "ctx").astype(jnp.float32),
        lax.psum(part_down.astype(jnp.bfloat16), "ctx").astype(jnp.float32),
        lax.psum(part_attn_gain.astype(jnp.bfloat16), "ctx").astype(jnp.float32),
        lax.psum(part_mlp_gain.astype(jnp.bfloat16), "ctx").astype(jnp.float32),
        lax.psum(part_bias.astype(jnp.bfloat16), "ctx").astype(jnp.float32),
    )
    output = result.astype(jnp.bfloat16).reshape(seq_count, row_count, width)
    return (
        output,
        grad_inputs,
        summed[0],
        summed[1],
        summed[2],
        summed[3],
        summed[4],
        summed[5],
        summed[6],
        summed[7],
        summed[8],
    )


MESH_ID = pl.DeviceIdType.MESH
BF = jnp.bfloat16
F32 = jnp.float32
WIDTH = 1024
TOKENS = 128
NT_DIMS = (((1,), (1,)), ((), ()))
TN_DIMS = (((0,), (0,)), ((), ()))


def dot_nn(left, right):
    return jnp.dot(left, right, preferred_element_type=F32)


def dot_nt(left, right):
    return lax.dot_general(left, right, NT_DIMS, preferred_element_type=F32)


def dot_tn(left, right):
    return lax.dot_general(left, right, TN_DIMS, preferred_element_type=F32)


def rows_at(start, count):
    return pl.ds(start if isinstance(start, int) else pl.multiple_of(start, count), count)


def remote(src, dst, send, recv, device):
    return pltpu.make_async_remote_copy(
        src_ref=src, dst_ref=dst, send_sem=send, recv_sem=recv, device_id=device, device_id_type=MESH_ID
    )


def steps(count, body, carry):
    for i in range(count):
        carry = body(i, carry)
    return carry


def fused_layer(
    x_in, cot_in, wq_in, wk_in, wv_in, wo_in, wi_in, wd_in, attn_in, mlp_in, table_in, bucket_in,
    out_ref, gin_ref, oqkv, oout, oin, odown, small_ref,
    XO, CO, PACK, BUCKET, STAGE, ACROSS, GP, XB, COT, N1, NTB, GAL, WQKV, WOUT, WIN, WDOWN,
    QKV, PROB, PLOW, BIAS, AT, ACT, SLOPE, GPRE, GATT, DQKV, DS, BACC,
    SA, SG, SO, SN, RA, RG, RO, RN, XA, XG, XS, XN, HID, GH, NTS, GALS,
    DQ, DO, DI, DD, SIBQ, SIBO, SIBI, SIBD, ZQ, ZO, ZI, ZD, REQ, REO, REI, RED, RCQ, RCO, RCI, RCD, FQ, FO, FI, FD,
    SMALL, RSMALL, PSMALL, RZSMALL,
    loc, gp_s, gp_r, xb_s, xb_r, xb_p, co_s, co_r, co_p, nt_s, nt_r, nt_p, ga_s, ga_r, ga_p,
    a_s, a_r, a_x, g_s, g_r, g_x, o_s, o_r, o_x, n_s, n_r, n_x,
    wx_s, wx_r, wqz_s, wqf_s, wqz_r, wqb_s, wqb_r, wiz_s, wif_s, wiz_r, wib_s, wib_r,
    wdz_s, wdf_s, wdz_r, wdb_s, wdb_r, woz_s, woz_r, wob_s, wob_r,
    sib_s, sib_r, sibd_r, zq_s, zqe_s, zq_r, zqc_r, zv_s, zve_s, zv_r, zvc_r, zo_s, zoe_s, zo_r, zoc_r,
    zi_s, zie_s, zi_r, zic_r, zd_s, zde_s, zd_r, zdc_r,
    fq_s, fqb_s, fq_r, fqb_r, fv_s, fvb_s, fv_r, fvb_r, fo_s, fo_r, fi_s, fib_s, fi_r, fib_r, fd_s, fd_r, sp_s, sp_r, sz_s, sz_r,
):
    c = lax.axis_index("ctx")
    f = lax.axis_index("fsdp")
    y, k = c // 2, lax.rem(c, 2)
    z, x = f // 2, lax.rem(f, 2)
    x1, y1, k1 = 1 - x, 1 - y, 1 - k
    f1 = 2 * z + x1
    q = 2 * x + y
    sib = (2 * y + k1, f)
    xdev = (c, f1)
    zs = [lax.rem(z + d, 4) for d in (1, 2, 3)]
    near = z + 1 - 2 * lax.rem(z, 2)
    other = 2 - 2 * (z // 2)
    others = (other, other + 1)
    far = 2 - z // 2
    middle = (z == 1) | (z == 2)
    at_end = jnp.logical_not(middle)

    def zdev(target):
        return (c, 2 * target + x)

    plane = []
    for i in range(4):
        ci = lax.rem(c + i, 4)
        for j, xj in enumerate((x, x1)):
            if i or j:
                plane.append((ci, 2 * z + xj))

    def recv(dst, sem):
        remote(dst, dst, sem, sem, sib).wait_recv()

    def sent(src, sem):
        remote(src, src, sem, sem, sib).wait_send()

    def block_half(buf, b, h):
        return buf.at[rows_at(b * TOKENS + 64 * h, 64)]

    def gather_send(src, dst, send, got, passed):
        halves = [src.at[pl.ds(64 * h, 64)] for h in range(2)]
        places = [block_half(dst, c, h) for h in range(2)]
        x_worker, y_worker = (2 * y + x, f1), (2 * y1 + x, f)
        remote(halves[0], places[0], send, passed.at[k], x_worker).start()
        remote(halves[1], places[1], send, passed.at[k], y_worker).start()
        remote(halves[1], places[1], send, got.at[c], x_worker).start()
        remote(halves[0], places[0], send, got.at[c], y_worker).start()
        whole = dst.at[rows_at(c * TOKENS, TOKENS)]

        @pl.when(k == x)
        def _():
            pltpu.make_async_copy(src, whole, got.at[c]).start()

        @pl.when(k != x)
        def _():
            remote(src, whole, send, got.at[c], sib).start()

    same = 1 - lax.rem(x + k, 2)
    pass_y = y + same * (1 - 2 * y)
    pass_to = (same * c + (1 - same) * (2 * y1 + k), same * f1 + (1 - same) * f)

    def gather_pass(dst, send, got, passed):
        for i in range(2):
            b = 2 * pass_y + i
            piece = block_half(dst, b, same)
            recv(piece, passed.at[i])
            remote(piece, piece, send, got.at[b], pass_to).start()

    def gather_wait(dst, got, b):
        @pl.when(b // 2 == pass_y)
        def _():
            recv(block_half(dst, b, 1 - same), got.at[b])

        @pl.when(b // 2 != pass_y)
        def _():
            recv(dst.at[rows_at(b * TOKENS, TOKENS)], got.at[b])

    def four_sent(buf, send):
        @pl.when(k == x)
        def _():
            sent(buf.at[pl.ds(0, 384)], send)

        @pl.when(k != x)
        def _():
            sent(buf, send)

    first_pair = 1 - pass_y

    def scatter_first(buf, dst, send, got, cross, cross_got, i):
        b = 2 * first_pair + i

        @pl.when(k != x)
        def _():
            remote(block_half(buf, b, 0), cross.at[i], send, cross_got.at[i], (2 * y1 + k, f)).start()
            remote(block_half(buf, b, 1), cross.at[i], send, cross_got.at[i], (c, f1)).start()

        whole = buf.at[rows_at(b * TOKENS, TOKENS)]

        @pl.when((k == x) & (i == k))
        def _():
            pltpu.make_async_copy(whole, dst.at[0], got).start()

        @pl.when((k == x) & (i != k))
        def _():
            remote(whole, dst.at[0], send, got, sib).start()

    def scatter_half(buf, dst, send, got, i, h):
        b = 2 * pass_y + i
        place = dst.at[1 + same, rows_at(64 * h, 64)]
        remote(block_half(buf, b, h), place, send, got, (b, 2 * z + k)).start()

    def scatter_second(buf, dst, send, got, i):
        scatter_half(buf, dst, send, got, i, 1 - same)

    def scatter_sums(buf, dst, send, got, cross, cross_got):
        for i in range(2):
            recv(cross.at[i], cross_got.at[i])
            rows = rows_at((2 * pass_y + i) * TOKENS + 64 * same, 64)
            buf[rows, :] = (buf[rows, :].astype(F32) + cross[i].astype(F32)).astype(BF)
            scatter_half(buf, dst, send, got, i, same)

    def half(fb, kk):
        return rows_at(fb * 128 + kk * 64, 64)

    def z_far(piece, send, got, src=None):
        remote(piece if src is None else src, piece, send, got, zdev(far)).start()

    def z_near(piece, send, got, src=None):
        remote(piece if src is None else src, piece, send, got, zdev(near)).start()

    def z_send(piece, send, got):
        z_far(piece, send, got)
        z_near(piece, send, got)

    def down_of(ref, t):
        return ref.at[t]

    def in_of(ref, t):
        return ref.at[pl.ds(2 * t, 2)]

    def value_of(ref, t):
        return ref.at[pl.ds(2 * t, 2), :, value_cols]

    def other_of(ref, t):
        return ref.at[pl.ds(2 * t, 2), :, other_cols]

    value_cols, other_cols = pl.ds(512, 256), pl.ds(0, 512)

    def reduce_others(of, terms, got, send, sem):
        @pl.when(at_end)
        def _():
            for t in others:
                remote(of(terms, t), of(got, t), send, sem.at[t], zdev(near)).start()

    def reduce_near(of, terms, got, send, sem):
        remote(of(terms, near), of(got, near), send, sem.at[near], zdev(near)).start()

    def reduce_middle(of, terms, got, final, send, sem, final_sem):
        @pl.when(middle)
        def _():
            for t in others:
                recv(of(got, t), sem.at[t])
                mine = of(terms, t)
                mine[...] = (mine[...].astype(F32) + of(got, t)[...].astype(F32)).astype(BF)
                remote(mine, final, send, final_sem, zdev(t)).start()

    def take(piece, got, bsend, bgot):
        recv(piece, got)
        remote(piece, piece, bsend, bgot, sib).start()

    def pass_on(piece, send, got):
        remote(piece, piece, send, got, zdev(near)).start()

    def of_row(t, xx):
        return 2 * t + xx

    own_x = pltpu.make_async_copy(x_in.at[0], XO, loc.at[0])
    own_c = pltpu.make_async_copy(cot_in.at[0], CO, loc.at[1])
    myrows = pl.ds(pl.multiple_of(128 * f, 128), 128)
    for w, proj in enumerate((wq_in, wk_in, wv_in)):
        pltpu.make_async_copy(proj, STAGE.at[w], loc.at[3]).start()
    for j in range(4):
        src = wi_in.at[:, pl.ds(pl.multiple_of(512 * (2 * j + x) + 256 * y, 256), 256)]
        pltpu.make_async_copy(src, WIN.at[myrows, pl.ds(256 * j, 256)], loc.at[4]).start()
    pltpu.make_async_copy(
        wd_in.at[rows_at(256 * y, 256)], WDOWN.at[rows_at(256 * z, 256)], loc.at[5]
    ).start()

    pltpu.make_async_copy(wo_in.at[rows_at(64 * y, 64)], WOUT.at[rows_at(64 * z, 64)], loc.at[6]).start()
    own_x.start()
    own_c.start()

    barrier = pltpu.get_barrier_semaphore()
    across = [(c, 2 * t + x1) for t in zs]
    for device in plane + [zdev(t) for t in zs] + across:
        pl.semaphore_signal(barrier, inc=1, device_id=device, device_id_type=MESH_ID)


    PACK[...] = jnp.zeros((8, 128), F32)
    PACK[0:1, :] = attn_in[...].astype(F32)
    PACK[1:2, :] = mlp_in[...].astype(F32)
    PACK[2:3, 0:64] = table_in[...].astype(F32)
    BUCKET[...] = jnp.full((1, WIDTH), -1, jnp.int32)
    BUCKET[0:1, 0 : WIDTH - 1] = bucket_in[...]
    GP[f] = PACK[...]

    pltpu.make_async_copy(STAGE, STAGE, loc.at[3]).wait()

    def pack_heads(dst, dst_rows, src_rows, xx, count):
        low = lax.broadcasted_iota(jnp.int32, (count, 128), 1) < 64
        for w in range(3):
            for j in range(2):
                first, second = [
                    STAGE[w, src_rows, pl.ds(pl.multiple_of(128 * (4 * j + 2 * n + xx), 128), 128)].astype(F32)
                    for n in range(2)
                ]
                left = jnp.where(y == 0, first, pltpu.roll(first, 64, 1))
                right = jnp.where(y == 0, pltpu.roll(second, 64, 1), second)
                dst[dst_rows, 256 * w + 128 * j : 256 * w + 128 * j + 128] = jnp.where(low, left, right).astype(BF)

    pack_heads(ACROSS, slice(0, 64), rows_at(64 * k, 64), x1, 64)
    pack_heads(WQKV, myrows, slice(0, 128), x, 128)
    pl.semaphore_wait(barrier, 13)
    for device in [xdev] + [zdev(t) for t in zs] + across:
        remote(PACK, GP.at[f], gp_s, gp_r, device).start()
    remote(ACROSS, WQKV.at[half(f, k)], wx_s.at[0], wx_r.at[0], xdev).start()
    z_send(WQKV.at[half(f, k)], wqz_s, wqz_r.at[f])
    gather_send(x_in.at[0], XB, xb_s, xb_r, xb_p)
    for j in range(4):
        src = wi_in.at[rows_at(64 * k, 64), pl.ds(pl.multiple_of(512 * (2 * j + x1) + 256 * y, 256), 256)]
        remote(src, WIN.at[half(f, k), pl.ds(256 * j, 256)], wx_s.at[1], wx_r.at[1], xdev).start()

    recv(WQKV.at[half(f1, k)], wx_r.at[0])
    z_send(WQKV.at[half(f1, k)], wqz_s, wqz_r.at[f1])
    remote(WQKV.at[half(f1, k)], WQKV.at[half(f1, k)], wqb_s, wqb_r, sib).start()
    down_half = rows_at(256 * z + 128 * k, 128)
    pltpu.make_async_copy(WIN.at[myrows], WIN.at[myrows], loc.at[4]).wait()

    def out_piece(t):
        return WOUT.at[rows_at(64 * t + 32 * k, 32)]

    out_own = wo_in.at[rows_at(64 * y + 32 * k, 32)]
    z_far(out_piece(z), woz_s, woz_r.at[z], out_own)

    @pl.when(at_end)
    def _():
        z_near(out_piece(z), woz_s, woz_r.at[z], out_own)

    z_far(WIN.at[half(f, k)], wiz_s, wiz_r.at[f])

    @pl.when(at_end)
    def _():
        z_near(WIN.at[half(f, k)], wiz_s, wiz_r.at[f])

    def take_proj(xx):
        for n in range(2):
            h = of_row(others[n], xx)
            piece = WQKV.at[half(h, k)]
            recv(piece, wqz_r.at[h])

            @pl.when(middle)
            def _():
                pass_on(piece, wqf_s, wqz_r.at[h])

            remote(piece, piece, wqb_s, wqb_r, sib).start()

    def take_near(xx):
        g = of_row(near, xx)
        take(WQKV.at[half(g, k)], wqz_r.at[g], wqb_s, wqb_r)

    @pl.when(middle)
    def _():
        take_proj(x)

    gather_pass(XB, xb_s, xb_r, xb_p)
    gather_send(cot_in.at[0], COT, co_s, co_r, co_p)
    take_near(x)

    @pl.when(middle)
    def _():
        take_proj(x1)
        take_near(x1)

        z_near(out_piece(z), woz_s, woz_r.at[z], out_own)

    recv(GP.at[pl.ds(0, 7)], gp_r)

    def row_of(index):
        return jnp.concatenate([GP[g, index : index + 1, :] for g in range(8)], axis=1)

    lane = lax.broadcasted_iota(jnp.int32, (8, 128), 1)
    head_row = lax.broadcasted_iota(jnp.int32, (8, 128), 0)
    head_of = 4 * head_row + 2 * x + y
    head_mask = (lax.rem(lane, 16) == head_of) & (head_row < 4)

    def bucket_hot(g):
        index = lax.broadcasted_iota(jnp.int32, (128, WIDTH), 0)
        wanted = jnp.where(index < 64, 4 * g + lax.div(index, 16), -1)
        return (BUCKET[0:1, :] == wanted)

    def add_bias(g, total):
        table = jnp.where(head_mask, jnp.broadcast_to(GP[g, 2:3, :], (8, 128)), 0.0).astype(BF)
        return total + dot_nn(table, bucket_hot(g).astype(BF))

    offsets = steps(8, add_bias, jnp.zeros((8, WIDTH), F32))
    for h in range(4):
        spread = jnp.broadcast_to(offsets[h : h + 1, :], (128, WIDTH))
        BIAS[h] = pltpu.roll(spread, WIDTH - 127, 1, stride=1, stride_axis=0)
        BACC[h] = jnp.zeros((128, WIDTH), F32)

    gain_one = row_of(0)

    def norm_block(i, carry):
        b = lax.rem(2 * y + i, 4)
        gather_wait(XB, xb_r, b)

        def chunk(r, inner):
            rows = rows_at(b * TOKENS + r * 32, 32)
            values = XB[rows, :].astype(F32)
            scale = lax.rsqrt(jnp.mean(values * values, axis=-1, keepdims=True) + EPS)
            N1[rows, :] = (values * scale * gain_one).astype(BF)
            return inner

        return steps(4, chunk, carry)

    steps(4, norm_block, 0)

    @pl.when(middle)
    def _():
        for t in others:
            recv(out_piece(t), woz_r.at[t])
            pass_on(out_piece(t), woz_s, woz_r.at[t])
            remote(out_piece(t), out_piece(t), wob_s, wob_r, sib).start()

        z_near(WIN.at[half(f, k)], wiz_s, wiz_r.at[f])

    recv(WIN.at[half(f1, k)], wx_r.at[1])
    z_far(WIN.at[half(f1, k)], wiz_s, wiz_r.at[f1])
    remote(WIN.at[half(f1, k)], WIN.at[half(f1, k)], wib_s, wib_r, sib).start()
    pltpu.make_async_copy(WDOWN.at[rows_at(256 * z, 256)], WDOWN.at[rows_at(256 * z, 256)], loc.at[5]).wait()
    z_far(WDOWN.at[down_half], wdz_s, wdz_r.at[z])

    z_near(WIN.at[half(f1, k)], wiz_s, wiz_r.at[f1])

    @pl.when(at_end)
    def _():
        z_near(WDOWN.at[down_half], wdz_s, wdz_r.at[z])
        take_near(x1)
        take_proj(x)
        take_proj(x1)

    recv(WQKV.at[pl.ds(0, 448)], wqb_r)

    def project(n, carry):
        cols = rows_at(256 * n, 256)
        QKV[:, cols] = dot_nn(N1[...], WQKV[:, cols]).astype(BF)
        return carry

    steps(3, project, 0)


    gather_pass(COT, co_s, co_r, co_p)

    @pl.when(middle)
    def _():
        z_near(WDOWN.at[down_half], wdz_s, wdz_r.at[z])

    low_lanes = lax.broadcasted_iota(jnp.int32, (TOKENS, 128), 1) < 64

    def pick(values, hh):
        keep = low_lanes if hh == 0 else jnp.logical_not(low_lanes)
        return jnp.where(keep, values, jnp.zeros_like(values))

    def attend(i, carry):
        b = lax.rem(2 * first_pair + i, 4)
        rows = rows_at(b * TOKENS, TOKENS)
        window = pl.ds(pl.multiple_of(384 - 128 * b, 128), 512)
        for j in range(2):
            outs = []
            for hh in range(2):
                h = 2 * j + hh
                query = pick(QKV[rows, 128 * j : 128 * j + 128], hh)
                scores = dot_nt(query, QKV[:, 256 + 128 * j : 384 + 128 * j]) + BIAS[h, :, window]
                weights = jnp.exp(scores - jnp.max(scores, axis=-1, keepdims=True))
                probs = weights * (1.0 / jnp.sum(weights, axis=-1, keepdims=True))
                PROB[h, rows, :] = probs
                low = probs.astype(BF)
                PLOW[h, rows, :] = low
                outs.append(dot_nn(low, QKV[:, 512 + 128 * j : 640 + 128 * j]))
            AT[rows, 128 * j : 128 * j + 128] = jnp.where(low_lanes, outs[0], outs[1]).astype(BF)

        @pl.when(i == 0)
        def _():
            take(out_piece(near), woz_r.at[near], wob_s, wob_r)

            @pl.when(at_end)
            def _():
                for t in others:
                    take(out_piece(t), woz_r.at[t], wob_s, wob_r)

            pltpu.make_async_copy(WOUT.at[rows_at(64 * z, 64)], WOUT.at[rows_at(64 * z, 64)], loc.at[6]).wait()
            recv(WOUT.at[pl.ds(0, 96)], wob_r)

        SA[rows, :] = dot_nn(AT[rows, :], WOUT[...]).astype(BF)

        @pl.when(i < 2)
        def _():
            scatter_first(SA, RA, a_s, a_r, XA, a_x, i)

        @pl.when(i >= 2)
        def _():
            scatter_second(SA, RA, a_s, a_r, i - 2)

        return carry

    lax.fori_loop(0, 4, attend, 0)
    scatter_sums(SA, RA, a_s, a_r, XA, a_x)

    for xx in (x, x1):
        g = of_row(near, xx)
        take(WIN.at[half(g, k)], wiz_r.at[g], wib_s, wib_r)

    @pl.when(middle)
    def _():
        for i, xx in enumerate((x, x1)):
            for n in range(2):
                g = of_row(others[n], xx)
                recv(WIN.at[half(g, k)], wiz_r.at[g])
                pass_on(WIN.at[half(g, k)], wif_s, wiz_r.at[g])
                remote(WIN.at[half(g, k)], WIN.at[half(g, k)], wib_s, wib_r, sib).start()

    own_x.wait()
    own_c.wait()
    gain_two = row_of(1)
    recv(RA, a_r)

    def home_forward(r, carry):
        rows = rows_at(r * 32, 32)
        hidden = XO[rows, :].astype(F32)
        for s in range(3):
            hidden = hidden + RA[s, rows, :].astype(F32)
        HID[rows, :] = hidden
        scale = lax.rsqrt(jnp.mean(hidden * hidden, axis=-1, keepdims=True) + EPS)
        NTS[rows, :] = (hidden * scale * gain_two).astype(BF)
        return carry

    steps(4, home_forward, 0)
    gather_send(NTS, NTB, nt_s, nt_r, nt_p)

    def down_piece(t, kk):
        return WDOWN.at[rows_at(256 * t + 128 * kk, 128)]

    take(down_piece(near, k), wdz_r.at[near], wdb_s, wdb_r)

    @pl.when(middle)
    def _():
        for n in range(2):
            t = others[n]
            recv(down_piece(t, k), wdz_r.at[t])
            pass_on(down_piece(t, k), wdf_s, wdz_r.at[t])
            remote(down_piece(t, k), down_piece(t, k), wdb_s, wdb_r, sib).start()

    @pl.when(at_end)
    def _():
        for xx in (x, x1):
            for t in others:
                g = of_row(t, xx)
                take(WIN.at[half(g, k)], wiz_r.at[g], wib_s, wib_r)

    recv(WIN.at[pl.ds(0, 448)], wib_r)

    gather_pass(NTB, nt_s, nt_r, nt_p)

    def feed(i, carry):
        yy = lax.rem(y + i, 2)
        rows = rows_at(256 * yy, 256)
        for b in (2 * yy, 2 * yy + 1):
            gather_wait(NTB, nt_r, b)

        def hidden_units(n, inner):
            cols = rows_at(256 * n, 256)
            pre = dot_nn(NTB[rows, :], WIN[:, cols])
            cdf = 0.5 * (1.0 + lax.erf(pre * 0.7071067811865476))
            ACT[rows, cols] = (pre * cdf).astype(BF)
            SLOPE[rows, cols] = cdf + pre * jnp.exp(-0.5 * pre * pre) * 0.3989422804014327
            return inner

        return steps(4, hidden_units, carry)

    lax.fori_loop(0, 2, feed, 0)

    for b in range(4):
        gather_wait(COT, co_r, b)

    order = (other, other + 1, near, z)

    def grad_down(i, carry):
        m = jnp.where(i < 2, other + i, jnp.where(i == 2, near, z))
        tile = dot_tn(ACT[:, rows_at(256 * m, 256)], COT[...]).astype(BF)
        DD[0, m] = tile[0:128]
        DD[1, m] = tile[128:256]
        remote(DD.at[k1, m], SIBD.at[m], sib_s.at[0], sibd_r.at[i], sib).start()
        return carry

    steps(4, grad_down, 0)

    def join_down(i, carry):
        m = jnp.where(i < 2, other + i, jnp.where(i == 2, near, z))
        recv(SIBD.at[m], sibd_r.at[i])
        ZD[m] = (DD[k, m].astype(F32) + SIBD[m].astype(F32)).astype(BF)

        @pl.when(at_end & (i < 2))
        def _():
            remote(ZD.at[m], RED.at[m], zde_s, zd_r.at[m], zdev(near)).start()

        @pl.when(middle & (i == 2))
        def _():
            remote(ZD.at[m], RED.at[m], zd_s, zd_r.at[m], zdev(near)).start()

        return carry

    steps(4, join_down, 0)

    @pl.when(at_end)
    def _():
        for t in others:
            take(down_piece(t, k), wdz_r.at[t], wdb_s, wdb_r)

    recv(WDOWN.at[pl.ds(0, 384)], wdb_r)

    def back_feed(i, carry):
        yy = lax.rem(first_pair + i, 2)
        rows = rows_at(256 * yy, 256)

        def back_act(n, inner):
            cols = rows_at(256 * n, 256)
            GPRE[rows, cols] = (dot_nt(COT[rows, :], WDOWN[cols, :]) * SLOPE[rows, cols]).astype(BF)
            return inner

        steps(4, back_act, 0)

        def back_normed(n, inner):
            cols = rows_at(256 * n, 256)
            SG[rows, cols] = dot_nt(GPRE[rows, :], WIN[cols, :]).astype(BF)
            return inner

        steps(4, back_normed, 0)

        @pl.when(i == 0)
        def _():
            for n in range(2):
                scatter_first(SG, RG, g_s, g_r, XG, g_x, n)

        @pl.when(i == 1)
        def _():
            for n in range(2):
                scatter_second(SG, RG, g_s, g_r, n)

        return carry

    lax.fori_loop(0, 2, back_feed, 0)

    def grad_in(m, carry):
        tile = dot_tn(NTB[:, rows_at(256 * m, 256)], GPRE[...]).astype(BF)
        for part in range(2):
            DI[0, 2 * m + part] = tile[128 * part : 128 * part + 64]
            DI[1, 2 * m + part] = tile[128 * part + 64 : 128 * part + 128]
        return carry

    steps(4, grad_in, 0)
    scatter_sums(SG, RG, g_s, g_r, XG, g_x)
    remote(DI.at[k1], SIBI, sib_s.at[1], sib_r.at[1], sib).start()

    def down_project(n, carry):
        cols = rows_at(256 * n, 256)
        SO[:, cols] = dot_nn(ACT[...], WDOWN[:, cols]).astype(BF)
        return carry

    steps(4, down_project, 0)
    for i in range(2):
        scatter_first(SO, RO, o_s, o_r, XS, o_x, i)


    recv(SIBI, sib_r.at[1])

    def join_in(m, carry):
        ZI[m] = (DI[k, m].astype(F32) + SIBI[m].astype(F32)).astype(BF)
        return carry

    steps(8, join_in, 0)
    reduce_others(in_of, ZI, REI, zie_s, zi_r)

    @pl.when(at_end)
    def _():
        reduce_near(down_of, ZD, RED, zd_s, zd_r)

    reduce_near(in_of, ZI, REI, zi_s, zi_r)

    recv(RG, g_r)

    def home_back(r, total):
        rows = rows_at(r * 32, 32)
        grad = RG[0, rows, :].astype(F32)
        for s in range(1, 3):
            grad = grad + RG[s, rows, :].astype(F32)
        hidden = HID[rows, :]
        scale = lax.rsqrt(jnp.mean(hidden * hidden, axis=-1, keepdims=True) + EPS)
        scaled = grad * gain_two
        inner = jnp.mean(scaled * hidden, axis=-1, keepdims=True)
        back = CO[rows, :].astype(F32) + scale * scaled - hidden * (scale * scale * scale * inner)
        GH[rows, :] = back
        GALS[rows, :] = back.astype(BF)
        return total + jnp.sum((grad * hidden * scale).reshape(4, 8, WIDTH), axis=0)

    mlp_gain_grad = steps(4, home_back, jnp.zeros((8, WIDTH), F32))
    gather_send(GALS, GAL, ga_s, ga_r, ga_p)
    reduce_middle(down_of, ZD, RED, RCD, zde_s, zd_r, zdc_r)

    mlp_gain_grad = jnp.sum(mlp_gain_grad, axis=0, keepdims=True)
    for g in range(8):
        SMALL[1, g : g + 1, :] = mlp_gain_grad[:, 128 * g : 128 * g + 128]

    gather_pass(GAL, ga_s, ga_r, ga_p)
    for i in range(2):
        scatter_second(SO, RO, o_s, o_r, i)

    scatter_sums(SO, RO, o_s, o_r, XS, o_x)

    all_low = lax.broadcasted_iota(jnp.int32, (512, 128), 1) < 64

    def pick_all(values, hh):
        keep = all_low if hh == 0 else jnp.logical_not(all_low)
        return jnp.where(keep, values, jnp.zeros_like(values))

    def attend_back(i, carry):
        b = lax.rem(2 * y + i, 4)
        rows = rows_at(b * TOKENS, TOKENS)
        gather_wait(GAL, ga_r, b)

        @pl.when(i == 2)
        def _():
            reduce_middle(in_of, ZI, REI, RCI, zie_s, zi_r, zic_r)

        GATT[rows, :] = dot_nt(GAL[rows, :], WOUT[...]).astype(BF)
        for j in range(2):
            pair = slice(128 * j, 128 * j + 128)
            keys = QKV[:, 256 + 128 * j : 384 + 128 * j]
            values = QKV[:, 512 + 128 * j : 640 + 128 * j]
            outs = []
            for hh in range(2):
                h = 2 * j + hh
                grad_att = pick(GATT[rows, pair], hh)
                probs = PROB[h, rows, :]
                grad_probs = dot_nt(grad_att, values)
                inner = jnp.sum(probs * grad_probs, axis=-1, keepdims=True)
                grad_scores = (probs * (grad_probs - inner)).astype(BF)
                DS[h, rows, :] = grad_scores
                outs.append(dot_nn(grad_scores, keys))
            DQKV[rows, pair] = jnp.where(low_lanes, outs[0], outs[1]).astype(BF)
        return carry

    lax.fori_loop(0, 4, attend_back, 0)

    def grad_keys(j, carry):
        query = QKV[:, rows_at(128 * j, 128)]
        first = dot_tn(DS[2 * j], pick_all(query, 0))
        second = dot_tn(DS[2 * j + 1], pick_all(query, 1))
        DQKV[:, pl.ds(pl.multiple_of(256 + 128 * j, 128), 128)] = jnp.where(all_low, first, second).astype(BF)
        return carry

    steps(2, grad_keys, 0)

    def grad_values(j, carry):
        grad_att = GATT[:, rows_at(128 * j, 128)]
        first = dot_tn(PLOW[2 * j], pick_all(grad_att, 0))
        second = dot_tn(PLOW[2 * j + 1], pick_all(grad_att, 1))
        DQKV[:, pl.ds(pl.multiple_of(512 + 128 * j, 128), 128)] = jnp.where(all_low, first, second).astype(BF)
        return carry

    steps(2, grad_values, 0)

    def grad_proj(first, width):
        def step(m, carry):
            tile = dot_tn(N1[:, rows_at(256 * m, 256)], DQKV[:, first : first + width]).astype(BF)
            for part in range(2):
                DQ[0, 2 * m + part, :, first : first + width] = tile[128 * part : 128 * part + 64]
                DQ[1, 2 * m + part, :, first : first + width] = tile[128 * part + 64 : 128 * part + 128]
            return carry

        steps(4, step, 0)

    def join_proj(first, width):
        def step(m, carry):
            total = DQ[k, m, :, first : first + width].astype(F32) + SIBQ[m, :, first : first + width].astype(F32)
            ZQ[m, :, first : first + width] = total.astype(BF)
            return carry

        steps(8, step, 0)

    def back_project(i, carry):
        yy = lax.rem(first_pair + i, 2)
        rows = rows_at(256 * yy, 256)
        SN[rows, :] = dot_nt(DQKV[rows, :], WQKV[...]).astype(BF)

        @pl.when(i == 0)
        def _():
            for n in range(2):
                scatter_first(SN, RN, n_s, n_r, XN, n_x, n)

        @pl.when(i == 1)
        def _():
            for n in range(2):
                scatter_second(SN, RN, n_s, n_r, n)

        return carry

    lax.fori_loop(0, 2, back_project, 0)

    grad_proj(0, 512)
    remote(DQ.at[k1, :, :, other_cols], SIBQ.at[:, :, other_cols], sib_s.at[4], sib_r.at[4], sib).start()
    grad_proj(512, 256)
    remote(DQ.at[k1, :, :, value_cols], SIBQ.at[:, :, value_cols], sib_s.at[2], sib_r.at[2], sib).start()


    recv(SIBQ.at[:, :, other_cols], sib_r.at[4])
    join_proj(0, 512)
    reduce_others(other_of, ZQ, REQ, zqe_s, zq_r)

    def grad_out_rows(m, carry):
        tile = dot_tn(AT[:, rows_at(128 * m, 128)], GAL[...]).astype(BF)
        for n in range(2):
            for kk in range(2):
                DO[kk, 2 * m + n] = tile[64 * n + 32 * kk : 64 * n + 32 * kk + 32]
        return carry

    steps(2, grad_out_rows, 0)
    remote(DO.at[k1], SIBO, sib_s.at[3], sib_r.at[3], sib).start()
    scatter_sums(SN, RN, n_s, n_r, XN, n_x)
    recv(SIBQ.at[:, :, value_cols], sib_r.at[2])
    join_proj(512, 256)
    reduce_others(value_of, ZQ, REQ, zve_s, zv_r)
    recv(SIBO, sib_r.at[3])
    ZO[...] = (DO[k].astype(F32) + SIBO[...].astype(F32)).astype(BF)
    reduce_others(down_of, ZO, REO, zoe_s, zo_r)
    reduce_near(other_of, ZQ, REQ, zq_s, zq_r)
    reduce_near(value_of, ZQ, REQ, zv_s, zv_r)
    reduce_near(down_of, ZO, REO, zo_s, zo_r)

    def place_scores(i, carry):
        rows = rows_at(i * TOKENS, TOKENS)
        window = pl.ds(pl.multiple_of(384 - 128 * i, 128), 512)
        for h in range(4):
            BACC[h, :, window] = BACC[h, :, window] + DS[h, rows, :].astype(F32)
        return carry

    steps(4, place_scores, 0)
    head_sums = []
    for h in range(4):
        rest = BACC[h]
        count = 64
        while count >= 8:
            rest = pltpu.roll(rest[0:count, :], count, 1) + rest[count : 2 * count, :]
            count //= 2
        for bit in (1, 2, 4):
            shift_row = 7 - lax.broadcasted_iota(jnp.int32, (8, WIDTH), 0)
            rest = jnp.where(lax.rem(lax.div(shift_row, bit), 2) == 1, pltpu.roll(rest, bit, 1), rest)
        head_sums.append(jnp.sum(rest, axis=0, keepdims=True))
    head_sums = jnp.concatenate(head_sums + [jnp.zeros((4, WIDTH), F32)], axis=0)
    coarse = head_sums.astype(BF)
    split_sums = jnp.concatenate([coarse, (head_sums - coarse.astype(F32)).astype(BF)], axis=0)
    both_masks = jnp.concatenate([head_mask.astype(F32)] * 2, axis=0) > 0.5

    def bucket_sums(g, carry):
        sums = dot_nt(split_sums, bucket_hot(g).astype(BF))
        SMALL[2, pl.ds(g, 1), :] = jnp.sum(jnp.where(both_masks, sums, 0.0), axis=0, keepdims=True)
        return carry

    steps(8, bucket_sums, 0)

    recv(RED.at[z], zd_r.at[z])
    recv(RCD, zdc_r)
    FD[...] = (ZD[z].astype(F32) + RED[z].astype(F32) + RCD[...].astype(F32)).astype(BF)

    def down_rows(cc):
        return odown.at[rows_at(128 * cc, 128)]

    y_core = (2 * y1 + k, f)
    remote(FD, down_rows(c), fd_s, fd_r.at[1], y_core).start()
    remote(FD, down_rows(c), fd_s, fd_r.at[2], sib).start()
    pltpu.make_async_copy(FD, down_rows(c), fd_r.at[0]).start()

    def spread(final, place, send, bsend, got, bgot):
        remote(final.at[x1], place(q, k), send, got.at[3], (2 * y1 + k, f1)).start()
        remote(final.at[x1], place(q, k), send, got.at[2], (c, f1)).start()
        remote(final.at[x], place(q, k), send, got.at[1], y_core).start()
        remote(final.at[x], place(q, k), bsend, bgot, sib).start()
        pltpu.make_async_copy(final.at[x], place(q, k), got.at[0]).start()

    chips = (2 * x + y1, 2 * x1 + y, 2 * x1 + y1)

    def spread_on(place, bsend, got, bgot):
        for i in range(3):
            piece = place(chips[i], k)
            recv(piece, got.at[i + 1])
            remote(piece, piece, bsend, bgot, sib).start()

    def in_place(qq, kk):
        return oin.at[:, qq, rows_at(64 * kk, 64), :]

    recv(RO, o_r)

    def home_out(r, carry):
        rows = rows_at(r * 32, 32)
        result = HID[rows, :]
        for s in range(3):
            result = result + RO[s, rows, :].astype(F32)
        out_ref[0, rows, :] = result.astype(BF)
        return carry

    steps(4, home_out, 0)
    recv(RN, n_r)

    def home_inputs(r, total):
        rows = rows_at(r * 32, 32)
        grad = RN[0, rows, :].astype(F32)
        for s in range(1, 3):
            grad = grad + RN[s, rows, :].astype(F32)
        values = XO[rows, :].astype(F32)
        scale = lax.rsqrt(jnp.mean(values * values, axis=-1, keepdims=True) + EPS)
        scaled = grad * gain_one
        inner = jnp.mean(scaled * values, axis=-1, keepdims=True)
        back = GH[rows, :] + scale * scaled - values * (scale * scale * scale * inner)
        gin_ref[0, rows, :] = back.astype(BF)
        return total + jnp.sum((grad * values * scale).reshape(4, 8, WIDTH), axis=0)

    attn_gain_grad = steps(4, home_inputs, jnp.zeros((8, WIDTH), F32))
    attn_gain_grad = jnp.sum(attn_gain_grad, axis=0, keepdims=True)
    for g in range(8):
        SMALL[0, g : g + 1, :] = attn_gain_grad[:, 128 * g : 128 * g + 128]

    for i in range(4):
        ci = lax.rem(c + i, 4)
        for j, xj in enumerate((x, x1)):
            if i or j:
                remote(SMALL, RSMALL.at[2 * c + x], sp_s, sp_r, (ci, 2 * z + xj)).start()

    recv(in_of(REI, z), zi_r.at[z])
    recv(RCI, zic_r)
    for xx in range(2):
        total = ZI[2 * z + xx].astype(F32) + REI[2 * z + xx].astype(F32) + RCI[xx].astype(F32)
        for j in range(4):
            FI[xx, j] = total[:, 256 * j : 256 * j + 256].astype(BF)
    spread(FI, in_place, fi_s, fib_s, fi_r, fib_r)

    reduce_middle(other_of, ZQ, REQ, RCQ.at[:, :, other_cols], zqe_s, zq_r, zqc_r)
    reduce_middle(value_of, ZQ, REQ, RCQ.at[:, :, value_cols], zve_s, zv_r, zvc_r)
    reduce_middle(down_of, ZO, REO, RCO, zoe_s, zo_r, zoc_r)

    def final_proj(of, cols, first, width, sem, final_sem):
        recv(of(REQ, z), sem.at[z])
        recv(RCQ.at[:, :, cols], final_sem)
        for xx in range(2):
            total = ZQ[2 * z + xx, :, first : first + width].astype(F32)
            total = total + REQ[2 * z + xx, :, first : first + width].astype(F32)
            total = total + RCQ[xx, :, first : first + width].astype(F32)
            FQ[xx, :, first : first + width] = total.astype(BF)

    def other_place(qq, kk):
        return oqkv.at[qq, rows_at(64 * kk, 64), other_cols]

    def value_place(qq, kk):
        return oqkv.at[qq, rows_at(64 * kk, 64), value_cols]

    def out_rows(cc):
        return oout.at[rows_at(32 * cc, 32)]

    y_rows = down_rows(2 * y1 + k)
    recv(y_rows, fd_r.at[1])
    remote(y_rows, y_rows, fd_s, fd_r.at[2], sib).start()
    recv(RSMALL.at[pl.ds(0, 7)], sp_r)
    plane_sum = SMALL[...]
    for i in range(4):
        ci = lax.rem(c + i, 4)
        for j, xj in enumerate((x, x1)):
            if i or j:
                plane_sum = plane_sum + RSMALL[2 * ci + xj]
    for t in range(4):
        for n in range(3):
            pair = plane_sum[n, 2 * t : 2 * t + 2, :]
            PSMALL[t, n : n + 1, :] = jnp.where(x == 0, pair[0:1], pair[1:2])
    for t in zs:
        remote(PSMALL.at[t], RZSMALL.at[z], sz_s, sz_r, zdev(t)).start()

    final_proj(other_of, other_cols, 0, 512, zq_r, zqc_r)
    spread(FQ.at[:, :, other_cols], other_place, fq_s, fqb_s, fq_r, fqb_r)
    final_proj(value_of, value_cols, 512, 256, zv_r, zvc_r)
    spread(FQ.at[:, :, value_cols], value_place, fv_s, fvb_s, fv_r, fvb_r)
    spread_on(in_place, fib_s, fi_r, fib_r)
    recv(REO.at[z], zo_r.at[z])
    recv(RCO, zoc_r)
    FO[...] = (ZO[z].astype(F32) + REO[z].astype(F32) + RCO[...].astype(F32)).astype(BF)
    remote(FO, out_rows(c), fo_s, fo_r.at[1], y_core).start()
    remote(FO, out_rows(c), fo_s, fo_r.at[2], sib).start()
    pltpu.make_async_copy(FO, out_rows(c), fo_r.at[0]).start()
    spread_on(other_place, fqb_s, fq_r, fqb_r)
    spread_on(value_place, fvb_s, fv_r, fvb_r)
    y_out = out_rows(2 * y1 + k)
    recv(y_out, fo_r.at[1])
    remote(y_out, y_out, fo_s, fo_r.at[2], sib).start()
    recv(RZSMALL.at[pl.ds(0, 3)], sz_r)
    total = PSMALL[z]
    for t in zs:
        total = total + RZSMALL[t]
    small_ref[...] = total

    recv(down_rows(c), fd_r.at[0])
    recv(odown.at[pl.ds(0, 256)], fd_r.at[2])
    recv(out_rows(c), fo_r.at[0])
    recv(oout.at[pl.ds(0, 64)], fo_r.at[2])
    recv(in_place(q, k), fi_r.at[0])
    recv(oin.at[:, :, rows_at(64 * k1, 64), :], fib_r)
    recv(other_place(q, k), fq_r.at[0])
    recv(oqkv.at[:, rows_at(64 * k1, 64), other_cols], fqb_r)
    recv(value_place(q, k), fv_r.at[0])
    recv(oqkv.at[:, rows_at(64 * k1, 64), value_cols], fvb_r)

    sent(GP.at[pl.ds(0, 7)], gp_s)
    four_sent(XB, xb_s)
    four_sent(COT, co_s)
    four_sent(NTB, nt_s)
    four_sent(GAL, ga_s)
    four_sent(SA, a_s)
    four_sent(SG, g_s)
    four_sent(SO, o_s)
    four_sent(SN, n_s)
    sent(WQKV.at[pl.ds(0, 256)], wqz_s)
    sent(WQKV.at[half(f, k)], wx_s.at[0])
    sent(WIN.at[half(f, k)], wx_s.at[1])
    sent(WIN.at[pl.ds(0, 256)], wiz_s)
    sent(WDOWN.at[pl.ds(0, 256)], wdz_s)
    sent(WQKV.at[pl.ds(0, 448)], wqb_s)
    sent(WIN.at[pl.ds(0, 448)], wib_s)
    sent(WDOWN.at[pl.ds(0, 384)], wdb_s)
    sent(value_of(ZQ, near), zv_s)
    sent(other_of(ZQ, near), zq_s)
    sent(ZQ.at[pl.ds(0, 4), :, value_cols], zve_s)
    sent(ZQ.at[pl.ds(0, 4), :, other_cols], zqe_s)
    sent(down_of(ZD, near), zd_s)
    sent(ZD.at[pl.ds(0, 2)], zde_s)
    sent(PSMALL.at[pl.ds(0, 3)], sz_s)
    sent(in_of(ZI, near), zi_s)
    sent(ZI.at[pl.ds(0, 4)], zie_s)

    @pl.when(middle)
    def _():
        sent(WDOWN.at[pl.ds(0, 256)], wdf_s)
        sent(WQKV.at[pl.ds(0, 256)], wqf_s)
        sent(WIN.at[pl.ds(0, 256)], wif_s)

    @pl.when(middle)
    def _():
        sent(WOUT.at[pl.ds(0, 128)], woz_s)

    @pl.when(at_end)
    def _():
        sent(WOUT.at[pl.ds(0, 64)], woz_s)

    sent(WOUT.at[pl.ds(0, 96)], wob_s)
    sent(ZO.at[near], zo_s)
    sent(ZO.at[pl.ds(0, 2)], zoe_s)
    sent(oout.at[pl.ds(0, 96)], fo_s)
    sent(DD.at[k1], sib_s.at[0])
    sent(DI.at[k1], sib_s.at[1])
    sent(DQ.at[k1, :, :, value_cols], sib_s.at[2])
    sent(DO.at[k1], sib_s.at[3])
    sent(DQ.at[k1, :, :, other_cols], sib_s.at[4])
    sent(odown.at[pl.ds(0, 384)], fd_s)
    sent(oin.at[:, pl.ds(0, 3), pl.ds(0, 64), :], fi_s)
    sent(oqkv.at[pl.ds(0, 3), pl.ds(0, 64), other_cols], fq_s)
    sent(oqkv.at[pl.ds(0, 3), pl.ds(0, 64), value_cols], fv_s)
    sent(oin.at[:, :, rows_at(64 * k, 64), :], fib_s)
    sent(oqkv.at[:, rows_at(64 * k, 64), other_cols], fqb_s)
    sent(oqkv.at[:, rows_at(64 * k, 64), value_cols], fvb_s)
    sent(RSMALL.at[pl.ds(0, 7)], sp_s)


def plane_shards(
    inputs, cotangent, w_query, w_key, w_value, w_out, w_in, w_down, gain_attn, gain_mlp, rel_bias, buckets
):
    vm = pltpu.VMEM
    dma = pltpu.SemaphoreType.DMA
    block = lambda kind: vm((TOKENS, WIDTH), kind)
    tokens = lambda width, kind: vm((512, width), kind)
    scratch = [
        block(BF), block(BF), vm((8, 128), F32), vm((1, 1024), jnp.int32),
        vm((3, 128, 1024), BF), vm((64, 768), BF), vm((8, 8, 128), F32),
        tokens(1024, BF), tokens(1024, BF), tokens(1024, BF), tokens(1024, BF), tokens(1024, BF),
        vm((1024, 768), BF), vm((256, 1024), BF), vm((1024, 1024), BF), vm((1024, 1024), BF),
        tokens(768, BF), vm((4, 512, 512), F32), vm((4, 512, 512), BF), vm((4, 128, 1024), F32),
        tokens(256, BF), tokens(1024, BF), tokens(1024, F32), tokens(1024, BF),
        tokens(256, BF), tokens(768, BF), vm((4, 512, 512), BF), vm((4, 128, 1024), F32),
        tokens(1024, BF), tokens(1024, BF), tokens(1024, BF), tokens(1024, BF),
        vm((3, 128, 1024), BF), vm((3, 128, 1024), BF), vm((3, 128, 1024), BF), vm((3, 128, 1024), BF),
        vm((2, 64, 1024), BF), vm((2, 64, 1024), BF), vm((2, 64, 1024), BF), vm((2, 64, 1024), BF),
        block(F32), block(F32), block(BF), block(BF),
        vm((2, 8, 64, 768), BF), vm((2, 4, 32, 1024), BF), vm((2, 8, 64, 1024), BF), vm((2, 4, 128, 1024), BF),
        vm((8, 64, 768), BF), vm((4, 32, 1024), BF), vm((8, 64, 1024), BF), vm((4, 128, 1024), BF),
        vm((8, 64, 768), BF), vm((4, 32, 1024), BF), vm((8, 64, 1024), BF), vm((4, 128, 1024), BF),
        vm((8, 64, 768), BF), vm((4, 32, 1024), BF), vm((8, 64, 1024), BF), vm((4, 128, 1024), BF),
        vm((2, 64, 768), BF), vm((32, 1024), BF), vm((2, 64, 1024), BF), vm((128, 1024), BF),
        vm((2, 64, 768), BF), vm((32, 1024), BF), vm((2, 4, 64, 256), BF), vm((128, 1024), BF),
        vm((3, 8, 128), F32), vm((8, 3, 8, 128), F32), vm((4, 8, 128), F32), vm((4, 8, 128), F32),
        dma((7,)), dma, dma, dma, dma((4,)), dma((2,)), dma, dma((4,)), dma((2,)), dma, dma((4,)), dma((2,)), dma, dma((4,)), dma((2,)),
        dma, dma, dma((2,)), dma, dma, dma((2,)), dma, dma, dma((2,)), dma, dma, dma((2,)),
        dma((2,)), dma((2,)), dma, dma, dma((8,)), dma, dma, dma, dma, dma((8,)), dma, dma,
        dma, dma, dma((4,)), dma, dma, dma, dma((4,)), dma, dma,
        dma((5,)), dma((5,)), dma((4,)), dma, dma, dma((4,)), dma, dma, dma, dma((4,)), dma, dma, dma, dma((4,)), dma,
        dma, dma, dma((4,)), dma, dma, dma, dma((4,)), dma,
        dma, dma, dma((4,)), dma, dma, dma, dma((4,)), dma, dma, dma((3,)), dma, dma, dma((4,)), dma, dma, dma((3,)), dma, dma, dma, dma,
    ]
    anywhere = pl.BlockSpec(memory_space=pl.ANY)
    in_vmem = pl.BlockSpec(memory_space=pltpu.VMEM)
    shape = jax.ShapeDtypeStruct
    output, grad_inputs, proj, out, hidden, down, small = pl.pallas_call(
        fused_layer,
        out_shape=(
            shape((1, TOKENS, WIDTH), BF),
            shape((1, TOKENS, WIDTH), BF),
            shape((4, 128, 768), BF),
            shape((128, 1024), BF),
            shape((4, 4, 128, 256), BF),
            shape((512, 1024), BF),
            shape((8, 128), F32),
        ),
        in_specs=[anywhere] * 8 + [in_vmem] * 4,
        out_specs=(in_vmem, in_vmem, anywhere, anywhere, anywhere, anywhere, in_vmem),
        scratch_shapes=scratch,
        compiler_params=pltpu.CompilerParams(
            collective_id=0, has_side_effects=True, vmem_limit_bytes=63 << 20
        ),
        cost_estimate=pl.CostEstimate(flops=11 * 10**9, bytes_accessed=16 * 2**20, transcendentals=3 * 2**20),
    )(inputs, cotangent, w_query, w_key, w_value, w_out, w_in, w_down, gain_attn[None], gain_mlp[None], rel_bias[None], buckets[None])
    return finish(output, grad_inputs, proj, out, hidden, down, small)


def finish_kernel(
    output, grad_inputs, proj, out, hidden, down, small,
    o_output, o_inputs, o_query, o_key, o_value, o_out, o_in, o_down, o_attn, o_mlp, o_bias,
    b_output, b_inputs, b_proj, b_out, b_hidden, b_down, b_small, w_proj, w_out, w_in, w_down, got, left,
):
    quarters = [pl.ds(128 * r, 128) for r in range(4)]
    downs = [pltpu.make_async_copy(down.at[rows], b_down.at[rows], got.at[6 + r]) for r, rows in enumerate(quarters)]
    moves = [
        pltpu.make_async_copy(proj, b_proj, got.at[0]),
        pltpu.make_async_copy(hidden, b_hidden, got.at[1]),
        pltpu.make_async_copy(out, b_out, got.at[2]),
        pltpu.make_async_copy(small, b_small, got.at[3]),
        pltpu.make_async_copy(output, b_output, got.at[4]),
        pltpu.make_async_copy(grad_inputs, b_inputs, got.at[5]),
    ]
    for move in downs + moves:
        move.start()
    sends = []

    def write(src, dst, slot):
        copy = pltpu.make_async_copy(src, dst, left.at[slot])
        copy.start()
        sends.append(copy)

    for r in range(4):
        downs[r].wait()
        rows = slice(128 * r, 128 * r + 128)
        w_down[rows, :] = b_down[rows, :].astype(F32)
        write(w_down.at[quarters[r]], o_down.at[quarters[r]], 7 + r)
    moves[0].wait()
    for w, place in enumerate((o_query, o_key, o_value)):
        for shard in range(8):
            z, x = shard // 2, shard % 2
            lanes = slice(256 * w + 64 * z, 256 * w + 64 * z + 64)
            parts = [b_proj[2 * x + y, :, lanes].astype(F32) for y in range(2)]
            w_proj[w, :, 128 * shard : 128 * shard + 128] = jnp.concatenate(parts, axis=1)
        write(w_proj.at[w], place, w)
    moves[1].wait()
    for r in range(4):
        rows = slice(32 * r, 32 * r + 32)
        for z in range(4):
            for q in range(4):
                w_in[rows, 256 * (4 * z + q) : 256 * (4 * z + q) + 256] = b_hidden[z, q, rows, :].astype(F32)
        write(w_in.at[pl.ds(32 * r, 32)], o_in.at[pl.ds(32 * r, 32)], 3 + r)
    moves[2].wait()
    w_out[...] = b_out[...].astype(F32)
    write(w_out, o_out, 11)
    moves[3].wait()
    o_attn[...] = b_small[0:1, :]
    o_mlp[...] = b_small[1:2, :]
    o_bias[...] = b_small[2:3, 0:64]
    moves[4].wait()
    write(b_output, o_output, 12)
    moves[5].wait()
    write(b_inputs, o_inputs, 13)
    for copy in sends:
        copy.wait()


def finish(output, grad_inputs, proj, out, hidden, down, small):
    shape = jax.ShapeDtypeStruct
    vm = pltpu.VMEM
    anywhere = pl.BlockSpec(memory_space=pl.ANY)
    in_vmem = pl.BlockSpec(memory_space=pltpu.VMEM)
    results = pl.pallas_call(
        finish_kernel,
        out_shape=(
            shape(output.shape, BF),
            shape(grad_inputs.shape, BF),
            shape((128, 1024), F32),
            shape((128, 1024), F32),
            shape((128, 1024), F32),
            shape((128, 1024), F32),
            shape((128, 4096), F32),
            shape((512, 1024), F32),
            shape((1, 128), F32),
            shape((1, 128), F32),
            shape((1, 64), F32),
        ),
        in_specs=[anywhere] * 7,
        out_specs=(anywhere,) * 8 + (in_vmem,) * 3,
        scratch_shapes=[
            vm(output.shape, BF), vm(grad_inputs.shape, BF), vm(proj.shape, BF), vm(out.shape, BF), vm(hidden.shape, BF), vm(down.shape, BF), vm(small.shape, F32),
            vm((3, 128, 1024), F32), vm((128, 1024), F32), vm((128, 4096), F32), vm((512, 1024), F32),
            pltpu.SemaphoreType.DMA((10,)), pltpu.SemaphoreType.DMA((14,)),
        ],
        compiler_params=pltpu.CompilerParams(vmem_limit_bytes=63 << 20),
        cost_estimate=pl.CostEstimate(flops=0, bytes_accessed=10 * 2**20, transcendentals=0),
    )(output, grad_inputs, proj, out, hidden, down, small)
    return results[:8] + (results[8].reshape(128), results[9].reshape(128), results[10].reshape(64))


def solution(mesh):
    placed = (
        P("fsdp", "ctx", None),
        P("fsdp", "ctx", None),
        P("fsdp", None),
        P("fsdp", None),
        P("fsdp", None),
        P("fsdp", None),
        P("fsdp", None),
        P("fsdp", None),
        P("fsdp"),
        P("fsdp"),
        P("fsdp"),
        P(),
    )
    by_planes = mesh.shape["ctx"] == 4 and mesh.shape["fsdp"] == 8
    return jax.shard_map(
        plane_shards if by_planes else shards,
        mesh=mesh,
        in_specs=placed,
        out_specs=(
            P("fsdp", "ctx", None),
            P("fsdp", "ctx", None),
            P("fsdp", None),
            P("fsdp", None),
            P("fsdp", None),
            P("fsdp", None),
            P("fsdp", None),
            P("fsdp", None),
            P("fsdp"),
            P("fsdp"),
            P("fsdp"),
        ),
        check_vma=False,
    )
```
